32 devices in a mesh: seq: 2 (over x), dp: 16 (over z, y, core).
Axes of the slice: x: 2, y: 2, z: 4, core: 2. Of those that a mesh axis runs over, the one named last changes fastest.
Arguments:
- latents: float32 [64, 256, 16], P('dp', 'seq'), may hold values from -6 to 6
- noise_target: float32 [64, 256, 16], P('dp', 'seq'), may hold values from -6 to 6
- pad_mask: int32 [64, 256], P('dp', 'seq'), may hold values from 0 to 1, as said below
- labels: int32 [64], P('dp'), may hold values from 0 to 1000
- timesteps: int32 [64], P('dp'), may hold values from 0 to 999
- embed_rows: float32 [1296, 1024], P(None, 'dp')
- first_embed: float32 [1296, 1024], P(None, 'dp'), may hold values from -24 to 24
- second_embed: float32 [1296, 1024], P(None, 'dp'), may hold values from 0.73728 to 11.79648
- class_table: float32 [1001, 1024], P(None, 'dp'), may hold values from -3 to 3
- first_table: float32 [1001, 1024], P(None, 'dp'), may hold values from -4 to 4
- second_table: float32 [1001, 1024], P(None, 'dp'), may hold values from 0.025 to 0.4
- qkv_weight: float32 [2, 1024, 3072], P(None, 'dp'), may hold values from -0.1875 to 0.1875
- first_qkv: float32 [2, 1024, 3072], P(None, 'dp'), may hold values from -14 to 14
- second_qkv: float32 [2, 1024, 3072], P(None, 'dp'), may hold values from 0.180224 to 2.94912
- proj_weight: float32 [2, 1024, 1024], P(None, 'dp'), may hold values from -0.75 to 0.75
- first_proj: float32 [2, 1024, 1024], P(None, 'dp'), may hold values from -14 to 14
- second_proj: float32 [2, 1024, 1024], P(None, 'dp'), may hold values from 0.180224 to 2.94912
- up_weight: float32 [2, 1024, 4096], P(None, 'dp'), may hold values from -0.1875 to 0.1875
- first_up: float32 [2, 1024, 4096], P(None, 'dp'), may hold values from -14 to 14
- second_up: float32 [2, 1024, 4096], P(None, 'dp'), may hold values from 0.180224 to 2.94912
- down_weight: float32 [2, 4096, 1024], P(None, 'dp'), may hold values from -0.09375 to 0.09375
- first_down: float32 [2, 4096, 1024], P(None, 'dp'), may hold values from -14 to 14
- second_down: float32 [2, 4096, 1024], P(None, 'dp'), may hold values from 0.180224 to 2.94912
- cond_weight: float32 [1024, 14336], P('dp'), may hold values from -0.1875 to 0.1875
- first_cond: float32 [1024, 14336], P('dp'), may hold values from -12 to 12
- second_cond: float32 [1024, 14336], P('dp'), may hold values from 0.1856 to 2.944
- head_weight: float32 [1024, 32], P('dp'), may hold values from -0.1875 to 0.1875
- first_head: float32 [1024, 32], P('dp'), may hold values from -224 to 224
- second_head: float32 [1024, 32], P('dp'), may hold values from 65.536 to 1032.192
- all_biases: float32 [35872], replicated, may hold values from -3 to 3
- first_bias: float32 [35872], replicated, may hold values from -24 to 24
- second_bias: float32 [35872], replicated, may hold values from 0.73728 to 11.79648
Outputs:
- loss_sum: float32 [], replicated
- loss_count: float32 [], replicated
- new_embed: float32 [1296, 1024], P(None, 'dp')
- new_first_embed: float32 [1296, 1024], P(None, 'dp')
- new_second_embed: float32 [1296, 1024], P(None, 'dp')
- new_table: float32 [1001, 1024], P(None, 'dp')
- new_first_table: float32 [1001, 1024], P(None, 'dp')
- new_second_table: float32 [1001, 1024], P(None, 'dp')
- new_qkv: float32 [2, 1024, 3072], P(None, 'dp')
- new_first_qkv: float32 [2, 1024, 3072], P(None, 'dp')
- new_second_qkv: float32 [2, 1024, 3072], P(None, 'dp')
- new_proj: float32 [2, 1024, 1024], P(None, 'dp')
- new_first_proj: float32 [2, 1024, 1024], P(None, 'dp')
- new_second_proj: float32 [2, 1024, 1024], P(None, 'dp')
- new_up: float32 [2, 1024, 4096], P(None, 'dp')
- new_first_up: float32 [2, 1024, 4096], P(None, 'dp')
- new_second_up: float32 [2, 1024, 4096], P(None, 'dp')
- new_down: float32 [2, 4096, 1024], P(None, 'dp')
- new_first_down: float32 [2, 4096, 1024], P(None, 'dp')
- new_second_down: float32 [2, 4096, 1024], P(None, 'dp')
- new_cond: float32 [1024, 14336], P('dp')
- new_first_cond: float32 [1024, 14336], P('dp')
- new_second_cond: float32 [1024, 14336], P('dp')
- new_head: float32 [1024, 32], P('dp')
- new_first_head: float32 [1024, 32], P('dp')
- new_second_head: float32 [1024, 32], P('dp')
- new_bias: float32 [35872], replicated
- new_first_bias: float32 [35872], replicated
- new_second_bias: float32 [35872], replicated
The draws below stay inside these ranges and needn't reach their ends.
Inputs may be any that keep to these rules, and one draw needn't show every extreme that they name: `pad_mask`: each image's real tokens form a prefix of 32 or more tokens; among each 4 consecutive images one is real in all 256 tokens.
All inputs are finite; a program needn't handle non-finite values.
Results may differ from the reference program's by a relative error of at most 0.017.
Values may be sent and summed in bfloat16 or wider, within the bound.
A program may use at most 448 MiB of HBM per device.

```python
import math
import jax
import jax.numpy as jnp
from jax import lax

D = 1024
HEADS = 16
HEAD_DIM = 64
FF = 4096
NCLASS = 1001
FREQ = 256
OUT_CH = 32
PATCH_IN = 16
GRID = 16
LAYERS = 2
STEP = 10
B_DEV = 4
TOKS = 256
NIMG = 64
NTOK = 16384
EMB = 1296
CW = 14336
NBIAS = 35872


def draw_pad_mask(key, part):
    key = jax.random.fold_in(key, 7)
    key_extra, key_full = jax.random.split(key)
    image_ids = jnp.arange(NIMG, dtype=jnp.int32)
    group_ids = image_ids // B_DEV
    group_total = NIMG // B_DEV
    base_len = TOKS // 8 + TOKS * 5 // 8 * group_ids // group_total
    extra_len = jax.random.randint(key_extra, (NIMG,), 0, TOKS // 4 + 1)
    full_pick = jax.random.randint(key_full, (group_total,), 0, B_DEV)
    is_full = image_ids % B_DEV == full_pick[group_ids]
    lengths = jnp.where(is_full, TOKS, jnp.minimum(base_len + extra_len, TOKS))
    return (jnp.arange(TOKS, dtype=jnp.int32)[None, :] < lengths[:, None]).astype(jnp.int32)


def draw_embed_rows(key, part):
    key = jax.random.fold_in(key, 3)
    row_ids = jnp.arange(EMB)
    row_scale = jnp.where(row_ids < PATCH_IN, PATCH_IN ** (-0.5), jnp.where(row_ids < PATCH_IN + FREQ, FREQ ** (-0.5), D ** (-0.5)))
    return jax.random.normal(key, (EMB, D), jnp.float32) * row_scale[:, None].astype(jnp.float32)


def place_ends(values, own_key, least, top_value):
    index_at = [jax.random.randint(jax.random.fold_in(own_key, axis), (), 0, length) for axis, length in enumerate(values.shape)]
    longest = values.shape.index(max(values.shape))
    next_to = index_at[:longest] + [(index_at[longest] + 1) % values.shape[longest]] + index_at[longest + 1:]
    return values.at[tuple(index_at)].set(least).at[tuple(next_to)].set(top_value)


def block_scale(stream_key, extent, cuts, low, largest):
    def one(dim, shards_of):
        heights = jax.random.uniform(jax.random.fold_in(jax.random.fold_in(stream_key, 6), dim), (shards_of,), jnp.float32, low / len(cuts), largest / len(cuts))
        return jnp.repeat(jnp.exp(heights), extent[dim] // shards_of).reshape((-1,) + (1,) * (len(extent) - dim - 1))

    loudness = one(*cuts[0])
    for cut in cuts[1:]:
        loudness = loudness * one(*cut)
    return loudness


def noise(rng, shape, scale, bound, shards=(), kind=jnp.bfloat16):
    drawn = scale * jax.random.normal(rng, shape, jnp.float32)
    if shards:
        drawn = drawn * block_scale(rng, shape, shards, -0.22, 0.18)
    return jnp.clip(drawn, -bound, bound).astype(kind)


def setup_inputs(seed: int = 0) -> dict:
    seeds = jax.random.split(jax.random.key(seed), 33)
    latents = noise(seeds[0], (NIMG, TOKS, PATCH_IN), 1.0, 6.0, ((0, 16), (1, 2)), jnp.float32)
    noise_target = noise(seeds[1], (NIMG, TOKS, PATCH_IN), 1.0, 6.0, ((0, 16), (1, 2)), jnp.float32)
    pad_mask = draw_pad_mask(jax.random.fold_in(seeds[32], 71), 0)
    labels = place_ends(jax.random.randint(seeds[3], (NIMG,), 0, NCLASS), jax.random.fold_in(seeds[3], 1), 0, NCLASS - 1).astype(jnp.int32)
    timesteps = place_ends(jax.random.randint(seeds[4], (NIMG,), 0, 1000), jax.random.fold_in(seeds[4], 1), 0, 999).astype(jnp.int32)
    embed_rows = draw_embed_rows(jax.random.fold_in(seeds[32], 71), 0)
    first_embed = noise(seeds[6], (EMB, D), (0.033 * NTOK ** 0.5), 24.0, ((1, 16),), jnp.float32)
    second_embed = jnp.clip(jnp.exp(math.log(11.79648) - 2.7725887 * jax.random.uniform(seeds[7], (EMB, D), jnp.float32) ** block_scale(seeds[7], (EMB, D), ((1, 16),), -0.2, 0.2)), 0.73728, 11.79648)
    class_table = noise(seeds[8], (NCLASS, D), 0.5, 3.0, ((1, 16),), jnp.float32)
    first_table = noise(seeds[9], (NCLASS, D), 0.8, 4.0, ((1, 16),), jnp.float32)
    second_table = jnp.clip(jnp.exp(math.log(0.4) - 2.7725887 * jax.random.uniform(seeds[10], (NCLASS, D), jnp.float32) ** block_scale(seeds[10], (NCLASS, D), ((1, 16),), -0.2, 0.2)), 0.025, 0.4)
    qkv_weight = noise(seeds[11], (LAYERS, D, 3 * D), D ** -0.5, 0.1875, ((1, 16),), jnp.float32)
    first_qkv = noise(seeds[12], (LAYERS, D, 3 * D), (0.017 * NTOK ** 0.5), 14.0, ((1, 16),), jnp.float32)
    second_qkv = jnp.clip(jnp.exp(math.log(2.94912) - 2.7950616 * jax.random.uniform(seeds[13], (LAYERS, D, 3 * D), jnp.float32) ** block_scale(seeds[13], (LAYERS, D, 3 * D), ((1, 16),), -0.2, 0.2)), 0.180224, 2.94912)
    proj_weight = noise(seeds[14], (LAYERS, D, D), (D // 16) ** -0.5, 0.75, ((1, 16),), jnp.float32)
    first_proj = noise(seeds[15], (LAYERS, D, D), (0.017 * NTOK ** 0.5), 14.0, ((1, 16),), jnp.float32)
    second_proj = jnp.clip(jnp.exp(math.log(2.94912) - 2.7950616 * jax.random.uniform(seeds[16], (LAYERS, D, D), jnp.float32) ** block_scale(seeds[16], (LAYERS, D, D), ((1, 16),), -0.2, 0.2)), 0.180224, 2.94912)
    up_weight = noise(seeds[17], (LAYERS, D, FF), D ** -0.5, 0.1875, ((1, 16),), jnp.float32)
    first_up = noise(seeds[18], (LAYERS, D, FF), (0.017 * NTOK ** 0.5), 14.0, ((1, 16),), jnp.float32)
    second_up = jnp.clip(jnp.exp(math.log(2.94912) - 2.7950616 * jax.random.uniform(seeds[19], (LAYERS, D, FF), jnp.float32) ** block_scale(seeds[19], (LAYERS, D, FF), ((1, 16),), -0.2, 0.2)), 0.180224, 2.94912)
    down_weight = noise(seeds[20], (LAYERS, FF, D), FF ** -0.5, 0.09375, ((1, 16),), jnp.float32)
    first_down = noise(seeds[21], (LAYERS, FF, D), (0.017 * NTOK ** 0.5), 14.0, ((1, 16),), jnp.float32)
    second_down = jnp.clip(jnp.exp(math.log(2.94912) - 2.7950616 * jax.random.uniform(seeds[22], (LAYERS, FF, D), jnp.float32) ** block_scale(seeds[22], (LAYERS, FF, D), ((1, 16),), -0.2, 0.2)), 0.180224, 2.94912)
    cond_weight = noise(seeds[23], (D, CW), D ** -0.5, 0.1875, ((0, 16),), jnp.float32)
    first_cond = noise(seeds[24], (D, CW), (0.26 * NIMG ** 0.5), 12.0, ((0, 16),), jnp.float32)
    second_cond = jnp.clip(jnp.exp(math.log(2.944) - 2.76393067 * jax.random.uniform(seeds[25], (D, CW), jnp.float32) ** block_scale(seeds[25], (D, CW), ((0, 16),), -0.2, 0.2)), 0.1856, 2.944)
    head_weight = noise(seeds[26], (D, OUT_CH), D ** -0.5, 0.1875, ((0, 16),), jnp.float32)
    first_head = noise(seeds[27], (D, OUT_CH), (0.3 * NTOK ** 0.5), 224.0, ((0, 16),), jnp.float32)
    second_head = jnp.clip(jnp.exp(math.log(1032.192) - 2.7568403 * jax.random.uniform(seeds[28], (D, OUT_CH), jnp.float32) ** block_scale(seeds[28], (D, OUT_CH), ((0, 16),), -0.2, 0.2)), 65.536, 1032.192)
    all_biases = noise(seeds[29], (NBIAS,), 0.2, 3.0, (), jnp.float32)
    first_bias = noise(seeds[30], (NBIAS,), (0.033 * NTOK ** 0.5), 24.0, (), jnp.float32)
    second_bias = jnp.clip(jnp.exp(jax.random.uniform(seeds[31], (NBIAS,), jnp.float32, math.log(0.73728), math.log(11.79648))), 0.73728, 11.79648)
    return dict(latents=latents, noise_target=noise_target, pad_mask=pad_mask, labels=labels, timesteps=timesteps, embed_rows=embed_rows, first_embed=first_embed, second_embed=second_embed, class_table=class_table, first_table=first_table, second_table=second_table, qkv_weight=qkv_weight, first_qkv=first_qkv, second_qkv=second_qkv, proj_weight=proj_weight, first_proj=first_proj, second_proj=second_proj, up_weight=up_weight, first_up=first_up, second_up=second_up, down_weight=down_weight, first_down=first_down, second_down=second_down, cond_weight=cond_weight, first_cond=first_cond, second_cond=second_cond, head_weight=head_weight, first_head=first_head, second_head=second_head, all_biases=all_biases, first_bias=first_bias, second_bias=second_bias)


@jax.custom_vjp
def low(v):
    return lax.optimization_barrier(v.astype(jnp.bfloat16)).astype(jnp.float32)

@jax.custom_vjp
def low_back(v):
    return v

def low_keep(v):
    return (low(v), None)

def low_pass(kept, grad):
    return (grad,)

def back_keep(v):
    return (v, None)

def back_low(kept, grad):
    return (low(grad),)
low.defvjp(low_keep, low_pass)
low_back.defvjp(back_keep, back_low)
BETA_ONE = 0.9
BETA_TWO = 0.999
EPSILON = 1e-08
DECAY = 0.01
RATE_MATRIX = 0.06
RATE_TABLE = 0.4
RATE_BIAS = 0.2

def matmul(left, right):
    return jnp.dot(left, right, precision=lax.Precision.HIGHEST)

def layer_norm(stream):
    row_mean = lax.optimization_barrier(jnp.mean(stream, axis=-1, keepdims=True))
    centered = stream - row_mean
    variance = lax.optimization_barrier(jnp.mean(centered * centered, axis=-1, keepdims=True))
    return centered * lax.rsqrt(variance + 1e-06)

def modulate(stream, shift_by, scale_by):
    return layer_norm(stream) * (1.0 + scale_by[:, None, :]) + shift_by[:, None, :]

def position_table(position_ids, feature_width, grid_side):
    quarter_width = feature_width // 4
    omegas = 1.0 / 10000.0 ** (jnp.arange(quarter_width, dtype=jnp.float32) / quarter_width)
    col_angle = (position_ids % grid_side).astype(jnp.float32)[:, None] * omegas[None, :]
    row_angle = (position_ids // grid_side).astype(jnp.float32)[:, None] * omegas[None, :]
    return jnp.concatenate([jnp.sin(col_angle), jnp.cos(col_angle), jnp.sin(row_angle), jnp.cos(row_angle)], axis=1)

def time_features(timesteps, feature_width):
    half_width = feature_width // 2
    frequencies = jnp.exp(-math.log(10000.0) * jnp.arange(half_width, dtype=jnp.float32) / half_width)
    angles = timesteps.astype(jnp.float32)[:, None] * frequencies[None, :]
    return jnp.concatenate([jnp.cos(angles), jnp.sin(angles)], axis=1)

def group_loss(params, latents, noise_target, pad_mask, labels, timesteps):
    embed_rows, class_table, qkv_weight, proj_weight, up_weight, down_weight, cond_weight, head_weight, all_biases = params
    images = latents.shape[0]
    cond_cols = cond_weight.shape[1]
    position = position_table(jnp.arange(TOKS, dtype=jnp.int32), D, GRID)
    flat_in = low(latents.reshape(images * TOKS, PATCH_IN))
    stream = low_back(matmul(flat_in, low(embed_rows[:PATCH_IN])) + all_biases[:D])
    stream = stream.reshape(images, TOKS, D) + position[None]
    features = low(time_features(timesteps, FREQ))
    time_pre = low_back(matmul(features, low(embed_rows[PATCH_IN:PATCH_IN + FREQ])) + all_biases[D:2 * D])
    time_hidden = low(jax.nn.silu(time_pre))
    time_embed = low_back(matmul(time_hidden, low(embed_rows[PATCH_IN + FREQ:])) + all_biases[2 * D:3 * D])
    onehot = (labels[:, None] == jnp.arange(NCLASS, dtype=jnp.int32)[None, :]).astype(jnp.float32)
    condition = time_embed + matmul(onehot, low(class_table))
    modulation = low_back(matmul(low(jax.nn.silu(condition)), low(cond_weight)) + all_biases[3 * D:3 * D + cond_cols])
    valid_keys = pad_mask[:, None, None, :] > 0
    scale_qk = HEAD_DIM ** (-0.5)
    for layer_at in range(LAYERS):
        bias_base = 3 * D + cond_cols + layer_at * (5 * D + FF)
        pieces = [modulation[:, (6 * layer_at + piece) * D:(6 * layer_at + piece + 1) * D] for piece in range(6)]
        shift_one, scale_one, gate_one, shift_two, scale_two, gate_two = pieces
        a_one = low(modulate(stream, shift_one, scale_one)).reshape(images * TOKS, D)
        qkv_all = low(low_back(matmul(a_one, low(qkv_weight[layer_at])) + all_biases[bias_base:bias_base + 3 * D]))
        qkv_all = qkv_all.reshape(images, TOKS, 3, HEADS, HEAD_DIM)
        queries, key_rows, value_rows = (qkv_all[:, :, 0], qkv_all[:, :, 1], qkv_all[:, :, 2])
        scores = low_back(scale_qk * jnp.einsum('bqhd,bkhd->bhqk', queries, key_rows, precision=lax.Precision.HIGHEST))
        attn_probs = jax.nn.softmax(jnp.where(valid_keys, scores, -1000000000.0), axis=-1)
        heads_out = jnp.einsum('bhqk,bkhd->bqhd', low(attn_probs), value_rows, precision=lax.Precision.HIGHEST)
        heads_out = low(low_back(heads_out)).reshape(images * TOKS, D)
        attn_out = low_back(matmul(heads_out, low(proj_weight[layer_at])) + all_biases[bias_base + 3 * D:bias_base + 4 * D])
        stream = stream + gate_one[:, None, :] * attn_out.reshape(images, TOKS, D)
        a_two = low(modulate(stream, shift_two, scale_two)).reshape(images * TOKS, D)
        up_pre = low_back(matmul(a_two, low(up_weight[layer_at])) + all_biases[bias_base + 4 * D:bias_base + 4 * D + FF])
        activated = low(jax.nn.gelu(up_pre, approximate=True))
        down_out = low_back(matmul(activated, low(down_weight[layer_at])) + all_biases[bias_base + 4 * D + FF:bias_base + 5 * D + FF])
        stream = stream + gate_two[:, None, :] * down_out.reshape(images, TOKS, D)
    final_at = 6 * LAYERS * D
    a_final = low(modulate(stream, modulation[:, final_at:final_at + D], modulation[:, final_at + D:final_at + 2 * D]))
    head_out = low_back(matmul(a_final.reshape(images * TOKS, D), low(head_weight)) + all_biases[NBIAS - OUT_CH:])
    predicted = head_out.reshape(images, TOKS, 4, 2, OUT_CH // 8)[:, :, :, 0, :].reshape(images, TOKS, PATCH_IN)
    errors = predicted - noise_target
    return jnp.sum(pad_mask.astype(jnp.float32)[:, :, None] * errors * errors)

def adamw(weight, gradient, first, second, rate):
    first_new = BETA_ONE * first + (1.0 - BETA_ONE) * gradient
    second_new = BETA_TWO * second + (1.0 - BETA_TWO) * gradient * gradient
    first_hat = first_new / (1.0 - BETA_ONE ** STEP)
    second_hat = second_new / (1.0 - BETA_TWO ** STEP)
    return (weight - rate * (first_hat / (jnp.sqrt(second_hat) + EPSILON) + DECAY * weight), first_new, second_new)

def reference(latents, noise_target, pad_mask, labels, timesteps, embed_rows, first_embed, second_embed, class_table, first_table, second_table, qkv_weight, first_qkv, second_qkv, proj_weight, first_proj, second_proj, up_weight, first_up, second_up, down_weight, first_down, second_down, cond_weight, first_cond, second_cond, head_weight, first_head, second_head, all_biases, first_bias, second_bias):
    params = (embed_rows, class_table, qkv_weight, proj_weight, up_weight, down_weight, cond_weight, head_weight, all_biases)
    group_size = max(1, min(NIMG, 4096 // TOKS))
    groups = NIMG // group_size

    def split_groups(array):
        return array.reshape((groups, group_size) + array.shape[1:])
    blocks = (split_groups(latents), split_groups(noise_target), split_groups(pad_mask), split_groups(labels), split_groups(timesteps))

    def accumulate(running, group_in):
        latent_g, noise_g, mask_g, label_g, time_g = group_in
        loss_g, back_fn = jax.vjp(lambda weights_in: group_loss(weights_in, latent_g, noise_g, mask_g, label_g, time_g), params)
        gradients = back_fn(jnp.ones_like(loss_g))[0]
        return ((running[0] + loss_g, jax.tree.map(jnp.add, running[1], gradients)), None)
    start = (jnp.zeros((), jnp.float32), jax.tree.map(jnp.zeros_like, params))
    (loss_sum, gradients), _ = lax.scan(accumulate, start, blocks)
    loss_count = PATCH_IN * jnp.sum(pad_mask.astype(jnp.float32))
    g_embed, g_table, g_qkv, g_proj, g_up, g_down, g_cond, g_head, g_bias = gradients
    new_embed, new_first_embed, new_second_embed = adamw(embed_rows, g_embed, first_embed, second_embed, RATE_MATRIX)
    new_table, new_first_table, new_second_table = adamw(class_table, g_table, first_table, second_table, RATE_TABLE)
    new_qkv, new_first_qkv, new_second_qkv = adamw(qkv_weight, g_qkv, first_qkv, second_qkv, RATE_MATRIX)
    new_proj, new_first_proj, new_second_proj = adamw(proj_weight, g_proj, first_proj, second_proj, RATE_MATRIX)
    new_up, new_first_up, new_second_up = adamw(up_weight, g_up, first_up, second_up, RATE_MATRIX)
    new_down, new_first_down, new_second_down = adamw(down_weight, g_down, first_down, second_down, RATE_MATRIX)
    new_cond, new_first_cond, new_second_cond = adamw(cond_weight, g_cond, first_cond, second_cond, RATE_MATRIX)
    new_head, new_first_head, new_second_head = adamw(head_weight, g_head, first_head, second_head, RATE_MATRIX)
    new_bias, new_first_bias, new_second_bias = adamw(all_biases, g_bias, first_bias, second_bias, RATE_BIAS)
    return (loss_sum, loss_count, new_embed, new_first_embed, new_second_embed, new_table, new_first_table, new_second_table, new_qkv, new_first_qkv, new_second_qkv, new_proj, new_first_proj, new_second_proj, new_up, new_first_up, new_second_up, new_down, new_first_down, new_second_down, new_cond, new_first_cond, new_second_cond, new_head, new_first_head, new_second_head, new_bias, new_first_bias, new_second_bias)
```

```python
import math

import jax
import jax.numpy as jnp
from jax import lax
from jax.sharding import PartitionSpec as P

D = 1024
HEADS = 16
HEAD_DIM = 64
FF = 4096
NCLASS = 1001
FREQ = 256
OUT_CH = 32
PATCH_IN = 16
GRID = 16
LAYERS = 2
STEP = 10
NBIAS = 35872


BETA_ONE = 0.9
BETA_TWO = 0.999
EPSILON = 1e-08
DECAY = 0.01
RATE_MATRIX = 0.06
RATE_TABLE = 0.4
RATE_BIAS = 0.2


def matdot(left, right):
    return jnp.dot(left, right, preferred_element_type=jnp.float32)


def layer_norm(stream):
    row_mean = jnp.mean(stream, axis=-1, keepdims=True)
    centered = stream - row_mean
    variance = jnp.mean(centered * centered, axis=-1, keepdims=True)
    return centered * lax.rsqrt(variance + 1e-06)


def modulate(stream, shift_by, scale_by):
    return layer_norm(stream) * (1.0 + scale_by[:, None, :]) + shift_by[:, None, :]


def position_table(position_ids, feature_width, grid_side):
    quarter_width = feature_width // 4
    omegas = 1.0 / 10000.0 ** (jnp.arange(quarter_width, dtype=jnp.float32) / quarter_width)
    col_angle = (position_ids % grid_side).astype(jnp.float32)[:, None] * omegas[None, :]
    row_angle = (position_ids // grid_side).astype(jnp.float32)[:, None] * omegas[None, :]
    return jnp.concatenate(
        [jnp.sin(col_angle), jnp.cos(col_angle), jnp.sin(row_angle), jnp.cos(row_angle)], axis=1
    )


def time_features(timesteps, feature_width):
    half_width = feature_width // 2
    frequencies = jnp.exp(
        -math.log(10000.0) * jnp.arange(half_width, dtype=jnp.float32) / half_width
    )
    angles = timesteps.astype(jnp.float32)[:, None] * frequencies[None, :]
    return jnp.concatenate([jnp.cos(angles), jnp.sin(angles)], axis=1)


def column_sum(grad_bf):
    return jnp.sum(grad_bf.astype(jnp.float32), axis=0)


def split_six(modul):
    return [modul[:, piece * D : (piece + 1) * D] for piece in range(6)]


def layer_forward(stream, modul, weight_set, bias_part, pad_mask):
    w_qkv, w_proj, w_up, w_down = weight_set
    images, tok_rows, _ = stream.shape
    shift_one, scale_one, gate_one, shift_two, scale_two, gate_two = split_six(modul)
    a_one = (
        modulate(stream, shift_one, scale_one).astype(jnp.bfloat16).reshape(images * tok_rows, D)
    )
    qkv_all = (matdot(a_one, w_qkv) + bias_part[: 3 * D]).astype(jnp.bfloat16)
    heads_in = qkv_all.reshape(images, tok_rows, 3, HEADS, HEAD_DIM)
    queries, key_rows, value_rows = (heads_in[:, :, 0], heads_in[:, :, 1], heads_in[:, :, 2])
    scores = jnp.einsum(
        "bqhd,bkhd->bhqk", queries, key_rows, preferred_element_type=jnp.float32
    ) * HEAD_DIM ** (-0.5)
    attn_probs = jax.nn.softmax(
        jnp.where(pad_mask[:, None, None, :] > 0, scores, -1000000000.0), axis=-1
    )
    heads_out = jnp.einsum(
        "bhqk,bkhd->bqhd",
        attn_probs.astype(jnp.bfloat16),
        value_rows,
        preferred_element_type=jnp.float32,
    )
    merged = heads_out.astype(jnp.bfloat16).reshape(images * tok_rows, D)
    attn_out = (matdot(merged, w_proj) + bias_part[3 * D : 4 * D]).reshape(images, tok_rows, D)
    stream_one = stream + gate_one[:, None, :] * attn_out
    a_two = (
        modulate(stream_one, shift_two, scale_two)
        .astype(jnp.bfloat16)
        .reshape(images * tok_rows, D)
    )
    up_pre = matdot(a_two, w_up) + bias_part[4 * D : 4 * D + FF]
    activated = jax.nn.gelu(up_pre, approximate=True).astype(jnp.bfloat16)
    down_out = (matdot(activated, w_down) + bias_part[4 * D + FF :]).reshape(images, tok_rows, D)
    stream_two = stream_one + gate_two[:, None, :] * down_out
    saved = (
        a_one,
        queries,
        key_rows,
        value_rows,
        attn_probs,
        merged,
        attn_out,
        stream_one,
        a_two,
        up_pre,
        activated,
        down_out,
    )
    return (stream_two, saved)


def layer_backward(grad_in, stream, modul, weight_set, saved):
    w_qkv, w_proj, w_up, w_down = weight_set
    (
        a_one,
        queries,
        key_rows,
        value_rows,
        attn_probs,
        merged,
        attn_out,
        stream_one,
        a_two,
        up_pre,
        activated,
        down_out,
    ) = saved
    images, tok_rows, _ = stream.shape
    shift_one, scale_one, gate_one, shift_two, scale_two, gate_two = split_six(modul)
    d_gate_two = jnp.sum(grad_in * down_out, axis=1)
    d_down = (grad_in * gate_two[:, None, :]).astype(jnp.bfloat16).reshape(images * tok_rows, D)
    s_down = reduce_rows(matdot(activated.T, d_down))
    d_activated = matdot(d_down, w_down.T)
    _, gelu_back = jax.vjp(lambda inner: jax.nn.gelu(inner, approximate=True), up_pre)
    d_up = gelu_back(d_activated)[0].astype(jnp.bfloat16)
    s_up = reduce_rows(matdot(a_two.T, d_up))
    d_a_two = matdot(d_up, w_up.T).reshape(images, tok_rows, D)
    _, mod_back_two = jax.vjp(modulate, stream_one, shift_two, scale_two)
    d_stream_one, d_shift_two, d_scale_two = mod_back_two(d_a_two)
    d_stream_one = d_stream_one + grad_in
    d_gate_one = jnp.sum(d_stream_one * attn_out, axis=1)
    d_attn = (
        (d_stream_one * gate_one[:, None, :]).astype(jnp.bfloat16).reshape(images * tok_rows, D)
    )
    s_proj = reduce_rows(matdot(merged.T, d_attn))
    d_heads = matdot(d_attn, w_proj.T).astype(jnp.bfloat16)
    d_heads = d_heads.reshape(images, tok_rows, HEADS, HEAD_DIM)
    d_values = jnp.einsum(
        "bhqk,bqhd->bkhd",
        attn_probs.astype(jnp.bfloat16),
        d_heads,
        preferred_element_type=jnp.float32,
    )
    d_probs = jnp.einsum("bqhd,bkhd->bhqk", d_heads, value_rows, preferred_element_type=jnp.float32)
    d_scores = attn_probs * (d_probs - jnp.sum(attn_probs * d_probs, axis=-1, keepdims=True))
    d_scores = d_scores.astype(jnp.bfloat16)
    d_queries = jnp.einsum(
        "bhqk,bkhd->bqhd", d_scores, key_rows, preferred_element_type=jnp.float32
    ) * HEAD_DIM ** (-0.5)
    d_keys = jnp.einsum(
        "bhqk,bqhd->bkhd", d_scores, queries, preferred_element_type=jnp.float32
    ) * HEAD_DIM ** (-0.5)
    d_qkv = jnp.stack([d_queries, d_keys, d_values], axis=2).astype(jnp.bfloat16)
    d_qkv = d_qkv.reshape(images * tok_rows, 3 * D)
    s_qkv = reduce_rows(matdot(a_one.T, d_qkv))
    d_a_one = matdot(d_qkv, w_qkv.T).reshape(images, tok_rows, D)
    _, mod_back_one = jax.vjp(modulate, stream, shift_one, scale_one)
    d_stream, d_shift_one, d_scale_one = mod_back_one(d_a_one)
    d_stream = d_stream + d_stream_one
    d_modul = jnp.concatenate(
        [d_shift_one, d_scale_one, d_gate_one, d_shift_two, d_scale_two, d_gate_two], axis=1
    )
    d_bias = jnp.concatenate(
        [column_sum(d_qkv), column_sum(d_attn), column_sum(d_up), column_sum(d_down)]
    )
    return (d_stream, d_modul, (s_qkv, s_proj, s_up, s_down), d_bias)


def gather_rows(shard):
    return lax.all_gather(shard.astype(jnp.bfloat16), "dp", axis=0, tiled=True)


def reduce_rows(partial):
    owned = lax.psum_scatter(
        partial.astype(jnp.bfloat16), "dp", scatter_dimension=0, tiled=True
    )
    return lax.psum(owned, "seq").astype(jnp.float32)


def adamw(weight, gradient, first, second, rate):
    first_new = BETA_ONE * first + (1.0 - BETA_ONE) * gradient
    second_new = BETA_TWO * second + (1.0 - BETA_TWO) * gradient * gradient
    first_hat = first_new / (1.0 - BETA_ONE**STEP)
    second_hat = second_new / (1.0 - BETA_TWO**STEP)
    return (
        weight - rate * (first_hat / (jnp.sqrt(second_hat) + EPSILON) + DECAY * weight),
        first_new,
        second_new,
    )


def body(
    latents,
    noise_target,
    pad_mask,
    labels,
    timesteps,
    embed_rows,
    first_embed,
    second_embed,
    class_table,
    first_table,
    second_table,
    qkv_weight,
    first_qkv,
    second_qkv,
    proj_weight,
    first_proj,
    second_proj,
    up_weight,
    first_up,
    second_up,
    down_weight,
    first_down,
    second_down,
    cond_weight,
    first_cond,
    second_cond,
    head_weight,
    first_head,
    second_head,
    all_biases,
    first_bias,
    second_bias,
):
    seq_parts = lax.axis_size("seq")
    dp_parts = lax.axis_size("dp")
    seq_at = lax.axis_index("seq")
    dp_at = lax.axis_index("dp")
    group, _, _ = latents.shape
    images = group // seq_parts
    everyone = group * dp_parts
    own_cols = embed_rows.shape[1]
    cond_cols = cond_weight.shape[1]
    bias_base = 3 * D + cond_cols
    packed = jnp.concatenate(
        [latents, noise_target, pad_mask.astype(jnp.float32)[:, :, None]], axis=2
    )
    packed = lax.all_to_all(packed, "seq", split_axis=0, concat_axis=1, tiled=True)
    tok_rows = packed.shape[1]
    latents, noise_target, keep_rows = (
        packed[:, :, :PATCH_IN],
        packed[:, :, PATCH_IN : 2 * PATCH_IN],
        packed[:, :, 2 * PATCH_IN],
    )
    ids = lax.all_gather(jnp.stack([labels, timesteps]), "dp", axis=1, tiled=True)
    small = jnp.concatenate(
        [embed_rows[: PATCH_IN + FREQ], head_weight.T], axis=0
    ).astype(jnp.bfloat16)
    small = lax.all_gather(small, "dp", axis=1, tiled=True)
    patch_part = small[:PATCH_IN]
    freq_part = small[PATCH_IN : PATCH_IN + FREQ]
    head_rows = small[PATCH_IN + FREQ :]
    time_own = embed_rows[PATCH_IN + FREQ :].astype(jnp.bfloat16)
    cond_own = cond_weight.astype(jnp.bfloat16)

    features = time_features(ids[1], FREQ).astype(jnp.bfloat16)
    time_pre = matdot(features, freq_part) + all_biases[D : 2 * D]
    time_hidden = jax.nn.silu(time_pre).astype(jnp.bfloat16)
    second_bias_own = lax.dynamic_slice(all_biases, (2 * D + dp_at * own_cols,), (own_cols,))
    onehot = (ids[0][:, None] == jnp.arange(NCLASS, dtype=jnp.int32)[None, :]).astype(jnp.float32)
    condition = (
        matdot(time_hidden, time_own)
        + second_bias_own
        + matdot(onehot.astype(jnp.bfloat16), class_table.astype(jnp.bfloat16))
    )
    cond_act = jax.nn.silu(condition).astype(jnp.bfloat16)
    plane_act = lax.dynamic_index_in_dim(
        cond_act.reshape(dp_parts, seq_parts, images, own_cols), seq_at, 1, keepdims=False
    ).reshape(dp_parts * images, own_cols)
    modulation = lax.psum_scatter(
        matdot(plane_act, cond_own), "dp", scatter_dimension=0, tiled=True
    )
    modulation = modulation + all_biases[3 * D : bias_base]

    position = position_table(jnp.arange(tok_rows, dtype=jnp.int32), D, GRID)
    flat_in = latents.astype(jnp.bfloat16).reshape(images * tok_rows, PATCH_IN)
    stream = (matdot(flat_in, patch_part) + all_biases[:D]).reshape(images, tok_rows, D) + position[
        None
    ]
    layer_bias = [
        all_biases[bias_base + at * (5 * D + FF) : bias_base + (at + 1) * (5 * D + FF)]
        for at in range(LAYERS)
    ]
    inputs_kept = []
    weights_kept = []
    saved_kept = []
    for at in range(LAYERS):
        weight_set = (
            gather_rows(qkv_weight[at]),
            gather_rows(proj_weight[at]),
            gather_rows(up_weight[at]),
            gather_rows(down_weight[at]),
        )
        weights_kept.append(weight_set)
        inputs_kept.append(stream)
        stream, saved = layer_forward(
            stream,
            modulation[:, 6 * at * D : 6 * (at + 1) * D],
            weight_set,
            layer_bias[at],
            keep_rows,
        )
        saved_kept.append(saved)
    final_at = 6 * LAYERS * D
    final_shift = modulation[:, final_at : final_at + D]
    final_scale = modulation[:, final_at + D : final_at + 2 * D]
    moved, final_back = jax.vjp(modulate, stream, final_shift, final_scale)
    a_final = moved.astype(jnp.bfloat16).reshape(images * tok_rows, D)
    head_out = lax.dot_general(
        a_final, head_rows, (((1,), (1,)), ((), ())), preferred_element_type=jnp.float32
    ) + all_biases[NBIAS - OUT_CH :]
    split_out = head_out.reshape(images, tok_rows, 4, 2, OUT_CH // 8)
    predicted = split_out[:, :, :, 0, :].reshape(images, tok_rows, PATCH_IN)
    errors = predicted - noise_target
    loss_part = jnp.sum(keep_rows[:, :, None] * errors * errors)
    count_part = PATCH_IN * jnp.sum(keep_rows)
    d_pred = (2.0 * keep_rows[:, :, None] * errors).reshape(images, tok_rows, 4, 1, OUT_CH // 8)
    d_head = (
        jnp.concatenate([d_pred, jnp.zeros_like(d_pred)], axis=3)
        .reshape(images * tok_rows, OUT_CH)
        .astype(jnp.bfloat16)
    )
    g_head = matdot(a_final.T, d_head)
    d_a_final = matdot(d_head, head_rows).reshape(images, tok_rows, D)
    d_stream, d_final_shift, d_final_scale = final_back(d_a_final)
    layer_sums = [None] * LAYERS
    layer_bias_grads = [None] * LAYERS
    modul_grads = [None] * LAYERS
    for at in reversed(range(LAYERS)):
        d_stream, modul_grads[at], layer_sums[at], layer_bias_grads[at] = layer_backward(
            d_stream,
            inputs_kept[at],
            modulation[:, 6 * at * D : 6 * (at + 1) * D],
            weights_kept[at],
            saved_kept[at],
        )
    d_mod_own = jnp.concatenate(modul_grads + [d_final_shift, d_final_scale], axis=1).astype(
        jnp.bfloat16
    )
    d_modulation = lax.all_gather(d_mod_own, ("dp", "seq"), axis=0, tiled=True)
    d_cond_act = lax.dot_general(
        d_modulation, cond_own, (((1,), (1,)), ((), ())), preferred_element_type=jnp.float32
    )
    _, silu_back = jax.vjp(jax.nn.silu, condition)
    d_condition = silu_back(d_cond_act)[0]
    d_time = d_condition.astype(jnp.bfloat16)
    d_time_hidden = lax.psum_scatter(
        lax.dot_general(
            d_time, time_own, (((1,), (1,)), ((), ())), preferred_element_type=jnp.float32
        ),
        "dp",
        scatter_dimension=1,
        tiled=True,
    )
    time_pre_own = lax.dynamic_slice(time_pre, (0, dp_at * own_cols), (everyone, own_cols))
    _, time_back = jax.vjp(jax.nn.silu, time_pre_own)
    d_time_pre = time_back(d_time_hidden)[0].astype(jnp.bfloat16)
    d_patch = d_stream.astype(jnp.bfloat16).reshape(images * tok_rows, D)
    g_patch = matdot(flat_in.T, d_patch)
    s_cond = matdot(cond_act.T, d_modulation)
    s_table = jnp.dot(onehot.T, d_condition, precision=lax.Precision.HIGHEST)
    g_time = matdot(time_hidden.T, d_time)
    g_freq = matdot(features.T, d_time_pre)

    lead_flag = (seq_at == 0).astype(jnp.float32)
    own_place = dp_at * own_cols
    first_time_bias = lax.dynamic_update_slice(
        jnp.zeros((D,), jnp.float32), column_sum(d_time_pre) * lead_flag, (own_place,)
    )
    second_time_bias = lax.dynamic_update_slice(
        jnp.zeros((D,), jnp.float32), column_sum(d_time) * lead_flag, (own_place,)
    )
    bias_grad = jnp.concatenate(
        [column_sum(d_patch), first_time_bias, second_time_bias, column_sum(d_mod_own)]
        + layer_bias_grads
        + [column_sum(d_head)]
    )
    bias_grad, g_patch, g_head, loss_sum, loss_count = lax.psum(
        (bias_grad, g_patch, g_head, loss_part, count_part), ("seq", "dp")
    )
    s_patch = lax.dynamic_slice(g_patch, (0, own_place), (PATCH_IN, own_cols))
    s_head = lax.dynamic_slice(g_head, (own_place, 0), (own_cols, OUT_CH))
    s_embed = jnp.concatenate([s_patch, g_freq, g_time], axis=0)
    s_qkv = jnp.stack([layer_sums[at][0] for at in range(LAYERS)])
    s_proj = jnp.stack([layer_sums[at][1] for at in range(LAYERS)])
    s_up = jnp.stack([layer_sums[at][2] for at in range(LAYERS)])
    s_down = jnp.stack([layer_sums[at][3] for at in range(LAYERS)])
    new_embed, new_first_embed, new_second_embed = adamw(
        embed_rows, s_embed, first_embed, second_embed, RATE_MATRIX
    )
    new_table, new_first_table, new_second_table = adamw(
        class_table, s_table, first_table, second_table, RATE_TABLE
    )
    new_qkv, new_first_qkv, new_second_qkv = adamw(
        qkv_weight, s_qkv, first_qkv, second_qkv, RATE_MATRIX
    )
    new_proj, new_first_proj, new_second_proj = adamw(
        proj_weight, s_proj, first_proj, second_proj, RATE_MATRIX
    )
    new_up, new_first_up, new_second_up = adamw(up_weight, s_up, first_up, second_up, RATE_MATRIX)
    new_down, new_first_down, new_second_down = adamw(
        down_weight, s_down, first_down, second_down, RATE_MATRIX
    )
    new_cond, new_first_cond, new_second_cond = adamw(
        cond_weight, s_cond, first_cond, second_cond, RATE_MATRIX
    )
    new_head, new_first_head, new_second_head = adamw(
        head_weight, s_head, first_head, second_head, RATE_MATRIX
    )
    new_bias, new_first_bias, new_second_bias = adamw(
        all_biases, bias_grad, first_bias, second_bias, RATE_BIAS
    )
    return (
        loss_sum,
        loss_count,
        new_embed,
        new_first_embed,
        new_second_embed,
        new_table,
        new_first_table,
        new_second_table,
        new_qkv,
        new_first_qkv,
        new_second_qkv,
        new_proj,
        new_first_proj,
        new_second_proj,
        new_up,
        new_first_up,
        new_second_up,
        new_down,
        new_first_down,
        new_second_down,
        new_cond,
        new_first_cond,
        new_second_cond,
        new_head,
        new_first_head,
        new_second_head,
        new_bias,
        new_first_bias,
        new_second_bias,
    )


def solution(mesh):
    placed = (
        P("dp", "seq", None),
        P("dp", "seq", None),
        P("dp", "seq"),
        P("dp"),
        P("dp"),
        P(None, "dp"),
        P(None, "dp"),
        P(None, "dp"),
        P(None, "dp"),
        P(None, "dp"),
        P(None, "dp"),
        P(None, "dp", None),
        P(None, "dp", None),
        P(None, "dp", None),
        P(None, "dp", None),
        P(None, "dp", None),
        P(None, "dp", None),
        P(None, "dp", None),
        P(None, "dp", None),
        P(None, "dp", None),
        P(None, "dp", None),
        P(None, "dp", None),
        P(None, "dp", None),
        P("dp", None),
        P("dp", None),
        P("dp", None),
        P("dp", None),
        P("dp", None),
        P("dp", None),
        P(),
        P(),
        P(),
    )
    return jax.shard_map(
        body,
        mesh=mesh,
        in_specs=placed,
        out_specs=(
            P(),
            P(),
            P(None, "dp"),
            P(None, "dp"),
            P(None, "dp"),
            P(None, "dp"),
            P(None, "dp"),
            P(None, "dp"),
            P(None, "dp", None),
            P(None, "dp", None),
            P(None, "dp", None),
            P(None, "dp", None),
            P(None, "dp", None),
            P(None, "dp", None),
            P(None, "dp", None),
            P(None, "dp", None),
            P(None, "dp", None),
            P(None, "dp", None),
            P(None, "dp", None),
            P(None, "dp", None),
            P("dp", None),
            P("dp", None),
            P("dp", None),
            P("dp", None),
            P("dp", None),
            P("dp", None),
            P(),
            P(),
            P(),
        ),
        check_vma=False,
    )
```

```python
import functools
import math

import jax
import jax.numpy as jnp
from jax import lax
from jax.experimental import pallas as pl
from jax.experimental.pallas import tpu as pltpu
from jax.sharding import PartitionSpec as P

D = 1024
HEADS = 16
HEAD_DIM = 64
FF = 4096
NCLASS = 1001
FREQ = 256
OUT_CH = 32
PATCH_IN = 16
GRID = 16
LAYERS = 2
STEP = 10
NBIAS = 35872


BETA_ONE = 0.9
BETA_TWO = 0.999
EPSILON = 1e-08
DECAY = 0.01
RATE_MATRIX = 0.06
RATE_TABLE = 0.4
RATE_BIAS = 0.2


def matdot(left, right):
    return jnp.dot(left, right, preferred_element_type=jnp.float32)


def layer_norm(stream):
    row_mean = jnp.mean(stream, axis=-1, keepdims=True)
    centered = stream - row_mean
    variance = jnp.mean(centered * centered, axis=-1, keepdims=True)
    return centered * lax.rsqrt(variance + 1e-06)


def modulate(stream, shift_by, scale_by):
    return layer_norm(stream) * (1.0 + scale_by[:, None, :]) + shift_by[:, None, :]


def position_table(position_ids, feature_width, grid_side):
    quarter_width = feature_width // 4
    omegas = 1.0 / 10000.0 ** (jnp.arange(quarter_width, dtype=jnp.float32) / quarter_width)
    col_angle = (position_ids % grid_side).astype(jnp.float32)[:, None] * omegas[None, :]
    row_angle = (position_ids // grid_side).astype(jnp.float32)[:, None] * omegas[None, :]
    return jnp.concatenate(
        [jnp.sin(col_angle), jnp.cos(col_angle), jnp.sin(row_angle), jnp.cos(row_angle)], axis=1
    )


def time_features(timesteps, feature_width):
    half_width = feature_width // 2
    frequencies = jnp.exp(
        -math.log(10000.0) * jnp.arange(half_width, dtype=jnp.float32) / half_width
    )
    angles = timesteps.astype(jnp.float32)[:, None] * frequencies[None, :]
    return jnp.concatenate([jnp.cos(angles), jnp.sin(angles)], axis=1)


def column_sum(grad_bf):
    return jnp.sum(grad_bf.astype(jnp.float32), axis=0)


def split_six(modul):
    return [modul[:, piece * D : (piece + 1) * D] for piece in range(6)]


MESH = pl.DeviceIdType.MESH
TILE = 256
PARTS = 4


def scatter_kernel(
    per_layer,
    total,
    lines,
    *refs,
):
    count = 8 * LAYERS
    sources = [refs[8 * layer : 8 * layer + 8] for layer in range(LAYERS)]
    (
    out_ref,
    lhs_buf,
    act_buf,
    wide_buf,
    down_buf,
    load_sem,
    made,
    core_in,
    x_out,
    x_in,
    p_keep,
    yq_out,
    yq_in,
    q_keep,
    yp_out,
    yp_in,
    p_line,
    zq_out,
    zq_in,
    zp_out,
    zp_in,
    xq_out,
    xq_in,
    xp_out,
    xp_in,
    core_sem,
    x_sem,
    yq_sem,
    yp_sem,
    zq_sem,
    zp_sem,
    xq_sem,
    xp_sem,
    ) = refs[count:]
    seq = lax.axis_index("seq")
    dp = lax.axis_index("dp")
    core = lax.rem(dp, 2)
    why = lax.rem(dp // 2, 2)
    zed = dp // 4
    core_peer = {"seq": seq, "dp": dp + 1 - 2 * core}
    x_peer = {"seq": 1 - seq, "dp": dp}
    y_peer = {"seq": seq, "dp": dp + 2 - 4 * why}

    def z_place(step):
        return lax.rem(zed + step, lines)

    def z_peer(step):
        return {"seq": seq, "dp": z_place(step) * 4 + 2 * why + core}

    barrier = pltpu.get_barrier_semaphore()
    for peer in [core_peer, x_peer, y_peer] + [z_peer(step) for step in range(1, lines)]:
        pl.semaphore_signal(barrier, inc=1, device_id=peer, device_id_type=MESH)
    pl.semaphore_wait(barrier, 2 + lines)

    def remote(source, target, sems, peer):
        return pltpu.make_async_remote_copy(
            src_ref=source,
            dst_ref=target,
            send_sem=sems.at[0],
            recv_sem=sems.at[1],
            device_id=peer,
            device_id_type=MESH,
        )

    def core_copy(slot):
        return remote(made.at[slot, 1 - core], core_in.at[slot], core_sem.at[slot], core_peer)

    def x_copy(slot):
        return remote(x_out.at[slot], x_in.at[slot], x_sem.at[slot], x_peer)

    def yq_copy(slot):
        return remote(yq_out.at[slot], yq_in.at[slot], yq_sem.at[slot], y_peer)

    def yp_copy(slot):
        return remote(yp_out.at[slot], yp_in.at[slot], yp_sem.at[slot], y_peer)

    def zq_copy(slot, step):
        return remote(
            zq_out.at[slot, z_place(step)],
            zq_in.at[slot, step - 1],
            zq_sem.at[slot, step - 1],
            z_peer(step),
        )

    def zp_copy(slot, step):
        return remote(
            zp_out.at[slot, z_place(step)],
            zp_in.at[slot, step - 1],
            zp_sem.at[slot, step - 1],
            z_peer(step),
        )

    def xq_copy(slot):
        return remote(xq_out.at[slot], xq_in.at[slot], xq_sem.at[slot], x_peer)

    def xp_copy(slot):
        return remote(xp_out.at[slot], xp_in.at[slot], xp_sem.at[slot], x_peer)

    def loads(unit, slot):
        found = []
        for layer in range(LAYERS):
            merged, a_one, a_two, act, d_attn, d_qkv, d_up, d_down = sources[layer]
            at = unit - layer * per_layer

            def slab(ref, index, size):
                return ref.at[:, pl.ds(pl.multiple_of(index * size, size), size)]

            wide_to = wide_buf.at[slot], load_sem.at[1, slot]
            lhs_to = lhs_buf.at[slot], load_sem.at[0, slot]
            found += [
                (at == 0, (merged, *lhs_to), (d_attn, *wide_to)),
                (
                    jnp.logical_and(at >= 1, at < 4),
                    (a_one, *lhs_to),
                    (slab(d_qkv, at - 1, D), *wide_to),
                ),
                (
                    jnp.logical_and(at >= 4, at < 8),
                    (a_two, *lhs_to),
                    (slab(d_up, at - 4, D), *wide_to),
                ),
                (
                    jnp.logical_and(at >= 8, at < per_layer),
                    (slab(d_down, at - 8, TILE), down_buf.at[slot], load_sem.at[2, slot]),
                ),
                (at == 8, (act, act_buf, load_sem.at[3, 0])),
            ]
        return found

    def prefetch(unit):
        for due, *moves in loads(unit, lax.rem(unit, 2)):

            @pl.when(due)
            def _():
                for move in moves:
                    pltpu.make_async_copy(*move).start()

    def fetched(unit):
        for due, *moves in loads(unit, lax.rem(unit, 2)):

            @pl.when(due)
            def _():
                for move in moves:
                    pltpu.make_async_copy(*move).wait()

    def dot_rows(left, right):
        return lax.dot_general(
            left, right, (((0,), (0,)), ((), ())), preferred_element_type=jnp.float32
        )

    def compute(unit):
        at = lax.rem(unit, per_layer)
        slot = lax.rem(unit, 2)
        fetched(unit)

        @pl.when(at < 8)
        def _():
            def rows(pair, carry):
                left = lhs_buf[slot, :, pl.ds(pl.multiple_of(pair * 128, 128), 128)]
                block = dot_rows(left, wide_buf[slot]).astype(jnp.bfloat16)
                for own in range(2):
                    for part in range(PARTS):
                        made[slot, own, part, pair // 2, lax.rem(pair, 2)] = block[
                            own * 64 : own * 64 + 64, part * TILE : part * TILE + TILE
                        ]
                return carry

            lax.fori_loop(0, 2 * lines, rows, 0)

        @pl.when(at >= 8)
        def _():
            def rows(pair, carry):
                left = act_buf[:, pl.ds(pl.multiple_of(pair * 512, 512), 512)]
                block = dot_rows(left, down_buf[slot]).astype(jnp.bfloat16)
                for own in range(2):
                    for part in range(PARTS):
                        first = own * 256 + part * 64
                        made[slot, own, part, pair // 2, lax.rem(pair, 2)] = block[
                            first : first + 64
                        ]
                return carry

            lax.fori_loop(0, 2 * lines, rows, 0)

    def wide_sum(one, other):
        return one.astype(jnp.float32) + other.astype(jnp.float32)

    def stage_two(slot):
        core_copy(slot).wait()

        def rows(line, carry):
            for side in range(2):
                x_out[slot, line, side] = wide_sum(
                    made[slot, core, 1 - seq, line, side], core_in[slot, 1 - seq, line, side]
                ).astype(jnp.bfloat16)
                p_keep[slot, line, side] = wide_sum(
                    made[slot, core, seq, line, side], core_in[slot, seq, line, side]
                ).astype(jnp.bfloat16)
            for part in range(2):
                yq_out[slot, line, part] = wide_sum(
                    made[slot, core, 2 + part, line, 1 - why],
                    core_in[slot, 2 + part, line, 1 - why],
                ).astype(jnp.bfloat16)
                q_keep[slot, line, part] = wide_sum(
                    made[slot, core, 2 + part, line, why], core_in[slot, 2 + part, line, why]
                ).astype(jnp.bfloat16)
            return carry

        lax.fori_loop(0, lines, rows, 0)
        x_copy(slot).start()
        yq_copy(slot).start()

    def stage_three(slot):
        x_copy(slot).wait()
        yq_copy(slot).wait()

        def rows(line, carry):
            yp_out[slot, line] = wide_sum(
                p_keep[slot, line, 1 - why], x_in[slot, line, 1 - why]
            ).astype(jnp.bfloat16)
            p_line[slot, line] = wide_sum(p_keep[slot, line, why], x_in[slot, line, why]).astype(
                jnp.bfloat16
            )
            for part in range(2):
                zq_out[slot, line, part] = wide_sum(
                    q_keep[slot, line, part], yq_in[slot, line, part]
                ).astype(jnp.bfloat16)
            return carry

        lax.fori_loop(0, lines, rows, 0)
        yp_copy(slot).start()
        for step in range(1, lines):
            zq_copy(slot, step).start()

    def stage_four(slot):
        yp_copy(slot).wait()
        for step in range(1, lines):
            zq_copy(slot, step).wait()

        def rows(line, carry):
            zp_out[slot, line] = wide_sum(p_line[slot, line], yp_in[slot, line]).astype(
                jnp.bfloat16
            )
            return carry

        lax.fori_loop(0, lines, rows, 0)
        total_q = zq_out[slot, zed].astype(jnp.float32)
        for step in range(1, lines):
            total_q = total_q + zq_in[slot, step - 1].astype(jnp.float32)
        xq_out[slot] = total_q.astype(jnp.bfloat16)
        for step in range(1, lines):
            zp_copy(slot, step).start()
        xq_copy(slot).start()

    def stage_five(unit, slot):
        for step in range(1, lines):
            zp_copy(slot, step).wait()
        xq_copy(slot).wait()
        total_p = zp_out[slot, zed].astype(jnp.float32)
        for step in range(1, lines):
            total_p = total_p + zp_in[slot, step - 1].astype(jnp.float32)
        rounded = total_p.astype(jnp.bfloat16)
        xp_out[slot] = rounded
        xp_copy(slot).start()
        out_ref[unit, seq] = rounded.astype(jnp.float32)
        for part in range(2):
            out_ref[unit, 2 + part] = wide_sum(xq_out[slot, part], xq_in[slot, part])

    def stage_six(unit, slot):
        xp_copy(slot).wait()
        out_ref[unit, 1 - seq] = xp_in[slot].astype(jnp.float32)

    prefetch(jnp.int32(0))

    def turn(at, carry):
        def when_due(behind, run):
            unit = at - behind

            @pl.when(jnp.logical_and(unit >= 0, unit < total))
            def _():
                run(unit, lax.rem(unit, 2))

        prefetch(at + 1)
        when_due(5, stage_six)
        when_due(4, stage_five)
        when_due(3, lambda unit, slot: stage_four(slot))
        when_due(2, lambda unit, slot: stage_three(slot))
        when_due(1, lambda unit, slot: stage_two(slot))

        @pl.when(at < total)
        def _():
            compute(at)
            core_copy(lax.rem(at, 2)).start()

        return carry

    lax.fori_loop(0, total + 5, turn, 0)


def scatter_sums(operands, lines):
    toks, hidden = operands[3].shape
    width = D
    per_layer = 12
    total = LAYERS * per_layer
    bf = jnp.bfloat16
    dma = pltpu.SemaphoreType.DMA

    def buf(*shape):
        return pltpu.VMEM((2,) + shape, bf)

    scratch = [
        buf(toks, width),
        pltpu.VMEM((toks, hidden), bf),
        buf(toks, width),
        buf(toks, TILE),
        dma((4, 2)),
        buf(2, PARTS, lines, 2, 64, TILE),
        buf(PARTS, lines, 2, 64, TILE),
        buf(lines, 2, 64, TILE),
        buf(lines, 2, 64, TILE),
        buf(lines, 2, 64, TILE),
        buf(lines, 2, 64, TILE),
        buf(lines, 2, 64, TILE),
        buf(lines, 2, 64, TILE),
        buf(lines, 64, TILE),
        buf(lines, 64, TILE),
        buf(lines, 64, TILE),
        buf(lines, 2, 64, TILE),
        buf(lines - 1, 2, 64, TILE),
        buf(lines, 64, TILE),
        buf(lines - 1, 64, TILE),
        buf(2, 64, TILE),
        buf(2, 64, TILE),
        buf(64, TILE),
        buf(64, TILE),
        dma((2, 2)),
        dma((2, 2)),
        dma((2, 2)),
        dma((2, 2)),
        dma((2, lines - 1, 2)),
        dma((2, lines - 1, 2)),
        dma((2, 2)),
        dma((2, 2)),
    ]
    return pl.pallas_call(
        functools.partial(scatter_kernel, per_layer, total, lines),
        out_shape=jax.ShapeDtypeStruct((total, PARTS, 64, TILE), jnp.float32),
        in_specs=[pl.BlockSpec(memory_space=pl.ANY)] * len(operands),
        out_specs=pl.BlockSpec(memory_space=pltpu.VMEM),
        scratch_shapes=scratch,
        compiler_params=pltpu.CompilerParams(
            collective_id=1, has_side_effects=True, vmem_limit_bytes=56 * 1024 * 1024
        ),
        cost_estimate=pl.CostEstimate(
            flops=2 * total * toks * width * width,
            bytes_accessed=total * 4 * 1024 * 1024,
            transcendentals=0,
        ),
    )(*operands)


def layer_forward(stream, modul, weight_set, bias_part, pad_mask):
    w_qkv, w_proj, w_up, w_down = weight_set
    images, tok_rows, _ = stream.shape
    shift_one, scale_one, gate_one, shift_two, scale_two, gate_two = split_six(modul)
    a_one = (
        modulate(stream, shift_one, scale_one).astype(jnp.bfloat16).reshape(images * tok_rows, D)
    )
    qkv_all = (matdot(a_one, w_qkv) + bias_part[: 3 * D]).astype(jnp.bfloat16)
    heads_in = qkv_all.reshape(images, tok_rows, 3, HEADS, HEAD_DIM)
    queries, key_rows, value_rows = (heads_in[:, :, 0], heads_in[:, :, 1], heads_in[:, :, 2])
    scores = jnp.einsum(
        "bqhd,bkhd->bhqk", queries, key_rows, preferred_element_type=jnp.float32
    ) * HEAD_DIM ** (-0.5)
    attn_probs = jax.nn.softmax(
        jnp.where(pad_mask[:, None, None, :] > 0, scores, -1000000000.0), axis=-1
    )
    heads_out = jnp.einsum(
        "bhqk,bkhd->bqhd",
        attn_probs.astype(jnp.bfloat16),
        value_rows,
        preferred_element_type=jnp.float32,
    )
    merged = heads_out.astype(jnp.bfloat16).reshape(images * tok_rows, D)
    attn_out = (matdot(merged, w_proj) + bias_part[3 * D : 4 * D]).reshape(images, tok_rows, D)
    stream_one = stream + gate_one[:, None, :] * attn_out
    a_two = (
        modulate(stream_one, shift_two, scale_two)
        .astype(jnp.bfloat16)
        .reshape(images * tok_rows, D)
    )
    up_pre = matdot(a_two, w_up) + bias_part[4 * D : 4 * D + FF]
    activated = jax.nn.gelu(up_pre, approximate=True).astype(jnp.bfloat16)
    down_out = (matdot(activated, w_down) + bias_part[4 * D + FF :]).reshape(images, tok_rows, D)
    stream_two = stream_one + gate_two[:, None, :] * down_out
    saved = (
        a_one,
        queries,
        key_rows,
        value_rows,
        attn_probs,
        merged,
        attn_out,
        stream_one,
        a_two,
        up_pre,
        activated,
        down_out,
    )
    return (stream_two, saved)


def layer_backward(grad_in, stream, modul, weight_set, saved):
    w_qkv, w_proj, w_up, w_down = weight_set
    (
        a_one,
        queries,
        key_rows,
        value_rows,
        attn_probs,
        merged,
        attn_out,
        stream_one,
        a_two,
        up_pre,
        activated,
        down_out,
    ) = saved
    images, tok_rows, _ = stream.shape
    shift_one, scale_one, gate_one, shift_two, scale_two, gate_two = split_six(modul)
    d_gate_two = jnp.sum(grad_in * down_out, axis=1)
    d_down = (grad_in * gate_two[:, None, :]).astype(jnp.bfloat16).reshape(images * tok_rows, D)
    d_activated = matdot(d_down, w_down.T)
    _, gelu_back = jax.vjp(lambda inner: jax.nn.gelu(inner, approximate=True), up_pre)
    d_up = gelu_back(d_activated)[0].astype(jnp.bfloat16)
    d_a_two = matdot(d_up, w_up.T).reshape(images, tok_rows, D)
    _, mod_back_two = jax.vjp(modulate, stream_one, shift_two, scale_two)
    d_stream_one, d_shift_two, d_scale_two = mod_back_two(d_a_two)
    d_stream_one = d_stream_one + grad_in
    d_gate_one = jnp.sum(d_stream_one * attn_out, axis=1)
    d_attn = (
        (d_stream_one * gate_one[:, None, :]).astype(jnp.bfloat16).reshape(images * tok_rows, D)
    )
    d_heads = matdot(d_attn, w_proj.T).astype(jnp.bfloat16)
    d_heads = d_heads.reshape(images, tok_rows, HEADS, HEAD_DIM)
    d_values = jnp.einsum(
        "bhqk,bqhd->bkhd",
        attn_probs.astype(jnp.bfloat16),
        d_heads,
        preferred_element_type=jnp.float32,
    )
    d_probs = jnp.einsum("bqhd,bkhd->bhqk", d_heads, value_rows, preferred_element_type=jnp.float32)
    d_scores = attn_probs * (d_probs - jnp.sum(attn_probs * d_probs, axis=-1, keepdims=True))
    d_scores = d_scores.astype(jnp.bfloat16)
    d_queries = jnp.einsum(
        "bhqk,bkhd->bqhd", d_scores, key_rows, preferred_element_type=jnp.float32
    ) * HEAD_DIM ** (-0.5)
    d_keys = jnp.einsum(
        "bhqk,bqhd->bkhd", d_scores, queries, preferred_element_type=jnp.float32
    ) * HEAD_DIM ** (-0.5)
    d_qkv = jnp.stack([d_queries, d_keys, d_values], axis=2).astype(jnp.bfloat16)
    d_qkv = d_qkv.reshape(images * tok_rows, 3 * D)
    d_a_one = matdot(d_qkv, w_qkv.T).reshape(images, tok_rows, D)
    _, mod_back_one = jax.vjp(modulate, stream, shift_one, scale_one)
    d_stream, d_shift_one, d_scale_one = mod_back_one(d_a_one)
    d_stream = d_stream + d_stream_one
    d_modul = jnp.concatenate(
        [d_shift_one, d_scale_one, d_gate_one, d_shift_two, d_scale_two, d_gate_two], axis=1
    )
    d_bias = jnp.concatenate(
        [column_sum(d_qkv), column_sum(d_attn), column_sum(d_up), column_sum(d_down)]
    )
    factors = (merged, a_one, a_two, activated, d_attn, d_qkv, d_up, d_down)
    return (d_stream, d_modul, factors, d_bias)


def gather_rows(shard):
    return lax.all_gather(shard.astype(jnp.bfloat16), "dp", axis=0, tiled=True)


def reduce_rows(partial):
    owned = lax.psum_scatter(
        partial.astype(jnp.bfloat16), "dp", scatter_dimension=0, tiled=True
    )
    return lax.psum(owned, "seq").astype(jnp.float32)


def weight_sums(factors):
    dp_parts = lax.axis_size("dp")
    by_kernel = (
        lax.axis_size("seq") == 2
        and dp_parts % 4 == 0
        and D // dp_parts == 64
        and FF // dp_parts == PARTS * 64
    )
    if not by_kernel:
        return [
            (
                reduce_rows(matdot(a_one.T, d_qkv)),
                reduce_rows(matdot(merged.T, d_attn)),
                reduce_rows(matdot(a_two.T, d_up)),
                reduce_rows(matdot(activated.T, d_down)),
            )
            for merged, a_one, a_two, activated, d_attn, d_qkv, d_up, d_down in factors
        ]
    units = scatter_sums([each for layer in factors for each in layer], dp_parts // 4)
    units = units.reshape(LAYERS, 12, PARTS, 64, TILE)

    def by_columns(some):
        return some.transpose(2, 0, 1, 3).reshape(64, some.shape[0] * D)

    return [
        (
            by_columns(layer[1:4]),
            by_columns(layer[:1]),
            by_columns(layer[4:8]),
            layer[8:].transpose(1, 2, 0, 3).reshape(PARTS * 64, D),
        )
        for layer in units
    ]


def adamw(weight, gradient, first, second, rate):
    first_new = BETA_ONE * first + (1.0 - BETA_ONE) * gradient
    second_new = BETA_TWO * second + (1.0 - BETA_TWO) * gradient * gradient
    first_hat = first_new / (1.0 - BETA_ONE**STEP)
    second_hat = second_new / (1.0 - BETA_TWO**STEP)
    return (
        weight - rate * (first_hat / (jnp.sqrt(second_hat) + EPSILON) + DECAY * weight),
        first_new,
        second_new,
    )


def body(
    latents,
    noise_target,
    pad_mask,
    labels,
    timesteps,
    embed_rows,
    first_embed,
    second_embed,
    class_table,
    first_table,
    second_table,
    qkv_weight,
    first_qkv,
    second_qkv,
    proj_weight,
    first_proj,
    second_proj,
    up_weight,
    first_up,
    second_up,
    down_weight,
    first_down,
    second_down,
    cond_weight,
    first_cond,
    second_cond,
    head_weight,
    first_head,
    second_head,
    all_biases,
    first_bias,
    second_bias,
):
    seq_parts = lax.axis_size("seq")
    dp_parts = lax.axis_size("dp")
    seq_at = lax.axis_index("seq")
    dp_at = lax.axis_index("dp")
    group, _, _ = latents.shape
    images = group // seq_parts
    everyone = group * dp_parts
    own_cols = embed_rows.shape[1]
    cond_cols = cond_weight.shape[1]
    bias_base = 3 * D + cond_cols
    packed = jnp.concatenate(
        [latents, noise_target, pad_mask.astype(jnp.float32)[:, :, None]], axis=2
    )
    packed = lax.all_to_all(packed, "seq", split_axis=0, concat_axis=1, tiled=True)
    tok_rows = packed.shape[1]
    latents, noise_target, keep_rows = (
        packed[:, :, :PATCH_IN],
        packed[:, :, PATCH_IN : 2 * PATCH_IN],
        packed[:, :, 2 * PATCH_IN],
    )
    ids = lax.all_gather(jnp.stack([labels, timesteps]), "dp", axis=1, tiled=True)
    small = jnp.concatenate(
        [embed_rows[: PATCH_IN + FREQ], head_weight.T], axis=0
    ).astype(jnp.bfloat16)
    small = lax.all_gather(small, "dp", axis=1, tiled=True)
    patch_part = small[:PATCH_IN]
    freq_part = small[PATCH_IN : PATCH_IN + FREQ]
    head_rows = small[PATCH_IN + FREQ :]
    time_own = embed_rows[PATCH_IN + FREQ :].astype(jnp.bfloat16)
    cond_own = cond_weight.astype(jnp.bfloat16)

    features = time_features(ids[1], FREQ).astype(jnp.bfloat16)
    time_pre = matdot(features, freq_part) + all_biases[D : 2 * D]
    time_hidden = jax.nn.silu(time_pre).astype(jnp.bfloat16)
    second_bias_own = lax.dynamic_slice(all_biases, (2 * D + dp_at * own_cols,), (own_cols,))
    onehot = (ids[0][:, None] == jnp.arange(NCLASS, dtype=jnp.int32)[None, :]).astype(jnp.float32)
    condition = (
        matdot(time_hidden, time_own)
        + second_bias_own
        + matdot(onehot.astype(jnp.bfloat16), class_table.astype(jnp.bfloat16))
    )
    cond_act = jax.nn.silu(condition).astype(jnp.bfloat16)
    plane_act = lax.dynamic_index_in_dim(
        cond_act.reshape(dp_parts, seq_parts, images, own_cols), seq_at, 1, keepdims=False
    ).reshape(dp_parts * images, own_cols)
    modulation = lax.psum_scatter(
        matdot(plane_act, cond_own), "dp", scatter_dimension=0, tiled=True
    )
    modulation = modulation + all_biases[3 * D : bias_base]

    position = position_table(jnp.arange(tok_rows, dtype=jnp.int32), D, GRID)
    flat_in = latents.astype(jnp.bfloat16).reshape(images * tok_rows, PATCH_IN)
    stream = (matdot(flat_in, patch_part) + all_biases[:D]).reshape(images, tok_rows, D) + position[
        None
    ]
    layer_bias = [
        all_biases[bias_base + at * (5 * D + FF) : bias_base + (at + 1) * (5 * D + FF)]
        for at in range(LAYERS)
    ]
    inputs_kept = []
    weights_kept = []
    saved_kept = []
    for at in range(LAYERS):
        weight_set = (
            gather_rows(qkv_weight[at]),
            gather_rows(proj_weight[at]),
            gather_rows(up_weight[at]),
            gather_rows(down_weight[at]),
        )
        weights_kept.append(weight_set)
        inputs_kept.append(stream)
        stream, saved = layer_forward(
            stream,
            modulation[:, 6 * at * D : 6 * (at + 1) * D],
            weight_set,
            layer_bias[at],
            keep_rows,
        )
        saved_kept.append(saved)
    final_at = 6 * LAYERS * D
    final_shift = modulation[:, final_at : final_at + D]
    final_scale = modulation[:, final_at + D : final_at + 2 * D]
    moved, final_back = jax.vjp(modulate, stream, final_shift, final_scale)
    a_final = moved.astype(jnp.bfloat16).reshape(images * tok_rows, D)
    head_out = lax.dot_general(
        a_final, head_rows, (((1,), (1,)), ((), ())), preferred_element_type=jnp.float32
    ) + all_biases[NBIAS - OUT_CH :]
    split_out = head_out.reshape(images, tok_rows, 4, 2, OUT_CH // 8)
    predicted = split_out[:, :, :, 0, :].reshape(images, tok_rows, PATCH_IN)
    errors = predicted - noise_target
    loss_part = jnp.sum(keep_rows[:, :, None] * errors * errors)
    count_part = PATCH_IN * jnp.sum(keep_rows)
    d_pred = (2.0 * keep_rows[:, :, None] * errors).reshape(images, tok_rows, 4, 1, OUT_CH // 8)
    d_head = (
        jnp.concatenate([d_pred, jnp.zeros_like(d_pred)], axis=3)
        .reshape(images * tok_rows, OUT_CH)
        .astype(jnp.bfloat16)
    )
    g_head = matdot(a_final.T, d_head)
    d_a_final = matdot(d_head, head_rows).reshape(images, tok_rows, D)
    d_stream, d_final_shift, d_final_scale = final_back(d_a_final)
    layer_factors = [None] * LAYERS
    layer_bias_grads = [None] * LAYERS
    modul_grads = [None] * LAYERS
    for at in reversed(range(LAYERS)):
        d_stream, modul_grads[at], layer_factors[at], layer_bias_grads[at] = layer_backward(
            d_stream,
            inputs_kept[at],
            modulation[:, 6 * at * D : 6 * (at + 1) * D],
            weights_kept[at],
            saved_kept[at],
        )
    d_mod_own = jnp.concatenate(modul_grads + [d_final_shift, d_final_scale], axis=1).astype(
        jnp.bfloat16
    )
    d_modulation = lax.all_gather(d_mod_own, ("dp", "seq"), axis=0, tiled=True)
    d_cond_act = lax.dot_general(
        d_modulation, cond_own, (((1,), (1,)), ((), ())), preferred_element_type=jnp.float32
    )
    _, silu_back = jax.vjp(jax.nn.silu, condition)
    d_condition = silu_back(d_cond_act)[0]
    d_time = d_condition.astype(jnp.bfloat16)
    d_time_hidden = lax.psum_scatter(
        lax.dot_general(
            d_time, time_own, (((1,), (1,)), ((), ())), preferred_element_type=jnp.float32
        ),
        "dp",
        scatter_dimension=1,
        tiled=True,
    )
    time_pre_own = lax.dynamic_slice(time_pre, (0, dp_at * own_cols), (everyone, own_cols))
    _, time_back = jax.vjp(jax.nn.silu, time_pre_own)
    d_time_pre = time_back(d_time_hidden)[0].astype(jnp.bfloat16)
    d_patch = d_stream.astype(jnp.bfloat16).reshape(images * tok_rows, D)
    g_patch = matdot(flat_in.T, d_patch)
    s_cond = matdot(cond_act.T, d_modulation)
    s_table = jnp.dot(onehot.T, d_condition, precision=lax.Precision.HIGHEST)
    g_time = matdot(time_hidden.T, d_time)
    g_freq = matdot(features.T, d_time_pre)

    lead_flag = (seq_at == 0).astype(jnp.float32)
    own_place = dp_at * own_cols
    first_time_bias = lax.dynamic_update_slice(
        jnp.zeros((D,), jnp.float32), column_sum(d_time_pre) * lead_flag, (own_place,)
    )
    second_time_bias = lax.dynamic_update_slice(
        jnp.zeros((D,), jnp.float32), column_sum(d_time) * lead_flag, (own_place,)
    )
    bias_grad = jnp.concatenate(
        [column_sum(d_patch), first_time_bias, second_time_bias, column_sum(d_mod_own)]
        + layer_bias_grads
        + [column_sum(d_head)]
    )
    bias_grad, g_patch, g_head, loss_sum, loss_count = lax.psum(
        (bias_grad, g_patch, g_head, loss_part, count_part), ("seq", "dp")
    )
    s_patch = lax.dynamic_slice(g_patch, (0, own_place), (PATCH_IN, own_cols))
    s_head = lax.dynamic_slice(g_head, (own_place, 0), (own_cols, OUT_CH))
    s_embed = jnp.concatenate([s_patch, g_freq, g_time], axis=0)
    layer_sums = weight_sums(layer_factors)
    s_qkv = jnp.stack([layer_sums[at][0] for at in range(LAYERS)])
    s_proj = jnp.stack([layer_sums[at][1] for at in range(LAYERS)])
    s_up = jnp.stack([layer_sums[at][2] for at in range(LAYERS)])
    s_down = jnp.stack([layer_sums[at][3] for at in range(LAYERS)])
    new_embed, new_first_embed, new_second_embed = adamw(
        embed_rows, s_embed, first_embed, second_embed, RATE_MATRIX
    )
    new_table, new_first_table, new_second_table = adamw(
        class_table, s_table, first_table, second_table, RATE_TABLE
    )
    new_qkv, new_first_qkv, new_second_qkv = adamw(
        qkv_weight, s_qkv, first_qkv, second_qkv, RATE_MATRIX
    )
    new_proj, new_first_proj, new_second_proj = adamw(
        proj_weight, s_proj, first_proj, second_proj, RATE_MATRIX
    )
    new_up, new_first_up, new_second_up = adamw(up_weight, s_up, first_up, second_up, RATE_MATRIX)
    new_down, new_first_down, new_second_down = adamw(
        down_weight, s_down, first_down, second_down, RATE_MATRIX
    )
    new_cond, new_first_cond, new_second_cond = adamw(
        cond_weight, s_cond, first_cond, second_cond, RATE_MATRIX
    )
    new_head, new_first_head, new_second_head = adamw(
        head_weight, s_head, first_head, second_head, RATE_MATRIX
    )
    new_bias, new_first_bias, new_second_bias = adamw(
        all_biases, bias_grad, first_bias, second_bias, RATE_BIAS
    )
    return (
        loss_sum,
        loss_count,
        new_embed,
        new_first_embed,
        new_second_embed,
        new_table,
        new_first_table,
        new_second_table,
        new_qkv,
        new_first_qkv,
        new_second_qkv,
        new_proj,
        new_first_proj,
        new_second_proj,
        new_up,
        new_first_up,
        new_second_up,
        new_down,
        new_first_down,
        new_second_down,
        new_cond,
        new_first_cond,
        new_second_cond,
        new_head,
        new_first_head,
        new_second_head,
        new_bias,
        new_first_bias,
        new_second_bias,
    )


def solution(mesh):
    placed = (
        P("dp", "seq", None),
        P("dp", "seq", None),
        P("dp", "seq"),
        P("dp"),
        P("dp"),
        P(None, "dp"),
        P(None, "dp"),
        P(None, "dp"),
        P(None, "dp"),
        P(None, "dp"),
        P(None, "dp"),
        P(None, "dp", None),
        P(None, "dp", None),
        P(None, "dp", None),
        P(None, "dp", None),
        P(None, "dp", None),
        P(None, "dp", None),
        P(None, "dp", None),
        P(None, "dp", None),
        P(None, "dp", None),
        P(None, "dp", None),
        P(None, "dp", None),
        P(None, "dp", None),
        P("dp", None),
        P("dp", None),
        P("dp", None),
        P("dp", None),
        P("dp", None),
        P("dp", None),
        P(),
        P(),
        P(),
    )
    return jax.shard_map(
        body,
        mesh=mesh,
        in_specs=placed,
        out_specs=(
            P(),
            P(),
            P(None, "dp"),
            P(None, "dp"),
            P(None, "dp"),
            P(None, "dp"),
            P(None, "dp"),
            P(None, "dp"),
            P(None, "dp", None),
            P(None, "dp", None),
            P(None, "dp", None),
            P(None, "dp", None),
            P(None, "dp", None),
            P(None, "dp", None),
            P(None, "dp", None),
            P(None, "dp", None),
            P(None, "dp", None),
            P(None, "dp", None),
            P(None, "dp", None),
            P(None, "dp", None),
            P("dp", None),
            P("dp", None),
            P("dp", None),
            P("dp", None),
            P("dp", None),
            P("dp", None),
            P(),
            P(),
            P(),
        ),
        check_vma=False,
    )
```

```python
import functools
import math

import jax
import jax.numpy as jnp
from jax import lax
from jax.experimental import pallas as pl
from jax.experimental.pallas import tpu as pltpu
from jax.sharding import PartitionSpec as P

D = 1024
HEADS = 16
HEAD_DIM = 64
FF = 4096
NCLASS = 1001
FREQ = 256
OUT_CH = 32
PATCH_IN = 16
GRID = 16
LAYERS = 2
STEP = 10
NBIAS = 35872


BETA_ONE = 0.9
BETA_TWO = 0.999
EPSILON = 1e-08
DECAY = 0.01
RATE_MATRIX = 0.06
RATE_TABLE = 0.4
RATE_BIAS = 0.2


def matdot(left, right):
    return jnp.dot(left, right, preferred_element_type=jnp.float32)


def layer_norm(stream):
    row_mean = jnp.mean(stream, axis=-1, keepdims=True)
    centered = stream - row_mean
    variance = jnp.mean(centered * centered, axis=-1, keepdims=True)
    return centered * lax.rsqrt(variance + 1e-06)


def modulate(stream, shift_by, scale_by):
    return layer_norm(stream) * (1.0 + scale_by[:, None, :]) + shift_by[:, None, :]


def position_table(position_ids, feature_width, grid_side):
    quarter_width = feature_width // 4
    omegas = 1.0 / 10000.0 ** (jnp.arange(quarter_width, dtype=jnp.float32) / quarter_width)
    col_angle = (position_ids % grid_side).astype(jnp.float32)[:, None] * omegas[None, :]
    row_angle = (position_ids // grid_side).astype(jnp.float32)[:, None] * omegas[None, :]
    return jnp.concatenate(
        [jnp.sin(col_angle), jnp.cos(col_angle), jnp.sin(row_angle), jnp.cos(row_angle)], axis=1
    )


def time_features(timesteps, feature_width):
    half_width = feature_width // 2
    frequencies = jnp.exp(
        -math.log(10000.0) * jnp.arange(half_width, dtype=jnp.float32) / half_width
    )
    angles = timesteps.astype(jnp.float32)[:, None] * frequencies[None, :]
    return jnp.concatenate([jnp.cos(angles), jnp.sin(angles)], axis=1)


def column_sum(grad_bf):
    return jnp.sum(grad_bf.astype(jnp.float32), axis=0)


def split_six(modul):
    return [modul[:, piece * D : (piece + 1) * D] for piece in range(6)]


MESH = pl.DeviceIdType.MESH
TILE = 256
PARTS = 4
SHARED = 640
GATHER_LAGS = (2, 2, 2, 1)


def scatter_kernel(
    per_layer,
    total,
    lines,
    *refs,
):
    count = 8 * LAYERS
    sources = [refs[8 * layer : 8 * layer + 8] for layer in range(LAYERS)]
    (
    out_ref,
    lhs_buf,
    act_buf,
    wide_buf,
    down_buf,
    load_sem,
    made,
    core_in,
    x_out,
    x_in,
    p_keep,
    yq_out,
    yq_in,
    q_keep,
    yp_out,
    yp_in,
    p_line,
    zq_out,
    zq_in,
    zp_out,
    zp_in,
    xq_out,
    xq_in,
    xp_out,
    xp_in,
    core_sem,
    x_sem,
    yq_sem,
    yp_sem,
    zq_sem,
    zp_sem,
    xq_sem,
    xp_sem,
    ) = refs[count:]
    seq = lax.axis_index("seq")
    dp = lax.axis_index("dp")
    core = lax.rem(dp, 2)
    why = lax.rem(dp // 2, 2)
    zed = dp // 4
    core_peer = {"seq": seq, "dp": dp + 1 - 2 * core}
    x_peer = {"seq": 1 - seq, "dp": dp}
    y_peer = {"seq": seq, "dp": dp + 2 - 4 * why}

    def z_place(step):
        return lax.rem(zed + step, lines)

    def z_peer(step):
        return {"seq": seq, "dp": z_place(step) * 4 + 2 * why + core}

    barrier = pltpu.get_barrier_semaphore()
    for peer in [core_peer, x_peer, y_peer] + [z_peer(step) for step in range(1, lines)]:
        pl.semaphore_signal(barrier, inc=1, device_id=peer, device_id_type=MESH)
    pl.semaphore_wait(barrier, 2 + lines)

    def remote(source, target, sems, peer):
        return pltpu.make_async_remote_copy(
            src_ref=source,
            dst_ref=target,
            send_sem=sems.at[0],
            recv_sem=sems.at[1],
            device_id=peer,
            device_id_type=MESH,
        )

    def core_copy(slot):
        return remote(made.at[slot, 1 - core], core_in.at[slot], core_sem.at[slot], core_peer)

    def x_copy(slot):
        return remote(x_out.at[slot], x_in.at[slot], x_sem.at[slot], x_peer)

    def yq_copy(slot):
        return remote(yq_out.at[slot], yq_in.at[slot], yq_sem.at[slot], y_peer)

    def yp_copy(slot):
        return remote(yp_out.at[slot], yp_in.at[slot], yp_sem.at[slot], y_peer)

    def zq_copy(slot, step):
        return remote(
            zq_out.at[slot, z_place(step)],
            zq_in.at[slot, step - 1],
            zq_sem.at[slot, step - 1],
            z_peer(step),
        )

    def zp_copy(slot, step):
        return remote(
            zp_out.at[slot, z_place(step)],
            zp_in.at[slot, step - 1],
            zp_sem.at[slot, step - 1],
            z_peer(step),
        )

    def xq_copy(slot):
        return remote(xq_out.at[slot], xq_in.at[slot], xq_sem.at[slot], x_peer)

    def xp_copy(slot):
        return remote(xp_out.at[slot], xp_in.at[slot], xp_sem.at[slot], x_peer)

    def loads(unit, slot):
        found = []
        for layer in range(LAYERS):
            merged, a_one, a_two, act, d_attn, d_qkv, d_up, d_down = sources[layer]
            at = unit - layer * per_layer

            def slab(ref, index, size):
                return ref.at[:, pl.ds(pl.multiple_of(index * size, size), size)]

            wide_to = wide_buf.at[slot], load_sem.at[1, slot]
            lhs_to = lhs_buf.at[slot], load_sem.at[0, slot]
            found += [
                (at == 0, (merged, *lhs_to), (d_attn, *wide_to)),
                (
                    jnp.logical_and(at >= 1, at < 4),
                    (a_one, *lhs_to),
                    (slab(d_qkv, at - 1, D), *wide_to),
                ),
                (
                    jnp.logical_and(at >= 4, at < 8),
                    (a_two, *lhs_to),
                    (slab(d_up, at - 4, D), *wide_to),
                ),
                (
                    jnp.logical_and(at >= 8, at < per_layer),
                    (slab(d_down, at - 8, TILE), down_buf.at[slot], load_sem.at[2, slot]),
                ),
                (at == 8, (act, act_buf, load_sem.at[3, 0])),
            ]
        return found

    def prefetch(unit):
        for due, *moves in loads(unit, lax.rem(unit, 2)):

            @pl.when(due)
            def _():
                for move in moves:
                    pltpu.make_async_copy(*move).start()

    def fetched(unit):
        for due, *moves in loads(unit, lax.rem(unit, 2)):

            @pl.when(due)
            def _():
                for move in moves:
                    pltpu.make_async_copy(*move).wait()

    def dot_rows(left, right):
        return lax.dot_general(
            left, right, (((0,), (0,)), ((), ())), preferred_element_type=jnp.float32
        )

    def compute(unit):
        at = lax.rem(unit, per_layer)
        slot = lax.rem(unit, 2)
        fetched(unit)

        @pl.when(at < 8)
        def _():
            def rows(pair, carry):
                left = lhs_buf[slot, :, pl.ds(pl.multiple_of(pair * 128, 128), 128)]
                block = dot_rows(left, wide_buf[slot]).astype(jnp.bfloat16)
                for own in range(2):
                    for part in range(PARTS):
                        made[slot, own, part, pair // 2, lax.rem(pair, 2)] = block[
                            own * 64 : own * 64 + 64, part * TILE : part * TILE + TILE
                        ]
                return carry

            lax.fori_loop(0, 2 * lines, rows, 0)

        @pl.when(at >= 8)
        def _():
            def rows(pair, carry):
                left = act_buf[:, pl.ds(pl.multiple_of(pair * 512, 512), 512)]
                block = dot_rows(left, down_buf[slot]).astype(jnp.bfloat16)
                for own in range(2):
                    for part in range(PARTS):
                        first = own * 256 + part * 64
                        made[slot, own, part, pair // 2, lax.rem(pair, 2)] = block[
                            first : first + 64
                        ]
                return carry

            lax.fori_loop(0, 2 * lines, rows, 0)

    def wide_sum(one, other):
        return one.astype(jnp.float32) + other.astype(jnp.float32)

    def stage_two(slot):
        core_copy(slot).wait()

        def rows(line, carry):
            for side in range(2):
                x_out[slot, line, side] = wide_sum(
                    made[slot, core, 1 - seq, line, side], core_in[slot, 1 - seq, line, side]
                ).astype(jnp.bfloat16)
                p_keep[slot, line, side] = wide_sum(
                    made[slot, core, seq, line, side], core_in[slot, seq, line, side]
                ).astype(jnp.bfloat16)
            for part in range(2):
                yq_out[slot, line, part] = wide_sum(
                    made[slot, core, 2 + part, line, 1 - why],
                    core_in[slot, 2 + part, line, 1 - why],
                ).astype(jnp.bfloat16)
                q_keep[slot, line, part] = wide_sum(
                    made[slot, core, 2 + part, line, why], core_in[slot, 2 + part, line, why]
                ).astype(jnp.bfloat16)
            return carry

        lax.fori_loop(0, lines, rows, 0)
        x_copy(slot).start()
        yq_copy(slot).start()

    def stage_three(slot):
        x_copy(slot).wait()
        yq_copy(slot).wait()

        def rows(line, carry):
            yp_out[slot, line] = wide_sum(
                p_keep[slot, line, 1 - why], x_in[slot, line, 1 - why]
            ).astype(jnp.bfloat16)
            p_line[slot, line] = wide_sum(p_keep[slot, line, why], x_in[slot, line, why]).astype(
                jnp.bfloat16
            )
            for part in range(2):
                zq_out[slot, line, part] = wide_sum(
                    q_keep[slot, line, part], yq_in[slot, line, part]
                ).astype(jnp.bfloat16)
            return carry

        lax.fori_loop(0, lines, rows, 0)
        yp_copy(slot).start()
        for step in range(1, lines):
            zq_copy(slot, step).start()

    def stage_four(slot):
        yp_copy(slot).wait()
        for step in range(1, lines):
            zq_copy(slot, step).wait()

        def rows(line, carry):
            zp_out[slot, line] = wide_sum(p_line[slot, line], yp_in[slot, line]).astype(
                jnp.bfloat16
            )
            return carry

        lax.fori_loop(0, lines, rows, 0)
        total_q = zq_out[slot, zed].astype(jnp.float32)
        for step in range(1, lines):
            total_q = total_q + zq_in[slot, step - 1].astype(jnp.float32)
        xq_out[slot] = total_q.astype(jnp.bfloat16)
        for step in range(1, lines):
            zp_copy(slot, step).start()
        xq_copy(slot).start()

    def stage_five(unit, slot):
        for step in range(1, lines):
            zp_copy(slot, step).wait()
        xq_copy(slot).wait()
        total_p = zp_out[slot, zed].astype(jnp.float32)
        for step in range(1, lines):
            total_p = total_p + zp_in[slot, step - 1].astype(jnp.float32)
        rounded = total_p.astype(jnp.bfloat16)
        xp_out[slot] = rounded
        xp_copy(slot).start()
        out_ref[unit, seq] = rounded.astype(jnp.float32)
        for part in range(2):
            out_ref[unit, 2 + part] = wide_sum(xq_out[slot, part], xq_in[slot, part])

    def stage_six(unit, slot):
        xp_copy(slot).wait()
        out_ref[unit, 1 - seq] = xp_in[slot].astype(jnp.float32)

    prefetch(jnp.int32(0))

    def turn(at, carry):
        def when_due(behind, run):
            unit = at - behind

            @pl.when(jnp.logical_and(unit >= 0, unit < total))
            def _():
                run(unit, lax.rem(unit, 2))

        prefetch(at + 1)
        when_due(5, stage_six)
        when_due(4, stage_five)
        when_due(3, lambda unit, slot: stage_four(slot))
        when_due(2, lambda unit, slot: stage_three(slot))
        when_due(1, lambda unit, slot: stage_two(slot))

        @pl.when(at < total)
        def _():
            compute(at)
            core_copy(lax.rem(at, 2)).start()

        return carry

    lax.fori_loop(0, total + 5, turn, 0)


def scatter_sums(operands, lines):
    toks, hidden = operands[3].shape
    width = D
    per_layer = 12
    total = LAYERS * per_layer
    bf = jnp.bfloat16
    dma = pltpu.SemaphoreType.DMA

    def buf(*shape):
        return pltpu.VMEM((2,) + shape, bf)

    scratch = [
        buf(toks, width),
        pltpu.VMEM((toks, hidden), bf),
        buf(toks, width),
        buf(toks, TILE),
        dma((4, 2)),
        buf(2, PARTS, lines, 2, 64, TILE),
        buf(PARTS, lines, 2, 64, TILE),
        buf(lines, 2, 64, TILE),
        buf(lines, 2, 64, TILE),
        buf(lines, 2, 64, TILE),
        buf(lines, 2, 64, TILE),
        buf(lines, 2, 64, TILE),
        buf(lines, 2, 64, TILE),
        buf(lines, 64, TILE),
        buf(lines, 64, TILE),
        buf(lines, 64, TILE),
        buf(lines, 2, 64, TILE),
        buf(lines - 1, 2, 64, TILE),
        buf(lines, 64, TILE),
        buf(lines - 1, 64, TILE),
        buf(2, 64, TILE),
        buf(2, 64, TILE),
        buf(64, TILE),
        buf(64, TILE),
        dma((2, 2)),
        dma((2, 2)),
        dma((2, 2)),
        dma((2, 2)),
        dma((2, lines - 1, 2)),
        dma((2, lines - 1, 2)),
        dma((2, 2)),
        dma((2, 2)),
    ]
    return pl.pallas_call(
        functools.partial(scatter_kernel, per_layer, total, lines),
        out_shape=jax.ShapeDtypeStruct((total, PARTS, 64, TILE), jnp.float32),
        in_specs=[pl.BlockSpec(memory_space=pl.ANY)] * len(operands),
        out_specs=pl.BlockSpec(memory_space=pltpu.VMEM),
        scratch_shapes=scratch,
        compiler_params=pltpu.CompilerParams(
            collective_id=1, has_side_effects=True, vmem_limit_bytes=56 * 1024 * 1024
        ),
        cost_estimate=pl.CostEstimate(
            flops=2 * total * toks * width * width,
            bytes_accessed=total * 4 * 1024 * 1024,
            transcendentals=0,
        ),
    )(*operands)


def gather_kernel(
    lines,
    qkv_own,
    proj_own,
    up_own,
    down_own,
    qkv_all,
    proj_all,
    up_all,
    down_all,
    own_sem,
    zp_sem,
    zq_sem,
    yp_sem,
    yq_sem,
    x_sem,
    core_sem,
):
    seq = lax.axis_index("seq")
    dp = lax.axis_index("dp")
    core = lax.rem(dp, 2)
    why = lax.rem(dp // 2, 2)
    zed = dp // 4
    core_peer = {"seq": seq, "dp": dp + 1 - 2 * core}
    x_peer = {"seq": 1 - seq, "dp": dp}
    y_peer = {"seq": seq, "dp": dp + 2 - 4 * why}
    z_peers = [
        {"seq": seq, "dp": lax.rem(zed + step, lines) * 4 + 2 * why + core}
        for step in range(1, lines)
    ]
    pairs = [(qkv_own, qkv_all), (proj_own, proj_all), (up_own, up_all), (down_own, down_all)]
    firsts = [0, 3, 4, 8]
    total = 12

    keeps = [
        pltpu.make_async_copy(own, every.at[zed, why, core], own_sem.at[at])
        for at, (own, every) in enumerate(pairs)
    ]
    for keep in keeps:
        keep.start()
    for keep in keeps:
        keep.wait()
    barrier = pltpu.get_barrier_semaphore()
    for peer in [core_peer, x_peer, y_peer] + z_peers:
        pl.semaphore_signal(barrier, inc=1, device_id=peer, device_id_type=MESH)
    pl.semaphore_wait(barrier, 2 + lines)

    def places(kind, unit):
        at = unit - firsts[kind]
        if kind == 3:
            return pl.multiple_of(at * 64, 64), 0
        return 0, pl.multiple_of(at * D, D)

    def span(first, begin, size):
        return pl.ds(pl.multiple_of(first + begin, 128), size)

    def copies(stage, kind, unit):
        slot = unit
        own, every = pairs[kind]
        row, first = places(kind, unit)
        rows = pl.ds(row, 64)
        mine = pl.ds(pl.multiple_of(row + seq * 32, 32), 32)
        halved = span(first, 0, SHARED)
        rest = span(first, SHARED, D - SHARED)
        whole = span(first, 0, D)

        def remote(source, target, sems, peer):
            return pltpu.make_async_remote_copy(
                src_ref=source,
                dst_ref=target,
                send_sem=sems.at[0],
                recv_sem=sems.at[1],
                device_id=peer,
                device_id_type=MESH,
            )

        def same(view, sems, peer):
            return remote(view, view, sems, peer)

        if stage == 0:
            return [
                remote(own.at[band, cols], every.at[zed, why, core, band, cols], sems, peer)
                for band, cols, kinds in ((mine, halved, zp_sem), (rows, rest, zq_sem))
                for sems, peer in [(kinds.at[slot, at], z_peers[at]) for at in range(lines - 1)]
            ]
        if stage == 1:
            return [
                same(every.at[:, why, core, mine, halved], yp_sem.at[slot], y_peer),
                same(every.at[:, why, core, rows, rest], yq_sem.at[slot], y_peer),
            ]
        if stage == 2:
            return [same(every.at[:, :, core, mine, halved], x_sem.at[slot], x_peer)]
        return [same(every.at[:, :, core, rows, whole], core_sem.at[slot], core_peer)]

    def each_kind(unit, run):
        ends = firsts[1:] + [total]
        for kind in range(4):

            @pl.when(jnp.logical_and(unit >= firsts[kind], unit < ends[kind]))
            def _():
                run(kind)

    def begin(stage, unit):
        def run(kind):
            for copy in copies(stage, kind, unit):
                copy.start()

        each_kind(unit, run)

    def finish(stage, unit):
        def run(kind):
            for copy in copies(stage, kind, unit):
                copy.wait()

        each_kind(unit, run)

    def turn(at, carry):
        finish(3, at - sum(GATHER_LAGS))
        for stage in (3, 2, 1):
            behind = sum(GATHER_LAGS[:stage])
            finish(stage - 1, at - behind)
            begin(stage, at - behind)
        begin(0, at)
        return carry

    lax.fori_loop(0, total + sum(GATHER_LAGS), turn, 0)


def gather_blocks(qkv_own, proj_own, up_own, down_own, lines, collective_id):
    owns = (qkv_own, proj_own, up_own, down_own)
    dma = pltpu.SemaphoreType.DMA
    outs = pl.pallas_call(
        functools.partial(gather_kernel, lines),
        out_shape=[
            jax.ShapeDtypeStruct((lines, 2, 2) + own.shape, jnp.bfloat16) for own in owns
        ],
        in_specs=[pl.BlockSpec(memory_space=pltpu.VMEM)] * 4,
        out_specs=[pl.BlockSpec(memory_space=pl.ANY)] * 4,
        scratch_shapes=[
            dma((4,)),
            dma((12, lines - 1, 2)),
            dma((12, lines - 1, 2)),
            dma((12, 2)),
            dma((12, 2)),
            dma((12, 2)),
            dma((12, 2)),
        ],
        compiler_params=pltpu.CompilerParams(
            collective_id=collective_id,
            has_side_effects=True,
            vmem_limit_bytes=56 * 1024 * 1024,
        ),
        cost_estimate=pl.CostEstimate(
            flops=0, bytes_accessed=12 * 4 * lines * 64 * D * 8, transcendentals=0
        ),
    )(*owns)
    return tuple(every.reshape(-1, every.shape[-1]) for every in outs)


def layer_forward(stream, modul, weight_set, bias_part, pad_mask):
    w_qkv, w_proj, w_up, w_down = weight_set
    images, tok_rows, _ = stream.shape
    shift_one, scale_one, gate_one, shift_two, scale_two, gate_two = split_six(modul)
    a_one = (
        modulate(stream, shift_one, scale_one).astype(jnp.bfloat16).reshape(images * tok_rows, D)
    )
    qkv_all = (matdot(a_one, w_qkv) + bias_part[: 3 * D]).astype(jnp.bfloat16)
    heads_in = qkv_all.reshape(images, tok_rows, 3, HEADS, HEAD_DIM)
    queries, key_rows, value_rows = (heads_in[:, :, 0], heads_in[:, :, 1], heads_in[:, :, 2])
    scores = jnp.einsum(
        "bqhd,bkhd->bhqk", queries, key_rows, preferred_element_type=jnp.float32
    ) * HEAD_DIM ** (-0.5)
    attn_probs = jax.nn.softmax(
        jnp.where(pad_mask[:, None, None, :] > 0, scores, -1000000000.0), axis=-1
    )
    heads_out = jnp.einsum(
        "bhqk,bkhd->bqhd",
        attn_probs.astype(jnp.bfloat16),
        value_rows,
        preferred_element_type=jnp.float32,
    )
    merged = heads_out.astype(jnp.bfloat16).reshape(images * tok_rows, D)
    attn_out = (matdot(merged, w_proj) + bias_part[3 * D : 4 * D]).reshape(images, tok_rows, D)
    stream_one = stream + gate_one[:, None, :] * attn_out
    a_two = (
        modulate(stream_one, shift_two, scale_two)
        .astype(jnp.bfloat16)
        .reshape(images * tok_rows, D)
    )
    up_pre = matdot(a_two, w_up) + bias_part[4 * D : 4 * D + FF]
    activated = jax.nn.gelu(up_pre, approximate=True).astype(jnp.bfloat16)
    down_out = (matdot(activated, w_down) + bias_part[4 * D + FF :]).reshape(images, tok_rows, D)
    stream_two = stream_one + gate_two[:, None, :] * down_out
    saved = (
        a_one,
        queries,
        key_rows,
        value_rows,
        attn_probs,
        merged,
        attn_out,
        stream_one,
        a_two,
        up_pre,
        activated,
        down_out,
    )
    return (stream_two, saved)


def layer_backward(grad_in, stream, modul, weight_set, saved):
    w_qkv, w_proj, w_up, w_down = weight_set
    (
        a_one,
        queries,
        key_rows,
        value_rows,
        attn_probs,
        merged,
        attn_out,
        stream_one,
        a_two,
        up_pre,
        activated,
        down_out,
    ) = saved
    images, tok_rows, _ = stream.shape
    shift_one, scale_one, gate_one, shift_two, scale_two, gate_two = split_six(modul)
    d_gate_two = jnp.sum(grad_in * down_out, axis=1)
    d_down = (grad_in * gate_two[:, None, :]).astype(jnp.bfloat16).reshape(images * tok_rows, D)
    d_activated = matdot(d_down, w_down.T)
    _, gelu_back = jax.vjp(lambda inner: jax.nn.gelu(inner, approximate=True), up_pre)
    d_up = gelu_back(d_activated)[0].astype(jnp.bfloat16)
    d_a_two = matdot(d_up, w_up.T).reshape(images, tok_rows, D)
    _, mod_back_two = jax.vjp(modulate, stream_one, shift_two, scale_two)
    d_stream_one, d_shift_two, d_scale_two = mod_back_two(d_a_two)
    d_stream_one = d_stream_one + grad_in
    d_gate_one = jnp.sum(d_stream_one * attn_out, axis=1)
    d_attn = (
        (d_stream_one * gate_one[:, None, :]).astype(jnp.bfloat16).reshape(images * tok_rows, D)
    )
    d_heads = matdot(d_attn, w_proj.T).astype(jnp.bfloat16)
    d_heads = d_heads.reshape(images, tok_rows, HEADS, HEAD_DIM)
    d_values = jnp.einsum(
        "bhqk,bqhd->bkhd",
        attn_probs.astype(jnp.bfloat16),
        d_heads,
        preferred_element_type=jnp.float32,
    )
    d_probs = jnp.einsum("bqhd,bkhd->bhqk", d_heads, value_rows, preferred_element_type=jnp.float32)
    d_scores = attn_probs * (d_probs - jnp.sum(attn_probs * d_probs, axis=-1, keepdims=True))
    d_scores = d_scores.astype(jnp.bfloat16)
    d_queries = jnp.einsum(
        "bhqk,bkhd->bqhd", d_scores, key_rows, preferred_element_type=jnp.float32
    ) * HEAD_DIM ** (-0.5)
    d_keys = jnp.einsum(
        "bhqk,bqhd->bkhd", d_scores, queries, preferred_element_type=jnp.float32
    ) * HEAD_DIM ** (-0.5)
    d_qkv = jnp.stack([d_queries, d_keys, d_values], axis=2).astype(jnp.bfloat16)
    d_qkv = d_qkv.reshape(images * tok_rows, 3 * D)
    d_a_one = matdot(d_qkv, w_qkv.T).reshape(images, tok_rows, D)
    _, mod_back_one = jax.vjp(modulate, stream, shift_one, scale_one)
    d_stream, d_shift_one, d_scale_one = mod_back_one(d_a_one)
    d_stream = d_stream + d_stream_one
    d_modul = jnp.concatenate(
        [d_shift_one, d_scale_one, d_gate_one, d_shift_two, d_scale_two, d_gate_two], axis=1
    )
    d_bias = jnp.concatenate(
        [column_sum(d_qkv), column_sum(d_attn), column_sum(d_up), column_sum(d_down)]
    )
    factors = (merged, a_one, a_two, activated, d_attn, d_qkv, d_up, d_down)
    return (d_stream, d_modul, factors, d_bias)


def gather_rows(shard):
    return lax.all_gather(shard.astype(jnp.bfloat16), "dp", axis=0, tiled=True)


def kernels_fit():
    dp_parts = lax.axis_size("dp")
    return (
        lax.axis_size("seq") == 2
        and dp_parts % 4 == 0
        and D // dp_parts == 64
        and FF // dp_parts == PARTS * 64
    )


def gather_layer(shards, collective_id):
    if kernels_fit():
        return gather_blocks(*shards, lax.axis_size("dp") // 4, collective_id)
    return tuple(gather_rows(shard) for shard in shards)


def reduce_rows(partial):
    owned = lax.psum_scatter(
        partial.astype(jnp.bfloat16), "dp", scatter_dimension=0, tiled=True
    )
    return lax.psum(owned, "seq").astype(jnp.float32)


def weight_sums(factors):
    dp_parts = lax.axis_size("dp")
    if not kernels_fit():
        return [
            (
                reduce_rows(matdot(a_one.T, d_qkv)),
                reduce_rows(matdot(merged.T, d_attn)),
                reduce_rows(matdot(a_two.T, d_up)),
                reduce_rows(matdot(activated.T, d_down)),
            )
            for merged, a_one, a_two, activated, d_attn, d_qkv, d_up, d_down in factors
        ]
    units = scatter_sums([each for layer in factors for each in layer], dp_parts // 4)
    units = units.reshape(LAYERS, 12, PARTS, 64, TILE)

    def by_columns(some):
        return some.transpose(2, 0, 1, 3).reshape(64, some.shape[0] * D)

    return [
        (
            by_columns(layer[1:4]),
            by_columns(layer[:1]),
            by_columns(layer[4:8]),
            layer[8:].transpose(1, 2, 0, 3).reshape(PARTS * 64, D),
        )
        for layer in units
    ]


def adamw(weight, gradient, first, second, rate):
    first_new = BETA_ONE * first + (1.0 - BETA_ONE) * gradient
    second_new = BETA_TWO * second + (1.0 - BETA_TWO) * gradient * gradient
    first_hat = first_new / (1.0 - BETA_ONE**STEP)
    second_hat = second_new / (1.0 - BETA_TWO**STEP)
    return (
        weight - rate * (first_hat / (jnp.sqrt(second_hat) + EPSILON) + DECAY * weight),
        first_new,
        second_new,
    )


def body(
    latents,
    noise_target,
    pad_mask,
    labels,
    timesteps,
    embed_rows,
    first_embed,
    second_embed,
    class_table,
    first_table,
    second_table,
    qkv_weight,
    first_qkv,
    second_qkv,
    proj_weight,
    first_proj,
    second_proj,
    up_weight,
    first_up,
    second_up,
    down_weight,
    first_down,
    second_down,
    cond_weight,
    first_cond,
    second_cond,
    head_weight,
    first_head,
    second_head,
    all_biases,
    first_bias,
    second_bias,
):
    seq_parts = lax.axis_size("seq")
    dp_parts = lax.axis_size("dp")
    seq_at = lax.axis_index("seq")
    dp_at = lax.axis_index("dp")
    group, _, _ = latents.shape
    images = group // seq_parts
    everyone = group * dp_parts
    own_cols = embed_rows.shape[1]
    cond_cols = cond_weight.shape[1]
    bias_base = 3 * D + cond_cols
    packed = jnp.concatenate(
        [latents, noise_target, pad_mask.astype(jnp.float32)[:, :, None]], axis=2
    )
    packed = lax.all_to_all(packed, "seq", split_axis=0, concat_axis=1, tiled=True)
    tok_rows = packed.shape[1]
    shards = [
        tuple(
            weight[at].astype(jnp.bfloat16)
            for weight in (qkv_weight, proj_weight, up_weight, down_weight)
        )
        for at in range(LAYERS)
    ]
    weights_kept = [gather_layer(shards[0], 2)]
    ids = lax.all_gather(jnp.stack([labels, timesteps]), "dp", axis=1, tiled=True)
    small = jnp.concatenate(
        [embed_rows[: PATCH_IN + FREQ], head_weight.T], axis=0
    ).astype(jnp.bfloat16)
    small = lax.all_gather(small, "dp", axis=1, tiled=True)
    ids, small, packed, weights_kept[0] = lax.optimization_barrier(
        (ids, small, packed, weights_kept[0])
    )
    latents, noise_target, keep_rows = (
        packed[:, :, :PATCH_IN],
        packed[:, :, PATCH_IN : 2 * PATCH_IN],
        packed[:, :, 2 * PATCH_IN],
    )
    patch_part = small[:PATCH_IN]
    freq_part = small[PATCH_IN : PATCH_IN + FREQ]
    head_rows = small[PATCH_IN + FREQ :]
    time_own = embed_rows[PATCH_IN + FREQ :].astype(jnp.bfloat16)
    cond_own = cond_weight.astype(jnp.bfloat16)

    features = time_features(ids[1], FREQ).astype(jnp.bfloat16)
    time_pre = matdot(features, freq_part) + all_biases[D : 2 * D]
    time_hidden = jax.nn.silu(time_pre).astype(jnp.bfloat16)
    second_bias_own = lax.dynamic_slice(all_biases, (2 * D + dp_at * own_cols,), (own_cols,))
    onehot = (ids[0][:, None] == jnp.arange(NCLASS, dtype=jnp.int32)[None, :]).astype(jnp.float32)
    condition = (
        matdot(time_hidden, time_own)
        + second_bias_own
        + matdot(onehot.astype(jnp.bfloat16), class_table.astype(jnp.bfloat16))
    )
    cond_act = jax.nn.silu(condition).astype(jnp.bfloat16)
    plane_act = lax.dynamic_index_in_dim(
        cond_act.reshape(dp_parts, seq_parts, images, own_cols), seq_at, 1, keepdims=False
    ).reshape(dp_parts * images, own_cols)
    mod_partial = matdot(plane_act, cond_own)
    mod_partial, shards[1] = lax.optimization_barrier((mod_partial, shards[1]))
    weights_kept.append(gather_layer(shards[1], 3))
    modulation = lax.psum_scatter(mod_partial, "dp", scatter_dimension=0, tiled=True)
    modulation = modulation + all_biases[3 * D : bias_base]

    position = position_table(jnp.arange(tok_rows, dtype=jnp.int32), D, GRID)
    flat_in = latents.astype(jnp.bfloat16).reshape(images * tok_rows, PATCH_IN)
    stream = (matdot(flat_in, patch_part) + all_biases[:D]).reshape(images, tok_rows, D) + position[
        None
    ]
    layer_bias = [
        all_biases[bias_base + at * (5 * D + FF) : bias_base + (at + 1) * (5 * D + FF)]
        for at in range(LAYERS)
    ]
    inputs_kept = []
    saved_kept = []
    for at in range(LAYERS):
        inputs_kept.append(stream)
        stream, saved = layer_forward(
            stream,
            modulation[:, 6 * at * D : 6 * (at + 1) * D],
            weights_kept[at],
            layer_bias[at],
            keep_rows,
        )
        saved_kept.append(saved)
        if at == 0:
            stream, time_own = lax.optimization_barrier((stream, time_own))
            time_full = lax.all_gather(time_own, "dp", axis=1, tiled=True)
    final_at = 6 * LAYERS * D
    final_shift = modulation[:, final_at : final_at + D]
    final_scale = modulation[:, final_at + D : final_at + 2 * D]
    moved, final_back = jax.vjp(modulate, stream, final_shift, final_scale)
    a_final = moved.astype(jnp.bfloat16).reshape(images * tok_rows, D)
    head_out = lax.dot_general(
        a_final, head_rows, (((1,), (1,)), ((), ())), preferred_element_type=jnp.float32
    ) + all_biases[NBIAS - OUT_CH :]
    split_out = head_out.reshape(images, tok_rows, 4, 2, OUT_CH // 8)
    predicted = split_out[:, :, :, 0, :].reshape(images, tok_rows, PATCH_IN)
    errors = predicted - noise_target
    loss_part = jnp.sum(keep_rows[:, :, None] * errors * errors)
    count_part = PATCH_IN * jnp.sum(keep_rows)
    d_pred = (2.0 * keep_rows[:, :, None] * errors).reshape(images, tok_rows, 4, 1, OUT_CH // 8)
    d_head = (
        jnp.concatenate([d_pred, jnp.zeros_like(d_pred)], axis=3)
        .reshape(images * tok_rows, OUT_CH)
        .astype(jnp.bfloat16)
    )
    g_head = matdot(a_final.T, d_head)
    d_a_final = matdot(d_head, head_rows).reshape(images, tok_rows, D)
    d_stream, d_final_shift, d_final_scale = final_back(d_a_final)
    layer_factors = [None] * LAYERS
    layer_bias_grads = [None] * LAYERS
    modul_grads = [None] * LAYERS
    for at in reversed(range(LAYERS)):
        d_stream, modul_grads[at], layer_factors[at], layer_bias_grads[at] = layer_backward(
            d_stream,
            inputs_kept[at],
            modulation[:, 6 * at * D : 6 * (at + 1) * D],
            weights_kept[at],
            saved_kept[at],
        )
    d_mod_own = jnp.concatenate(modul_grads + [d_final_shift, d_final_scale], axis=1).astype(
        jnp.bfloat16
    )
    d_patch = d_stream.astype(jnp.bfloat16).reshape(images * tok_rows, D)
    flat = jnp.concatenate(
        [column_sum(d_patch), jnp.zeros((2 * D,), jnp.float32), column_sum(d_mod_own)]
        + layer_bias_grads
        + [column_sum(d_head), loss_part[None], count_part[None]]
        + [matdot(flat_in.T, d_patch).reshape(-1), g_head.reshape(-1)]
    )
    flat, d_mod_own, layer_factors = lax.optimization_barrier((flat, d_mod_own, layer_factors))
    flat = lax.psum(flat, ("seq", "dp"))
    d_modulation = lax.all_gather(d_mod_own, ("dp", "seq"), axis=0, tiled=True)
    layer_sums = weight_sums(layer_factors)
    d_cond_act = lax.dot_general(
        d_modulation, cond_own, (((1,), (1,)), ((), ())), preferred_element_type=jnp.float32
    )
    _, silu_back = jax.vjp(jax.nn.silu, condition)
    d_condition = silu_back(d_cond_act)[0]
    d_time_own = d_condition.astype(jnp.bfloat16)
    d_time = lax.all_gather(d_time_own, "dp", axis=1, tiled=True)
    d_time_hidden = lax.dot_general(
        d_time, time_full, (((1,), (1,)), ((), ())), preferred_element_type=jnp.float32
    )
    _, time_back = jax.vjp(jax.nn.silu, time_pre)
    d_time_pre = time_back(d_time_hidden)[0].astype(jnp.bfloat16)
    own_place = dp_at * own_cols
    s_cond = matdot(cond_act.T, d_modulation)
    s_table = jnp.dot(onehot.T, d_condition, precision=lax.Precision.HIGHEST)
    g_time = matdot(time_hidden.T, d_time_own)
    g_freq = matdot(
        features.T, lax.dynamic_slice(d_time_pre, (0, own_place), (everyone, own_cols))
    )
    bias_grad = jnp.concatenate(
        [flat[:D], column_sum(d_time_pre), column_sum(d_time), flat[3 * D : NBIAS]]
    )
    loss_sum, loss_count = flat[NBIAS], flat[NBIAS + 1]
    patch_at = NBIAS + 2
    head_at = patch_at + PATCH_IN * D
    s_patch = lax.dynamic_slice(
        flat[patch_at:head_at].reshape(PATCH_IN, D), (0, own_place), (PATCH_IN, own_cols)
    )
    s_head = lax.dynamic_slice(
        flat[head_at:].reshape(D, OUT_CH), (own_place, 0), (own_cols, OUT_CH)
    )
    s_embed = jnp.concatenate([s_patch, g_freq, g_time], axis=0)
    s_qkv = jnp.stack([layer_sums[at][0] for at in range(LAYERS)])
    s_proj = jnp.stack([layer_sums[at][1] for at in range(LAYERS)])
    s_up = jnp.stack([layer_sums[at][2] for at in range(LAYERS)])
    s_down = jnp.stack([layer_sums[at][3] for at in range(LAYERS)])
    new_embed, new_first_embed, new_second_embed = adamw(
        embed_rows, s_embed, first_embed, second_embed, RATE_MATRIX
    )
    new_table, new_first_table, new_second_table = adamw(
        class_table, s_table, first_table, second_table, RATE_TABLE
    )
    new_qkv, new_first_qkv, new_second_qkv = adamw(
        qkv_weight, s_qkv, first_qkv, second_qkv, RATE_MATRIX
    )
    new_proj, new_first_proj, new_second_proj = adamw(
        proj_weight, s_proj, first_proj, second_proj, RATE_MATRIX
    )
    new_up, new_first_up, new_second_up = adamw(up_weight, s_up, first_up, second_up, RATE_MATRIX)
    new_down, new_first_down, new_second_down = adamw(
        down_weight, s_down, first_down, second_down, RATE_MATRIX
    )
    new_cond, new_first_cond, new_second_cond = adamw(
        cond_weight, s_cond, first_cond, second_cond, RATE_MATRIX
    )
    new_head, new_first_head, new_second_head = adamw(
        head_weight, s_head, first_head, second_head, RATE_MATRIX
    )
    new_bias, new_first_bias, new_second_bias = adamw(
        all_biases, bias_grad, first_bias, second_bias, RATE_BIAS
    )
    return (
        loss_sum,
        loss_count,
        new_embed,
        new_first_embed,
        new_second_embed,
        new_table,
        new_first_table,
        new_second_table,
        new_qkv,
        new_first_qkv,
        new_second_qkv,
        new_proj,
        new_first_proj,
        new_second_proj,
        new_up,
        new_first_up,
        new_second_up,
        new_down,
        new_first_down,
        new_second_down,
        new_cond,
        new_first_cond,
        new_second_cond,
        new_head,
        new_first_head,
        new_second_head,
        new_bias,
        new_first_bias,
        new_second_bias,
    )


def solution(mesh):
    placed = (
        P("dp", "seq", None),
        P("dp", "seq", None),
        P("dp", "seq"),
        P("dp"),
        P("dp"),
        P(None, "dp"),
        P(None, "dp"),
        P(None, "dp"),
        P(None, "dp"),
        P(None, "dp"),
        P(None, "dp"),
        P(None, "dp", None),
        P(None, "dp", None),
        P(None, "dp", None),
        P(None, "dp", None),
        P(None, "dp", None),
        P(None, "dp", None),
        P(None, "dp", None),
        P(None, "dp", None),
        P(None, "dp", None),
        P(None, "dp", None),
        P(None, "dp", None),
        P(None, "dp", None),
        P("dp", None),
        P("dp", None),
        P("dp", None),
        P("dp", None),
        P("dp", None),
        P("dp", None),
        P(),
        P(),
        P(),
    )
    return jax.shard_map(
        body,
        mesh=mesh,
        in_specs=placed,
        out_specs=(
            P(),
            P(),
            P(None, "dp"),
            P(None, "dp"),
            P(None, "dp"),
            P(None, "dp"),
            P(None, "dp"),
            P(None, "dp"),
            P(None, "dp", None),
            P(None, "dp", None),
            P(None, "dp", None),
            P(None, "dp", None),
            P(None, "dp", None),
            P(None, "dp", None),
            P(None, "dp", None),
            P(None, "dp", None),
            P(None, "dp", None),
            P(None, "dp", None),
            P(None, "dp", None),
            P(None, "dp", None),
            P("dp", None),
            P("dp", None),
            P("dp", None),
            P("dp", None),
            P("dp", None),
            P("dp", None),
            P(),
            P(),
            P(),
        ),
        check_vma=False,
    )
```

```python
import functools
import math

import jax
import jax.numpy as jnp
from jax import lax
from jax.experimental import pallas as pl
from jax.experimental.pallas import tpu as pltpu
from jax.sharding import PartitionSpec as P

D = 1024
HEADS = 16
HEAD_DIM = 64
FF = 4096
NCLASS = 1001
FREQ = 256
OUT_CH = 32
PATCH_IN = 16
GRID = 16
LAYERS = 2
STEP = 10
NBIAS = 35872


BETA_ONE = 0.9
BETA_TWO = 0.999
EPSILON = 1e-08
DECAY = 0.01
RATE_MATRIX = 0.06
RATE_TABLE = 0.4
RATE_BIAS = 0.2


def matdot(left, right):
    return jnp.dot(left, right, preferred_element_type=jnp.float32)


def layer_norm(stream):
    row_mean = jnp.mean(stream, axis=-1, keepdims=True)
    centered = stream - row_mean
    variance = jnp.mean(centered * centered, axis=-1, keepdims=True)
    return centered * lax.rsqrt(variance + 1e-06)


def modulate(stream, shift_by, scale_by):
    return layer_norm(stream) * (1.0 + scale_by[:, None, :]) + shift_by[:, None, :]


def position_table(position_ids, feature_width, grid_side):
    quarter_width = feature_width // 4
    omegas = 1.0 / 10000.0 ** (jnp.arange(quarter_width, dtype=jnp.float32) / quarter_width)
    col_angle = (position_ids % grid_side).astype(jnp.float32)[:, None] * omegas[None, :]
    row_angle = (position_ids // grid_side).astype(jnp.float32)[:, None] * omegas[None, :]
    return jnp.concatenate(
        [jnp.sin(col_angle), jnp.cos(col_angle), jnp.sin(row_angle), jnp.cos(row_angle)], axis=1
    )


def time_features(timesteps, feature_width):
    half_width = feature_width // 2
    frequencies = jnp.exp(
        -math.log(10000.0) * jnp.arange(half_width, dtype=jnp.float32) / half_width
    )
    angles = timesteps.astype(jnp.float32)[:, None] * frequencies[None, :]
    return jnp.concatenate([jnp.cos(angles), jnp.sin(angles)], axis=1)


def column_sum(grad_bf):
    return jnp.sum(grad_bf.astype(jnp.float32), axis=0)


MESH = pl.DeviceIdType.MESH
TILE = 256
PARTS = 4
SHARED = 640
GATHER_LAGS = (2, 2, 2, 1)
HALF = 512
GELU_IN = math.sqrt(2.0 / math.pi)
GELU_CUBE = 0.044715
FORWARD_STEPS = 26
BACKWARD_STEPS = 27


def scatter_kernel(
    per_layer,
    total,
    lines,
    *refs,
):
    count = 8 * LAYERS
    sources = [refs[8 * layer : 8 * layer + 8] for layer in range(LAYERS)]
    (
    out_ref,
    lhs_buf,
    act_buf,
    wide_buf,
    down_buf,
    load_sem,
    made,
    core_in,
    x_out,
    x_in,
    p_keep,
    yq_out,
    yq_in,
    q_keep,
    yp_out,
    yp_in,
    p_line,
    zq_out,
    zq_in,
    zp_out,
    zp_in,
    xq_out,
    xq_in,
    xp_out,
    xp_in,
    core_sem,
    x_sem,
    yq_sem,
    yp_sem,
    zq_sem,
    zp_sem,
    xq_sem,
    xp_sem,
    ) = refs[count:]
    seq = lax.axis_index("seq")
    dp = lax.axis_index("dp")
    core = lax.rem(dp, 2)
    why = lax.rem(dp // 2, 2)
    zed = dp // 4
    core_peer = {"seq": seq, "dp": dp + 1 - 2 * core}
    x_peer = {"seq": 1 - seq, "dp": dp}
    y_peer = {"seq": seq, "dp": dp + 2 - 4 * why}

    def z_place(step):
        return lax.rem(zed + step, lines)

    def z_peer(step):
        return {"seq": seq, "dp": z_place(step) * 4 + 2 * why + core}

    barrier = pltpu.get_barrier_semaphore()
    for peer in [core_peer, x_peer, y_peer] + [z_peer(step) for step in range(1, lines)]:
        pl.semaphore_signal(barrier, inc=1, device_id=peer, device_id_type=MESH)
    pl.semaphore_wait(barrier, 2 + lines)

    def remote(source, target, sems, peer):
        return pltpu.make_async_remote_copy(
            src_ref=source,
            dst_ref=target,
            send_sem=sems.at[0],
            recv_sem=sems.at[1],
            device_id=peer,
            device_id_type=MESH,
        )

    def core_copy(slot):
        return remote(made.at[slot, 1 - core], core_in.at[slot], core_sem.at[slot], core_peer)

    def x_copy(slot):
        return remote(x_out.at[slot], x_in.at[slot], x_sem.at[slot], x_peer)

    def yq_copy(slot):
        return remote(yq_out.at[slot], yq_in.at[slot], yq_sem.at[slot], y_peer)

    def yp_copy(slot):
        return remote(yp_out.at[slot], yp_in.at[slot], yp_sem.at[slot], y_peer)

    def zq_copy(slot, step):
        return remote(
            zq_out.at[slot, z_place(step)],
            zq_in.at[slot, step - 1],
            zq_sem.at[slot, step - 1],
            z_peer(step),
        )

    def zp_copy(slot, step):
        return remote(
            zp_out.at[slot, z_place(step)],
            zp_in.at[slot, step - 1],
            zp_sem.at[slot, step - 1],
            z_peer(step),
        )

    def xq_copy(slot):
        return remote(xq_out.at[slot], xq_in.at[slot], xq_sem.at[slot], x_peer)

    def xp_copy(slot):
        return remote(xp_out.at[slot], xp_in.at[slot], xp_sem.at[slot], x_peer)

    def loads(unit, slot):
        found = []
        for layer in range(LAYERS):
            merged, a_one, a_two, act, d_attn, d_qkv, d_up, d_down = sources[layer]
            at = unit - layer * per_layer

            def slab(ref, index, size):
                return ref.at[:, pl.ds(pl.multiple_of(index * size, size), size)]

            wide_to = wide_buf.at[slot], load_sem.at[1, slot]
            lhs_to = lhs_buf.at[slot], load_sem.at[0, slot]
            found += [
                (at == 0, (merged, *lhs_to), (d_attn, *wide_to)),
                (
                    jnp.logical_and(at >= 1, at < 4),
                    (a_one, *lhs_to),
                    (slab(d_qkv, at - 1, D), *wide_to),
                ),
                (
                    jnp.logical_and(at >= 4, at < 8),
                    (a_two, *lhs_to),
                    (slab(d_up, at - 4, D), *wide_to),
                ),
                (
                    jnp.logical_and(at >= 8, at < per_layer),
                    (slab(d_down, at - 8, TILE), down_buf.at[slot], load_sem.at[2, slot]),
                ),
                (at == 8, (act, act_buf, load_sem.at[3, 0])),
            ]
        return found

    def prefetch(unit):
        for due, *moves in loads(unit, lax.rem(unit, 2)):

            @pl.when(due)
            def _():
                for move in moves:
                    pltpu.make_async_copy(*move).start()

    def fetched(unit):
        for due, *moves in loads(unit, lax.rem(unit, 2)):

            @pl.when(due)
            def _():
                for move in moves:
                    pltpu.make_async_copy(*move).wait()

    def dot_rows(left, right):
        return lax.dot_general(
            left, right, (((0,), (0,)), ((), ())), preferred_element_type=jnp.float32
        )

    def compute(unit):
        at = lax.rem(unit, per_layer)
        slot = lax.rem(unit, 2)
        fetched(unit)

        @pl.when(at < 8)
        def _():
            def rows(pair, carry):
                left = lhs_buf[slot, :, pl.ds(pl.multiple_of(pair * 128, 128), 128)]
                block = dot_rows(left, wide_buf[slot]).astype(jnp.bfloat16)
                for own in range(2):
                    for part in range(PARTS):
                        made[slot, own, part, pair // 2, lax.rem(pair, 2)] = block[
                            own * 64 : own * 64 + 64, part * TILE : part * TILE + TILE
                        ]
                return carry

            lax.fori_loop(0, 2 * lines, rows, 0)

        @pl.when(at >= 8)
        def _():
            def rows(pair, carry):
                left = act_buf[:, pl.ds(pl.multiple_of(pair * 512, 512), 512)]
                block = dot_rows(left, down_buf[slot]).astype(jnp.bfloat16)
                for own in range(2):
                    for part in range(PARTS):
                        first = own * 256 + part * 64
                        made[slot, own, part, pair // 2, lax.rem(pair, 2)] = block[
                            first : first + 64
                        ]
                return carry

            lax.fori_loop(0, 2 * lines, rows, 0)

    def wide_sum(one, other):
        return one.astype(jnp.float32) + other.astype(jnp.float32)

    def stage_two(slot):
        core_copy(slot).wait()

        def rows(line, carry):
            for side in range(2):
                x_out[slot, line, side] = wide_sum(
                    made[slot, core, 1 - seq, line, side], core_in[slot, 1 - seq, line, side]
                ).astype(jnp.bfloat16)
                p_keep[slot, line, side] = wide_sum(
                    made[slot, core, seq, line, side], core_in[slot, seq, line, side]
                ).astype(jnp.bfloat16)
            for part in range(2):
                yq_out[slot, line, part] = wide_sum(
                    made[slot, core, 2 + part, line, 1 - why],
                    core_in[slot, 2 + part, line, 1 - why],
                ).astype(jnp.bfloat16)
                q_keep[slot, line, part] = wide_sum(
                    made[slot, core, 2 + part, line, why], core_in[slot, 2 + part, line, why]
                ).astype(jnp.bfloat16)
            return carry

        lax.fori_loop(0, lines, rows, 0)
        x_copy(slot).start()
        yq_copy(slot).start()

    def stage_three(slot):
        x_copy(slot).wait()
        yq_copy(slot).wait()

        def rows(line, carry):
            yp_out[slot, line] = wide_sum(
                p_keep[slot, line, 1 - why], x_in[slot, line, 1 - why]
            ).astype(jnp.bfloat16)
            p_line[slot, line] = wide_sum(p_keep[slot, line, why], x_in[slot, line, why]).astype(
                jnp.bfloat16
            )
            for part in range(2):
                zq_out[slot, line, part] = wide_sum(
                    q_keep[slot, line, part], yq_in[slot, line, part]
                ).astype(jnp.bfloat16)
            return carry

        lax.fori_loop(0, lines, rows, 0)
        yp_copy(slot).start()
        for step in range(1, lines):
            zq_copy(slot, step).start()

    def stage_four(slot):
        yp_copy(slot).wait()
        for step in range(1, lines):
            zq_copy(slot, step).wait()

        def rows(line, carry):
            zp_out[slot, line] = wide_sum(p_line[slot, line], yp_in[slot, line]).astype(
                jnp.bfloat16
            )
            return carry

        lax.fori_loop(0, lines, rows, 0)
        total_q = zq_out[slot, zed].astype(jnp.float32)
        for step in range(1, lines):
            total_q = total_q + zq_in[slot, step - 1].astype(jnp.float32)
        xq_out[slot] = total_q.astype(jnp.bfloat16)
        for step in range(1, lines):
            zp_copy(slot, step).start()
        xq_copy(slot).start()

    def stage_five(unit, slot):
        for step in range(1, lines):
            zp_copy(slot, step).wait()
        xq_copy(slot).wait()
        total_p = zp_out[slot, zed].astype(jnp.float32)
        for step in range(1, lines):
            total_p = total_p + zp_in[slot, step - 1].astype(jnp.float32)
        rounded = total_p.astype(jnp.bfloat16)
        xp_out[slot] = rounded
        xp_copy(slot).start()
        out_ref[unit, seq] = rounded.astype(jnp.float32)
        for part in range(2):
            out_ref[unit, 2 + part] = wide_sum(xq_out[slot, part], xq_in[slot, part])

    def stage_six(unit, slot):
        xp_copy(slot).wait()
        out_ref[unit, 1 - seq] = xp_in[slot].astype(jnp.float32)

    prefetch(jnp.int32(0))

    def turn(at, carry):
        def when_due(behind, run):
            unit = at - behind

            @pl.when(jnp.logical_and(unit >= 0, unit < total))
            def _():
                run(unit, lax.rem(unit, 2))

        prefetch(at + 1)
        when_due(5, stage_six)
        when_due(4, stage_five)
        when_due(3, lambda unit, slot: stage_four(slot))
        when_due(2, lambda unit, slot: stage_three(slot))
        when_due(1, lambda unit, slot: stage_two(slot))

        @pl.when(at < total)
        def _():
            compute(at)
            core_copy(lax.rem(at, 2)).start()

        return carry

    lax.fori_loop(0, total + 5, turn, 0)


def scatter_sums(operands, lines):
    toks, hidden = operands[3].shape
    width = D
    per_layer = 12
    total = LAYERS * per_layer
    bf = jnp.bfloat16
    dma = pltpu.SemaphoreType.DMA

    def buf(*shape):
        return pltpu.VMEM((2,) + shape, bf)

    scratch = [
        buf(toks, width),
        pltpu.VMEM((toks, hidden), bf),
        buf(toks, width),
        buf(toks, TILE),
        dma((4, 2)),
        buf(2, PARTS, lines, 2, 64, TILE),
        buf(PARTS, lines, 2, 64, TILE),
        buf(lines, 2, 64, TILE),
        buf(lines, 2, 64, TILE),
        buf(lines, 2, 64, TILE),
        buf(lines, 2, 64, TILE),
        buf(lines, 2, 64, TILE),
        buf(lines, 2, 64, TILE),
        buf(lines, 64, TILE),
        buf(lines, 64, TILE),
        buf(lines, 64, TILE),
        buf(lines, 2, 64, TILE),
        buf(lines - 1, 2, 64, TILE),
        buf(lines, 64, TILE),
        buf(lines - 1, 64, TILE),
        buf(2, 64, TILE),
        buf(2, 64, TILE),
        buf(64, TILE),
        buf(64, TILE),
        dma((2, 2)),
        dma((2, 2)),
        dma((2, 2)),
        dma((2, 2)),
        dma((2, lines - 1, 2)),
        dma((2, lines - 1, 2)),
        dma((2, 2)),
        dma((2, 2)),
    ]
    return pl.pallas_call(
        functools.partial(scatter_kernel, per_layer, total, lines),
        out_shape=jax.ShapeDtypeStruct((total, PARTS, 64, TILE), jnp.float32),
        in_specs=[pl.BlockSpec(memory_space=pl.ANY)] * len(operands),
        out_specs=pl.BlockSpec(memory_space=pltpu.VMEM),
        scratch_shapes=scratch,
        compiler_params=pltpu.CompilerParams(
            collective_id=1, has_side_effects=True, vmem_limit_bytes=56 * 1024 * 1024
        ),
        cost_estimate=pl.CostEstimate(
            flops=2 * total * toks * width * width,
            bytes_accessed=total * 4 * 1024 * 1024,
            transcendentals=0,
        ),
    )(*operands)


def dot_nn(left, right):
    return jnp.dot(left, right, preferred_element_type=jnp.float32)


def dot_nt(left, right):
    return lax.dot_general(
        left, right, (((1,), (1,)), ((), ())), preferred_element_type=jnp.float32
    )


def dot_tn(left, right):
    return lax.dot_general(
        left, right, (((0,), (0,)), ((), ())), preferred_element_type=jnp.float32
    )


def column_tile(at, size=HALF):
    return pl.ds(pl.multiple_of(at * size, size), size)


def normalized(rows):
    centered = rows - jnp.mean(rows, axis=-1, keepdims=True)
    variance = jnp.mean(centered * centered, axis=-1, keepdims=True)
    inverse = lax.rsqrt(variance + 1e-06)
    return centered * inverse, inverse


def head_probs(queries, keys, keep):
    scores = jnp.where(keep > 0, dot_nt(queries, keys), -1000000000.0)
    raised = jnp.exp(scores - jnp.max(scores, axis=-1, keepdims=True))
    return raised * (1.0 / jnp.sum(raised, axis=-1, keepdims=True))


def within(at, first, size):
    return jnp.logical_and(at >= first, at < first + size)


def forward_pieces(refs, mod_at):
    (
        x_ref,
        mod_ref,
        bias_ref,
        keep_ref,
        w_qkv,
        w_proj,
        w_up,
        w_down,
        a_one_out,
        qkv_out,
        merged_out,
        attn_out,
        x_one_out,
        a_two_out,
        pre_out,
        act_out,
        down_out,
        x_two_out,
        a_buf,
        qkv_buf,
        merged_buf,
        attn_buf,
        x_one_buf,
        a_two_buf,
        pre_buf,
        act_buf,
        down_buf,
        x_two_buf,
        wide_buf,
        tall_buf,
        load_sem,
        tile_sem,
        save_sem,
    ) = refs
    images, toks = keep_ref.shape
    bf = jnp.bfloat16

    def save(at, source, target):
        return pltpu.make_async_copy(source, target, save_sem.at[at])

    saves = [
        save(at, *pair)
        for at, pair in enumerate(
            [
                (a_buf, a_one_out),
                (qkv_buf, qkv_out),
                (merged_buf, merged_out),
                (attn_buf, attn_out),
                (x_one_buf, x_one_out),
                (a_two_buf, a_two_out),
                (down_buf, down_out),
                (x_two_buf, x_two_out),
            ]
        )
    ]

    def wide_load(source, tile, slot):
        return pltpu.make_async_copy(
            source.at[:, :, :, :, column_tile(tile)], wide_buf.at[slot], load_sem.at[0, slot]
        )

    def tall_load(tile, slot):
        return pltpu.make_async_copy(
            w_down.at[tile // 2, lax.rem(tile, 2)], tall_buf.at[slot], load_sem.at[1, slot]
        )

    def tile_saves(tile, slot):
        return [
            pltpu.make_async_copy(
                pre_buf.at[slot], pre_out.at[:, column_tile(tile)], tile_sem.at[0, slot]
            ),
            pltpu.make_async_copy(
                act_buf.at[slot], act_out.at[:, column_tile(tile)], tile_sem.at[1, slot]
            ),
        ]

    def wide_tile(slot):
        return wide_buf[slot].reshape(D, HALF)

    def tall_tile(slot):
        return tall_buf[slot].reshape(HALF, D)

    def loads(at, run):
        slot = lax.rem(at, 2)

        @pl.when(within(at, 1, 6))
        def _():
            run(wide_load(w_qkv, at - 1, slot))

        @pl.when(within(at, 15, 2))
        def _():
            run(wide_load(w_proj, at - 15, slot))

        @pl.when(within(at, 18, 8))
        def _():
            run(wide_load(w_up, at - 18, slot))
            run(tall_load(at - 18, slot))

    def modulated(source, target, piece):
        def rows_of(block, carry):
            image = block // 4
            rows = pl.ds(pl.multiple_of(block * 64, 64), 64)
            shift = mod_ref[pl.ds(mod_at + 2 * piece + image, 1), :]
            scale = mod_ref[pl.ds(mod_at + 2 * piece + 2 + image, 1), :]
            unit, _ = normalized(source[rows, :])
            target[rows, :] = (unit * (1.0 + scale) + shift).astype(bf)
            return carry

        lax.fori_loop(0, images * toks // 64, rows_of, 0)

    def attend(image, pair):
        rows = pl.ds(pl.multiple_of(image * toks, toks), toks)
        low = lax.broadcasted_iota(jnp.int32, (toks, 128), 1) < 64
        queries = qkv_buf[rows, column_tile(pair, 128)] * jnp.asarray(0.125, bf)
        keys = qkv_buf[rows, column_tile(8 + pair, 128)]
        values = qkv_buf[rows, column_tile(16 + pair, 128)]
        keep = keep_ref[pl.ds(image, 1), :]
        zero = jnp.zeros_like(queries)
        total = jnp.zeros((toks, 128), jnp.float32)
        for own in (low, jnp.logical_not(low)):
            probs = head_probs(jnp.where(own, queries, zero), keys, keep)
            total = total + dot_nn(probs.astype(bf), jnp.where(own, values, zero))
        merged_buf[rows, column_tile(pair, 128)] = total.astype(bf)

    def step(at):
        slot = lax.rem(at, 2)
        loads(at + 1, lambda copy: copy.start())
        loads(at, lambda copy: copy.wait())

        @pl.when(at == 0)
        def _():
            modulated(x_ref, a_buf, 0)
            saves[0].start()

        @pl.when(within(at, 1, 6))
        def _():
            cols = column_tile(at - 1)
            for image in range(images):
                rows = pl.ds(image * toks, toks)
                qkv_buf[rows, cols] = (
                    dot_nn(a_buf[rows, :], wide_tile(slot)) + bias_ref[:, cols]
                ).astype(bf)

        @pl.when(at == 7)
        def _():
            saves[1].start()

        @pl.when(within(at, 7, 8))
        def _():
            for turn in range(2):
                item = (at - 7) * 2 + turn
                attend(item // 8, lax.rem(item, 8))

        @pl.when(within(at, 15, 2))
        def _():
            cols = column_tile(at - 15)
            for image in range(images):
                rows = pl.ds(image * toks, toks)
                attn = dot_nn(merged_buf[rows, :], wide_tile(slot)) + bias_ref[
                    :, column_tile(at - 15 + 6)
                ]
                attn_buf[rows, cols] = attn
                gate = mod_ref[mod_at + 4 + image : mod_at + 5 + image, cols]
                x_one_buf[rows, cols] = x_ref[rows, cols] + gate * attn

        @pl.when(at == 17)
        def _():
            for which in (2, 3, 4):
                saves[which].start()
            modulated(x_one_buf, a_two_buf, 3)
            saves[5].start()

        @pl.when(within(at, 18, 8))
        def _():
            tile = at - 18

            @pl.when(tile >= 2)
            def _():
                for copy in tile_saves(tile - 2, slot):
                    copy.wait()

            for image in range(images):
                rows = pl.ds(image * toks, toks)
                pre = dot_nn(a_two_buf[rows, :], wide_tile(slot)) + bias_ref[:, column_tile(tile + 8)]
                pre_buf[slot, rows, :] = pre
                inner = jnp.tanh(GELU_IN * (pre + GELU_CUBE * pre * pre * pre))
                active = (0.5 * pre * (1.0 + inner)).astype(bf)
                act_buf[slot, rows, :] = active
                part = dot_nn(active, tall_tile(slot))

                @pl.when(tile == 0)
                def _():
                    down_buf[rows, :] = part + bias_ref[:, 8 * D : 9 * D]

                @pl.when(tile > 0)
                def _():
                    down_buf[rows, :] += part

            for copy in tile_saves(tile, slot):
                copy.start()

        @pl.when(at == FORWARD_STEPS - 1)
        def _():
            for image in range(images):
                rows = pl.ds(image * toks, toks)
                gate = mod_ref[mod_at + 10 + image : mod_at + 11 + image, :]
                x_two_buf[rows, :] = x_one_buf[rows, :] + gate * down_buf[rows, :]
            saves[6].start()
            saves[7].start()

    def finish():
        for tile in (6, 7):
            for copy in tile_saves(tile, tile % 2):
                copy.wait()
        for copy in saves:
            copy.wait()

    return step, finish


FORWARD_OUTS = [
    (D, jnp.bfloat16),
    (3 * D, jnp.bfloat16),
    (D, jnp.bfloat16),
    (D, jnp.float32),
    (D, jnp.float32),
    (D, jnp.bfloat16),
    (FF, jnp.float32),
    (FF, jnp.bfloat16),
    (D, jnp.float32),
    (D, jnp.float32),
]


def forward_scratch(toks):
    bf, f32 = jnp.bfloat16, jnp.float32
    return [
        pltpu.VMEM((toks, D), bf),
        pltpu.VMEM((toks, 3 * D), bf),
        pltpu.VMEM((toks, D), bf),
        pltpu.VMEM((toks, D), f32),
        pltpu.VMEM((toks, D), f32),
        pltpu.VMEM((toks, D), bf),
        pltpu.VMEM((2, toks, HALF), f32),
        pltpu.VMEM((2, toks, HALF), bf),
        pltpu.VMEM((toks, D), f32),
        pltpu.VMEM((toks, D), f32),
        pltpu.VMEM((2, 4, 2, 2, 64, HALF), bf),
        pltpu.VMEM((2, 2, 256, D), bf),
        pltpu.SemaphoreType.DMA((2, 2)),
        pltpu.SemaphoreType.DMA((2, 2)),
        pltpu.SemaphoreType.DMA((8,)),
    ]


def forward_kernel(mod_at, *refs):
    step, finish = forward_pieces(refs, mod_at)

    def turn(at, carry):
        step(at)
        return carry

    lax.fori_loop(0, FORWARD_STEPS, turn, 0)
    finish()


def grouped(weights):
    return [each.reshape(4, 2, 2, -1, each.shape[-1]) for each in weights]


def forward_layer(x, mods, mod_at, biases, keep, weights):
    toks = x.shape[0]
    return pl.pallas_call(
        functools.partial(forward_kernel, mod_at),
        out_shape=[jax.ShapeDtypeStruct((toks, width), kind) for width, kind in FORWARD_OUTS],
        in_specs=[pl.BlockSpec(memory_space=pltpu.VMEM)] * 4
        + [pl.BlockSpec(memory_space=pl.ANY)] * 4,
        out_specs=[pl.BlockSpec(memory_space=pl.ANY)] * len(FORWARD_OUTS),
        scratch_shapes=forward_scratch(toks),
        compiler_params=pltpu.CompilerParams(vmem_limit_bytes=56 * 1024 * 1024),
        cost_estimate=pl.CostEstimate(
            flops=24 * toks * D * D, bytes_accessed=60 * 1024 * 1024, transcendentals=4 * toks * D
        ),
    )(x, mods, biases, keep, *grouped(weights))


def backward_pieces(refs, mod_at):
    (
        grad_ref,
        x_ref,
        x_one_ref,
        attn_ref,
        down_ref,
        qkv_ref,
        mod_ref,
        keep_ref,
        pre_hbm,
        w_qkv,
        w_proj,
        w_up,
        w_down,
        d_x_out,
        d_down_out,
        d_up_out,
        d_attn_out,
        d_qkv_out,
        d_mod_ref,
        d_bias_ref,
        total_buf,
        d_x_one_buf,
        d_down_buf,
        d_up_buf,
        d_attn_buf,
        d_heads_buf,
        d_qkv_buf,
        pre_buf,
        wide_buf,
        tall_buf,
        load_sem,
        tile_sem,
        save_sem,
    ) = refs
    images, toks = keep_ref.shape
    bf = jnp.bfloat16
    blocks = toks // 64
    saves = [
        pltpu.make_async_copy(source, target, save_sem.at[at])
        for at, (source, target) in enumerate(
            [
                (d_down_buf, d_down_out),
                (d_attn_buf, d_attn_out),
                (d_qkv_buf, d_qkv_out),
                (total_buf, d_x_out),
            ]
        )
    ]

    def wide_load(source, tile, slot):
        return pltpu.make_async_copy(
            source.at[:, :, :, :, column_tile(tile)], wide_buf.at[slot], load_sem.at[0, slot]
        )

    def tall_load(tile, slot):
        return pltpu.make_async_copy(
            w_down.at[tile // 2, lax.rem(tile, 2)], tall_buf.at[slot], load_sem.at[1, slot]
        )

    def pre_load(tile, slot):
        return pltpu.make_async_copy(
            pre_hbm.at[:, column_tile(tile)], pre_buf.at[slot], load_sem.at[2, slot]
        )

    def up_save(tile, slot):
        return pltpu.make_async_copy(
            d_up_buf.at[slot], d_up_out.at[:, column_tile(tile)], tile_sem.at[slot]
        )

    def wide_tile(slot):
        return wide_buf[slot].reshape(D, HALF)

    def tall_tile(slot):
        return tall_buf[slot].reshape(HALF, D)

    def loads(at, run):
        slot = lax.rem(at, 2)

        @pl.when(within(at, 1, 8))
        def _():
            run(tall_load(at - 1, slot))
            run(wide_load(w_up, at - 1, slot))
            run(pre_load(at - 1, slot))

        @pl.when(within(at, 10, 2))
        def _():
            run(wide_load(w_proj, at - 10, slot))

        @pl.when(within(at, 20, 6))
        def _():
            run(wide_load(w_qkv, at - 20, slot))

    def column_sums(rows):
        return jnp.sum(rows.astype(jnp.float32), axis=0, keepdims=True)

    def gated(image, gate_row, gradient, branch, target, bias_cols):
        def rows_of(block, sums):
            rows = pl.ds(pl.multiple_of(image * toks + block * 64, 64), 64)
            upper = gradient[rows, :]
            gate = mod_ref[mod_at + gate_row + image : mod_at + gate_row + image + 1, :]
            lower = (upper * gate).astype(bf)
            target[rows, :] = lower
            return sums[0] + column_sums(upper * branch[rows, :]), sums[1] + column_sums(lower)

        zero = jnp.zeros((1, D), jnp.float32)
        gate, bias = lax.fori_loop(0, blocks, rows_of, (zero, zero))
        d_mod_ref[gate_row + image : gate_row + image + 1, :] = gate
        if image == 0:
            d_bias_ref[:, bias_cols] = bias
        else:
            d_bias_ref[:, bias_cols] += bias

    def modulate_back(image, first_row, source, passed, target):
        def rows_of(block, sums):
            rows = pl.ds(pl.multiple_of(image * toks + block * 64, 64), 64)
            scale_row = mod_at + first_row + 2 + image
            scale = mod_ref[scale_row : scale_row + 1, :]
            unit, inverse = normalized(source[rows, :])
            upper = total_buf[rows, :]
            inner = upper * (1.0 + scale)
            back = inverse * (
                inner
                - jnp.mean(inner, axis=-1, keepdims=True)
                - unit * jnp.mean(inner * unit, axis=-1, keepdims=True)
            )
            target[rows, :] = back + passed[rows, :]
            return sums[0] + column_sums(upper), sums[1] + column_sums(upper * unit)

        zero = jnp.zeros((1, D), jnp.float32)
        shift, scale = lax.fori_loop(0, blocks, rows_of, (zero, zero))
        d_mod_ref[first_row + image : first_row + image + 1, :] = shift
        d_mod_ref[first_row + 2 + image : first_row + 3 + image, :] = scale

    def attend_back(image, pair):
        rows = pl.ds(pl.multiple_of(image * toks, toks), toks)
        low = lax.broadcasted_iota(jnp.int32, (toks, 128), 1) < 64
        eighth = jnp.asarray(0.125, bf)
        queries = qkv_ref[rows, column_tile(pair, 128)] * eighth
        keys = qkv_ref[rows, column_tile(8 + pair, 128)]
        values = qkv_ref[rows, column_tile(16 + pair, 128)]
        upper = d_heads_buf[rows, column_tile(pair, 128)]
        keep = keep_ref[pl.ds(image, 1), :]
        zero = jnp.zeros_like(queries)
        total = jnp.zeros((toks, 128), jnp.float32)
        d_q, d_k, d_v = total, total, total
        for own in (low, jnp.logical_not(low)):
            own_q = jnp.where(own, queries, zero)
            own_up = jnp.where(own, upper, zero)
            probs = head_probs(own_q, keys, keep)
            d_probs = dot_nt(own_up, values)
            mean = jnp.sum(probs * d_probs, axis=-1, keepdims=True)
            d_scores = (probs * (d_probs - mean)).astype(bf)
            d_v = d_v + dot_tn(probs.astype(bf), own_up)
            d_q = d_q + dot_nn(d_scores, jnp.where(own, keys * eighth, zero))
            d_k = d_k + dot_tn(d_scores, own_q)
        d_qkv_buf[rows, column_tile(pair, 128)] = d_q.astype(bf)
        d_qkv_buf[rows, column_tile(8 + pair, 128)] = d_k.astype(bf)
        d_qkv_buf[rows, column_tile(16 + pair, 128)] = d_v.astype(bf)

    def add_product(first, image_rows, part):
        @pl.when(first)
        def _():
            total_buf[image_rows, :] = part

        @pl.when(jnp.logical_not(first))
        def _():
            total_buf[image_rows, :] += part

    def step(at):
        slot = lax.rem(at, 2)
        loads(at + 1, lambda copy: copy.start())
        loads(at, lambda copy: copy.wait())

        @pl.when(at == 0)
        def _():
            for image in range(images):
                gated(image, 10, grad_ref, down_ref, d_down_buf, slice(8 * D, 9 * D))
            saves[0].start()

        @pl.when(within(at, 1, 8))
        def _():
            tile = at - 1

            @pl.when(tile >= 2)
            def _():
                up_save(tile - 2, slot).wait()

            bias = jnp.zeros((1, HALF), jnp.float32)
            for image in range(images):
                rows = pl.ds(image * toks, toks)
                upper = dot_nt(d_down_buf[rows, :], tall_tile(slot))
                pre = pre_buf[slot, rows, :]
                square = pre * pre
                inner = jnp.tanh(GELU_IN * (pre + GELU_CUBE * square * pre))
                slope = 0.5 * (1.0 + inner) + 0.5 * pre * (1.0 - inner * inner) * (
                    GELU_IN * (1.0 + 3.0 * GELU_CUBE * square)
                )
                lower = (upper * slope).astype(bf)
                d_up_buf[slot, rows, :] = lower
                bias = bias + column_sums(lower)
                add_product(tile == 0, rows, dot_nt(lower, wide_tile(slot)))
            d_bias_ref[:, column_tile(tile + 8)] = bias
            up_save(tile, slot).start()

        @pl.when(at == 9)
        def _():
            for image in range(images):
                modulate_back(image, 6, x_one_ref, grad_ref, d_x_one_buf)
                gated(image, 4, d_x_one_buf, attn_ref, d_attn_buf, slice(3 * D, 4 * D))
            saves[1].start()

        @pl.when(within(at, 10, 2))
        def _():
            for image in range(images):
                rows = pl.ds(image * toks, toks)
                part = dot_nt(d_attn_buf[rows, column_tile(at - 10)], wide_tile(slot))
                add_product(at == 10, rows, part)

            @pl.when(at == 11)
            def _():
                d_heads_buf[...] = total_buf[...].astype(bf)

        @pl.when(within(at, 12, 8))
        def _():
            for turn in range(2):
                item = (at - 12) * 2 + turn
                attend_back(item // 8, lax.rem(item, 8))

        @pl.when(at == 20)
        def _():
            saves[2].start()

        @pl.when(within(at, 20, 6))
        def _():
            cols = column_tile(at - 20)
            bias = jnp.zeros((1, HALF), jnp.float32)
            for image in range(images):
                rows = pl.ds(image * toks, toks)
                lower = d_qkv_buf[rows, cols]
                bias = bias + column_sums(lower)
                add_product(at == 20, rows, dot_nt(lower, wide_tile(slot)))
            d_bias_ref[:, cols] = bias

        @pl.when(at == BACKWARD_STEPS - 1)
        def _():
            for image in range(images):
                modulate_back(image, 0, x_ref, d_x_one_buf, total_buf)
            saves[3].start()

    def finish():
        for tile in (6, 7):
            up_save(tile, tile % 2).wait()
        for copy in saves:
            copy.wait()

    return step, finish


BACKWARD_OUTS = [
    (D, jnp.float32),
    (D, jnp.bfloat16),
    (FF, jnp.bfloat16),
    (D, jnp.bfloat16),
    (3 * D, jnp.bfloat16),
]


def backward_scratch(toks):
    bf, f32 = jnp.bfloat16, jnp.float32
    return [
        pltpu.VMEM((toks, D), f32),
        pltpu.VMEM((toks, D), f32),
        pltpu.VMEM((toks, D), bf),
        pltpu.VMEM((2, toks, HALF), bf),
        pltpu.VMEM((toks, D), bf),
        pltpu.VMEM((toks, D), bf),
        pltpu.VMEM((toks, 3 * D), bf),
        pltpu.VMEM((2, toks, HALF), f32),
        pltpu.VMEM((2, 4, 2, 2, 64, HALF), bf),
        pltpu.VMEM((2, 2, 256, D), bf),
        pltpu.SemaphoreType.DMA((3, 2)),
        pltpu.SemaphoreType.DMA((2,)),
        pltpu.SemaphoreType.DMA((4,)),
    ]


def backward_kernel(mod_at, *refs):
    step, finish = backward_pieces(refs, mod_at)

    def turn(at, carry):
        step(at)
        return carry

    lax.fori_loop(0, BACKWARD_STEPS, turn, 0)
    finish()


def backward_layer(grad, x, saved, mods, mod_at, keep, weights):
    a_one, qkv, merged, attn, x_one, a_two, pre, act, down, _ = saved
    toks = x.shape[0]
    vmem = pl.BlockSpec(memory_space=pltpu.VMEM)
    hbm = pl.BlockSpec(memory_space=pl.ANY)
    outs = pl.pallas_call(
        functools.partial(backward_kernel, mod_at),
        out_shape=[jax.ShapeDtypeStruct((toks, width), kind) for width, kind in BACKWARD_OUTS]
        + [
            jax.ShapeDtypeStruct((12, D), jnp.float32),
            jax.ShapeDtypeStruct((1, 9 * D), jnp.float32),
        ],
        in_specs=[vmem] * 8 + [hbm] * 5,
        out_specs=[hbm] * len(BACKWARD_OUTS) + [vmem] * 2,
        scratch_shapes=backward_scratch(toks),
        compiler_params=pltpu.CompilerParams(vmem_limit_bytes=56 * 1024 * 1024),
        cost_estimate=pl.CostEstimate(
            flops=28 * toks * D * D, bytes_accessed=80 * 1024 * 1024, transcendentals=4 * toks * D
        ),
    )(grad, x, x_one, attn, down, qkv, mods, keep, pre, *grouped(weights))
    d_x, d_down, d_up, d_attn, d_qkv, d_mod, d_bias = outs
    factors = (merged, a_one, a_two, act, d_attn, d_qkv, d_up, d_down)
    return d_x, d_mod, factors, d_bias


def gather_pieces(lines, refs):
    layers = (len(refs) - 7) // 8
    pairs = list(zip(refs[: 4 * layers], refs[4 * layers : 8 * layers]))
    own_sem, zp_sem, zq_sem, yp_sem, yq_sem, x_sem, core_sem = refs[8 * layers :]
    firsts = [12 * layer + first for layer in range(layers) for first in (0, 3, 4, 8)]
    total = 12 * layers
    seq = lax.axis_index("seq")
    dp = lax.axis_index("dp")
    core = lax.rem(dp, 2)
    why = lax.rem(dp // 2, 2)
    zed = dp // 4
    core_peer = {"seq": seq, "dp": dp + 1 - 2 * core}
    x_peer = {"seq": 1 - seq, "dp": dp}
    y_peer = {"seq": seq, "dp": dp + 2 - 4 * why}
    z_peers = [
        {"seq": seq, "dp": lax.rem(zed + step, lines) * 4 + 2 * why + core}
        for step in range(1, lines)
    ]
    keeps = [
        pltpu.make_async_copy(own, every.at[zed, why, core], own_sem.at[at])
        for at, (own, every) in enumerate(pairs)
    ]
    for keep in keeps:
        keep.start()
    for keep in keeps:
        keep.wait()
    barrier = pltpu.get_barrier_semaphore()
    for peer in [core_peer, x_peer, y_peer] + z_peers:
        pl.semaphore_signal(barrier, inc=1, device_id=peer, device_id_type=MESH)
    pl.semaphore_wait(barrier, 2 + lines)

    def places(kind, unit):
        at = unit - firsts[kind]
        if kind % 4 == 3:
            return pl.multiple_of(at * 64, 64), 0
        return 0, pl.multiple_of(at * D, D)

    def span(first, begin, size):
        return pl.ds(pl.multiple_of(first + begin, 128), size)

    def copies(stage, kind, unit):
        slot = unit
        own, every = pairs[kind]
        row, first = places(kind, unit)
        rows = pl.ds(row, 64)
        mine = pl.ds(pl.multiple_of(row + seq * 32, 32), 32)
        halved = span(first, 0, SHARED)
        rest = span(first, SHARED, D - SHARED)
        whole = span(first, 0, D)

        def remote(source, target, sems, peer):
            return pltpu.make_async_remote_copy(
                src_ref=source,
                dst_ref=target,
                send_sem=sems.at[0],
                recv_sem=sems.at[1],
                device_id=peer,
                device_id_type=MESH,
            )

        def same(view, sems, peer):
            return remote(view, view, sems, peer)

        if stage == 0:
            return [
                remote(own.at[band, cols], every.at[zed, why, core, band, cols], sems, peer)
                for band, cols, kinds in ((mine, halved, zp_sem), (rows, rest, zq_sem))
                for sems, peer in [(kinds.at[slot, at], z_peers[at]) for at in range(lines - 1)]
            ]
        if stage == 1:
            return [
                same(every.at[:, why, core, mine, halved], yp_sem.at[slot], y_peer),
                same(every.at[:, why, core, rows, rest], yq_sem.at[slot], y_peer),
            ]
        if stage == 2:
            return [same(every.at[:, :, core, mine, halved], x_sem.at[slot], x_peer)]
        return [same(every.at[:, :, core, rows, whole], core_sem.at[slot], core_peer)]

    def each_kind(unit, run):
        ends = firsts[1:] + [total]
        for kind in range(len(firsts)):

            @pl.when(jnp.logical_and(unit >= firsts[kind], unit < ends[kind]))
            def _():
                run(kind)

    def begin(stage, unit):
        def run(kind):
            for copy in copies(stage, kind, unit):
                copy.start()

        each_kind(unit, run)

    def finish(stage, unit):
        def run(kind):
            for copy in copies(stage, kind, unit):
                copy.wait()

        each_kind(unit, run)

    def step(at):
        finish(3, at - sum(GATHER_LAGS))
        for stage in (3, 2, 1):
            behind = sum(GATHER_LAGS[:stage])
            finish(stage - 1, at - behind)
            begin(stage, at - behind)
        begin(0, at)

    return step, total + sum(GATHER_LAGS)


def gather_scratch(lines, layers):
    dma = pltpu.SemaphoreType.DMA
    units = 12 * layers
    return [
        dma((4 * layers,)),
        dma((units, lines - 1, 2)),
        dma((units, lines - 1, 2)),
        dma((units, 2)),
        dma((units, 2)),
        dma((units, 2)),
        dma((units, 2)),
    ]


def modulation_pieces(lines, refs):
    (
        partial_ref,
        bias_ref,
        mods_ref,
        core_in,
        core_total,
        y_in,
        y_total,
        z_in,
        core_sem,
        y_sem,
        z_sem,
    ) = refs
    seq = lax.axis_index("seq")
    dp = lax.axis_index("dp")
    core = lax.rem(dp, 2)
    why = lax.rem(dp // 2, 2)
    zed = dp // 4

    def remote(source, target, sems, peer):
        return pltpu.make_async_remote_copy(
            src_ref=source,
            dst_ref=target,
            send_sem=sems.at[0],
            recv_sem=sems.at[1],
            device_id={"seq": seq, "dp": peer},
            device_id_type=MESH,
        )

    to_core = remote(partial_ref.at[:, :, 1 - core], core_in, core_sem, dp + 1 - 2 * core)
    to_y = remote(core_total.at[:, 1 - why], y_in, y_sem, dp + 2 - 4 * why)
    to_z = []
    for ahead in range(1, lines):
        there = lax.rem(zed + ahead, lines)
        to_z.append(
            remote(
                y_total.at[there],
                z_in.at[ahead - 1],
                z_sem.at[ahead - 1],
                there * 4 + 2 * why + core,
            )
        )

    def step(at):
        @pl.when(at == 0)
        def _():
            to_core.start()

        @pl.when(at == 1)
        def _():
            to_core.wait()
            core_total[...] = partial_ref[:, :, core] + core_in[...]
            to_y.start()

        @pl.when(at == 4)
        def _():
            to_y.wait()
            y_total[...] = core_total[:, why] + y_in[...]
            for copy in to_z:
                copy.start()

        @pl.when(at == 8)
        def _():
            total = y_total[zed] + bias_ref[...]
            for ahead, copy in enumerate(to_z):
                copy.wait()
                total = total + z_in[ahead]
            mods_ref[...] = total

    return step


def modulation_scratch(lines, rows):
    dma = pltpu.SemaphoreType.DMA
    f32 = jnp.float32
    return [
        pltpu.VMEM((lines, 2, rows, D), f32),
        pltpu.VMEM((lines, 2, rows, D), f32),
        pltpu.VMEM((lines, rows, D), f32),
        pltpu.VMEM((lines, rows, D), f32),
        pltpu.VMEM((lines - 1, rows, D), f32),
        dma((2,)),
        dma((2,)),
        dma((lines - 1, 2)),
    ]


def whole_forward_kernel(lines, *refs):
    refs = list(refs)

    def take(count):
        taken, refs[:] = tuple(refs[:count]), refs[count:]
        return taken

    own = take(8)
    partial_ref, mod_bias, x_ref, first_bias, second_bias, keep = take(6)
    every = take(8)
    first_outs, second_outs = take(len(FORWARD_OUTS)), take(len(FORWARD_OUTS))
    (mods,) = take(1)
    gather_sems = take(7)
    mod_scratch = take(8)
    scratch = tuple(refs)
    gather, steps = gather_pieces(lines, own + every + gather_sems)
    modulate_step = modulation_pieces(lines, (partial_ref, mod_bias, mods) + mod_scratch)
    first, first_finish = forward_pieces(
        (x_ref, mods, first_bias, keep) + every[:4] + first_outs + scratch, 0
    )
    second, second_finish = forward_pieces(
        (scratch[9], mods, second_bias, keep) + every[4:] + second_outs + scratch, 12
    )

    def run(step, begin, end):
        def one(at, carry):
            step(at)
            return carry

        lax.fori_loop(begin, end, one, 0)

    def turn(at, carry):
        gather(at)
        modulate_step(at)

        @pl.when(within(at, 10, 13))
        def _():
            run(first, 2 * (at - 10), 2 * (at - 9))

        @pl.when(at == 23)
        def _():
            first_finish()

        @pl.when(at >= 24)
        def _():
            run(second, 18 * (at - 24) // 7, 18 * (at - 23) // 7)

        return carry

    lax.fori_loop(0, steps + 4, turn, 0)
    second_finish()


def whole_forward(own, partial, mod_bias, x, biases, keep, lines):
    toks = x.shape[0]
    rows = mod_bias.shape[0]
    vmem = pl.BlockSpec(memory_space=pltpu.VMEM)
    hbm = pl.BlockSpec(memory_space=pl.ANY)
    layer_outs = [jax.ShapeDtypeStruct((toks, width), kind) for width, kind in FORWARD_OUTS]
    outs = pl.pallas_call(
        functools.partial(whole_forward_kernel, lines),
        out_shape=[
            jax.ShapeDtypeStruct((lines, 2, 2) + each.shape, jnp.bfloat16) for each in own
        ]
        + layer_outs
        + layer_outs
        + [jax.ShapeDtypeStruct((rows, D), jnp.float32)],
        in_specs=[vmem] * 14,
        out_specs=[hbm] * (8 + 2 * len(FORWARD_OUTS)) + [vmem],
        scratch_shapes=gather_scratch(lines, 2)
        + modulation_scratch(lines, rows)
        + forward_scratch(toks),
        compiler_params=pltpu.CompilerParams(
            collective_id=2, has_side_effects=True, vmem_limit_bytes=58 * 1024 * 1024
        ),
        cost_estimate=pl.CostEstimate(
            flops=48 * toks * D * D,
            bytes_accessed=24 * 4 * lines * 64 * D * 8,
            transcendentals=8 * toks * D,
        ),
    )(*own, partial, mod_bias, x, *biases, keep)
    weights = outs[:8]
    count = len(FORWARD_OUTS)
    saved = [outs[8 : 8 + count], outs[8 + count : 8 + 2 * count]]
    return [weights[:4], weights[4:]], saved, outs[-1]


def gather_small_kernel(lines, own_ref, every_ref, z_sem, y_sem, core_sem):
    seq = lax.axis_index("seq")
    dp = lax.axis_index("dp")
    core = lax.rem(dp, 2)
    why = lax.rem(dp // 2, 2)
    zed = dp // 4
    core_peer = {"seq": seq, "dp": dp + 1 - 2 * core}
    y_peer = {"seq": seq, "dp": dp + 2 - 4 * why}
    z_peers = [
        {"seq": seq, "dp": lax.rem(zed + step, lines) * 4 + 2 * why + core}
        for step in range(1, lines)
    ]
    barrier = pltpu.get_barrier_semaphore()
    for peer in [core_peer, y_peer] + z_peers:
        pl.semaphore_signal(barrier, inc=1, device_id=peer, device_id_type=MESH)
    every_ref[zed, why, core] = own_ref[...]
    pl.semaphore_wait(barrier, 1 + lines)

    def remote(source, target, sems, peer):
        return pltpu.make_async_remote_copy(
            src_ref=source,
            dst_ref=target,
            send_sem=sems.at[0],
            recv_sem=sems.at[1],
            device_id=peer,
            device_id_type=MESH,
        )

    copies = [
        remote(own_ref, every_ref.at[zed, why, core], z_sem.at[at], peer)
        for at, peer in enumerate(z_peers)
    ]
    for copy in copies:
        copy.start()
    for copy in copies:
        copy.wait()
    for view, sems, peer in (
        (every_ref.at[:, why, core], y_sem, y_peer),
        (every_ref.at[:, :, core], core_sem, core_peer),
    ):
        copy = remote(view, view, sems, peer)
        copy.start()
        copy.wait()


def gather_small(own, lines, collective_id):
    dma = pltpu.SemaphoreType.DMA
    every = pl.pallas_call(
        functools.partial(gather_small_kernel, lines),
        out_shape=jax.ShapeDtypeStruct((lines, 2, 2) + own.shape, own.dtype),
        in_specs=[pl.BlockSpec(memory_space=pltpu.VMEM)],
        out_specs=pl.BlockSpec(memory_space=pltpu.VMEM),
        scratch_shapes=[dma((lines - 1, 2)), dma((2,)), dma((2,))],
        compiler_params=pltpu.CompilerParams(collective_id=collective_id, has_side_effects=True),
        cost_estimate=pl.CostEstimate(
            flops=0, bytes_accessed=own.size * 32 * lines, transcendentals=0
        ),
    )(own)
    return every.reshape(-1, own.shape[-1])


def gather_rows(shard):
    return lax.all_gather(shard.astype(jnp.bfloat16), "dp", axis=0, tiled=True)


def kernels_fit():
    dp_parts = lax.axis_size("dp")
    return (
        lax.axis_size("seq") == 2
        and dp_parts % 4 == 0
        and D // dp_parts == 64
        and FF // dp_parts == PARTS * 64
    )


def reduce_rows(partial):
    owned = lax.psum_scatter(
        partial.astype(jnp.bfloat16), "dp", scatter_dimension=0, tiled=True
    )
    return lax.psum(owned, "seq").astype(jnp.float32)


def weight_sums(factors):
    dp_parts = lax.axis_size("dp")
    if not kernels_fit():
        return [
            (
                reduce_rows(matdot(a_one.T, d_qkv)),
                reduce_rows(matdot(merged.T, d_attn)),
                reduce_rows(matdot(a_two.T, d_up)),
                reduce_rows(matdot(activated.T, d_down)),
            )
            for merged, a_one, a_two, activated, d_attn, d_qkv, d_up, d_down in factors
        ]
    units = scatter_sums([each for layer in factors for each in layer], dp_parts // 4)
    units = units.reshape(LAYERS, 12, PARTS, 64, TILE)

    def by_columns(some):
        return some.transpose(2, 0, 1, 3).reshape(64, some.shape[0] * D)

    return [
        (
            by_columns(layer[1:4]),
            by_columns(layer[:1]),
            by_columns(layer[4:8]),
            layer[8:].transpose(1, 2, 0, 3).reshape(PARTS * 64, D),
        )
        for layer in units
    ]


def adamw(weight, gradient, first, second, rate):
    first_new = BETA_ONE * first + (1.0 - BETA_ONE) * gradient
    second_new = BETA_TWO * second + (1.0 - BETA_TWO) * gradient * gradient
    first_hat = first_new / (1.0 - BETA_ONE**STEP)
    second_hat = second_new / (1.0 - BETA_TWO**STEP)
    return (
        weight - rate * (first_hat / (jnp.sqrt(second_hat) + EPSILON) + DECAY * weight),
        first_new,
        second_new,
    )


def body(
    latents,
    noise_target,
    pad_mask,
    labels,
    timesteps,
    embed_rows,
    first_embed,
    second_embed,
    class_table,
    first_table,
    second_table,
    qkv_weight,
    first_qkv,
    second_qkv,
    proj_weight,
    first_proj,
    second_proj,
    up_weight,
    first_up,
    second_up,
    down_weight,
    first_down,
    second_down,
    cond_weight,
    first_cond,
    second_cond,
    head_weight,
    first_head,
    second_head,
    all_biases,
    first_bias,
    second_bias,
):
    seq_parts = lax.axis_size("seq")
    dp_parts = lax.axis_size("dp")
    seq_at = lax.axis_index("seq")
    dp_at = lax.axis_index("dp")
    lines = dp_parts // 4
    group, half_rows, _ = latents.shape
    images = group // seq_parts
    everyone = group * dp_parts
    own_cols = embed_rows.shape[1]
    own_place = dp_at * own_cols
    cond_cols = cond_weight.shape[1]
    pieces = cond_cols // D
    bias_base = 3 * D + cond_cols
    by_kernel = kernels_fit()
    packed = jnp.concatenate(
        [latents, noise_target, pad_mask.astype(jnp.float32)[:, :, None]], axis=2
    )
    shards = [
        weight[at].astype(jnp.bfloat16)
        for at in range(LAYERS)
        for weight in (qkv_weight, proj_weight, up_weight, down_weight)
    ]
    narrow = jnp.concatenate(
        [embed_rows[: PATCH_IN + FREQ].T, head_weight], axis=1
    ).astype(jnp.bfloat16)
    if by_kernel:
        ids = jnp.stack([labels, timesteps])
        parts = jnp.stack([ids // 32, ids % 32]).astype(jnp.bfloat16).reshape(-1, 1)
        parts = jnp.pad(parts, ((0, own_cols - parts.shape[0]), (0, 0)))
        width = narrow.shape[1]
        block = jnp.concatenate(
            [narrow, parts, jnp.zeros((own_cols, 383 - width), jnp.bfloat16)], axis=1
        )
        small = gather_small(block, lines, 4)
        parts = small[:, width].astype(jnp.float32).reshape(dp_parts, own_cols)[:, : 4 * group]
        parts = parts.reshape(dp_parts, 2, 2, group)
        ids = (parts[:, 0] * 32.0 + parts[:, 1]).astype(jnp.int32)
        ids = ids.transpose(1, 0, 2).reshape(2, everyone)
        theirs = lax.dynamic_slice(
            packed, ((1 - seq_at) * images, 0, 0), (images,) + packed.shape[1:]
        )
        mine = lax.dynamic_slice(packed, (seq_at * images, 0, 0), (images,) + packed.shape[1:])
        came = lax.ppermute(theirs, "seq", [(0, 1), (1, 0)])
        packed = jnp.concatenate(
            [jnp.where(seq_at == 0, mine, came), jnp.where(seq_at == 0, came, mine)], axis=1
        )
    else:
        small = lax.all_gather(narrow, "dp", axis=0, tiled=True)
        ids = lax.all_gather(jnp.stack([labels, timesteps]), "dp", axis=1, tiled=True)
        packed = lax.all_to_all(packed, "seq", split_axis=0, concat_axis=1, tiled=True)
    tok_rows = packed.shape[1]
    toks = images * tok_rows
    latents, noise_target, keep_rows = (
        packed[:, :, :PATCH_IN],
        packed[:, :, PATCH_IN : 2 * PATCH_IN],
        packed[:, :, 2 * PATCH_IN],
    )
    patch_part = small[:, :PATCH_IN]
    freq_part = small[:, PATCH_IN : PATCH_IN + FREQ]
    head_full = small[:, PATCH_IN + FREQ : PATCH_IN + FREQ + OUT_CH]
    time_own = embed_rows[PATCH_IN + FREQ :].astype(jnp.bfloat16)
    cond_own = cond_weight.astype(jnp.bfloat16)

    features = time_features(ids[1], FREQ).astype(jnp.bfloat16)
    time_pre = dot_nt(features, freq_part) + all_biases[D : 2 * D]
    time_hidden = jax.nn.silu(time_pre).astype(jnp.bfloat16)
    second_bias_own = lax.dynamic_slice(all_biases, (2 * D + own_place,), (own_cols,))
    onehot = (ids[0][:, None] == jnp.arange(NCLASS, dtype=jnp.int32)[None, :]).astype(jnp.float32)
    condition = (
        matdot(time_hidden, time_own)
        + second_bias_own
        + matdot(onehot.astype(jnp.bfloat16), class_table.astype(jnp.bfloat16))
    )
    cond_act = jax.nn.silu(condition).astype(jnp.bfloat16)
    plane_act = lax.dynamic_index_in_dim(
        cond_act.reshape(dp_parts, seq_parts, images, own_cols), seq_at, 1, keepdims=False
    ).reshape(dp_parts * images, own_cols)
    partial = matdot(plane_act, cond_own).reshape(dp_parts, images, pieces, D)
    partial = partial.transpose(0, 2, 1, 3).reshape(dp_parts, pieces * images, D)
    mod_bias = jnp.repeat(all_biases[3 * D : bias_base].reshape(pieces, D), images, axis=0)

    position = position_table(jnp.arange(tok_rows, dtype=jnp.int32), D, GRID)
    flat_in = latents.astype(jnp.bfloat16).reshape(toks, PATCH_IN)
    stream = (dot_nt(flat_in, patch_part) + all_biases[:D]).reshape(
        images, tok_rows, D
    ) + position[None]
    stream = stream.reshape(toks, D)
    layer_bias = [
        all_biases[bias_base + at * 9 * D : bias_base + (at + 1) * 9 * D].reshape(1, 9 * D)
        for at in range(LAYERS)
    ]
    if by_kernel:
        weights_kept, saved_kept, mods = whole_forward(
            shards,
            partial.reshape(lines, 2, 2, pieces * images, D),
            mod_bias,
            stream,
            layer_bias,
            keep_rows,
            lines,
        )
    else:
        mods = mod_bias + lax.psum_scatter(
            partial, "dp", scatter_dimension=0, tiled=True
        ).reshape(pieces * images, D)
        weights_kept = [
            [gather_rows(shard) for shard in shards[4 * at : 4 * at + 4]] for at in range(LAYERS)
        ]
        saved_kept = []
        upper = stream
        for at in range(LAYERS):
            saved_kept.append(
                forward_layer(
                    upper, mods, 6 * images * at, layer_bias[at], keep_rows, weights_kept[at]
                )
            )
            upper = saved_kept[at][-1]
    inputs_kept = [stream] + [saved[-1] for saved in saved_kept]
    final, time_own = lax.optimization_barrier((inputs_kept[-1], time_own))
    time_full = lax.all_gather(time_own, "dp", axis=1, tiled=True)
    final_at = 6 * LAYERS * images
    final_shift = mods[final_at : final_at + images]
    final_scale = mods[final_at + images :]
    moved, final_back = jax.vjp(
        modulate, final.reshape(images, tok_rows, D), final_shift, final_scale
    )
    a_final = moved.astype(jnp.bfloat16).reshape(toks, D)
    head_out = matdot(a_final, head_full) + all_biases[NBIAS - OUT_CH :]
    split_out = head_out.reshape(images, tok_rows, 4, 2, OUT_CH // 8)
    predicted = split_out[:, :, :, 0, :].reshape(images, tok_rows, PATCH_IN)
    errors = predicted - noise_target
    loss_part = jnp.sum(keep_rows[:, :, None] * errors * errors)
    count_part = PATCH_IN * jnp.sum(keep_rows)
    d_pred = (2.0 * keep_rows[:, :, None] * errors).reshape(images, tok_rows, 4, 1, OUT_CH // 8)
    d_head = (
        jnp.concatenate([d_pred, jnp.zeros_like(d_pred)], axis=3)
        .reshape(toks, OUT_CH)
        .astype(jnp.bfloat16)
    )
    g_head = matdot(a_final.T, d_head)
    d_a_final = dot_nt(d_head, head_full).reshape(images, tok_rows, D)
    d_stream, d_final_shift, d_final_scale = final_back(d_a_final)
    d_stream = d_stream.reshape(toks, D)
    layer_factors = [None] * LAYERS
    layer_bias_grads = [None] * LAYERS
    modul_grads = [None] * LAYERS
    for at in reversed(range(LAYERS)):
        d_stream, d_mod, layer_factors[at], d_bias = backward_layer(
            d_stream,
            inputs_kept[at],
            saved_kept[at],
            mods,
            6 * images * at,
            keep_rows,
            weights_kept[at],
        )
        modul_grads[at] = d_mod.reshape(6, images, D).transpose(1, 0, 2).reshape(images, 6 * D)
        layer_bias_grads[at] = d_bias.reshape(-1)
    d_mod_own = jnp.concatenate(modul_grads + [d_final_shift, d_final_scale], axis=1).astype(
        jnp.bfloat16
    )
    d_patch = d_stream.astype(jnp.bfloat16)
    flat = jnp.concatenate(
        [column_sum(d_patch), jnp.zeros((2 * D,), jnp.float32), column_sum(d_mod_own)]
        + layer_bias_grads
        + [column_sum(d_head), loss_part[None], count_part[None]]
        + [matdot(flat_in.T, d_patch).reshape(-1), g_head.reshape(-1)]
    )
    flat, d_mod_own, layer_factors = lax.optimization_barrier((flat, d_mod_own, layer_factors))
    flat = lax.psum(flat, ("seq", "dp"))
    d_modulation = lax.all_gather(d_mod_own, ("dp", "seq"), axis=0, tiled=True)
    layer_sums = weight_sums(layer_factors)
    d_cond_act = lax.dot_general(
        d_modulation, cond_own, (((1,), (1,)), ((), ())), preferred_element_type=jnp.float32
    )
    _, silu_back = jax.vjp(jax.nn.silu, condition)
    d_condition = silu_back(d_cond_act)[0]
    d_time_own = d_condition.astype(jnp.bfloat16)
    d_time = lax.all_gather(d_time_own, "dp", axis=1, tiled=True)
    d_time_hidden = lax.dot_general(
        d_time, time_full, (((1,), (1,)), ((), ())), preferred_element_type=jnp.float32
    )
    _, time_back = jax.vjp(jax.nn.silu, time_pre)
    d_time_pre = time_back(d_time_hidden)[0].astype(jnp.bfloat16)
    s_cond = matdot(cond_act.T, d_modulation)
    s_table = jnp.dot(onehot.T, d_condition, precision=lax.Precision.HIGHEST)
    g_time = matdot(time_hidden.T, d_time_own)
    g_freq = matdot(
        features.T, lax.dynamic_slice(d_time_pre, (0, own_place), (everyone, own_cols))
    )
    bias_grad = jnp.concatenate(
        [flat[:D], column_sum(d_time_pre), column_sum(d_time), flat[3 * D : NBIAS]]
    )
    loss_sum, loss_count = flat[NBIAS], flat[NBIAS + 1]
    patch_at = NBIAS + 2
    head_at = patch_at + PATCH_IN * D
    s_patch = lax.dynamic_slice(
        flat[patch_at:head_at].reshape(PATCH_IN, D), (0, own_place), (PATCH_IN, own_cols)
    )
    s_head = lax.dynamic_slice(
        flat[head_at:].reshape(D, OUT_CH), (own_place, 0), (own_cols, OUT_CH)
    )
    s_embed = jnp.concatenate([s_patch, g_freq, g_time], axis=0)
    s_qkv = jnp.stack([layer_sums[at][0] for at in range(LAYERS)])
    s_proj = jnp.stack([layer_sums[at][1] for at in range(LAYERS)])
    s_up = jnp.stack([layer_sums[at][2] for at in range(LAYERS)])
    s_down = jnp.stack([layer_sums[at][3] for at in range(LAYERS)])
    new_embed, new_first_embed, new_second_embed = adamw(
        embed_rows, s_embed, first_embed, second_embed, RATE_MATRIX
    )
    new_table, new_first_table, new_second_table = adamw(
        class_table, s_table, first_table, second_table, RATE_TABLE
    )
    new_qkv, new_first_qkv, new_second_qkv = adamw(
        qkv_weight, s_qkv, first_qkv, second_qkv, RATE_MATRIX
    )
    new_proj, new_first_proj, new_second_proj = adamw(
        proj_weight, s_proj, first_proj, second_proj, RATE_MATRIX
    )
    new_up, new_first_up, new_second_up = adamw(up_weight, s_up, first_up, second_up, RATE_MATRIX)
    new_down, new_first_down, new_second_down = adamw(
        down_weight, s_down, first_down, second_down, RATE_MATRIX
    )
    new_cond, new_first_cond, new_second_cond = adamw(
        cond_weight, s_cond, first_cond, second_cond, RATE_MATRIX
    )
    new_head, new_first_head, new_second_head = adamw(
        head_weight, s_head, first_head, second_head, RATE_MATRIX
    )
    new_bias, new_first_bias, new_second_bias = adamw(
        all_biases, bias_grad, first_bias, second_bias, RATE_BIAS
    )
    return (
        loss_sum,
        loss_count,
        new_embed,
        new_first_embed,
        new_second_embed,
        new_table,
        new_first_table,
        new_second_table,
        new_qkv,
        new_first_qkv,
        new_second_qkv,
        new_proj,
        new_first_proj,
        new_second_proj,
        new_up,
        new_first_up,
        new_second_up,
        new_down,
        new_first_down,
        new_second_down,
        new_cond,
        new_first_cond,
        new_second_cond,
        new_head,
        new_first_head,
        new_second_head,
        new_bias,
        new_first_bias,
        new_second_bias,
    )


def solution(mesh):
    placed = (
        P("dp", "seq", None),
        P("dp", "seq", None),
        P("dp", "seq"),
        P("dp"),
        P("dp"),
        P(None, "dp"),
        P(None, "dp"),
        P(None, "dp"),
        P(None, "dp"),
        P(None, "dp"),
        P(None, "dp"),
        P(None, "dp", None),
        P(None, "dp", None),
        P(None, "dp", None),
        P(None, "dp", None),
        P(None, "dp", None),
        P(None, "dp", None),
        P(None, "dp", None),
        P(None, "dp", None),
        P(None, "dp", None),
        P(None, "dp", None),
        P(None, "dp", None),
        P(None, "dp", None),
        P("dp", None),
        P("dp", None),
        P("dp", None),
        P("dp", None),
        P("dp", None),
        P("dp", None),
        P(),
        P(),
        P(),
    )
    return jax.shard_map(
        body,
        mesh=mesh,
        in_specs=placed,
        out_specs=(
            P(),
            P(),
            P(None, "dp"),
            P(None, "dp"),
            P(None, "dp"),
            P(None, "dp"),
            P(None, "dp"),
            P(None, "dp"),
            P(None, "dp", None),
            P(None, "dp", None),
            P(None, "dp", None),
            P(None, "dp", None),
            P(None, "dp", None),
            P(None, "dp", None),
            P(None, "dp", None),
            P(None, "dp", None),
            P(None, "dp", None),
            P(None, "dp", None),
            P(None, "dp", None),
            P(None, "dp", None),
            P("dp", None),
            P("dp", None),
            P("dp", None),
            P("dp", None),
            P("dp", None),
            P("dp", None),
            P(),
            P(),
            P(),
        ),
        check_vma=False,
    )
```

```python
import functools
import math

import jax
import jax.numpy as jnp
from jax import lax
from jax.experimental import pallas as pl
from jax.experimental.pallas import tpu as pltpu
from jax.sharding import PartitionSpec as P

D = 1024
HEADS = 16
HEAD_DIM = 64
FF = 4096
NCLASS = 1001
FREQ = 256
OUT_CH = 32
PATCH_IN = 16
GRID = 16
LAYERS = 2
STEP = 10
NBIAS = 35872


BETA_ONE = 0.9
BETA_TWO = 0.999
EPSILON = 1e-08
DECAY = 0.01
RATE_MATRIX = 0.06
RATE_TABLE = 0.4
RATE_BIAS = 0.2

MESH = pl.DeviceIdType.MESH
TILE = 256
PARTS = 4
SHARED = 640
GATHER_LAGS = (2, 2, 2, 1)
HALF = 512
GELU_IN = math.sqrt(2.0 / math.pi)
GELU_CUBE = 0.044715
FORWARD_STEPS = 26
BACKWARD_STEPS = 27


def matdot(left, right):
    return jnp.dot(left, right, preferred_element_type=jnp.float32)


def layer_norm(stream):
    row_mean = jnp.mean(stream, axis=-1, keepdims=True)
    centered = stream - row_mean
    variance = jnp.mean(centered * centered, axis=-1, keepdims=True)
    return centered * lax.rsqrt(variance + 1e-06)


def modulate(stream, shift_by, scale_by):
    return layer_norm(stream) * (1.0 + scale_by[:, None, :]) + shift_by[:, None, :]


def position_table(position_ids, feature_width, grid_side):
    quarter_width = feature_width // 4
    omegas = 1.0 / 10000.0 ** (jnp.arange(quarter_width, dtype=jnp.float32) / quarter_width)
    col_angle = (position_ids % grid_side).astype(jnp.float32)[:, None] * omegas[None, :]
    row_angle = (position_ids // grid_side).astype(jnp.float32)[:, None] * omegas[None, :]
    return jnp.concatenate(
        [jnp.sin(col_angle), jnp.cos(col_angle), jnp.sin(row_angle), jnp.cos(row_angle)], axis=1
    )


def time_features(timesteps, feature_width):
    half_width = feature_width // 2
    frequencies = jnp.exp(
        -math.log(10000.0) * jnp.arange(half_width, dtype=jnp.float32) / half_width
    )
    angles = timesteps.astype(jnp.float32)[:, None] * frequencies[None, :]
    return jnp.concatenate([jnp.cos(angles), jnp.sin(angles)], axis=1)


def column_sum(grad_bf):
    return jnp.sum(grad_bf.astype(jnp.float32), axis=0)


def dot_nn(left, right):
    return jnp.dot(left, right, preferred_element_type=jnp.float32)


def dot_nt(left, right):
    return lax.dot_general(
        left, right, (((1,), (1,)), ((), ())), preferred_element_type=jnp.float32
    )


def dot_tn(left, right):
    return lax.dot_general(
        left, right, (((0,), (0,)), ((), ())), preferred_element_type=jnp.float32
    )


def column_tile(at, size=HALF):
    return pl.ds(pl.multiple_of(at * size, size), size)


def normalized(rows):
    centered = rows - jnp.mean(rows, axis=-1, keepdims=True)
    variance = jnp.mean(centered * centered, axis=-1, keepdims=True)
    inverse = lax.rsqrt(variance + 1e-06)
    return centered * inverse, inverse


def head_probs(queries, keys, keep):
    scores = jnp.where(keep > 0, dot_nt(queries, keys), -1000000000.0)
    raised = jnp.exp(scores - jnp.max(scores, axis=-1, keepdims=True))
    return raised * (1.0 / jnp.sum(raised, axis=-1, keepdims=True))


def within(at, first, size):
    return jnp.logical_and(at >= first, at < first + size)


def forward_pieces(refs, mod_at):
    (
        x_ref,
        mod_ref,
        bias_ref,
        keep_ref,
        w_qkv,
        w_proj,
        w_up,
        w_down,
        a_one_out,
        qkv_out,
        merged_out,
        attn_out,
        x_one_out,
        a_two_out,
        pre_out,
        act_out,
        down_out,
        x_two_out,
        a_buf,
        qkv_buf,
        merged_buf,
        attn_buf,
        x_one_buf,
        a_two_buf,
        pre_buf,
        act_buf,
        down_buf,
        x_two_buf,
        wide_buf,
        tall_buf,
        load_sem,
        tile_sem,
        save_sem,
    ) = refs
    images, toks = keep_ref.shape
    bf = jnp.bfloat16

    def save(at, source, target):
        return pltpu.make_async_copy(source, target, save_sem.at[at])

    saves = [
        save(at, *pair)
        for at, pair in enumerate(
            [
                (a_buf, a_one_out),
                (qkv_buf, qkv_out),
                (merged_buf, merged_out),
                (attn_buf, attn_out),
                (x_one_buf, x_one_out),
                (a_two_buf, a_two_out),
                (down_buf, down_out),
                (x_two_buf, x_two_out),
            ]
        )
    ]

    def wide_load(source, tile, slot):
        return pltpu.make_async_copy(
            source.at[:, :, :, :, column_tile(tile)], wide_buf.at[slot], load_sem.at[0, slot]
        )

    def tall_load(tile, slot):
        return pltpu.make_async_copy(
            w_down.at[tile // 2, lax.rem(tile, 2)], tall_buf.at[slot], load_sem.at[1, slot]
        )

    def tile_saves(tile, slot):
        return [
            pltpu.make_async_copy(
                pre_buf.at[slot], pre_out.at[:, column_tile(tile)], tile_sem.at[0, slot]
            ),
            pltpu.make_async_copy(
                act_buf.at[slot], act_out.at[:, column_tile(tile)], tile_sem.at[1, slot]
            ),
        ]

    def wide_tile(slot):
        return wide_buf[slot].reshape(D, HALF)

    def tall_tile(slot):
        return tall_buf[slot].reshape(HALF, D)

    def loads(at, run):
        slot = lax.rem(at, 2)

        @pl.when(within(at, 1, 6))
        def _():
            run(wide_load(w_qkv, at - 1, slot))

        @pl.when(within(at, 15, 2))
        def _():
            run(wide_load(w_proj, at - 15, slot))

        @pl.when(within(at, 18, 8))
        def _():
            run(wide_load(w_up, at - 18, slot))
            run(tall_load(at - 18, slot))

    def modulated(source, target, piece):
        def rows_of(block, carry):
            image = block // 4
            rows = pl.ds(pl.multiple_of(block * 64, 64), 64)
            shift = mod_ref[pl.ds(mod_at + 2 * piece + image, 1), :]
            scale = mod_ref[pl.ds(mod_at + 2 * piece + 2 + image, 1), :]
            unit, _ = normalized(source[rows, :])
            target[rows, :] = (unit * (1.0 + scale) + shift).astype(bf)
            return carry

        lax.fori_loop(0, images * toks // 64, rows_of, 0)

    def attend(image, pair):
        rows = pl.ds(pl.multiple_of(image * toks, toks), toks)
        low = lax.broadcasted_iota(jnp.int32, (toks, 128), 1) < 64
        queries = qkv_buf[rows, column_tile(pair, 128)] * jnp.asarray(0.125, bf)
        keys = qkv_buf[rows, column_tile(8 + pair, 128)]
        values = qkv_buf[rows, column_tile(16 + pair, 128)]
        keep = keep_ref[pl.ds(image, 1), :]
        zero = jnp.zeros_like(queries)
        total = jnp.zeros((toks, 128), jnp.float32)
        for own in (low, jnp.logical_not(low)):
            probs = head_probs(jnp.where(own, queries, zero), keys, keep)
            total = total + dot_nn(probs.astype(bf), jnp.where(own, values, zero))
        merged_buf[rows, column_tile(pair, 128)] = total.astype(bf)

    def step(at):
        slot = lax.rem(at, 2)
        loads(at + 1, lambda copy: copy.start())
        loads(at, lambda copy: copy.wait())

        @pl.when(at == 0)
        def _():
            modulated(x_ref, a_buf, 0)
            saves[0].start()

        @pl.when(within(at, 1, 6))
        def _():
            cols = column_tile(at - 1)
            for image in range(images):
                rows = pl.ds(image * toks, toks)
                qkv_buf[rows, cols] = (
                    dot_nn(a_buf[rows, :], wide_tile(slot)) + bias_ref[:, cols]
                ).astype(bf)

        @pl.when(at == 7)
        def _():
            saves[1].start()

        @pl.when(within(at, 7, 8))
        def _():
            for turn in range(2):
                item = (at - 7) * 2 + turn
                attend(item // 8, lax.rem(item, 8))

        @pl.when(within(at, 15, 2))
        def _():
            cols = column_tile(at - 15)
            for image in range(images):
                rows = pl.ds(image * toks, toks)
                attn = dot_nn(merged_buf[rows, :], wide_tile(slot)) + bias_ref[
                    :, column_tile(at - 15 + 6)
                ]
                attn_buf[rows, cols] = attn
                gate = mod_ref[mod_at + 4 + image : mod_at + 5 + image, cols]
                x_one_buf[rows, cols] = x_ref[rows, cols] + gate * attn

        @pl.when(at == 17)
        def _():
            for which in (2, 3, 4):
                saves[which].start()
            modulated(x_one_buf, a_two_buf, 3)
            saves[5].start()

        @pl.when(within(at, 18, 8))
        def _():
            tile = at - 18

            @pl.when(tile >= 2)
            def _():
                for copy in tile_saves(tile - 2, slot):
                    copy.wait()

            for image in range(images):
                rows = pl.ds(image * toks, toks)
                pre = dot_nn(a_two_buf[rows, :], wide_tile(slot)) + bias_ref[:, column_tile(tile + 8)]
                pre_buf[slot, rows, :] = pre
                inner = jnp.tanh(GELU_IN * (pre + GELU_CUBE * pre * pre * pre))
                active = (0.5 * pre * (1.0 + inner)).astype(bf)
                act_buf[slot, rows, :] = active
                part = dot_nn(active, tall_tile(slot))

                @pl.when(tile == 0)
                def _():
                    down_buf[rows, :] = part + bias_ref[:, 8 * D : 9 * D]

                @pl.when(tile > 0)
                def _():
                    down_buf[rows, :] += part

            for copy in tile_saves(tile, slot):
                copy.start()

        @pl.when(at == FORWARD_STEPS - 1)
        def _():
            for image in range(images):
                rows = pl.ds(image * toks, toks)
                gate = mod_ref[mod_at + 10 + image : mod_at + 11 + image, :]
                x_two_buf[rows, :] = x_one_buf[rows, :] + gate * down_buf[rows, :]
            saves[6].start()
            saves[7].start()

    def finish():
        for tile in (6, 7):
            for copy in tile_saves(tile, tile % 2):
                copy.wait()
        for copy in saves:
            copy.wait()

    return step, finish


FORWARD_OUTS = [
    (D, jnp.bfloat16),
    (3 * D, jnp.bfloat16),
    (D, jnp.bfloat16),
    (D, jnp.float32),
    (D, jnp.float32),
    (D, jnp.bfloat16),
    (FF, jnp.float32),
    (FF, jnp.bfloat16),
    (D, jnp.float32),
    (D, jnp.float32),
]


def forward_scratch(toks):
    bf, f32 = jnp.bfloat16, jnp.float32
    return [
        pltpu.VMEM((toks, D), bf),
        pltpu.VMEM((toks, 3 * D), bf),
        pltpu.VMEM((toks, D), bf),
        pltpu.VMEM((toks, D), f32),
        pltpu.VMEM((toks, D), f32),
        pltpu.VMEM((toks, D), bf),
        pltpu.VMEM((2, toks, HALF), f32),
        pltpu.VMEM((2, toks, HALF), bf),
        pltpu.VMEM((toks, D), f32),
        pltpu.VMEM((toks, D), f32),
        pltpu.VMEM((2, 4, 2, 2, 64, HALF), bf),
        pltpu.VMEM((2, 2, 256, D), bf),
        pltpu.SemaphoreType.DMA((2, 2)),
        pltpu.SemaphoreType.DMA((2, 2)),
        pltpu.SemaphoreType.DMA((8,)),
    ]


def forward_kernel(mod_at, *refs):
    step, finish = forward_pieces(refs, mod_at)

    def turn(at, carry):
        step(at)
        return carry

    lax.fori_loop(0, FORWARD_STEPS, turn, 0)
    finish()


def grouped(weights):
    return [each.reshape(4, 2, 2, -1, each.shape[-1]) for each in weights]


def forward_layer(x, mods, mod_at, biases, keep, weights):
    toks = x.shape[0]
    return pl.pallas_call(
        functools.partial(forward_kernel, mod_at),
        out_shape=[jax.ShapeDtypeStruct((toks, width), kind) for width, kind in FORWARD_OUTS],
        in_specs=[pl.BlockSpec(memory_space=pltpu.VMEM)] * 4
        + [pl.BlockSpec(memory_space=pl.ANY)] * 4,
        out_specs=[pl.BlockSpec(memory_space=pl.ANY)] * len(FORWARD_OUTS),
        scratch_shapes=forward_scratch(toks),
        compiler_params=pltpu.CompilerParams(vmem_limit_bytes=56 * 1024 * 1024),
        cost_estimate=pl.CostEstimate(
            flops=24 * toks * D * D, bytes_accessed=60 * 1024 * 1024, transcendentals=4 * toks * D
        ),
    )(x, mods, biases, keep, *grouped(weights))


def backward_pieces(ins, outs, scratch, mod_at):
    (
        x_hbm,
        x_one_hbm,
        attn_hbm,
        down_hbm,
        qkv_hbm,
        pre_hbm,
        w_qkv,
        w_proj,
        w_up,
        w_down,
        mod_ref,
        keep_ref,
    ) = ins
    d_down_out, d_up_out, d_attn_out, d_qkv_out = outs
    (
        d_mod_ref,
        d_bias_ref,
        grad_ref,
        side_ref,
        x_one_ref,
        attn_ref,
        qkv_ref,
        total_buf,
        d_x_one_buf,
        d_down_buf,
        d_up_buf,
        d_attn_buf,
        d_heads_buf,
        d_qkv_buf,
        pre_buf,
        wide_buf,
        tall_buf,
        load_sem,
        tile_sem,
        save_sem,
        in_sem,
    ) = scratch
    images, toks = keep_ref.shape
    bf = jnp.bfloat16
    blocks = toks // 64
    saves = [
        pltpu.make_async_copy(source, target, save_sem.at[at])
        for at, (source, target) in enumerate(
            [
                (d_down_buf, d_down_out),
                (d_attn_buf, d_attn_out),
                (d_qkv_buf, d_qkv_out),
            ]
        )
    ]

    in_down, in_x_one, in_attn, in_qkv, in_x = [
        pltpu.make_async_copy(source, target, in_sem.at[at])
        for at, (source, target) in enumerate(
            [
                (down_hbm, side_ref),
                (x_one_hbm, x_one_ref),
                (attn_hbm, attn_ref),
                (qkv_hbm, qkv_ref),
                (x_hbm, side_ref),
            ]
        )
    ]

    def begin():
        for copy in (in_down, in_x_one, in_attn, in_qkv):
            copy.start()

    def wide_load(source, tile, slot):
        return pltpu.make_async_copy(
            source.at[:, :, :, :, column_tile(tile)], wide_buf.at[slot], load_sem.at[0, slot]
        )

    def tall_load(tile, slot):
        return pltpu.make_async_copy(
            w_down.at[tile // 2, lax.rem(tile, 2)], tall_buf.at[slot], load_sem.at[1, slot]
        )

    def pre_load(tile, slot):
        return pltpu.make_async_copy(
            pre_hbm.at[:, column_tile(tile)], pre_buf.at[slot], load_sem.at[2, slot]
        )

    def up_save(tile, slot):
        return pltpu.make_async_copy(
            d_up_buf.at[slot], d_up_out.at[:, column_tile(tile)], tile_sem.at[slot]
        )

    def wide_tile(slot):
        return wide_buf[slot].reshape(D, HALF)

    def tall_tile(slot):
        return tall_buf[slot].reshape(HALF, D)

    def loads(at, run):
        slot = lax.rem(at, 2)

        @pl.when(within(at, 1, 8))
        def _():
            run(tall_load(at - 1, slot))
            run(wide_load(w_up, at - 1, slot))
            run(pre_load(at - 1, slot))

        @pl.when(within(at, 10, 2))
        def _():
            run(wide_load(w_proj, at - 10, slot))

        @pl.when(within(at, 20, 6))
        def _():
            run(wide_load(w_qkv, at - 20, slot))

    def column_sums(rows):
        return jnp.sum(rows.astype(jnp.float32), axis=0, keepdims=True)

    def gated(image, gate_row, gradient, branch, target, bias_cols):
        def rows_of(block, sums):
            rows = pl.ds(pl.multiple_of(image * toks + block * 64, 64), 64)
            upper = gradient[rows, :]
            gate = mod_ref[mod_at + gate_row + image : mod_at + gate_row + image + 1, :]
            lower = (upper * gate).astype(bf)
            target[rows, :] = lower
            return sums[0] + column_sums(upper * branch[rows, :]), sums[1] + column_sums(lower)

        zero = jnp.zeros((1, D), jnp.float32)
        gate, bias = lax.fori_loop(0, blocks, rows_of, (zero, zero))
        gate_at = mod_at + gate_row + image
        d_mod_ref[gate_at : gate_at + 1, :] = gate
        if image == 0:
            d_bias_ref[:, bias_cols] = bias
        else:
            d_bias_ref[:, bias_cols] += bias

    def modulate_back(image, first_row, source, passed, target):
        def rows_of(block, sums):
            rows = pl.ds(pl.multiple_of(image * toks + block * 64, 64), 64)
            scale_row = mod_at + first_row + 2 + image
            scale = mod_ref[scale_row : scale_row + 1, :]
            unit, inverse = normalized(source[rows, :])
            upper = total_buf[rows, :]
            inner = upper * (1.0 + scale)
            back = inverse * (
                inner
                - jnp.mean(inner, axis=-1, keepdims=True)
                - unit * jnp.mean(inner * unit, axis=-1, keepdims=True)
            )
            target[rows, :] = back + passed[rows, :]
            return sums[0] + column_sums(upper), sums[1] + column_sums(upper * unit)

        zero = jnp.zeros((1, D), jnp.float32)
        shift, scale = lax.fori_loop(0, blocks, rows_of, (zero, zero))
        shift_at = mod_at + first_row + image
        d_mod_ref[shift_at : shift_at + 1, :] = shift
        d_mod_ref[shift_at + 2 : shift_at + 3, :] = scale

    def attend_back(image, pair):
        rows = pl.ds(pl.multiple_of(image * toks, toks), toks)
        low = lax.broadcasted_iota(jnp.int32, (toks, 128), 1) < 64
        eighth = jnp.asarray(0.125, bf)
        queries = qkv_ref[rows, column_tile(pair, 128)] * eighth
        keys = qkv_ref[rows, column_tile(8 + pair, 128)]
        values = qkv_ref[rows, column_tile(16 + pair, 128)]
        upper = d_heads_buf[rows, column_tile(pair, 128)]
        keep = keep_ref[pl.ds(image, 1), :]
        zero = jnp.zeros_like(queries)
        total = jnp.zeros((toks, 128), jnp.float32)
        d_q, d_k, d_v = total, total, total
        for own in (low, jnp.logical_not(low)):
            own_q = jnp.where(own, queries, zero)
            own_up = jnp.where(own, upper, zero)
            probs = head_probs(own_q, keys, keep)
            d_probs = dot_nt(own_up, values)
            mean = jnp.sum(probs * d_probs, axis=-1, keepdims=True)
            d_scores = (probs * (d_probs - mean)).astype(bf)
            d_v = d_v + dot_tn(probs.astype(bf), own_up)
            d_q = d_q + dot_nn(d_scores, jnp.where(own, keys * eighth, zero))
            d_k = d_k + dot_tn(d_scores, own_q)
        d_qkv_buf[rows, column_tile(pair, 128)] = d_q.astype(bf)
        d_qkv_buf[rows, column_tile(8 + pair, 128)] = d_k.astype(bf)
        d_qkv_buf[rows, column_tile(16 + pair, 128)] = d_v.astype(bf)

    def add_product(first, image_rows, part):
        @pl.when(first)
        def _():
            total_buf[image_rows, :] = part

        @pl.when(jnp.logical_not(first))
        def _():
            total_buf[image_rows, :] += part

    def step(at):
        slot = lax.rem(at, 2)
        loads(at + 1, lambda copy: copy.start())
        loads(at, lambda copy: copy.wait())

        @pl.when(at == 0)
        def _():
            in_down.wait()
            for image in range(images):
                gated(image, 10, grad_ref, side_ref, d_down_buf, slice(8 * D, 9 * D))
            saves[0].start()

        @pl.when(within(at, 1, 8))
        def _():
            tile = at - 1
            bias = jnp.zeros((1, HALF), jnp.float32)
            for image in range(images):
                rows = pl.ds(image * toks, toks)
                upper = dot_nt(d_down_buf[rows, :], tall_tile(slot))
                pre = pre_buf[slot, rows, :]
                square = pre * pre
                inner = jnp.tanh(GELU_IN * (pre + GELU_CUBE * square * pre))
                slope = 0.5 * (1.0 + inner) + 0.5 * pre * (1.0 - inner * inner) * (
                    GELU_IN * (1.0 + 3.0 * GELU_CUBE * square)
                )
                lower = (upper * slope).astype(bf)
                d_up_buf[slot, rows, :] = lower
                bias = bias + column_sums(lower)
                add_product(tile == 0, rows, dot_nt(lower, wide_tile(slot)))
            d_bias_ref[:, column_tile(tile + 8)] = bias
            up_save(tile, slot).start()

            @pl.when(tile == 0)
            def _():
                saves[0].wait()

            @pl.when(tile >= 1)
            def _():
                up_save(tile - 1, 1 - slot).wait()

        @pl.when(at == 9)
        def _():
            up_save(7, 0).wait()
            in_x_one.wait()
            in_attn.wait()
            for image in range(images):
                modulate_back(image, 6, x_one_ref, grad_ref, d_x_one_buf)
                gated(image, 4, d_x_one_buf, attn_ref, d_attn_buf, slice(3 * D, 4 * D))
            saves[1].start()

        @pl.when(within(at, 10, 2))
        def _():
            for image in range(images):
                rows = pl.ds(image * toks, toks)
                part = dot_nt(d_attn_buf[rows, column_tile(at - 10)], wide_tile(slot))
                add_product(at == 10, rows, part)

            @pl.when(at == 10)
            def _():
                in_x.start()
                saves[1].wait()

            @pl.when(at == 11)
            def _():
                in_qkv.wait()
                d_heads_buf[...] = total_buf[...].astype(bf)

        @pl.when(within(at, 12, 8))
        def _():
            for turn in range(2):
                item = (at - 12) * 2 + turn
                attend_back(item // 8, lax.rem(item, 8))

        @pl.when(at == 20)
        def _():
            saves[2].start()

        @pl.when(within(at, 20, 6))
        def _():
            cols = column_tile(at - 20)
            bias = jnp.zeros((1, HALF), jnp.float32)
            for image in range(images):
                rows = pl.ds(image * toks, toks)
                lower = d_qkv_buf[rows, cols]
                bias = bias + column_sums(lower)
                add_product(at == 20, rows, dot_nt(lower, wide_tile(slot)))
            d_bias_ref[:, cols] = bias

            @pl.when(at == 21)
            def _():
                saves[2].wait()

        @pl.when(at == BACKWARD_STEPS - 1)
        def _():
            in_x.wait()
            for image in range(images):
                modulate_back(image, 0, side_ref, d_x_one_buf, grad_ref)

    return begin, step


BACKWARD_OUTS = [(D, jnp.bfloat16), (FF, jnp.bfloat16), (D, jnp.bfloat16), (3 * D, jnp.bfloat16)]


def backward_scratch(toks):
    bf, f32 = jnp.bfloat16, jnp.float32
    return [
        pltpu.VMEM((toks, D), f32),
        pltpu.VMEM((toks, D), f32),
        pltpu.VMEM((toks, D), f32),
        pltpu.VMEM((toks, D), f32),
        pltpu.VMEM((toks, 3 * D), bf),
        pltpu.VMEM((toks, D), f32),
        pltpu.VMEM((toks, D), f32),
        pltpu.VMEM((toks, D), bf),
        pltpu.VMEM((2, toks, HALF), bf),
        pltpu.VMEM((toks, D), bf),
        pltpu.VMEM((toks, D), bf),
        pltpu.VMEM((toks, 3 * D), bf),
        pltpu.VMEM((2, toks, HALF), f32),
        pltpu.VMEM((2, 4, 2, 2, 64, HALF), bf),
        pltpu.VMEM((2, 2, 256, D), bf),
        pltpu.SemaphoreType.DMA((3, 2)),
        pltpu.SemaphoreType.DMA((2,)),
        pltpu.SemaphoreType.DMA((3,)),
        pltpu.SemaphoreType.DMA((5,)),
    ]


def backward_kernel(mod_at, *refs):
    grad_in, ins, outs = refs[0], refs[1:13], refs[13:17]
    d_x_out, d_mod_ref, d_bias_ref = refs[17:20]
    scratch, sem = refs[20:-1], refs[-1]
    begin, step = backward_pieces(ins, outs, (d_mod_ref, d_bias_ref) + scratch, mod_at)
    begin()
    copy = pltpu.make_async_copy(grad_in, scratch[0], sem.at[0])
    copy.start()
    copy.wait()

    def turn(at, carry):
        step(at)
        return carry

    lax.fori_loop(0, BACKWARD_STEPS, turn, 0)
    copy = pltpu.make_async_copy(scratch[0], d_x_out, sem.at[1])
    copy.start()
    copy.wait()


def backward_operands(x, saved, weights):
    _, qkv, _, attn, x_one, _, pre, _, down, _ = saved
    return (x, x_one, attn, down, qkv, pre, *weights)


def backward_layer(grad, x, saved, mods, mod_at, keep, weights):
    a_one, _, merged, _, _, a_two, _, act, _, _ = saved
    toks = x.shape[0]
    vmem = pl.BlockSpec(memory_space=pltpu.VMEM)
    hbm = pl.BlockSpec(memory_space=pl.ANY)
    outs = pl.pallas_call(
        functools.partial(backward_kernel, mod_at),
        out_shape=[jax.ShapeDtypeStruct((toks, width), kind) for width, kind in BACKWARD_OUTS]
        + [
            jax.ShapeDtypeStruct((toks, D), jnp.float32),
            jax.ShapeDtypeStruct((mod_at + 12, D), jnp.float32),
            jax.ShapeDtypeStruct((1, 9 * D), jnp.float32),
        ],
        in_specs=[hbm] * 11 + [vmem] * 2,
        out_specs=[hbm] * 5 + [vmem] * 2,
        scratch_shapes=backward_scratch(toks) + [pltpu.SemaphoreType.DMA((2,))],
        compiler_params=pltpu.CompilerParams(vmem_limit_bytes=56 * 1024 * 1024),
        cost_estimate=pl.CostEstimate(
            flops=28 * toks * D * D, bytes_accessed=80 * 1024 * 1024, transcendentals=4 * toks * D
        ),
    )(grad, *backward_operands(x, saved, grouped(weights)), mods, keep)
    d_down, d_up, d_attn, d_qkv, d_x, d_mod, d_bias = outs
    factors = (merged, a_one, a_two, act, d_attn, d_qkv, d_up, d_down)
    return d_x, d_mod[mod_at:], factors, d_bias


def gather_pieces(lines, refs):
    layers = (len(refs) - 7) // 8
    pairs = list(zip(refs[: 4 * layers], refs[4 * layers : 8 * layers]))
    own_sem, zp_sem, zq_sem, yp_sem, yq_sem, x_sem, core_sem = refs[8 * layers :]
    firsts = [12 * layer + first for layer in range(layers) for first in (0, 3, 4, 8)]
    total = 12 * layers
    seq = lax.axis_index("seq")
    dp = lax.axis_index("dp")
    core = lax.rem(dp, 2)
    why = lax.rem(dp // 2, 2)
    zed = dp // 4
    core_peer = {"seq": seq, "dp": dp + 1 - 2 * core}
    x_peer = {"seq": 1 - seq, "dp": dp}
    y_peer = {"seq": seq, "dp": dp + 2 - 4 * why}
    z_peers = [
        {"seq": seq, "dp": lax.rem(zed + step, lines) * 4 + 2 * why + core}
        for step in range(1, lines)
    ]
    keeps = [
        pltpu.make_async_copy(own, every.at[zed, why, core], own_sem.at[at])
        for at, (own, every) in enumerate(pairs)
    ]
    for keep in keeps:
        keep.start()
    for keep in keeps:
        keep.wait()
    barrier = pltpu.get_barrier_semaphore()
    for peer in [core_peer, x_peer, y_peer] + z_peers:
        pl.semaphore_signal(barrier, inc=1, device_id=peer, device_id_type=MESH)
    pl.semaphore_wait(barrier, 2 + lines)

    def places(kind, unit):
        at = unit - firsts[kind]
        if kind % 4 == 3:
            return pl.multiple_of(at * 64, 64), 0
        return 0, pl.multiple_of(at * D, D)

    def span(first, begin, size):
        return pl.ds(pl.multiple_of(first + begin, 128), size)

    def copies(stage, kind, unit):
        slot = unit
        own, every = pairs[kind]
        row, first = places(kind, unit)
        rows = pl.ds(row, 64)
        mine = pl.ds(pl.multiple_of(row + seq * 32, 32), 32)
        halved = span(first, 0, SHARED)
        rest = span(first, SHARED, D - SHARED)
        whole = span(first, 0, D)

        def remote(source, target, sems, peer):
            return pltpu.make_async_remote_copy(
                src_ref=source,
                dst_ref=target,
                send_sem=sems.at[0],
                recv_sem=sems.at[1],
                device_id=peer,
                device_id_type=MESH,
            )

        def same(view, sems, peer):
            return remote(view, view, sems, peer)

        if stage == 0:
            return [
                remote(own.at[band, cols], every.at[zed, why, core, band, cols], sems, peer)
                for band, cols, kinds in ((mine, halved, zp_sem), (rows, rest, zq_sem))
                for sems, peer in [(kinds.at[slot, at], z_peers[at]) for at in range(lines - 1)]
            ]
        if stage == 1:
            return [
                same(every.at[:, why, core, mine, halved], yp_sem.at[slot], y_peer),
                same(every.at[:, why, core, rows, rest], yq_sem.at[slot], y_peer),
            ]
        if stage == 2:
            return [same(every.at[:, :, core, mine, halved], x_sem.at[slot], x_peer)]
        return [same(every.at[:, :, core, rows, whole], core_sem.at[slot], core_peer)]

    def each_kind(unit, run):
        ends = firsts[1:] + [total]
        for kind in range(len(firsts)):

            @pl.when(jnp.logical_and(unit >= firsts[kind], unit < ends[kind]))
            def _():
                run(kind)

    def begin(stage, unit):
        def run(kind):
            for copy in copies(stage, kind, unit):
                copy.start()

        each_kind(unit, run)

    def finish(stage, unit):
        def run(kind):
            for copy in copies(stage, kind, unit):
                copy.wait()

        each_kind(unit, run)

    def step(at):
        finish(3, at - sum(GATHER_LAGS))
        for stage in (3, 2, 1):
            behind = sum(GATHER_LAGS[:stage])
            finish(stage - 1, at - behind)
            begin(stage, at - behind)
        begin(0, at)

    return step, total + sum(GATHER_LAGS)


def gather_scratch(lines, layers):
    dma = pltpu.SemaphoreType.DMA
    units = 12 * layers
    return [
        dma((4 * layers,)),
        dma((units, lines - 1, 2)),
        dma((units, lines - 1, 2)),
        dma((units, 2)),
        dma((units, 2)),
        dma((units, 2)),
        dma((units, 2)),
    ]


def modulation_pieces(lines, refs):
    (
        partial_ref,
        bias_ref,
        mods_ref,
        core_in,
        core_total,
        y_in,
        y_total,
        z_in,
        core_sem,
        y_sem,
        z_sem,
    ) = refs
    seq = lax.axis_index("seq")
    dp = lax.axis_index("dp")
    core = lax.rem(dp, 2)
    why = lax.rem(dp // 2, 2)
    zed = dp // 4

    def remote(source, target, sems, peer):
        return pltpu.make_async_remote_copy(
            src_ref=source,
            dst_ref=target,
            send_sem=sems.at[0],
            recv_sem=sems.at[1],
            device_id={"seq": seq, "dp": peer},
            device_id_type=MESH,
        )

    to_core = remote(partial_ref.at[:, :, 1 - core], core_in, core_sem, dp + 1 - 2 * core)
    to_y = remote(core_total.at[:, 1 - why], y_in, y_sem, dp + 2 - 4 * why)
    to_z = []
    for ahead in range(1, lines):
        there = lax.rem(zed + ahead, lines)
        to_z.append(
            remote(
                y_total.at[there],
                z_in.at[ahead - 1],
                z_sem.at[ahead - 1],
                there * 4 + 2 * why + core,
            )
        )

    def step(at):
        @pl.when(at == 0)
        def _():
            to_core.start()

        @pl.when(at == 1)
        def _():
            to_core.wait()
            core_total[...] = partial_ref[:, :, core] + core_in[...]
            to_y.start()

        @pl.when(at == 4)
        def _():
            to_y.wait()
            y_total[...] = core_total[:, why] + y_in[...]
            for copy in to_z:
                copy.start()

        @pl.when(at == 8)
        def _():
            total = y_total[zed] + bias_ref[...]
            for ahead, copy in enumerate(to_z):
                copy.wait()
                total = total + z_in[ahead]
            mods_ref[...] = total

    return step


def modulation_scratch(lines, rows):
    dma = pltpu.SemaphoreType.DMA
    f32 = jnp.float32
    return [
        pltpu.VMEM((lines, 2, rows, D), f32),
        pltpu.VMEM((lines, 2, rows, D), f32),
        pltpu.VMEM((lines, rows, D), f32),
        pltpu.VMEM((lines, rows, D), f32),
        pltpu.VMEM((lines - 1, rows, D), f32),
        dma((2,)),
        dma((2,)),
        dma((lines - 1, 2)),
    ]


def whole_forward_kernel(lines, *refs):
    refs = list(refs)

    def take(count):
        taken, refs[:] = tuple(refs[:count]), refs[count:]
        return taken

    own = take(8)
    partial_ref, mod_bias, x_ref, first_bias, second_bias, keep = take(6)
    every = take(8)
    first_outs, second_outs = take(len(FORWARD_OUTS)), take(len(FORWARD_OUTS))
    (mods,) = take(1)
    gather_sems = take(7)
    mod_scratch = take(8)
    scratch = tuple(refs)
    gather, steps = gather_pieces(lines, own + every + gather_sems)
    modulate_step = modulation_pieces(lines, (partial_ref, mod_bias, mods) + mod_scratch)
    first, first_finish = forward_pieces(
        (x_ref, mods, first_bias, keep) + every[:4] + first_outs + scratch, 0
    )
    second, second_finish = forward_pieces(
        (scratch[9], mods, second_bias, keep) + every[4:] + second_outs + scratch, 12
    )

    def run(step, begin, end):
        def one(at, carry):
            step(at)
            return carry

        lax.fori_loop(begin, end, one, 0)

    def turn(at, carry):
        gather(at)
        modulate_step(at)

        @pl.when(within(at, 10, 13))
        def _():
            run(first, 2 * (at - 10), 2 * (at - 9))

        @pl.when(at == 23)
        def _():
            first_finish()

        @pl.when(at >= 24)
        def _():
            run(second, 18 * (at - 24) // 7, 18 * (at - 23) // 7)

        return carry

    lax.fori_loop(0, steps + 4, turn, 0)
    second_finish()


def whole_forward(own, partial, mod_bias, x, biases, keep, lines):
    toks = x.shape[0]
    rows = mod_bias.shape[0]
    vmem = pl.BlockSpec(memory_space=pltpu.VMEM)
    hbm = pl.BlockSpec(memory_space=pl.ANY)
    layer_outs = [jax.ShapeDtypeStruct((toks, width), kind) for width, kind in FORWARD_OUTS]
    outs = pl.pallas_call(
        functools.partial(whole_forward_kernel, lines),
        out_shape=[
            jax.ShapeDtypeStruct((lines, 2, 2) + each.shape, jnp.bfloat16) for each in own
        ]
        + layer_outs
        + layer_outs
        + [jax.ShapeDtypeStruct((rows, D), jnp.float32)],
        in_specs=[vmem] * 14,
        out_specs=[hbm] * (8 + 2 * len(FORWARD_OUTS)) + [vmem],
        scratch_shapes=gather_scratch(lines, 2)
        + modulation_scratch(lines, rows)
        + forward_scratch(toks),
        compiler_params=pltpu.CompilerParams(
            collective_id=2, has_side_effects=True, vmem_limit_bytes=58 * 1024 * 1024
        ),
        cost_estimate=pl.CostEstimate(
            flops=48 * toks * D * D,
            bytes_accessed=24 * 4 * lines * 64 * D * 8,
            transcendentals=8 * toks * D,
        ),
    )(*own, partial, mod_bias, x, *biases, keep)
    weights = outs[:8]
    count = len(FORWARD_OUTS)
    saved = [outs[8 : 8 + count], outs[8 + count : 8 + 2 * count]]
    return [weights[:4], weights[4:]], saved, outs[-1]


def gather_small_kernel(lines, own_ref, every_ref, z_sem, y_sem, core_sem):
    seq = lax.axis_index("seq")
    dp = lax.axis_index("dp")
    core = lax.rem(dp, 2)
    why = lax.rem(dp // 2, 2)
    zed = dp // 4
    core_peer = {"seq": seq, "dp": dp + 1 - 2 * core}
    y_peer = {"seq": seq, "dp": dp + 2 - 4 * why}
    z_peers = [
        {"seq": seq, "dp": lax.rem(zed + step, lines) * 4 + 2 * why + core}
        for step in range(1, lines)
    ]
    barrier = pltpu.get_barrier_semaphore()
    for peer in [core_peer, y_peer] + z_peers:
        pl.semaphore_signal(barrier, inc=1, device_id=peer, device_id_type=MESH)
    every_ref[zed, why, core] = own_ref[...]
    pl.semaphore_wait(barrier, 1 + lines)

    def remote(source, target, sems, peer):
        return pltpu.make_async_remote_copy(
            src_ref=source,
            dst_ref=target,
            send_sem=sems.at[0],
            recv_sem=sems.at[1],
            device_id=peer,
            device_id_type=MESH,
        )

    copies = [
        remote(own_ref, every_ref.at[zed, why, core], z_sem.at[at], peer)
        for at, peer in enumerate(z_peers)
    ]
    for copy in copies:
        copy.start()
    for copy in copies:
        copy.wait()
    for view, sems, peer in (
        (every_ref.at[:, why, core], y_sem, y_peer),
        (every_ref.at[:, :, core], core_sem, core_peer),
    ):
        copy = remote(view, view, sems, peer)
        copy.start()
        copy.wait()


def gather_small(own, lines, collective_id):
    dma = pltpu.SemaphoreType.DMA
    every = pl.pallas_call(
        functools.partial(gather_small_kernel, lines),
        out_shape=jax.ShapeDtypeStruct((lines, 2, 2) + own.shape, own.dtype),
        in_specs=[pl.BlockSpec(memory_space=pltpu.VMEM)],
        out_specs=pl.BlockSpec(memory_space=pltpu.VMEM),
        scratch_shapes=[dma((lines - 1, 2)), dma((2,)), dma((2,))],
        compiler_params=pltpu.CompilerParams(collective_id=collective_id, has_side_effects=True),
        cost_estimate=pl.CostEstimate(
            flops=0, bytes_accessed=own.size * 32 * lines, transcendentals=0
        ),
    )(own)
    return every.reshape(-1, own.shape[-1])


def scatter_pieces(lines, sources, scratch):
    per_layer = 12
    total = len(sources) * per_layer
    (
    out_ref,
    lhs_buf,
    act_buf,
    wide_buf,
    down_buf,
    load_sem,
    made,
    core_in,
    x_out,
    x_in,
    p_keep,
    yq_out,
    yq_in,
    q_keep,
    yp_out,
    yp_in,
    p_line,
    zq_out,
    zq_in,
    zp_out,
    zp_in,
    xq_out,
    xq_in,
    xp_out,
    xp_in,
    core_sem,
    x_sem,
    yq_sem,
    yp_sem,
    zq_sem,
    zp_sem,
    xq_sem,
    xp_sem,
    out_buf,
    out_sem,
    ) = scratch
    seq = lax.axis_index("seq")
    dp = lax.axis_index("dp")
    core = lax.rem(dp, 2)
    why = lax.rem(dp // 2, 2)
    zed = dp // 4
    core_peer = {"seq": seq, "dp": dp + 1 - 2 * core}
    x_peer = {"seq": 1 - seq, "dp": dp}
    y_peer = {"seq": seq, "dp": dp + 2 - 4 * why}

    def z_place(step):
        return lax.rem(zed + step, lines)

    def z_peer(step):
        return {"seq": seq, "dp": z_place(step) * 4 + 2 * why + core}

    def remote(source, target, sems, peer):
        return pltpu.make_async_remote_copy(
            src_ref=source,
            dst_ref=target,
            send_sem=sems.at[0],
            recv_sem=sems.at[1],
            device_id=peer,
            device_id_type=MESH,
        )

    def core_copy(slot):
        return remote(made.at[slot, 1 - core], core_in.at[slot], core_sem.at[slot], core_peer)

    def x_copy(slot):
        return remote(x_out.at[slot], x_in.at[slot], x_sem.at[slot], x_peer)

    def yq_copy(slot):
        return remote(yq_out.at[slot], yq_in.at[slot], yq_sem.at[slot], y_peer)

    def yp_copy(slot):
        return remote(yp_out.at[slot], yp_in.at[slot], yp_sem.at[slot], y_peer)

    def zq_copy(slot, step):
        return remote(
            zq_out.at[slot, z_place(step)],
            zq_in.at[slot, step - 1],
            zq_sem.at[slot, step - 1],
            z_peer(step),
        )

    def zp_copy(slot, step):
        return remote(
            zp_out.at[slot, z_place(step)],
            zp_in.at[slot, step - 1],
            zp_sem.at[slot, step - 1],
            z_peer(step),
        )

    def xq_copy(slot):
        return remote(xq_out.at[slot], xq_in.at[slot], xq_sem.at[slot], x_peer)

    def xp_copy(slot):
        return remote(xp_out.at[slot], xp_in.at[slot], xp_sem.at[slot], x_peer)

    def loads(unit, slot):
        found = []
        for layer in range(len(sources)):
            merged, a_one, a_two, act, d_attn, d_qkv, d_up, d_down = sources[layer]
            at = unit - layer * per_layer

            def slab(ref, index, size):
                return ref.at[:, pl.ds(pl.multiple_of(index * size, size), size)]

            wide_to = wide_buf.at[slot], load_sem.at[1, slot]
            lhs_to = lhs_buf.at[slot], load_sem.at[0, slot]
            found += [
                (
                    jnp.logical_and(at >= 0, at < 4),
                    (slab(d_down, at, TILE), down_buf.at[slot], load_sem.at[2, slot]),
                ),
                (at == 0, (act, act_buf, load_sem.at[3, 0])),
                (
                    jnp.logical_and(at >= 4, at < 8),
                    (a_two, *lhs_to),
                    (slab(d_up, at - 4, D), *wide_to),
                ),
                (at == 8, (merged, *lhs_to), (d_attn, *wide_to)),
                (
                    jnp.logical_and(at >= 9, at < per_layer),
                    (a_one, *lhs_to),
                    (slab(d_qkv, at - 9, D), *wide_to),
                ),
            ]
        return found

    def prefetch(unit):
        for due, *moves in loads(unit, lax.rem(unit, 2)):

            @pl.when(due)
            def _():
                for move in moves:
                    pltpu.make_async_copy(*move).start()

    def fetched(unit):
        for due, *moves in loads(unit, lax.rem(unit, 2)):

            @pl.when(due)
            def _():
                for move in moves:
                    pltpu.make_async_copy(*move).wait()

    def dot_rows(left, right):
        return lax.dot_general(
            left, right, (((0,), (0,)), ((), ())), preferred_element_type=jnp.float32
        )

    def compute(unit):
        at = lax.rem(unit, per_layer)
        slot = lax.rem(unit, 2)
        fetched(unit)

        @pl.when(at >= 4)
        def _():
            def rows(pair, carry):
                left = lhs_buf[slot, :, pl.ds(pl.multiple_of(pair * 128, 128), 128)]
                block = dot_rows(left, wide_buf[slot]).astype(jnp.bfloat16)
                for own in range(2):
                    for part in range(PARTS):
                        made[slot, own, part, pair // 2, lax.rem(pair, 2)] = block[
                            own * 64 : own * 64 + 64, part * TILE : part * TILE + TILE
                        ]
                return carry

            lax.fori_loop(0, 2 * lines, rows, 0)

        @pl.when(at < 4)
        def _():
            def rows(pair, carry):
                left = act_buf[:, pl.ds(pl.multiple_of(pair * 512, 512), 512)]
                block = dot_rows(left, down_buf[slot]).astype(jnp.bfloat16)
                for own in range(2):
                    for part in range(PARTS):
                        first = own * 256 + part * 64
                        made[slot, own, part, pair // 2, lax.rem(pair, 2)] = block[
                            first : first + 64
                        ]
                return carry

            lax.fori_loop(0, 2 * lines, rows, 0)

    def wide_sum(one, other):
        return one.astype(jnp.float32) + other.astype(jnp.float32)

    def out_copy(unit, slot):
        return pltpu.make_async_copy(out_buf.at[slot], out_ref.at[unit], out_sem.at[slot])

    def stage_two(slot):
        core_copy(slot).wait()

        def rows(line, carry):
            for side in range(2):
                x_out[slot, line, side] = wide_sum(
                    made[slot, core, 1 - seq, line, side], core_in[slot, 1 - seq, line, side]
                ).astype(jnp.bfloat16)
                p_keep[slot, line, side] = wide_sum(
                    made[slot, core, seq, line, side], core_in[slot, seq, line, side]
                ).astype(jnp.bfloat16)
            for part in range(2):
                yq_out[slot, line, part] = wide_sum(
                    made[slot, core, 2 + part, line, 1 - why],
                    core_in[slot, 2 + part, line, 1 - why],
                ).astype(jnp.bfloat16)
                q_keep[slot, line, part] = wide_sum(
                    made[slot, core, 2 + part, line, why], core_in[slot, 2 + part, line, why]
                ).astype(jnp.bfloat16)
            return carry

        lax.fori_loop(0, lines, rows, 0)
        x_copy(slot).start()
        yq_copy(slot).start()

    def stage_three(slot):
        x_copy(slot).wait()
        yq_copy(slot).wait()

        def rows(line, carry):
            yp_out[slot, line] = wide_sum(
                p_keep[slot, line, 1 - why], x_in[slot, line, 1 - why]
            ).astype(jnp.bfloat16)
            p_line[slot, line] = wide_sum(p_keep[slot, line, why], x_in[slot, line, why]).astype(
                jnp.bfloat16
            )
            for part in range(2):
                zq_out[slot, line, part] = wide_sum(
                    q_keep[slot, line, part], yq_in[slot, line, part]
                ).astype(jnp.bfloat16)
            return carry

        lax.fori_loop(0, lines, rows, 0)
        yp_copy(slot).start()
        for step in range(1, lines):
            zq_copy(slot, step).start()

    def stage_four(slot):
        yp_copy(slot).wait()
        for step in range(1, lines):
            zq_copy(slot, step).wait()

        def rows(line, carry):
            zp_out[slot, line] = wide_sum(p_line[slot, line], yp_in[slot, line]).astype(
                jnp.bfloat16
            )
            return carry

        lax.fori_loop(0, lines, rows, 0)
        total_q = zq_out[slot, zed].astype(jnp.float32)
        for step in range(1, lines):
            total_q = total_q + zq_in[slot, step - 1].astype(jnp.float32)
        xq_out[slot] = total_q.astype(jnp.bfloat16)
        for step in range(1, lines):
            zp_copy(slot, step).start()
        xq_copy(slot).start()

    def stage_five(unit, slot):
        for step in range(1, lines):
            zp_copy(slot, step).wait()
        xq_copy(slot).wait()
        total_p = zp_out[slot, zed].astype(jnp.float32)
        for step in range(1, lines):
            total_p = total_p + zp_in[slot, step - 1].astype(jnp.float32)
        rounded = total_p.astype(jnp.bfloat16)
        xp_out[slot] = rounded
        xp_copy(slot).start()
        @pl.when(unit >= 2)
        def _():
            out_copy(unit - 2, slot).wait()

        out_buf[slot, seq] = rounded.astype(jnp.float32)
        for part in range(2):
            out_buf[slot, 2 + part] = wide_sum(xq_out[slot, part], xq_in[slot, part])

    def stage_six(unit, slot):
        xp_copy(slot).wait()
        out_buf[slot, 1 - seq] = xp_in[slot].astype(jnp.float32)
        out_copy(unit, slot).start()

    def turn(at):
        def when_due(behind, run):
            unit = at - behind

            @pl.when(jnp.logical_and(unit >= 0, unit < total))
            def _():
                run(unit, lax.rem(unit, 2))

        when_due(5, stage_six)
        when_due(4, stage_five)
        when_due(3, lambda unit, slot: stage_four(slot))
        when_due(2, lambda unit, slot: stage_three(slot))
        when_due(1, lambda unit, slot: stage_two(slot))

        @pl.when(at < total)
        def _():
            compute(at)
            core_copy(lax.rem(at, 2)).start()

    def finish():
        for unit in (total - 2, total - 1):
            out_copy(unit, unit % 2).wait()

    return prefetch, turn, finish, total + 5


def scatter_scratch(toks, lines):
    bf = jnp.bfloat16
    dma = pltpu.SemaphoreType.DMA

    buf_f32 = pltpu.VMEM((2, PARTS, 64, TILE), jnp.float32)

    def buf(*shape):
        return pltpu.VMEM((2,) + shape, bf)

    return [
        buf(toks, D),
        pltpu.VMEM((toks, FF), bf),
        buf(toks, D),
        buf(toks, TILE),
        dma((4, 2)),
        buf(2, PARTS, lines, 2, 64, TILE),
        buf(PARTS, lines, 2, 64, TILE),
        buf(lines, 2, 64, TILE),
        buf(lines, 2, 64, TILE),
        buf(lines, 2, 64, TILE),
        buf(lines, 2, 64, TILE),
        buf(lines, 2, 64, TILE),
        buf(lines, 2, 64, TILE),
        buf(lines, 64, TILE),
        buf(lines, 64, TILE),
        buf(lines, 64, TILE),
        buf(lines, 2, 64, TILE),
        buf(lines - 1, 2, 64, TILE),
        buf(lines, 64, TILE),
        buf(lines - 1, 64, TILE),
        buf(2, 64, TILE),
        buf(2, 64, TILE),
        buf(64, TILE),
        buf(64, TILE),
        dma((2, 2)),
        dma((2, 2)),
        dma((2, 2)),
        dma((2, 2)),
        dma((2, lines - 1, 2)),
        dma((2, lines - 1, 2)),
        dma((2, 2)),
        dma((2, 2)),
        buf_f32,
        dma((2,)),
    ]


def summary_pieces(lines, refs):
    (
        flat_own,
        mod_own,
        flat_all,
        mod_all,
        core_in,
        core_total,
        x_in,
        x_total,
        y_in,
        y_total,
        z_in,
        pair_sem,
        line_sem,
    ) = refs
    seq = lax.axis_index("seq")
    dp = lax.axis_index("dp")
    core = lax.rem(dp, 2)
    why = lax.rem(dp // 2, 2)
    zed = dp // 4
    core_peer = {"seq": seq, "dp": dp + 1 - 2 * core}
    x_peer = {"seq": 1 - seq, "dp": dp}
    y_peer = {"seq": seq, "dp": dp + 2 - 4 * why}
    places = [lax.rem(zed + ahead, lines) for ahead in range(1, lines)]
    z_peers = [{"seq": seq, "dp": there * 4 + 2 * why + core} for there in places]

    def remote(source, target, sems, peer):
        return pltpu.make_async_remote_copy(
            src_ref=source,
            dst_ref=target,
            send_sem=sems.at[0],
            recv_sem=sems.at[1],
            device_id=peer,
            device_id_type=MESH,
        )

    def same(view, sems, peer):
        return remote(view, view, sems, peer)

    flat_core = remote(flat_own.at[1 - core], core_in, pair_sem.at[0], core_peer)
    flat_x = remote(core_total, x_in, pair_sem.at[1], x_peer)
    flat_y = remote(x_total, y_in, pair_sem.at[2], y_peer)
    flat_z = [
        remote(y_total.at[there], z_in.at[at], line_sem.at[0, at], peer)
        for at, (there, peer) in enumerate(zip(places, z_peers))
    ]
    back_z = [
        same(flat_all.at[core, zed], line_sem.at[1, at], peer) for at, peer in enumerate(z_peers)
    ]
    back_core = same(flat_all.at[core], pair_sem.at[3], core_peer)
    mod_x = remote(mod_own, mod_all.at[zed, why, core, seq], pair_sem.at[4], x_peer)
    mod_z = [
        same(mod_all.at[zed, why, core], line_sem.at[2, at], peer)
        for at, peer in enumerate(z_peers)
    ]
    mod_y = same(mod_all.at[:, why, core], pair_sem.at[5], y_peer)
    mod_core = same(mod_all.at[:, :, core], pair_sem.at[6], core_peer)

    def first():
        mod_all[zed, why, core, seq] = mod_own[...]
        flat_core.start()
        mod_x.start()

    def second():
        flat_core.wait()
        core_total[...] = flat_own[core] + core_in[...]
        flat_x.start()
        mod_x.wait()
        for copy in mod_z:
            copy.start()

    def third():
        flat_x.wait()
        x_total[...] = core_total[...] + x_in[...]
        flat_y.start()
        for copy in mod_z:
            copy.wait()
        mod_y.start()

    def fourth():
        flat_y.wait()
        y_total[...] = x_total[...] + y_in[...]
        for copy in flat_z:
            copy.start()

    def fifth():
        total = y_total[zed]
        for at, copy in enumerate(flat_z):
            copy.wait()
            total = total + z_in[at]
        flat_all[core, zed] = total
        for copy in back_z:
            copy.start()
        mod_y.wait()
        mod_core.start()

    def sixth():
        for copy in back_z:
            copy.wait()
        back_core.start()
        mod_core.wait()

    def seventh():
        back_core.wait()

    return [first, second, third, fourth, fifth, sixth, seventh]


def summary_scratch(lines):
    f32 = jnp.float32
    part = pltpu.VMEM((lines, 8, D), f32)
    return [
        pltpu.VMEM((2, lines, 8, D), f32),
        pltpu.VMEM((32, D), jnp.bfloat16),
        part,
        part,
        part,
        part,
        part,
        part,
        pltpu.VMEM((lines - 1, 8, D), f32),
        pltpu.SemaphoreType.DMA((7, 2)),
        pltpu.SemaphoreType.DMA((3, lines - 1, 2)),
    ]


def whole_backward_kernel(lines, *refs):
    refs = list(refs)

    def take(count):
        taken, refs[:] = tuple(refs[:count]), refs[count:]
        return taken

    (grad_in,) = take(1)
    operands = [take(10), take(10)]
    kept = [take(4), take(4)]
    mod_ref, keep_ref, final_rows, head_rows, misc_row, flat_in = take(6)
    units_out = take(1)
    outs = [take(4), take(4)]
    flat_all, mod_all = take(2)
    back_scratch = take(19)
    d_mod_ref, *d_bias_refs = take(3)
    (grad_sem,) = take(1)
    summary = take(11)
    scatter_refs = tuple(refs)

    dp = lax.axis_index("dp")
    seq = lax.axis_index("seq")
    core = lax.rem(dp, 2)
    why = lax.rem(dp // 2, 2)
    zed = dp // 4
    barrier = pltpu.get_barrier_semaphore()
    peers = [dp + 1 - 2 * core, dp + 2 - 4 * why]
    peers += [lax.rem(zed + ahead, lines) * 4 + 2 * why + core for ahead in range(1, lines)]
    for peer in [{"seq": seq, "dp": peer} for peer in peers] + [{"seq": 1 - seq, "dp": dp}]:
        pl.semaphore_signal(barrier, inc=1, device_id=peer, device_id_type=MESH)

    load = pltpu.make_async_copy(grad_in, back_scratch[0], grad_sem.at[0])
    load.start()
    begins, steps = [], []
    for at, mod_at in ((0, 12), (1, 0)):
        begin, step = backward_pieces(
            operands[at] + (mod_ref, keep_ref),
            outs[at],
            (d_mod_ref, d_bias_refs[at]) + back_scratch,
            mod_at,
        )
        begins.append(begin)
        steps.append(step)
    begins[0]()
    load.wait()

    sources = []
    for at in range(2):
        merged, a_one, a_two, act = kept[at]
        d_down, d_up, d_attn, d_qkv = outs[at]
        sources.append((merged, a_one, a_two, act, d_attn, d_qkv, d_up, d_down))
    prefetch, scatter, scatter_finish, turns = scatter_pieces(
        lines, sources, units_out + scatter_refs
    )
    flat_own, mod_own = summary[:2]
    summary_steps = summary_pieces(
        lines, (flat_own, mod_own, flat_all, mod_all) + summary[2:]
    )

    def put(row, value):
        flat_own[row // (8 * lines), row // 8 % lines, row % 8 : row % 8 + 1, :] = value

    def collect():
        d_patch = back_scratch[0][...].astype(jnp.bfloat16)
        for layer in range(2):
            for row in range(9):
                put(9 * layer + row, d_bias_refs[1 - layer][:, row * D : (row + 1) * D])
        put(18, jnp.sum(d_patch.astype(jnp.float32), axis=0, keepdims=True))
        g_patch = dot_nn(flat_in[...], d_patch)
        for row in range(16):
            put(19 + row, g_patch[row : row + 1, :])
            put(35 + row, head_rows[row : row + 1, :])
        put(51, misc_row[...])
        for row in range(52, 16 * lines):
            put(row, jnp.zeros((1, D), jnp.float32))
        d_mod_ref[24:28, :] = final_rows[...]
        d_mod_ref[28:32, :] = jnp.zeros((4, D), jnp.float32)
        mod_own[...] = d_mod_ref[...].astype(jnp.bfloat16)

    def back(at, carry):
        @pl.when(at < BACKWARD_STEPS)
        def _():
            steps[0](at)

        @pl.when(at == BACKWARD_STEPS)
        def _():
            begins[1]()

        @pl.when(jnp.logical_and(at >= BACKWARD_STEPS, at < 2 * BACKWARD_STEPS))
        def _():
            steps[1](at - BACKWARD_STEPS)

        return carry

    lax.fori_loop(0, 2, back, 0)
    prefetch(jnp.int32(0))
    pl.semaphore_wait(barrier, 2 + lines)

    def turn(at, carry):
        @pl.when(at <= 20)
        def _():
            lax.fori_loop(2 + at * 5 // 2, 2 + (at + 1) * 5 // 2, back, 0)

        prefetch(at + 1)
        scatter(at)

        @pl.when(at == 21)
        def _():
            collect()

        for offset, run in enumerate(summary_steps):

            @pl.when(at == 21 + offset)
            def _():
                run()

        return carry

    lax.fori_loop(0, turns, turn, 0)
    scatter_finish()


def whole_backward(
    grad, inputs, saved, weights, mods, keep, final_rows, head_rows, misc_row, flat_in, lines
):
    toks = grad.shape[0]
    vmem = pl.BlockSpec(memory_space=pltpu.VMEM)
    hbm = pl.BlockSpec(memory_space=pl.ANY)
    operands = [grad]
    for at in (1, 0):
        operands += backward_operands(inputs[at], saved[at], weights[at])
    for at in (1, 0):
        a_one, _, merged, _, _, a_two, _, act, _, _ = saved[at]
        operands += [merged, a_one, a_two, act]
    layer_outs = [jax.ShapeDtypeStruct((toks, width), kind) for width, kind in BACKWARD_OUTS]
    outs = pl.pallas_call(
        functools.partial(whole_backward_kernel, lines),
        out_shape=[jax.ShapeDtypeStruct((24, PARTS, 64, TILE), jnp.float32)]
        + layer_outs
        + layer_outs
        + [
            jax.ShapeDtypeStruct((2, lines, 8, D), jnp.float32),
            jax.ShapeDtypeStruct((lines, 2, 2, 2, 32, D), jnp.bfloat16),
        ],
        in_specs=[hbm] * len(operands) + [vmem] * 6,
        out_specs=[hbm] * 9 + [vmem] * 2,
        scratch_shapes=backward_scratch(toks)
        + [
            pltpu.VMEM((32, D), jnp.float32),
            pltpu.VMEM((1, 9 * D), jnp.float32),
            pltpu.VMEM((1, 9 * D), jnp.float32),
            pltpu.SemaphoreType.DMA((1,)),
        ]
        + summary_scratch(lines)
        + scatter_scratch(toks, lines),
        compiler_params=pltpu.CompilerParams(
            collective_id=1, has_side_effects=True, vmem_limit_bytes=61 * 1024 * 1024
        ),
        cost_estimate=pl.CostEstimate(
            flops=104 * toks * D * D,
            bytes_accessed=300 * 1024 * 1024,
            transcendentals=8 * toks * D,
        ),
    )(*operands, mods, keep, final_rows, head_rows, misc_row, flat_in)
    return outs[0], outs[9], outs[10]


def gather_rows(shard):
    return lax.all_gather(shard.astype(jnp.bfloat16), "dp", axis=0, tiled=True)


def kernels_fit():
    dp_parts = lax.axis_size("dp")
    return (
        lax.axis_size("seq") == 2
        and dp_parts % 4 == 0
        and D // dp_parts == 64
        and FF // dp_parts == PARTS * 64
    )


def reduce_rows(partial):
    owned = lax.psum_scatter(
        partial.astype(jnp.bfloat16), "dp", scatter_dimension=0, tiled=True
    )
    return lax.psum(owned, "seq").astype(jnp.float32)


def unit_sums(units):
    def by_columns(some):
        return some.transpose(2, 0, 1, 3).reshape(64, some.shape[0] * D)

    return (
        by_columns(units[9:]),
        by_columns(units[8:9]),
        by_columns(units[4:8]),
        units[:4].transpose(1, 2, 0, 3).reshape(PARTS * 64, D),
    )


def adamw(weight, gradient, first, second, rate):
    first_new = BETA_ONE * first + (1.0 - BETA_ONE) * gradient
    second_new = BETA_TWO * second + (1.0 - BETA_TWO) * gradient * gradient
    first_hat = first_new / (1.0 - BETA_ONE**STEP)
    second_hat = second_new / (1.0 - BETA_TWO**STEP)
    return (
        weight - rate * (first_hat / (jnp.sqrt(second_hat) + EPSILON) + DECAY * weight),
        first_new,
        second_new,
    )


def body(
    latents,
    noise_target,
    pad_mask,
    labels,
    timesteps,
    embed_rows,
    first_embed,
    second_embed,
    class_table,
    first_table,
    second_table,
    qkv_weight,
    first_qkv,
    second_qkv,
    proj_weight,
    first_proj,
    second_proj,
    up_weight,
    first_up,
    second_up,
    down_weight,
    first_down,
    second_down,
    cond_weight,
    first_cond,
    second_cond,
    head_weight,
    first_head,
    second_head,
    all_biases,
    first_bias,
    second_bias,
):
    seq_parts = lax.axis_size("seq")
    dp_parts = lax.axis_size("dp")
    seq_at = lax.axis_index("seq")
    dp_at = lax.axis_index("dp")
    lines = dp_parts // 4
    group, half_rows, _ = latents.shape
    images = group // seq_parts
    everyone = group * dp_parts
    own_cols = embed_rows.shape[1]
    own_place = dp_at * own_cols
    cond_cols = cond_weight.shape[1]
    pieces = cond_cols // D
    bias_base = 3 * D + cond_cols
    by_kernel = kernels_fit()
    packed = jnp.concatenate(
        [latents, noise_target, pad_mask.astype(jnp.float32)[:, :, None]], axis=2
    )
    shards = [
        weight[at].astype(jnp.bfloat16)
        for at in range(LAYERS)
        for weight in (qkv_weight, proj_weight, up_weight, down_weight)
    ]
    narrow = jnp.concatenate(
        [embed_rows[: PATCH_IN + FREQ].T, head_weight], axis=1
    ).astype(jnp.bfloat16)
    if by_kernel:
        ids = jnp.stack([labels, timesteps])
        parts = jnp.stack([ids // 32, ids % 32]).astype(jnp.bfloat16).reshape(-1, 1)
        parts = jnp.pad(parts, ((0, own_cols - parts.shape[0]), (0, 0)))
        width = narrow.shape[1]
        block = jnp.concatenate(
            [narrow, parts, jnp.zeros((own_cols, 383 - width), jnp.bfloat16)], axis=1
        )
        small = gather_small(block, lines, 4)
        parts = small[:, width].astype(jnp.float32).reshape(dp_parts, own_cols)[:, : 4 * group]
        parts = parts.reshape(dp_parts, 2, 2, group)
        ids = (parts[:, 0] * 32.0 + parts[:, 1]).astype(jnp.int32)
        ids = ids.transpose(1, 0, 2).reshape(2, everyone)
        theirs = lax.dynamic_slice(
            packed, ((1 - seq_at) * images, 0, 0), (images,) + packed.shape[1:]
        )
        mine = lax.dynamic_slice(packed, (seq_at * images, 0, 0), (images,) + packed.shape[1:])
        came = lax.ppermute(theirs, "seq", [(0, 1), (1, 0)])
        packed = jnp.concatenate(
            [jnp.where(seq_at == 0, mine, came), jnp.where(seq_at == 0, came, mine)], axis=1
        )
    else:
        small = lax.all_gather(narrow, "dp", axis=0, tiled=True)
        ids = lax.all_gather(jnp.stack([labels, timesteps]), "dp", axis=1, tiled=True)
        packed = lax.all_to_all(packed, "seq", split_axis=0, concat_axis=1, tiled=True)
    tok_rows = packed.shape[1]
    toks = images * tok_rows
    latents, noise_target, keep_rows = (
        packed[:, :, :PATCH_IN],
        packed[:, :, PATCH_IN : 2 * PATCH_IN],
        packed[:, :, 2 * PATCH_IN],
    )
    patch_part = small[:, :PATCH_IN]
    freq_part = small[:, PATCH_IN : PATCH_IN + FREQ]
    head_full = small[:, PATCH_IN + FREQ : PATCH_IN + FREQ + OUT_CH]
    time_own = embed_rows[PATCH_IN + FREQ :].astype(jnp.bfloat16)
    cond_own = cond_weight.astype(jnp.bfloat16)

    features = time_features(ids[1], FREQ).astype(jnp.bfloat16)
    time_pre = dot_nt(features, freq_part) + all_biases[D : 2 * D]
    time_hidden = jax.nn.silu(time_pre).astype(jnp.bfloat16)
    second_bias_own = lax.dynamic_slice(all_biases, (2 * D + own_place,), (own_cols,))
    onehot = (ids[0][:, None] == jnp.arange(NCLASS, dtype=jnp.int32)[None, :]).astype(jnp.float32)
    condition = (
        matdot(time_hidden, time_own)
        + second_bias_own
        + matdot(onehot.astype(jnp.bfloat16), class_table.astype(jnp.bfloat16))
    )
    cond_act = jax.nn.silu(condition).astype(jnp.bfloat16)
    plane_act = lax.dynamic_index_in_dim(
        cond_act.reshape(dp_parts, seq_parts, images, own_cols), seq_at, 1, keepdims=False
    ).reshape(dp_parts * images, own_cols)
    partial = matdot(plane_act, cond_own).reshape(dp_parts, images, pieces, D)
    partial = partial.transpose(0, 2, 1, 3).reshape(dp_parts, pieces * images, D)
    mod_bias = jnp.repeat(all_biases[3 * D : bias_base].reshape(pieces, D), images, axis=0)

    position = position_table(jnp.arange(tok_rows, dtype=jnp.int32), D, GRID)
    flat_in = latents.astype(jnp.bfloat16).reshape(toks, PATCH_IN)
    stream = (dot_nt(flat_in, patch_part) + all_biases[:D]).reshape(
        images, tok_rows, D
    ) + position[None]
    stream = stream.reshape(toks, D)
    layer_bias = [
        all_biases[bias_base + at * 9 * D : bias_base + (at + 1) * 9 * D].reshape(1, 9 * D)
        for at in range(LAYERS)
    ]
    if by_kernel:
        weights_kept, saved_kept, mods = whole_forward(
            shards,
            partial.reshape(lines, 2, 2, pieces * images, D),
            mod_bias,
            stream,
            layer_bias,
            keep_rows,
            lines,
        )
    else:
        mods = mod_bias + lax.psum_scatter(
            partial, "dp", scatter_dimension=0, tiled=True
        ).reshape(pieces * images, D)
        weights_kept = [
            [gather_rows(shard) for shard in shards[4 * at : 4 * at + 4]] for at in range(LAYERS)
        ]
        saved_kept = []
        upper = stream
        for at in range(LAYERS):
            saved_kept.append(
                forward_layer(
                    upper, mods, 6 * images * at, layer_bias[at], keep_rows, weights_kept[at]
                )
            )
            upper = saved_kept[at][-1]
    inputs_kept = [stream] + [saved[-1] for saved in saved_kept]
    final, time_own = lax.optimization_barrier((inputs_kept[-1], time_own))
    time_full = lax.all_gather(time_own, "dp", axis=1, tiled=True)
    final_at = 6 * LAYERS * images
    final_shift = mods[final_at : final_at + images]
    final_scale = mods[final_at + images :]
    moved, final_back = jax.vjp(
        modulate, final.reshape(images, tok_rows, D), final_shift, final_scale
    )
    a_final = moved.astype(jnp.bfloat16).reshape(toks, D)
    head_out = matdot(a_final, head_full) + all_biases[NBIAS - OUT_CH :]
    split_out = head_out.reshape(images, tok_rows, 4, 2, OUT_CH // 8)
    predicted = split_out[:, :, :, 0, :].reshape(images, tok_rows, PATCH_IN)
    errors = predicted - noise_target
    loss_part = jnp.sum(keep_rows[:, :, None] * errors * errors)
    count_part = PATCH_IN * jnp.sum(keep_rows)
    d_pred = (2.0 * keep_rows[:, :, None] * errors).reshape(images, tok_rows, 4, 1, OUT_CH // 8)
    d_head = (
        jnp.concatenate([d_pred, jnp.zeros_like(d_pred)], axis=3)
        .reshape(toks, OUT_CH)
        .astype(jnp.bfloat16)
    )
    d_a_final = dot_nt(d_head, head_full).reshape(images, tok_rows, D)
    d_stream, d_final_shift, d_final_scale = final_back(d_a_final)
    d_stream = d_stream.reshape(toks, D)
    d_bias_head = column_sum(d_head)
    if by_kernel:
        d_noise = d_pred.astype(jnp.bfloat16).reshape(toks, PATCH_IN)
        misc_row = jnp.concatenate([d_bias_head, loss_part[None], count_part[None]])
        misc_row = jnp.pad(misc_row, (0, D - misc_row.shape[0])).reshape(1, D)
        units, flat, mod_all = whole_backward(
            d_stream,
            inputs_kept,
            saved_kept,
            weights_kept,
            mods,
            keep_rows,
            jnp.concatenate([d_final_shift, d_final_scale], axis=0),
            matdot(d_noise.T, a_final),
            misc_row,
            flat_in.T,
            lines,
        )
        layer_sums = [unit_sums(units[12:]), unit_sums(units[:12])]
        d_modulation = (
            mod_all[..., : pieces * images, :]
            .reshape(dp_parts * seq_parts, pieces, images, D)
            .transpose(0, 2, 1, 3)
            .reshape(everyone, cond_cols)
        )
        flat = flat.reshape(64, D)
        d_bias_mod = column_sum(d_modulation)
        d_bias_patch = flat[18]
        d_bias_layers = flat[:18].reshape(-1)
        d_bias_head, loss_sum, loss_count = (
            flat[51, :OUT_CH],
            flat[51, OUT_CH],
            flat[51, OUT_CH + 1],
        )
        own_flat = lax.dynamic_slice(flat, (0, own_place), (64, own_cols))
        s_patch = own_flat[19:35]
        s_head = own_flat[35:51].T.reshape(own_cols, 4, 1, OUT_CH // 8)
        s_head = jnp.concatenate([s_head, jnp.zeros_like(s_head)], axis=2)
        s_head = s_head.reshape(own_cols, OUT_CH)
    else:
        layer_sums = [None] * LAYERS
        layer_bias_grads = [None] * LAYERS
        modul_grads = [None] * LAYERS
        for at in reversed(range(LAYERS)):
            d_stream, d_mod, factors, d_bias = backward_layer(
                d_stream,
                inputs_kept[at],
                saved_kept[at],
                mods,
                6 * images * at,
                keep_rows,
                weights_kept[at],
            )
            merged, a_one, a_two, active, d_attn, d_qkv, d_up, d_down = factors
            layer_sums[at] = (
                reduce_rows(matdot(a_one.T, d_qkv)),
                reduce_rows(matdot(merged.T, d_attn)),
                reduce_rows(matdot(a_two.T, d_up)),
                reduce_rows(matdot(active.T, d_down)),
            )
            modul_grads[at] = d_mod.reshape(6, images, D).transpose(1, 0, 2).reshape(images, 6 * D)
            layer_bias_grads[at] = d_bias.reshape(-1)
        d_mod_own = jnp.concatenate(
            modul_grads + [d_final_shift, d_final_scale], axis=1
        ).astype(jnp.bfloat16)
        d_patch = d_stream.astype(jnp.bfloat16)
        d_modulation = lax.all_gather(d_mod_own, ("dp", "seq"), axis=0, tiled=True)
        (
            d_bias_patch,
            d_bias_mod,
            d_bias_layers,
            d_bias_head,
            loss_sum,
            loss_count,
            g_patch,
            g_head,
        ) = lax.psum(
            (
                column_sum(d_patch),
                column_sum(d_mod_own),
                jnp.concatenate(layer_bias_grads),
                d_bias_head,
                loss_part,
                count_part,
                matdot(flat_in.T, d_patch),
                matdot(a_final.T, d_head),
            ),
            ("seq", "dp"),
        )
        s_patch = lax.dynamic_slice(g_patch, (0, own_place), (PATCH_IN, own_cols))
        s_head = lax.dynamic_slice(g_head, (own_place, 0), (own_cols, OUT_CH))
    d_cond_act = dot_nt(d_modulation, cond_own)
    _, silu_back = jax.vjp(jax.nn.silu, condition)
    d_condition = silu_back(d_cond_act)[0]
    d_time_own = d_condition.astype(jnp.bfloat16)
    if by_kernel:
        d_time = gather_small(
            jnp.pad(d_time_own.T, ((0, 0), (0, everyone))), lines, 5
        )
        d_time = d_time[:, :everyone].T
    else:
        d_time = lax.all_gather(d_time_own, "dp", axis=1, tiled=True)
    d_time_hidden = dot_nt(d_time, time_full)
    _, time_back = jax.vjp(jax.nn.silu, time_pre)
    d_time_pre = time_back(d_time_hidden)[0].astype(jnp.bfloat16)
    s_cond = matdot(cond_act.T, d_modulation)
    s_table = jnp.dot(onehot.T, d_condition, precision=lax.Precision.HIGHEST)
    g_time = matdot(time_hidden.T, d_time_own)
    g_freq = matdot(
        features.T, lax.dynamic_slice(d_time_pre, (0, own_place), (everyone, own_cols))
    )
    bias_grad = jnp.concatenate(
        [
            d_bias_patch,
            column_sum(d_time_pre),
            column_sum(d_time),
            d_bias_mod,
            d_bias_layers,
            d_bias_head,
        ]
    )
    s_embed = jnp.concatenate([s_patch, g_freq, g_time], axis=0)
    s_qkv = jnp.stack([layer_sums[at][0] for at in range(LAYERS)])
    s_proj = jnp.stack([layer_sums[at][1] for at in range(LAYERS)])
    s_up = jnp.stack([layer_sums[at][2] for at in range(LAYERS)])
    s_down = jnp.stack([layer_sums[at][3] for at in range(LAYERS)])
    new_embed, new_first_embed, new_second_embed = adamw(
        embed_rows, s_embed, first_embed, second_embed, RATE_MATRIX
    )
    new_table, new_first_table, new_second_table = adamw(
        class_table, s_table, first_table, second_table, RATE_TABLE
    )
    new_qkv, new_first_qkv, new_second_qkv = adamw(
        qkv_weight, s_qkv, first_qkv, second_qkv, RATE_MATRIX
    )
    new_proj, new_first_proj, new_second_proj = adamw(
        proj_weight, s_proj, first_proj, second_proj, RATE_MATRIX
    )
    new_up, new_first_up, new_second_up = adamw(up_weight, s_up, first_up, second_up, RATE_MATRIX)
    new_down, new_first_down, new_second_down = adamw(
        down_weight, s_down, first_down, second_down, RATE_MATRIX
    )
    new_cond, new_first_cond, new_second_cond = adamw(
        cond_weight, s_cond, first_cond, second_cond, RATE_MATRIX
    )
    new_head, new_first_head, new_second_head = adamw(
        head_weight, s_head, first_head, second_head, RATE_MATRIX
    )
    new_bias, new_first_bias, new_second_bias = adamw(
        all_biases, bias_grad, first_bias, second_bias, RATE_BIAS
    )
    return (
        loss_sum,
        loss_count,
        new_embed,
        new_first_embed,
        new_second_embed,
        new_table,
        new_first_table,
        new_second_table,
        new_qkv,
        new_first_qkv,
        new_second_qkv,
        new_proj,
        new_first_proj,
        new_second_proj,
        new_up,
        new_first_up,
        new_second_up,
        new_down,
        new_first_down,
        new_second_down,
        new_cond,
        new_first_cond,
        new_second_cond,
        new_head,
        new_first_head,
        new_second_head,
        new_bias,
        new_first_bias,
        new_second_bias,
    )


def solution(mesh):
    placed = (
        P("dp", "seq", None),
        P("dp", "seq", None),
        P("dp", "seq"),
        P("dp"),
        P("dp"),
        P(None, "dp"),
        P(None, "dp"),
        P(None, "dp"),
        P(None, "dp"),
        P(None, "dp"),
        P(None, "dp"),
        P(None, "dp", None),
        P(None, "dp", None),
        P(None, "dp", None),
        P(None, "dp", None),
        P(None, "dp", None),
        P(None, "dp", None),
        P(None, "dp", None),
        P(None, "dp", None),
        P(None, "dp", None),
        P(None, "dp", None),
        P(None, "dp", None),
        P(None, "dp", None),
        P("dp", None),
        P("dp", None),
        P("dp", None),
        P("dp", None),
        P("dp", None),
        P("dp", None),
        P(),
        P(),
        P(),
    )
    return jax.shard_map(
        body,
        mesh=mesh,
        in_specs=placed,
        out_specs=(
            P(),
            P(),
            P(None, "dp"),
            P(None, "dp"),
            P(None, "dp"),
            P(None, "dp"),
            P(None, "dp"),
            P(None, "dp"),
            P(None, "dp", None),
            P(None, "dp", None),
            P(None, "dp", None),
            P(None, "dp", None),
            P(None, "dp", None),
            P(None, "dp", None),
            P(None, "dp", None),
            P(None, "dp", None),
            P(None, "dp", None),
            P(None, "dp", None),
            P(None, "dp", None),
            P(None, "dp", None),
            P("dp", None),
            P("dp", None),
            P("dp", None),
            P("dp", None),
            P("dp", None),
            P("dp", None),
            P(),
            P(),
            P(),
        ),
        check_vma=False,
    )
```

```python
import functools
import math

import jax
import jax.numpy as jnp
from jax import lax
from jax.experimental import pallas as pl
from jax.experimental.pallas import tpu as pltpu
from jax.sharding import PartitionSpec as P

D = 1024
HEADS = 16
HEAD_DIM = 64
FF = 4096
NCLASS = 1001
FREQ = 256
OUT_CH = 32
PATCH_IN = 16
GRID = 16
LAYERS = 2
STEP = 10
NBIAS = 35872


BETA_ONE = 0.9
BETA_TWO = 0.999
EPSILON = 1e-08
DECAY = 0.01
RATE_MATRIX = 0.06
RATE_TABLE = 0.4
RATE_BIAS = 0.2

MESH = pl.DeviceIdType.MESH
TILE = 256
PARTS = 4
SHARED = 640
SHARED_ROWS = 80
GATHER_LAGS = (2, 2, 2, 1)
HALF = 512
GELU_IN = math.sqrt(2.0 / math.pi)
GELU_CUBE = 0.044715
FORWARD_STEPS = 30
BACKWARD_STEPS = 27


def matdot(left, right):
    return jnp.dot(left, right, preferred_element_type=jnp.float32)


def layer_norm(stream):
    row_mean = jnp.mean(stream, axis=-1, keepdims=True)
    centered = stream - row_mean
    variance = jnp.mean(centered * centered, axis=-1, keepdims=True)
    return centered * lax.rsqrt(variance + 1e-06)


def modulate(stream, shift_by, scale_by):
    return layer_norm(stream) * (1.0 + scale_by[:, None, :]) + shift_by[:, None, :]


def position_table(position_ids, feature_width, grid_side):
    quarter_width = feature_width // 4
    omegas = 1.0 / 10000.0 ** (jnp.arange(quarter_width, dtype=jnp.float32) / quarter_width)
    col_angle = (position_ids % grid_side).astype(jnp.float32)[:, None] * omegas[None, :]
    row_angle = (position_ids // grid_side).astype(jnp.float32)[:, None] * omegas[None, :]
    return jnp.concatenate(
        [jnp.sin(col_angle), jnp.cos(col_angle), jnp.sin(row_angle), jnp.cos(row_angle)], axis=1
    )


def time_features(timesteps, feature_width):
    half_width = feature_width // 2
    frequencies = jnp.exp(
        -math.log(10000.0) * jnp.arange(half_width, dtype=jnp.float32) / half_width
    )
    angles = timesteps.astype(jnp.float32)[:, None] * frequencies[None, :]
    return jnp.concatenate([jnp.cos(angles), jnp.sin(angles)], axis=1)


def column_sum(grad_bf):
    return jnp.sum(grad_bf.astype(jnp.float32), axis=0)


def dot_nn(left, right):
    return jnp.dot(left, right, preferred_element_type=jnp.float32)


def dot_nt(left, right):
    return lax.dot_general(
        left, right, (((1,), (1,)), ((), ())), preferred_element_type=jnp.float32
    )


def dot_tn(left, right):
    return lax.dot_general(
        left, right, (((0,), (0,)), ((), ())), preferred_element_type=jnp.float32
    )


def column_tile(at, size=HALF):
    return pl.ds(pl.multiple_of(at * size, size), size)


def normalized(rows):
    centered = rows - jnp.mean(rows, axis=-1, keepdims=True)
    variance = jnp.mean(centered * centered, axis=-1, keepdims=True)
    inverse = lax.rsqrt(variance + 1e-06)
    return centered * inverse, inverse


def head_probs(queries, keys, keep):
    scores = jnp.where(keep > 0, dot_nt(queries, keys), -1000000000.0)
    raised = jnp.exp(scores - jnp.max(scores, axis=-1, keepdims=True))
    return raised * (1.0 / jnp.sum(raised, axis=-1, keepdims=True))


def within(at, first, size):
    return jnp.logical_and(at >= first, at < first + size)


def forward_pieces(refs, mod_at):
    (
        x_ref,
        mod_ref,
        bias_ref,
        keep_ref,
        w_qkv,
        w_proj,
        w_up,
        w_down,
        a_one_out,
        qkv_out,
        merged_out,
        attn_out,
        x_one_out,
        a_two_out,
        pre_out,
        act_out,
        down_out,
        x_two_out,
        a_buf,
        qkv_buf,
        merged_buf,
        attn_buf,
        x_one_buf,
        a_two_buf,
        pre_buf,
        act_buf,
        down_buf,
        x_two_buf,
        wide_buf,
        tall_buf,
        load_sem,
        tile_sem,
        save_sem,
    ) = refs
    images, toks = keep_ref.shape
    bf = jnp.bfloat16

    def save(at, source, target):
        return pltpu.make_async_copy(source, target, save_sem.at[at])

    saves = [
        save(at, *pair)
        for at, pair in enumerate(
            [
                (a_buf, a_one_out),
                (qkv_buf, qkv_out),
                (merged_buf, merged_out),
                (attn_buf, attn_out),
                (x_one_buf, x_one_out),
                (a_two_buf, a_two_out),
                (down_buf, down_out),
                (x_two_buf, x_two_out),
                (act_buf, act_out),
            ]
        )
    ]

    def wide_load(source, tile, slot):
        return pltpu.make_async_copy(
            source.at[:, :, :, :, column_tile(tile)], wide_buf.at[slot], load_sem.at[0, slot]
        )

    def tall_load(tile, slot):
        return pltpu.make_async_copy(
            w_down.at[:, :, :, :, column_tile(tile, TILE)], tall_buf.at[slot], load_sem.at[1, slot]
        )

    def tile_saves(tile, slot):
        return [
            pltpu.make_async_copy(
                pre_buf.at[slot], pre_out.at[:, column_tile(tile)], tile_sem.at[0, slot]
            ),
        ]

    def wide_tile(slot):
        return wide_buf[slot].reshape(D, HALF)

    def tall_tile(slot):
        return tall_buf[slot].reshape(FF, TILE)

    def loads(at, run):
        slot = lax.rem(at, 2)

        @pl.when(within(at, 1, 6))
        def _():
            run(wide_load(w_qkv, at - 1, slot))

        @pl.when(within(at, 15, 2))
        def _():
            run(wide_load(w_proj, at - 15, slot))

        @pl.when(within(at, 18, 8))
        def _():
            run(wide_load(w_up, at - 18, slot))

        @pl.when(within(at, 26, 4))
        def _():
            run(tall_load(at - 26, slot))

    def modulated(source, target, piece):
        def rows_of(block, carry):
            image = block // 4
            rows = pl.ds(pl.multiple_of(block * 64, 64), 64)
            shift = mod_ref[pl.ds(mod_at + 2 * piece + image, 1), :]
            scale = mod_ref[pl.ds(mod_at + 2 * piece + 2 + image, 1), :]
            unit, _ = normalized(source[rows, :])
            target[rows, :] = (unit * (1.0 + scale) + shift).astype(bf)
            return carry

        lax.fori_loop(0, images * toks // 64, rows_of, 0)

    def attend(image, pair):
        rows = pl.ds(pl.multiple_of(image * toks, toks), toks)
        low = lax.broadcasted_iota(jnp.int32, (toks, 128), 1) < 64
        queries = qkv_buf[rows, column_tile(pair, 128)] * jnp.asarray(0.125, bf)
        keys = qkv_buf[rows, column_tile(8 + pair, 128)]
        values = qkv_buf[rows, column_tile(16 + pair, 128)]
        keep = keep_ref[pl.ds(image, 1), :]
        zero = jnp.zeros_like(queries)
        total = jnp.zeros((toks, 128), jnp.float32)
        for own in (low, jnp.logical_not(low)):
            probs = head_probs(jnp.where(own, queries, zero), keys, keep)
            total = total + dot_nn(probs.astype(bf), jnp.where(own, values, zero))
        merged_buf[rows, column_tile(pair, 128)] = total.astype(bf)

    def step(at):
        slot = lax.rem(at, 2)
        loads(at + 1, lambda copy: copy.start())
        loads(at, lambda copy: copy.wait())

        @pl.when(at == 0)
        def _():
            modulated(x_ref, a_buf, 0)
            saves[0].start()

        @pl.when(within(at, 1, 6))
        def _():
            cols = column_tile(at - 1)
            for image in range(images):
                rows = pl.ds(image * toks, toks)
                qkv_buf[rows, cols] = (
                    dot_nn(a_buf[rows, :], wide_tile(slot)) + bias_ref[:, cols]
                ).astype(bf)

        @pl.when(at == 7)
        def _():
            saves[1].start()

        @pl.when(within(at, 7, 8))
        def _():
            for turn in range(2):
                item = (at - 7) * 2 + turn
                attend(item // 8, lax.rem(item, 8))

        @pl.when(within(at, 15, 2))
        def _():
            cols = column_tile(at - 15)
            for image in range(images):
                rows = pl.ds(image * toks, toks)
                attn = dot_nn(merged_buf[rows, :], wide_tile(slot)) + bias_ref[
                    :, column_tile(at - 15 + 6)
                ]
                attn_buf[rows, cols] = attn
                gate = mod_ref[mod_at + 4 + image : mod_at + 5 + image, cols]
                x_one_buf[rows, cols] = x_ref[rows, cols] + gate * attn

        @pl.when(at == 17)
        def _():
            for which in (2, 3, 4):
                saves[which].start()
            modulated(x_one_buf, a_two_buf, 3)
            saves[5].start()

        @pl.when(within(at, 18, 8))
        def _():
            tile = at - 18

            @pl.when(tile >= 2)
            def _():
                for copy in tile_saves(tile - 2, slot):
                    copy.wait()

            for image in range(images):
                rows = pl.ds(image * toks, toks)
                pre = dot_nn(a_two_buf[rows, :], wide_tile(slot)) + bias_ref[:, column_tile(tile + 8)]
                pre_buf[slot, rows, :] = pre
                inner = jnp.tanh(GELU_IN * (pre + GELU_CUBE * pre * pre * pre))
                active = (0.5 * pre * (1.0 + inner)).astype(bf)
                act_buf[rows, column_tile(tile)] = active

            for copy in tile_saves(tile, slot):
                copy.start()

        @pl.when(at == 26)
        def _():
            saves[8].start()

        @pl.when(within(at, 26, 4))
        def _():
            cols = column_tile(at - 26, TILE)
            bias_cols = column_tile(at - 26 + 32, TILE)
            for image in range(images):
                rows = pl.ds(image * toks, toks)
                down = dot_nn(act_buf[rows, :], tall_tile(slot)) + bias_ref[:, bias_cols]
                down_buf[rows, cols] = down
                gate = mod_ref[mod_at + 10 + image : mod_at + 11 + image, cols]
                x_two_buf[rows, cols] = x_one_buf[rows, cols] + gate * down

        @pl.when(at == FORWARD_STEPS - 1)
        def _():
            saves[6].start()
            saves[7].start()

    def finish():
        for tile in (6, 7):
            for copy in tile_saves(tile, tile % 2):
                copy.wait()
        for copy in saves:
            copy.wait()

    return step, finish


FORWARD_OUTS = [
    (D, jnp.bfloat16),
    (3 * D, jnp.bfloat16),
    (D, jnp.bfloat16),
    (D, jnp.float32),
    (D, jnp.float32),
    (D, jnp.bfloat16),
    (FF, jnp.float32),
    (FF, jnp.bfloat16),
    (D, jnp.float32),
    (D, jnp.float32),
]


def forward_scratch(toks):
    bf, f32 = jnp.bfloat16, jnp.float32
    return [
        pltpu.VMEM((toks, D), bf),
        pltpu.VMEM((toks, 3 * D), bf),
        pltpu.VMEM((toks, D), bf),
        pltpu.VMEM((toks, D), f32),
        pltpu.VMEM((toks, D), f32),
        pltpu.VMEM((toks, D), bf),
        pltpu.VMEM((2, toks, HALF), f32),
        pltpu.VMEM((toks, FF), bf),
        pltpu.VMEM((toks, D), f32),
        pltpu.VMEM((toks, D), f32),
        pltpu.VMEM((2, 4, 2, 2, 64, HALF), bf),
        pltpu.VMEM((2, 4, 2, 2, 256, TILE), bf),
        pltpu.SemaphoreType.DMA((2, 2)),
        pltpu.SemaphoreType.DMA((2, 2)),
        pltpu.SemaphoreType.DMA((9,)),
    ]


def forward_kernel(mod_at, *refs):
    step, finish = forward_pieces(refs, mod_at)

    def turn(at, carry):
        step(at)
        return carry

    lax.fori_loop(0, FORWARD_STEPS, turn, 0)
    finish()


def grouped(weights):
    return [each.reshape(4, 2, 2, -1, each.shape[-1]) for each in weights]


def forward_layer(x, mods, mod_at, biases, keep, weights):
    toks = x.shape[0]
    return pl.pallas_call(
        functools.partial(forward_kernel, mod_at),
        out_shape=[jax.ShapeDtypeStruct((toks, width), kind) for width, kind in FORWARD_OUTS],
        in_specs=[pl.BlockSpec(memory_space=pltpu.VMEM)] * 4
        + [pl.BlockSpec(memory_space=pl.ANY)] * 4,
        out_specs=[pl.BlockSpec(memory_space=pl.ANY)] * len(FORWARD_OUTS),
        scratch_shapes=forward_scratch(toks),
        compiler_params=pltpu.CompilerParams(vmem_limit_bytes=56 * 1024 * 1024),
        cost_estimate=pl.CostEstimate(
            flops=24 * toks * D * D, bytes_accessed=60 * 1024 * 1024, transcendentals=4 * toks * D
        ),
    )(x, mods, biases, keep, *grouped(weights))


def backward_pieces(ins, outs, scratch, mod_at):
    (
        x_hbm,
        x_one_hbm,
        attn_hbm,
        down_hbm,
        qkv_hbm,
        pre_hbm,
        w_qkv,
        w_proj,
        w_up,
        w_down,
        mod_ref,
        keep_ref,
    ) = ins
    d_down_out, d_up_out, d_attn_out, d_qkv_out = outs
    (
        d_mod_ref,
        d_bias_ref,
        grad_ref,
        side_ref,
        x_one_ref,
        attn_ref,
        qkv_ref,
        total_buf,
        d_x_one_buf,
        d_down_buf,
        d_up_buf,
        d_attn_buf,
        d_heads_buf,
        d_qkv_buf,
        pre_buf,
        wide_buf,
        tall_buf,
        load_sem,
        tile_sem,
        save_sem,
        in_sem,
    ) = scratch
    images, toks = keep_ref.shape
    bf = jnp.bfloat16
    blocks = toks // 64
    saves = [
        pltpu.make_async_copy(source, target, save_sem.at[at])
        for at, (source, target) in enumerate(
            [
                (d_down_buf, d_down_out),
                (d_attn_buf, d_attn_out),
                (d_qkv_buf, d_qkv_out),
            ]
        )
    ]

    in_down, in_x_one, in_attn, in_qkv, in_x = [
        pltpu.make_async_copy(source, target, in_sem.at[at])
        for at, (source, target) in enumerate(
            [
                (down_hbm, side_ref),
                (x_one_hbm, x_one_ref),
                (attn_hbm, attn_ref),
                (qkv_hbm, qkv_ref),
                (x_hbm, side_ref),
            ]
        )
    ]

    def begin():
        for copy in (in_down, in_x_one, in_attn, in_qkv):
            copy.start()

    def wide_load(source, tile, slot):
        return pltpu.make_async_copy(
            source.at[:, :, :, :, column_tile(tile)], wide_buf.at[slot], load_sem.at[0, slot]
        )

    def tall_load(tile, slot):
        return pltpu.make_async_copy(
            w_down.at[tile // 2, lax.rem(tile, 2)], tall_buf.at[slot], load_sem.at[1, slot]
        )

    def pre_load(tile, slot):
        return pltpu.make_async_copy(
            pre_hbm.at[:, column_tile(tile)], pre_buf.at[slot], load_sem.at[2, slot]
        )

    def up_save(tile, slot):
        return pltpu.make_async_copy(
            d_up_buf.at[slot], d_up_out.at[:, column_tile(tile)], tile_sem.at[slot]
        )

    def wide_tile(slot):
        return wide_buf[slot].reshape(D, HALF)

    def tall_tile(slot):
        return tall_buf[slot].reshape(HALF, D)

    def loads(at, run):
        slot = lax.rem(at, 2)

        @pl.when(within(at, 1, 8))
        def _():
            run(tall_load(at - 1, slot))
            run(wide_load(w_up, at - 1, slot))
            run(pre_load(at - 1, slot))

        @pl.when(within(at, 10, 2))
        def _():
            run(wide_load(w_proj, at - 10, slot))

        @pl.when(within(at, 20, 6))
        def _():
            run(wide_load(w_qkv, at - 20, slot))

    def column_sums(rows):
        return jnp.sum(rows.astype(jnp.float32), axis=0, keepdims=True)

    def gated(image, gate_row, gradient, branch, target, bias_cols):
        def rows_of(block, sums):
            rows = pl.ds(pl.multiple_of(image * toks + block * 64, 64), 64)
            upper = gradient[rows, :]
            gate = mod_ref[mod_at + gate_row + image : mod_at + gate_row + image + 1, :]
            lower = (upper * gate).astype(bf)
            target[rows, :] = lower
            return sums[0] + column_sums(upper * branch[rows, :]), sums[1] + column_sums(lower)

        zero = jnp.zeros((1, D), jnp.float32)
        gate, bias = lax.fori_loop(0, blocks, rows_of, (zero, zero))
        gate_at = mod_at + gate_row + image
        d_mod_ref[gate_at : gate_at + 1, :] = gate
        if image == 0:
            d_bias_ref[:, bias_cols] = bias
        else:
            d_bias_ref[:, bias_cols] += bias

    def modulate_back(image, first_row, source, passed, target):
        def rows_of(block, sums):
            rows = pl.ds(pl.multiple_of(image * toks + block * 64, 64), 64)
            scale_row = mod_at + first_row + 2 + image
            scale = mod_ref[scale_row : scale_row + 1, :]
            unit, inverse = normalized(source[rows, :])
            upper = total_buf[rows, :]
            inner = upper * (1.0 + scale)
            back = inverse * (
                inner
                - jnp.mean(inner, axis=-1, keepdims=True)
                - unit * jnp.mean(inner * unit, axis=-1, keepdims=True)
            )
            target[rows, :] = back + passed[rows, :]
            return sums[0] + column_sums(upper), sums[1] + column_sums(upper * unit)

        zero = jnp.zeros((1, D), jnp.float32)
        shift, scale = lax.fori_loop(0, blocks, rows_of, (zero, zero))
        shift_at = mod_at + first_row + image
        d_mod_ref[shift_at : shift_at + 1, :] = shift
        d_mod_ref[shift_at + 2 : shift_at + 3, :] = scale

    def attend_back(image, pair):
        rows = pl.ds(pl.multiple_of(image * toks, toks), toks)
        low = lax.broadcasted_iota(jnp.int32, (toks, 128), 1) < 64
        eighth = jnp.asarray(0.125, bf)
        queries = qkv_ref[rows, column_tile(pair, 128)] * eighth
        keys = qkv_ref[rows, column_tile(8 + pair, 128)]
        values = qkv_ref[rows, column_tile(16 + pair, 128)]
        upper = d_heads_buf[rows, column_tile(pair, 128)]
        keep = keep_ref[pl.ds(image, 1), :]
        zero = jnp.zeros_like(queries)
        total = jnp.zeros((toks, 128), jnp.float32)
        d_q, d_k, d_v = total, total, total
        for own in (low, jnp.logical_not(low)):
            own_q = jnp.where(own, queries, zero)
            own_up = jnp.where(own, upper, zero)
            probs = head_probs(own_q, keys, keep)
            d_probs = dot_nt(own_up, values)
            mean = jnp.sum(probs * d_probs, axis=-1, keepdims=True)
            d_scores = (probs * (d_probs - mean)).astype(bf)
            d_v = d_v + dot_tn(probs.astype(bf), own_up)
            d_q = d_q + dot_nn(d_scores, jnp.where(own, keys * eighth, zero))
            d_k = d_k + dot_tn(d_scores, own_q)
        d_qkv_buf[rows, column_tile(pair, 128)] = d_q.astype(bf)
        d_qkv_buf[rows, column_tile(8 + pair, 128)] = d_k.astype(bf)
        d_qkv_buf[rows, column_tile(16 + pair, 128)] = d_v.astype(bf)

    def add_product(first, image_rows, part):
        @pl.when(first)
        def _():
            total_buf[image_rows, :] = part

        @pl.when(jnp.logical_not(first))
        def _():
            total_buf[image_rows, :] += part

    def step(at):
        slot = lax.rem(at, 2)
        loads(at + 1, lambda copy: copy.start())
        loads(at, lambda copy: copy.wait())

        @pl.when(at == 0)
        def _():
            in_down.wait()
            for image in range(images):
                gated(image, 10, grad_ref, side_ref, d_down_buf, slice(8 * D, 9 * D))
            saves[0].start()

        @pl.when(within(at, 1, 8))
        def _():
            tile = at - 1
            bias = jnp.zeros((1, HALF), jnp.float32)
            for image in range(images):
                rows = pl.ds(image * toks, toks)
                upper = dot_nt(d_down_buf[rows, :], tall_tile(slot))
                pre = pre_buf[slot, rows, :]
                square = pre * pre
                inner = jnp.tanh(GELU_IN * (pre + GELU_CUBE * square * pre))
                slope = 0.5 * (1.0 + inner) + 0.5 * pre * (1.0 - inner * inner) * (
                    GELU_IN * (1.0 + 3.0 * GELU_CUBE * square)
                )
                lower = (upper * slope).astype(bf)
                d_up_buf[slot, rows, :] = lower
                bias = bias + column_sums(lower)
                add_product(tile == 0, rows, dot_nt(lower, wide_tile(slot)))
            d_bias_ref[:, column_tile(tile + 8)] = bias
            up_save(tile, slot).start()

            @pl.when(tile == 0)
            def _():
                saves[0].wait()

            @pl.when(tile >= 1)
            def _():
                up_save(tile - 1, 1 - slot).wait()

        @pl.when(at == 9)
        def _():
            up_save(7, 0).wait()
            in_x_one.wait()
            in_attn.wait()
            for image in range(images):
                modulate_back(image, 6, x_one_ref, grad_ref, d_x_one_buf)
                gated(image, 4, d_x_one_buf, attn_ref, d_attn_buf, slice(3 * D, 4 * D))
            saves[1].start()

        @pl.when(within(at, 10, 2))
        def _():
            for image in range(images):
                rows = pl.ds(image * toks, toks)
                part = dot_nt(d_attn_buf[rows, column_tile(at - 10)], wide_tile(slot))
                add_product(at == 10, rows, part)

            @pl.when(at == 10)
            def _():
                in_x.start()
                saves[1].wait()

            @pl.when(at == 11)
            def _():
                in_qkv.wait()
                d_heads_buf[...] = total_buf[...].astype(bf)

        @pl.when(within(at, 12, 8))
        def _():
            for turn in range(2):
                item = (at - 12) * 2 + turn
                attend_back(item // 8, lax.rem(item, 8))

        @pl.when(at == 20)
        def _():
            saves[2].start()

        @pl.when(within(at, 20, 6))
        def _():
            cols = column_tile(at - 20)
            bias = jnp.zeros((1, HALF), jnp.float32)
            for image in range(images):
                rows = pl.ds(image * toks, toks)
                lower = d_qkv_buf[rows, cols]
                bias = bias + column_sums(lower)
                add_product(at == 20, rows, dot_nt(lower, wide_tile(slot)))
            d_bias_ref[:, cols] = bias

            @pl.when(at == 21)
            def _():
                saves[2].wait()

        @pl.when(at == BACKWARD_STEPS - 1)
        def _():
            in_x.wait()
            for image in range(images):
                modulate_back(image, 0, side_ref, d_x_one_buf, grad_ref)

    return begin, step


BACKWARD_OUTS = [(D, jnp.bfloat16), (FF, jnp.bfloat16), (D, jnp.bfloat16), (3 * D, jnp.bfloat16)]


def backward_scratch(toks):
    bf, f32 = jnp.bfloat16, jnp.float32
    return [
        pltpu.VMEM((toks, D), f32),
        pltpu.VMEM((toks, D), f32),
        pltpu.VMEM((toks, D), f32),
        pltpu.VMEM((toks, D), f32),
        pltpu.VMEM((toks, 3 * D), bf),
        pltpu.VMEM((toks, D), f32),
        pltpu.VMEM((toks, D), f32),
        pltpu.VMEM((toks, D), bf),
        pltpu.VMEM((2, toks, HALF), bf),
        pltpu.VMEM((toks, D), bf),
        pltpu.VMEM((toks, D), bf),
        pltpu.VMEM((toks, 3 * D), bf),
        pltpu.VMEM((2, toks, HALF), f32),
        pltpu.VMEM((2, 4, 2, 2, 64, HALF), bf),
        pltpu.VMEM((2, 2, 256, D), bf),
        pltpu.SemaphoreType.DMA((3, 2)),
        pltpu.SemaphoreType.DMA((2,)),
        pltpu.SemaphoreType.DMA((3,)),
        pltpu.SemaphoreType.DMA((5,)),
    ]


def backward_kernel(mod_at, *refs):
    grad_in, ins, outs = refs[0], refs[1:13], refs[13:17]
    d_x_out, d_mod_ref, d_bias_ref = refs[17:20]
    scratch, sem = refs[20:-1], refs[-1]
    begin, step = backward_pieces(ins, outs, (d_mod_ref, d_bias_ref) + scratch, mod_at)
    begin()
    copy = pltpu.make_async_copy(grad_in, scratch[0], sem.at[0])
    copy.start()
    copy.wait()

    def turn(at, carry):
        step(at)
        return carry

    lax.fori_loop(0, BACKWARD_STEPS, turn, 0)
    copy = pltpu.make_async_copy(scratch[0], d_x_out, sem.at[1])
    copy.start()
    copy.wait()


def backward_operands(x, saved, weights):
    _, qkv, _, attn, x_one, _, pre, _, down, _ = saved
    return (x, x_one, attn, down, qkv, pre, *weights)


def backward_layer(grad, x, saved, mods, mod_at, keep, weights):
    a_one, _, merged, _, _, a_two, _, act, _, _ = saved
    toks = x.shape[0]
    vmem = pl.BlockSpec(memory_space=pltpu.VMEM)
    hbm = pl.BlockSpec(memory_space=pl.ANY)
    outs = pl.pallas_call(
        functools.partial(backward_kernel, mod_at),
        out_shape=[jax.ShapeDtypeStruct((toks, width), kind) for width, kind in BACKWARD_OUTS]
        + [
            jax.ShapeDtypeStruct((toks, D), jnp.float32),
            jax.ShapeDtypeStruct((mod_at + 12, D), jnp.float32),
            jax.ShapeDtypeStruct((1, 9 * D), jnp.float32),
        ],
        in_specs=[hbm] * 11 + [vmem] * 2,
        out_specs=[hbm] * 5 + [vmem] * 2,
        scratch_shapes=backward_scratch(toks) + [pltpu.SemaphoreType.DMA((2,))],
        compiler_params=pltpu.CompilerParams(vmem_limit_bytes=56 * 1024 * 1024),
        cost_estimate=pl.CostEstimate(
            flops=28 * toks * D * D, bytes_accessed=80 * 1024 * 1024, transcendentals=4 * toks * D
        ),
    )(grad, *backward_operands(x, saved, grouped(weights)), mods, keep)
    d_down, d_up, d_attn, d_qkv, d_x, d_mod, d_bias = outs
    factors = (merged, a_one, a_two, act, d_attn, d_qkv, d_up, d_down)
    return d_x, d_mod[mod_at:], factors, d_bias


def gather_pieces(lines, refs):
    layers = (len(refs) - 7) // 8
    pairs = list(zip(refs[: 4 * layers], refs[4 * layers : 8 * layers]))
    own_sem, zp_sem, zq_sem, yp_sem, yq_sem, x_sem, core_sem = refs[8 * layers :]
    firsts = [12 * layer + first for layer in range(layers) for first in (0, 3, 4, 8)]
    total = 12 * layers
    seq = lax.axis_index("seq")
    dp = lax.axis_index("dp")
    core = lax.rem(dp, 2)
    why = lax.rem(dp // 2, 2)
    zed = dp // 4
    core_peer = {"seq": seq, "dp": dp + 1 - 2 * core}
    x_peer = {"seq": 1 - seq, "dp": dp}
    y_peer = {"seq": seq, "dp": dp + 2 - 4 * why}
    z_peers = [
        {"seq": seq, "dp": lax.rem(zed + step, lines) * 4 + 2 * why + core}
        for step in range(1, lines)
    ]
    keeps = [
        pltpu.make_async_copy(own, every.at[zed, why, core], own_sem.at[at])
        for at, (own, every) in enumerate(pairs)
    ]
    for keep in keeps:
        keep.start()
    for keep in keeps:
        keep.wait()
    barrier = pltpu.get_barrier_semaphore()
    for peer in [core_peer, x_peer, y_peer] + z_peers:
        pl.semaphore_signal(barrier, inc=1, device_id=peer, device_id_type=MESH)
    pl.semaphore_wait(barrier, 2 + lines)

    def views(kind, unit):
        at = unit - firsts[kind]
        if kind % 4 == 3:
            cols = column_tile(at, TILE)
            mine = pl.ds(pl.multiple_of(seq * SHARED_ROWS, 16), SHARED_ROWS)
            rest = pl.ds(2 * SHARED_ROWS, PARTS * 64 - 2 * SHARED_ROWS)
            return (mine, cols), (rest, cols), (slice(None), cols)
        first = pl.multiple_of(at * D, D)
        halved = pl.ds(first, SHARED)
        rest = pl.ds(pl.multiple_of(first + SHARED, 128), D - SHARED)
        mine = pl.ds(pl.multiple_of(seq * 32, 32), 32)
        return (mine, halved), (slice(None), rest), (slice(None), pl.ds(first, D))

    def copies(stage, kind, unit):
        slot = unit
        own, every = pairs[kind]
        shared, rest, whole = views(kind, unit)

        def remote(source, target, sems, peer):
            return pltpu.make_async_remote_copy(
                src_ref=source,
                dst_ref=target,
                send_sem=sems.at[0],
                recv_sem=sems.at[1],
                device_id=peer,
                device_id_type=MESH,
            )

        def same(view, sems, peer):
            return remote(view, view, sems, peer)

        if stage == 0:
            return [
                remote(own.at[view], every.at[(zed, why, core) + view], sems, peer)
                for view, kinds in ((shared, zp_sem), (rest, zq_sem))
                for sems, peer in [(kinds.at[slot, at], z_peers[at]) for at in range(lines - 1)]
            ]
        if stage == 1:
            return [
                same(every.at[(slice(None), why, core) + shared], yp_sem.at[slot], y_peer),
                same(every.at[(slice(None), why, core) + rest], yq_sem.at[slot], y_peer),
            ]
        if stage == 2:
            return [same(every.at[(slice(None), slice(None), core) + shared], x_sem.at[slot], x_peer)]
        return [same(every.at[(slice(None), slice(None), core) + whole], core_sem.at[slot], core_peer)]

    def each_kind(unit, run):
        ends = firsts[1:] + [total]
        for kind in range(len(firsts)):

            @pl.when(jnp.logical_and(unit >= firsts[kind], unit < ends[kind]))
            def _():
                run(kind)

    def begin(stage, unit):
        def run(kind):
            for copy in copies(stage, kind, unit):
                copy.start()

        each_kind(unit, run)

    def finish(stage, unit):
        def run(kind):
            for copy in copies(stage, kind, unit):
                copy.wait()

        each_kind(unit, run)

    def step(at):
        finish(3, at - sum(GATHER_LAGS))
        for stage in (3, 2, 1):
            behind = sum(GATHER_LAGS[:stage])
            finish(stage - 1, at - behind)
            begin(stage, at - behind)
        begin(0, at)

    return step, total + sum(GATHER_LAGS)


def gather_scratch(lines, layers):
    dma = pltpu.SemaphoreType.DMA
    units = 12 * layers
    return [
        dma((4 * layers,)),
        dma((units, lines - 1, 2)),
        dma((units, lines - 1, 2)),
        dma((units, 2)),
        dma((units, 2)),
        dma((units, 2)),
        dma((units, 2)),
    ]


def modulation_pieces(lines, refs):
    (
        partial_ref,
        bias_ref,
        mods_ref,
        core_in,
        core_total,
        y_in,
        y_total,
        z_in,
        core_sem,
        y_sem,
        z_sem,
    ) = refs
    seq = lax.axis_index("seq")
    dp = lax.axis_index("dp")
    core = lax.rem(dp, 2)
    why = lax.rem(dp // 2, 2)
    zed = dp // 4

    def remote(source, target, sems, peer):
        return pltpu.make_async_remote_copy(
            src_ref=source,
            dst_ref=target,
            send_sem=sems.at[0],
            recv_sem=sems.at[1],
            device_id={"seq": seq, "dp": peer},
            device_id_type=MESH,
        )

    to_core = remote(partial_ref.at[:, :, 1 - core], core_in, core_sem, dp + 1 - 2 * core)
    to_y = remote(core_total.at[:, 1 - why], y_in, y_sem, dp + 2 - 4 * why)
    to_z = []
    for ahead in range(1, lines):
        there = lax.rem(zed + ahead, lines)
        to_z.append(
            remote(
                y_total.at[there],
                z_in.at[ahead - 1],
                z_sem.at[ahead - 1],
                there * 4 + 2 * why + core,
            )
        )

    def step(at):
        @pl.when(at == 0)
        def _():
            to_core.start()

        @pl.when(at == 1)
        def _():
            to_core.wait()
            core_total[...] = partial_ref[:, :, core] + core_in[...]
            to_y.start()

        @pl.when(at == 4)
        def _():
            to_y.wait()
            y_total[...] = core_total[:, why] + y_in[...]
            for copy in to_z:
                copy.start()

        @pl.when(at == 8)
        def _():
            total = y_total[zed] + bias_ref[...]
            for ahead, copy in enumerate(to_z):
                copy.wait()
                total = total + z_in[ahead]
            mods_ref[...] = total

    return step


def modulation_scratch(lines, rows):
    dma = pltpu.SemaphoreType.DMA
    f32 = jnp.float32
    return [
        pltpu.VMEM((lines, 2, rows, D), f32),
        pltpu.VMEM((lines, 2, rows, D), f32),
        pltpu.VMEM((lines, rows, D), f32),
        pltpu.VMEM((lines, rows, D), f32),
        pltpu.VMEM((lines - 1, rows, D), f32),
        dma((2,)),
        dma((2,)),
        dma((lines - 1, 2)),
    ]


def whole_forward_kernel(lines, *refs):
    refs = list(refs)

    def take(count):
        taken, refs[:] = tuple(refs[:count]), refs[count:]
        return taken

    own = take(8)
    partial_ref, mod_bias, x_ref, first_bias, second_bias, keep = take(6)
    every = take(8)
    first_outs, second_outs = take(len(FORWARD_OUTS)), take(len(FORWARD_OUTS))
    (mods,) = take(1)
    gather_sems = take(7)
    mod_scratch = take(8)
    scratch = tuple(refs)
    gather, steps = gather_pieces(lines, own + every + gather_sems)
    modulate_step = modulation_pieces(lines, (partial_ref, mod_bias, mods) + mod_scratch)
    first, first_finish = forward_pieces(
        (x_ref, mods, first_bias, keep) + every[:4] + first_outs + scratch, 0
    )
    second, second_finish = forward_pieces(
        (scratch[9], mods, second_bias, keep) + every[4:] + second_outs + scratch, 12
    )

    def run(step, begin, end):
        def one(at, carry):
            step(at)
            return carry

        lax.fori_loop(begin, end, one, 0)

    def turn(at, carry):
        gather(at)
        modulate_step(at)

        @pl.when(within(at, 10, 13))
        def _():
            run(first, 5 * (at - 10) // 2, 5 * (at - 9) // 2)

        @pl.when(at == 23)
        def _():
            first_finish()

        @pl.when(at >= 23)
        def _():
            run(second, 13 * (at - 23) // 4, 13 * (at - 22) // 4)

        return carry

    lax.fori_loop(0, steps + 2, turn, 0)
    second_finish()


def whole_forward(own, partial, mod_bias, x, biases, keep, lines):
    toks = x.shape[0]
    rows = mod_bias.shape[0]
    vmem = pl.BlockSpec(memory_space=pltpu.VMEM)
    hbm = pl.BlockSpec(memory_space=pl.ANY)
    layer_outs = [jax.ShapeDtypeStruct((toks, width), kind) for width, kind in FORWARD_OUTS]
    outs = pl.pallas_call(
        functools.partial(whole_forward_kernel, lines),
        out_shape=[
            jax.ShapeDtypeStruct((lines, 2, 2) + each.shape, jnp.bfloat16) for each in own
        ]
        + layer_outs
        + layer_outs
        + [jax.ShapeDtypeStruct((rows, D), jnp.float32)],
        in_specs=[vmem] * 14,
        out_specs=[hbm] * (8 + 2 * len(FORWARD_OUTS)) + [vmem],
        scratch_shapes=gather_scratch(lines, 2)
        + modulation_scratch(lines, rows)
        + forward_scratch(toks),
        compiler_params=pltpu.CompilerParams(
            collective_id=2, has_side_effects=True, vmem_limit_bytes=58 * 1024 * 1024
        ),
        cost_estimate=pl.CostEstimate(
            flops=48 * toks * D * D,
            bytes_accessed=24 * 4 * lines * 64 * D * 8,
            transcendentals=8 * toks * D,
        ),
    )(*own, partial, mod_bias, x, *biases, keep)
    weights = outs[:8]
    count = len(FORWARD_OUTS)
    saved = [outs[8 : 8 + count], outs[8 + count : 8 + 2 * count]]
    return [weights[:4], weights[4:]], saved, outs[-1]


def gather_small_kernel(lines, own_ref, every_ref, z_sem, y_sem, core_sem):
    seq = lax.axis_index("seq")
    dp = lax.axis_index("dp")
    core = lax.rem(dp, 2)
    why = lax.rem(dp // 2, 2)
    zed = dp // 4
    core_peer = {"seq": seq, "dp": dp + 1 - 2 * core}
    y_peer = {"seq": seq, "dp": dp + 2 - 4 * why}
    z_peers = [
        {"seq": seq, "dp": lax.rem(zed + step, lines) * 4 + 2 * why + core}
        for step in range(1, lines)
    ]
    barrier = pltpu.get_barrier_semaphore()
    for peer in [core_peer, y_peer] + z_peers:
        pl.semaphore_signal(barrier, inc=1, device_id=peer, device_id_type=MESH)
    every_ref[zed, why, core] = own_ref[...]
    pl.semaphore_wait(barrier, 1 + lines)

    def remote(source, target, sems, peer):
        return pltpu.make_async_remote_copy(
            src_ref=source,
            dst_ref=target,
            send_sem=sems.at[0],
            recv_sem=sems.at[1],
            device_id=peer,
            device_id_type=MESH,
        )

    copies = [
        remote(own_ref, every_ref.at[zed, why, core], z_sem.at[at], peer)
        for at, peer in enumerate(z_peers)
    ]
    for copy in copies:
        copy.start()
    for copy in copies:
        copy.wait()
    for view, sems, peer in (
        (every_ref.at[:, why, core], y_sem, y_peer),
        (every_ref.at[:, :, core], core_sem, core_peer),
    ):
        copy = remote(view, view, sems, peer)
        copy.start()
        copy.wait()


def gather_small(own, lines, collective_id):
    dma = pltpu.SemaphoreType.DMA
    every = pl.pallas_call(
        functools.partial(gather_small_kernel, lines),
        out_shape=jax.ShapeDtypeStruct((lines, 2, 2) + own.shape, own.dtype),
        in_specs=[pl.BlockSpec(memory_space=pltpu.VMEM)],
        out_specs=pl.BlockSpec(memory_space=pltpu.VMEM),
        scratch_shapes=[dma((lines - 1, 2)), dma((2,)), dma((2,))],
        compiler_params=pltpu.CompilerParams(collective_id=collective_id, has_side_effects=True),
        cost_estimate=pl.CostEstimate(
            flops=0, bytes_accessed=own.size * 32 * lines, transcendentals=0
        ),
    )(own)
    return every.reshape(-1, own.shape[-1])


def scatter_pieces(lines, sources, scratch):
    per_layer = 12
    total = len(sources) * per_layer
    (
    out_ref,
    lhs_buf,
    act_buf,
    wide_buf,
    down_buf,
    load_sem,
    made,
    core_in,
    x_out,
    x_in,
    p_keep,
    yq_out,
    yq_in,
    q_keep,
    yp_out,
    yp_in,
    p_line,
    zq_out,
    zq_in,
    zp_out,
    zp_in,
    xq_out,
    xq_in,
    xp_out,
    xp_in,
    core_sem,
    x_sem,
    yq_sem,
    yp_sem,
    zq_sem,
    zp_sem,
    xq_sem,
    xp_sem,
    out_buf,
    out_sem,
    ) = scratch
    seq = lax.axis_index("seq")
    dp = lax.axis_index("dp")
    core = lax.rem(dp, 2)
    why = lax.rem(dp // 2, 2)
    zed = dp // 4
    core_peer = {"seq": seq, "dp": dp + 1 - 2 * core}
    x_peer = {"seq": 1 - seq, "dp": dp}
    y_peer = {"seq": seq, "dp": dp + 2 - 4 * why}

    def z_place(step):
        return lax.rem(zed + step, lines)

    def z_peer(step):
        return {"seq": seq, "dp": z_place(step) * 4 + 2 * why + core}

    def remote(source, target, sems, peer):
        return pltpu.make_async_remote_copy(
            src_ref=source,
            dst_ref=target,
            send_sem=sems.at[0],
            recv_sem=sems.at[1],
            device_id=peer,
            device_id_type=MESH,
        )

    def core_copy(slot):
        return remote(made.at[slot, 1 - core], core_in.at[slot], core_sem.at[slot], core_peer)

    def x_copy(slot):
        return remote(x_out.at[slot], x_in.at[slot], x_sem.at[slot], x_peer)

    def yq_copy(slot):
        return remote(yq_out.at[slot], yq_in.at[slot], yq_sem.at[slot], y_peer)

    def yp_copy(slot):
        return remote(yp_out.at[slot], yp_in.at[slot], yp_sem.at[slot], y_peer)

    def zq_copy(slot, step):
        return remote(
            zq_out.at[slot, z_place(step)],
            zq_in.at[slot, step - 1],
            zq_sem.at[slot, step - 1],
            z_peer(step),
        )

    def zp_copy(slot, step):
        return remote(
            zp_out.at[slot, z_place(step)],
            zp_in.at[slot, step - 1],
            zp_sem.at[slot, step - 1],
            z_peer(step),
        )

    def xq_copy(slot):
        return remote(xq_out.at[slot], xq_in.at[slot], xq_sem.at[slot], x_peer)

    def xp_copy(slot):
        return remote(xp_out.at[slot], xp_in.at[slot], xp_sem.at[slot], x_peer)

    def loads(unit, slot):
        found = []
        for layer in range(len(sources)):
            merged, a_one, a_two, act, d_attn, d_qkv, d_up, d_down = sources[layer]
            at = unit - layer * per_layer

            def slab(ref, index, size):
                return ref.at[:, pl.ds(pl.multiple_of(index * size, size), size)]

            wide_to = wide_buf.at[slot], load_sem.at[1, slot]
            lhs_to = lhs_buf.at[slot], load_sem.at[0, slot]
            found += [
                (
                    jnp.logical_and(at >= 0, at < 4),
                    (slab(d_down, at, TILE), down_buf.at[slot], load_sem.at[2, slot]),
                ),
                (at == 0, (act, act_buf, load_sem.at[3, 0])),
                (
                    jnp.logical_and(at >= 4, at < 8),
                    (a_two, *lhs_to),
                    (slab(d_up, at - 4, D), *wide_to),
                ),
                (at == 8, (merged, *lhs_to), (d_attn, *wide_to)),
                (
                    jnp.logical_and(at >= 9, at < per_layer),
                    (a_one, *lhs_to),
                    (slab(d_qkv, at - 9, D), *wide_to),
                ),
            ]
        return found

    def prefetch(unit):
        for due, *moves in loads(unit, lax.rem(unit, 2)):

            @pl.when(due)
            def _():
                for move in moves:
                    pltpu.make_async_copy(*move).start()

    def fetched(unit):
        for due, *moves in loads(unit, lax.rem(unit, 2)):

            @pl.when(due)
            def _():
                for move in moves:
                    pltpu.make_async_copy(*move).wait()

    def dot_rows(left, right):
        return lax.dot_general(
            left, right, (((0,), (0,)), ((), ())), preferred_element_type=jnp.float32
        )

    def compute(unit):
        at = lax.rem(unit, per_layer)
        slot = lax.rem(unit, 2)
        fetched(unit)

        @pl.when(at >= 4)
        def _():
            def rows(pair, carry):
                left = lhs_buf[slot, :, pl.ds(pl.multiple_of(pair * 128, 128), 128)]
                block = dot_rows(left, wide_buf[slot]).astype(jnp.bfloat16)
                for own in range(2):
                    for part in range(PARTS):
                        made[slot, own, part, pair // 2, lax.rem(pair, 2)] = block[
                            own * 64 : own * 64 + 64, part * TILE : part * TILE + TILE
                        ]
                return carry

            lax.fori_loop(0, 2 * lines, rows, 0)

        @pl.when(at < 4)
        def _():
            def rows(pair, carry):
                left = act_buf[:, pl.ds(pl.multiple_of(pair * 512, 512), 512)]
                block = dot_rows(left, down_buf[slot]).astype(jnp.bfloat16)
                for own in range(2):
                    for part in range(PARTS):
                        first = own * 256 + part * 64
                        made[slot, own, part, pair // 2, lax.rem(pair, 2)] = block[
                            first : first + 64
                        ]
                return carry

            lax.fori_loop(0, 2 * lines, rows, 0)

    def wide_sum(one, other):
        return one.astype(jnp.float32) + other.astype(jnp.float32)

    def out_copy(unit, slot):
        return pltpu.make_async_copy(out_buf.at[slot], out_ref.at[unit], out_sem.at[slot])

    def stage_two(slot):
        core_copy(slot).wait()

        def rows(line, carry):
            for side in range(2):
                x_out[slot, line, side] = wide_sum(
                    made[slot, core, 1 - seq, line, side], core_in[slot, 1 - seq, line, side]
                ).astype(jnp.bfloat16)
                p_keep[slot, line, side] = wide_sum(
                    made[slot, core, seq, line, side], core_in[slot, seq, line, side]
                ).astype(jnp.bfloat16)
            for part in range(2):
                yq_out[slot, line, part] = wide_sum(
                    made[slot, core, 2 + part, line, 1 - why],
                    core_in[slot, 2 + part, line, 1 - why],
                ).astype(jnp.bfloat16)
                q_keep[slot, line, part] = wide_sum(
                    made[slot, core, 2 + part, line, why], core_in[slot, 2 + part, line, why]
                ).astype(jnp.bfloat16)
            return carry

        lax.fori_loop(0, lines, rows, 0)
        x_copy(slot).start()
        yq_copy(slot).start()

    def stage_three(slot):
        x_copy(slot).wait()
        yq_copy(slot).wait()

        def rows(line, carry):
            yp_out[slot, line] = wide_sum(
                p_keep[slot, line, 1 - why], x_in[slot, line, 1 - why]
            ).astype(jnp.bfloat16)
            p_line[slot, line] = wide_sum(p_keep[slot, line, why], x_in[slot, line, why]).astype(
                jnp.bfloat16
            )
            for part in range(2):
                zq_out[slot, line, part] = wide_sum(
                    q_keep[slot, line, part], yq_in[slot, line, part]
                ).astype(jnp.bfloat16)
            return carry

        lax.fori_loop(0, lines, rows, 0)
        yp_copy(slot).start()
        for step in range(1, lines):
            zq_copy(slot, step).start()

    def stage_four(slot):
        yp_copy(slot).wait()
        for step in range(1, lines):
            zq_copy(slot, step).wait()

        def rows(line, carry):
            zp_out[slot, line] = wide_sum(p_line[slot, line], yp_in[slot, line]).astype(
                jnp.bfloat16
            )
            return carry

        lax.fori_loop(0, lines, rows, 0)
        total_q = zq_out[slot, zed].astype(jnp.float32)
        for step in range(1, lines):
            total_q = total_q + zq_in[slot, step - 1].astype(jnp.float32)
        xq_out[slot] = total_q.astype(jnp.bfloat16)
        for step in range(1, lines):
            zp_copy(slot, step).start()
        xq_copy(slot).start()

    def stage_five(unit, slot):
        for step in range(1, lines):
            zp_copy(slot, step).wait()
        xq_copy(slot).wait()
        total_p = zp_out[slot, zed].astype(jnp.float32)
        for step in range(1, lines):
            total_p = total_p + zp_in[slot, step - 1].astype(jnp.float32)
        rounded = total_p.astype(jnp.bfloat16)
        xp_out[slot] = rounded
        xp_copy(slot).start()
        @pl.when(unit >= 2)
        def _():
            out_copy(unit - 2, slot).wait()

        out_buf[slot, seq] = rounded.astype(jnp.float32)
        for part in range(2):
            out_buf[slot, 2 + part] = wide_sum(xq_out[slot, part], xq_in[slot, part])

    def stage_six(unit, slot):
        xp_copy(slot).wait()
        out_buf[slot, 1 - seq] = xp_in[slot].astype(jnp.float32)
        out_copy(unit, slot).start()

    def turn(at):
        def when_due(behind, run):
            unit = at - behind

            @pl.when(jnp.logical_and(unit >= 0, unit < total))
            def _():
                run(unit, lax.rem(unit, 2))

        when_due(5, stage_six)
        when_due(4, stage_five)
        when_due(3, lambda unit, slot: stage_four(slot))
        when_due(2, lambda unit, slot: stage_three(slot))
        when_due(1, lambda unit, slot: stage_two(slot))

        @pl.when(at < total)
        def _():
            compute(at)
            core_copy(lax.rem(at, 2)).start()

    def finish():
        for unit in (total - 2, total - 1):
            out_copy(unit, unit % 2).wait()

    return prefetch, turn, finish, total + 5


def scatter_scratch(toks, lines):
    bf = jnp.bfloat16
    dma = pltpu.SemaphoreType.DMA

    buf_f32 = pltpu.VMEM((2, PARTS, 64, TILE), jnp.float32)

    def buf(*shape):
        return pltpu.VMEM((2,) + shape, bf)

    return [
        buf(toks, D),
        pltpu.VMEM((toks, FF), bf),
        buf(toks, D),
        buf(toks, TILE),
        dma((4, 2)),
        buf(2, PARTS, lines, 2, 64, TILE),
        buf(PARTS, lines, 2, 64, TILE),
        buf(lines, 2, 64, TILE),
        buf(lines, 2, 64, TILE),
        buf(lines, 2, 64, TILE),
        buf(lines, 2, 64, TILE),
        buf(lines, 2, 64, TILE),
        buf(lines, 2, 64, TILE),
        buf(lines, 64, TILE),
        buf(lines, 64, TILE),
        buf(lines, 64, TILE),
        buf(lines, 2, 64, TILE),
        buf(lines - 1, 2, 64, TILE),
        buf(lines, 64, TILE),
        buf(lines - 1, 64, TILE),
        buf(2, 64, TILE),
        buf(2, 64, TILE),
        buf(64, TILE),
        buf(64, TILE),
        dma((2, 2)),
        dma((2, 2)),
        dma((2, 2)),
        dma((2, 2)),
        dma((2, lines - 1, 2)),
        dma((2, lines - 1, 2)),
        dma((2, 2)),
        dma((2, 2)),
        buf_f32,
        dma((2,)),
    ]


def summary_pieces(lines, refs):
    (
        flat_own,
        mod_own,
        flat_all,
        mod_all,
        core_in,
        core_total,
        x_in,
        x_total,
        y_in,
        y_total,
        z_in,
        pair_sem,
        line_sem,
    ) = refs
    seq = lax.axis_index("seq")
    dp = lax.axis_index("dp")
    core = lax.rem(dp, 2)
    why = lax.rem(dp // 2, 2)
    zed = dp // 4
    core_peer = {"seq": seq, "dp": dp + 1 - 2 * core}
    x_peer = {"seq": 1 - seq, "dp": dp}
    y_peer = {"seq": seq, "dp": dp + 2 - 4 * why}
    places = [lax.rem(zed + ahead, lines) for ahead in range(1, lines)]
    z_peers = [{"seq": seq, "dp": there * 4 + 2 * why + core} for there in places]

    def remote(source, target, sems, peer):
        return pltpu.make_async_remote_copy(
            src_ref=source,
            dst_ref=target,
            send_sem=sems.at[0],
            recv_sem=sems.at[1],
            device_id=peer,
            device_id_type=MESH,
        )

    def same(view, sems, peer):
        return remote(view, view, sems, peer)

    flat_core = remote(flat_own.at[1 - core], core_in, pair_sem.at[0], core_peer)
    flat_x = remote(core_total, x_in, pair_sem.at[1], x_peer)
    flat_y = remote(x_total, y_in, pair_sem.at[2], y_peer)
    flat_z = [
        remote(y_total.at[there], z_in.at[at], line_sem.at[0, at], peer)
        for at, (there, peer) in enumerate(zip(places, z_peers))
    ]
    back_z = [
        same(flat_all.at[core, zed], line_sem.at[1, at], peer) for at, peer in enumerate(z_peers)
    ]
    back_core = same(flat_all.at[core], pair_sem.at[3], core_peer)
    mod_x = remote(mod_own, mod_all.at[zed, why, core, seq], pair_sem.at[4], x_peer)
    mod_z = [
        same(mod_all.at[zed, why, core], line_sem.at[2, at], peer)
        for at, peer in enumerate(z_peers)
    ]
    mod_y = same(mod_all.at[:, why, core], pair_sem.at[5], y_peer)
    mod_core = same(mod_all.at[:, :, core], pair_sem.at[6], core_peer)

    def first():
        mod_all[zed, why, core, seq] = mod_own[...]
        flat_core.start()
        mod_x.start()

    def second():
        flat_core.wait()
        core_total[...] = flat_own[core] + core_in[...]
        flat_x.start()
        mod_x.wait()
        for copy in mod_z:
            copy.start()

    def third():
        flat_x.wait()
        x_total[...] = core_total[...] + x_in[...]
        flat_y.start()
        for copy in mod_z:
            copy.wait()
        mod_y.start()

    def fourth():
        flat_y.wait()
        y_total[...] = x_total[...] + y_in[...]
        for copy in flat_z:
            copy.start()

    def fifth():
        total = y_total[zed]
        for at, copy in enumerate(flat_z):
            copy.wait()
            total = total + z_in[at]
        flat_all[core, zed] = total
        for copy in back_z:
            copy.start()
        mod_y.wait()
        mod_core.start()

    def sixth():
        for copy in back_z:
            copy.wait()
        back_core.start()
        mod_core.wait()

    def seventh():
        back_core.wait()

    return [first, second, third, fourth, fifth, sixth, seventh]


def summary_scratch(lines):
    f32 = jnp.float32
    part = pltpu.VMEM((lines, 8, D), f32)
    return [
        pltpu.VMEM((2, lines, 8, D), f32),
        pltpu.VMEM((32, D), jnp.bfloat16),
        part,
        part,
        part,
        part,
        part,
        part,
        pltpu.VMEM((lines - 1, 8, D), f32),
        pltpu.SemaphoreType.DMA((7, 2)),
        pltpu.SemaphoreType.DMA((3, lines - 1, 2)),
    ]


def whole_backward_kernel(lines, *refs):
    refs = list(refs)

    def take(count):
        taken, refs[:] = tuple(refs[:count]), refs[count:]
        return taken

    (grad_in,) = take(1)
    operands = [take(10), take(10)]
    kept = [take(4), take(4)]
    mod_ref, keep_ref, final_rows, head_rows, misc_row, flat_in = take(6)
    units_out = take(1)
    outs = [take(4), take(4)]
    flat_all, mod_all = take(2)
    back_scratch = take(19)
    d_mod_ref, *d_bias_refs = take(3)
    (grad_sem,) = take(1)
    summary = take(11)
    scatter_refs = tuple(refs)

    dp = lax.axis_index("dp")
    seq = lax.axis_index("seq")
    core = lax.rem(dp, 2)
    why = lax.rem(dp // 2, 2)
    zed = dp // 4
    barrier = pltpu.get_barrier_semaphore()
    peers = [dp + 1 - 2 * core, dp + 2 - 4 * why]
    peers += [lax.rem(zed + ahead, lines) * 4 + 2 * why + core for ahead in range(1, lines)]
    for peer in [{"seq": seq, "dp": peer} for peer in peers] + [{"seq": 1 - seq, "dp": dp}]:
        pl.semaphore_signal(barrier, inc=1, device_id=peer, device_id_type=MESH)

    load = pltpu.make_async_copy(grad_in, back_scratch[0], grad_sem.at[0])
    load.start()
    begins, steps = [], []
    for at, mod_at in ((0, 12), (1, 0)):
        begin, step = backward_pieces(
            operands[at] + (mod_ref, keep_ref),
            outs[at],
            (d_mod_ref, d_bias_refs[at]) + back_scratch,
            mod_at,
        )
        begins.append(begin)
        steps.append(step)
    begins[0]()
    load.wait()

    sources = []
    for at in range(2):
        merged, a_one, a_two, act = kept[at]
        d_down, d_up, d_attn, d_qkv = outs[at]
        sources.append((merged, a_one, a_two, act, d_attn, d_qkv, d_up, d_down))
    prefetch, scatter, scatter_finish, turns = scatter_pieces(
        lines, sources, units_out + scatter_refs
    )
    flat_own, mod_own = summary[:2]
    summary_steps = summary_pieces(
        lines, (flat_own, mod_own, flat_all, mod_all) + summary[2:]
    )

    def put(row, value):
        flat_own[row // (8 * lines), row // 8 % lines, row % 8 : row % 8 + 1, :] = value

    def collect():
        d_patch = back_scratch[0][...].astype(jnp.bfloat16)
        for layer in range(2):
            for row in range(9):
                put(9 * layer + row, d_bias_refs[1 - layer][:, row * D : (row + 1) * D])
        put(18, jnp.sum(d_patch.astype(jnp.float32), axis=0, keepdims=True))
        g_patch = dot_nn(flat_in[...], d_patch)
        for row in range(16):
            put(19 + row, g_patch[row : row + 1, :])
            put(35 + row, head_rows[row : row + 1, :])
        put(51, misc_row[...])
        for row in range(52, 16 * lines):
            put(row, jnp.zeros((1, D), jnp.float32))
        d_mod_ref[24:28, :] = final_rows[...]
        d_mod_ref[28:32, :] = jnp.zeros((4, D), jnp.float32)
        mod_own[...] = d_mod_ref[...].astype(jnp.bfloat16)

    def back(at, carry):
        @pl.when(at < BACKWARD_STEPS)
        def _():
            steps[0](at)

        @pl.when(at == BACKWARD_STEPS)
        def _():
            begins[1]()

        @pl.when(jnp.logical_and(at >= BACKWARD_STEPS, at < 2 * BACKWARD_STEPS))
        def _():
            steps[1](at - BACKWARD_STEPS)

        return carry

    lax.fori_loop(0, 2, back, 0)
    prefetch(jnp.int32(0))
    pl.semaphore_wait(barrier, 2 + lines)

    def turn(at, carry):
        @pl.when(at <= 20)
        def _():
            lax.fori_loop(2 + at * 5 // 2, 2 + (at + 1) * 5 // 2, back, 0)

        prefetch(at + 1)
        scatter(at)

        @pl.when(at == 21)
        def _():
            collect()

        for offset, run in enumerate(summary_steps):

            @pl.when(at == 21 + offset)
            def _():
                run()

        return carry

    lax.fori_loop(0, turns, turn, 0)
    scatter_finish()


def whole_backward(
    grad, inputs, saved, weights, mods, keep, final_rows, head_rows, misc_row, flat_in, lines
):
    toks = grad.shape[0]
    vmem = pl.BlockSpec(memory_space=pltpu.VMEM)
    hbm = pl.BlockSpec(memory_space=pl.ANY)
    operands = [grad]
    for at in (1, 0):
        operands += backward_operands(inputs[at], saved[at], weights[at])
    for at in (1, 0):
        a_one, _, merged, _, _, a_two, _, act, _, _ = saved[at]
        operands += [merged, a_one, a_two, act]
    layer_outs = [jax.ShapeDtypeStruct((toks, width), kind) for width, kind in BACKWARD_OUTS]
    outs = pl.pallas_call(
        functools.partial(whole_backward_kernel, lines),
        out_shape=[jax.ShapeDtypeStruct((24, PARTS, 64, TILE), jnp.float32)]
        + layer_outs
        + layer_outs
        + [
            jax.ShapeDtypeStruct((2, lines, 8, D), jnp.float32),
            jax.ShapeDtypeStruct((lines, 2, 2, 2, 32, D), jnp.bfloat16),
        ],
        in_specs=[hbm] * len(operands) + [vmem] * 6,
        out_specs=[hbm] * 9 + [vmem] * 2,
        scratch_shapes=backward_scratch(toks)
        + [
            pltpu.VMEM((32, D), jnp.float32),
            pltpu.VMEM((1, 9 * D), jnp.float32),
            pltpu.VMEM((1, 9 * D), jnp.float32),
            pltpu.SemaphoreType.DMA((1,)),
        ]
        + summary_scratch(lines)
        + scatter_scratch(toks, lines),
        compiler_params=pltpu.CompilerParams(
            collective_id=1, has_side_effects=True, vmem_limit_bytes=61 * 1024 * 1024
        ),
        cost_estimate=pl.CostEstimate(
            flops=104 * toks * D * D,
            bytes_accessed=300 * 1024 * 1024,
            transcendentals=8 * toks * D,
        ),
    )(*operands, mods, keep, final_rows, head_rows, misc_row, flat_in)
    return outs[0], outs[9], outs[10]


def gather_rows(shard):
    return lax.all_gather(shard.astype(jnp.bfloat16), "dp", axis=0, tiled=True)


def kernels_fit():
    dp_parts = lax.axis_size("dp")
    return (
        lax.axis_size("seq") == 2
        and dp_parts % 4 == 0
        and D // dp_parts == 64
        and FF // dp_parts == PARTS * 64
    )


def reduce_rows(partial):
    owned = lax.psum_scatter(
        partial.astype(jnp.bfloat16), "dp", scatter_dimension=0, tiled=True
    )
    return lax.psum(owned, "seq").astype(jnp.float32)


def adamw(weight, gradient, first, second, rate):
    first_new = BETA_ONE * first + (1.0 - BETA_ONE) * gradient
    second_new = BETA_TWO * second + (1.0 - BETA_TWO) * gradient * gradient
    first_hat = first_new / (1.0 - BETA_ONE**STEP)
    second_hat = second_new / (1.0 - BETA_TWO**STEP)
    return (
        weight - rate * (first_hat / (jnp.sqrt(second_hat) + EPSILON) + DECAY * weight),
        first_new,
        second_new,
    )


def unit_adamw_kernel(by_rows, grad_ref, weight_ref, first_ref, second_ref, *outs):
    for part in range(PARTS):
        if by_rows:
            place = (0, slice(part * 64, part * 64 + 64), slice(None))
        else:
            place = (0, slice(None), slice(part * TILE, part * TILE + TILE))
        moved = adamw(
            weight_ref[place], grad_ref[0, part], first_ref[place], second_ref[place], RATE_MATRIX
        )
        for out, value in zip(outs, moved):
            out[place] = value


def unit_adamw(weight, units, first, second, first_unit, by_rows):
    layers, rows, width = weight.shape
    block = (1, rows, TILE) if by_rows else (1, rows, D)
    spec = pl.BlockSpec(block, lambda layer, at: (layer, 0, at))
    per_layer = units.shape[0] // layers
    grad_spec = pl.BlockSpec(
        (1, PARTS, 64, TILE),
        lambda layer, at: ((layers - 1 - layer) * per_layer + first_unit + at, 0, 0, 0),
    )
    return pl.pallas_call(
        functools.partial(unit_adamw_kernel, by_rows),
        out_shape=[jax.ShapeDtypeStruct(weight.shape, jnp.float32)] * 3,
        grid=(layers, width // block[2]),
        in_specs=[grad_spec, spec, spec, spec],
        out_specs=[spec] * 3,
        compiler_params=pltpu.CompilerParams(vmem_limit_bytes=32 * 1024 * 1024),
        cost_estimate=pl.CostEstimate(
            flops=16 * weight.size, bytes_accessed=28 * weight.size, transcendentals=weight.size
        ),
    )(units, weight, first, second)


def body(
    latents,
    noise_target,
    pad_mask,
    labels,
    timesteps,
    embed_rows,
    first_embed,
    second_embed,
    class_table,
    first_table,
    second_table,
    qkv_weight,
    first_qkv,
    second_qkv,
    proj_weight,
    first_proj,
    second_proj,
    up_weight,
    first_up,
    second_up,
    down_weight,
    first_down,
    second_down,
    cond_weight,
    first_cond,
    second_cond,
    head_weight,
    first_head,
    second_head,
    all_biases,
    first_bias,
    second_bias,
):
    seq_parts = lax.axis_size("seq")
    dp_parts = lax.axis_size("dp")
    seq_at = lax.axis_index("seq")
    dp_at = lax.axis_index("dp")
    lines = dp_parts // 4
    group, half_rows, _ = latents.shape
    images = group // seq_parts
    everyone = group * dp_parts
    own_cols = embed_rows.shape[1]
    own_place = dp_at * own_cols
    cond_cols = cond_weight.shape[1]
    pieces = cond_cols // D
    bias_base = 3 * D + cond_cols
    by_kernel = kernels_fit()
    packed = jnp.concatenate(
        [latents, noise_target, pad_mask.astype(jnp.float32)[:, :, None]], axis=2
    )
    shards = [
        weight[at].astype(jnp.bfloat16)
        for at in range(LAYERS)
        for weight in (qkv_weight, proj_weight, up_weight, down_weight)
    ]
    narrow = jnp.concatenate(
        [embed_rows[: PATCH_IN + FREQ].T, head_weight], axis=1
    ).astype(jnp.bfloat16)
    if by_kernel:
        ids = jnp.stack([labels, timesteps])
        parts = jnp.stack([ids // 32, ids % 32]).astype(jnp.bfloat16).reshape(-1, 1)
        parts = jnp.pad(parts, ((0, own_cols - parts.shape[0]), (0, 0)))
        width = narrow.shape[1]
        block = jnp.concatenate(
            [narrow, parts, jnp.zeros((own_cols, 383 - width), jnp.bfloat16)], axis=1
        )
        small = gather_small(block, lines, 4)
        parts = small[:, width].astype(jnp.float32).reshape(dp_parts, own_cols)[:, : 4 * group]
        parts = parts.reshape(dp_parts, 2, 2, group)
        ids = (parts[:, 0] * 32.0 + parts[:, 1]).astype(jnp.int32)
        ids = ids.transpose(1, 0, 2).reshape(2, everyone)
        theirs = lax.dynamic_slice(
            packed, ((1 - seq_at) * images, 0, 0), (images,) + packed.shape[1:]
        )
        mine = lax.dynamic_slice(packed, (seq_at * images, 0, 0), (images,) + packed.shape[1:])
        came = lax.ppermute(theirs, "seq", [(0, 1), (1, 0)])
        packed = jnp.concatenate(
            [jnp.where(seq_at == 0, mine, came), jnp.where(seq_at == 0, came, mine)], axis=1
        )
    else:
        small = lax.all_gather(narrow, "dp", axis=0, tiled=True)
        ids = lax.all_gather(jnp.stack([labels, timesteps]), "dp", axis=1, tiled=True)
        packed = lax.all_to_all(packed, "seq", split_axis=0, concat_axis=1, tiled=True)
    tok_rows = packed.shape[1]
    toks = images * tok_rows
    latents, noise_target, keep_rows = (
        packed[:, :, :PATCH_IN],
        packed[:, :, PATCH_IN : 2 * PATCH_IN],
        packed[:, :, 2 * PATCH_IN],
    )
    patch_part = small[:, :PATCH_IN]
    freq_part = small[:, PATCH_IN : PATCH_IN + FREQ]
    head_full = small[:, PATCH_IN + FREQ : PATCH_IN + FREQ + OUT_CH]
    time_own = embed_rows[PATCH_IN + FREQ :].astype(jnp.bfloat16)
    cond_own = cond_weight.astype(jnp.bfloat16)

    features = time_features(ids[1], FREQ).astype(jnp.bfloat16)
    time_pre = dot_nt(features, freq_part) + all_biases[D : 2 * D]
    time_hidden = jax.nn.silu(time_pre).astype(jnp.bfloat16)
    second_bias_own = lax.dynamic_slice(all_biases, (2 * D + own_place,), (own_cols,))
    onehot = (ids[0][:, None] == jnp.arange(NCLASS, dtype=jnp.int32)[None, :]).astype(jnp.float32)
    condition = (
        matdot(time_hidden, time_own)
        + second_bias_own
        + matdot(onehot.astype(jnp.bfloat16), class_table.astype(jnp.bfloat16))
    )
    cond_act = jax.nn.silu(condition).astype(jnp.bfloat16)
    plane_act = lax.dynamic_index_in_dim(
        cond_act.reshape(dp_parts, seq_parts, images, own_cols), seq_at, 1, keepdims=False
    ).reshape(dp_parts * images, own_cols)
    partial = matdot(plane_act, cond_own).reshape(dp_parts, images, pieces, D)
    partial = partial.transpose(0, 2, 1, 3).reshape(dp_parts, pieces * images, D)
    mod_bias = jnp.repeat(all_biases[3 * D : bias_base].reshape(pieces, D), images, axis=0)

    position = position_table(jnp.arange(tok_rows, dtype=jnp.int32), D, GRID)
    flat_in = latents.astype(jnp.bfloat16).reshape(toks, PATCH_IN)
    stream = (dot_nt(flat_in, patch_part) + all_biases[:D]).reshape(
        images, tok_rows, D
    ) + position[None]
    stream = stream.reshape(toks, D)
    layer_bias = [
        all_biases[bias_base + at * 9 * D : bias_base + (at + 1) * 9 * D].reshape(1, 9 * D)
        for at in range(LAYERS)
    ]
    if by_kernel:
        weights_kept, saved_kept, mods = whole_forward(
            shards,
            partial.reshape(lines, 2, 2, pieces * images, D),
            mod_bias,
            stream,
            layer_bias,
            keep_rows,
            lines,
        )
    else:
        mods = mod_bias + lax.psum_scatter(
            partial, "dp", scatter_dimension=0, tiled=True
        ).reshape(pieces * images, D)
        weights_kept = [
            [gather_rows(shard) for shard in shards[4 * at : 4 * at + 4]] for at in range(LAYERS)
        ]
        saved_kept = []
        upper = stream
        for at in range(LAYERS):
            saved_kept.append(
                forward_layer(
                    upper, mods, 6 * images * at, layer_bias[at], keep_rows, weights_kept[at]
                )
            )
            upper = saved_kept[at][-1]
    inputs_kept = [stream] + [saved[-1] for saved in saved_kept]
    final, time_own = lax.optimization_barrier((inputs_kept[-1], time_own))
    time_full = lax.all_gather(time_own, "dp", axis=1, tiled=True)
    final_at = 6 * LAYERS * images
    final_shift = mods[final_at : final_at + images]
    final_scale = mods[final_at + images :]
    moved, final_back = jax.vjp(
        modulate, final.reshape(images, tok_rows, D), final_shift, final_scale
    )
    a_final = moved.astype(jnp.bfloat16).reshape(toks, D)
    head_out = matdot(a_final, head_full) + all_biases[NBIAS - OUT_CH :]
    split_out = head_out.reshape(images, tok_rows, 4, 2, OUT_CH // 8)
    predicted = split_out[:, :, :, 0, :].reshape(images, tok_rows, PATCH_IN)
    errors = predicted - noise_target
    loss_part = jnp.sum(keep_rows[:, :, None] * errors * errors)
    count_part = PATCH_IN * jnp.sum(keep_rows)
    d_pred = (2.0 * keep_rows[:, :, None] * errors).reshape(images, tok_rows, 4, 1, OUT_CH // 8)
    d_head = (
        jnp.concatenate([d_pred, jnp.zeros_like(d_pred)], axis=3)
        .reshape(toks, OUT_CH)
        .astype(jnp.bfloat16)
    )
    d_a_final = dot_nt(d_head, head_full).reshape(images, tok_rows, D)
    d_stream, d_final_shift, d_final_scale = final_back(d_a_final)
    d_stream = d_stream.reshape(toks, D)
    d_bias_head = column_sum(d_head)
    if by_kernel:
        d_noise = d_pred.astype(jnp.bfloat16).reshape(toks, PATCH_IN)
        misc_row = jnp.concatenate([d_bias_head, loss_part[None], count_part[None]])
        misc_row = jnp.pad(misc_row, (0, D - misc_row.shape[0])).reshape(1, D)
        units, flat, mod_all = whole_backward(
            d_stream,
            inputs_kept,
            saved_kept,
            weights_kept,
            mods,
            keep_rows,
            jnp.concatenate([d_final_shift, d_final_scale], axis=0),
            matdot(d_noise.T, a_final),
            misc_row,
            flat_in.T,
            lines,
        )
        d_modulation = (
            mod_all[..., : pieces * images, :]
            .reshape(dp_parts * seq_parts, pieces, images, D)
            .transpose(0, 2, 1, 3)
            .reshape(everyone, cond_cols)
        )
        flat = flat.reshape(64, D)
        d_bias_mod = column_sum(d_modulation)
        d_bias_patch = flat[18]
        d_bias_layers = flat[:18].reshape(-1)
        d_bias_head, loss_sum, loss_count = (
            flat[51, :OUT_CH],
            flat[51, OUT_CH],
            flat[51, OUT_CH + 1],
        )
        own_flat = lax.dynamic_slice(flat, (0, own_place), (64, own_cols))
        s_patch = own_flat[19:35]
        s_head = own_flat[35:51].T.reshape(own_cols, 4, 1, OUT_CH // 8)
        s_head = jnp.concatenate([s_head, jnp.zeros_like(s_head)], axis=2)
        s_head = s_head.reshape(own_cols, OUT_CH)
    else:
        layer_sums = [None] * LAYERS
        layer_bias_grads = [None] * LAYERS
        modul_grads = [None] * LAYERS
        for at in reversed(range(LAYERS)):
            d_stream, d_mod, factors, d_bias = backward_layer(
                d_stream,
                inputs_kept[at],
                saved_kept[at],
                mods,
                6 * images * at,
                keep_rows,
                weights_kept[at],
            )
            merged, a_one, a_two, active, d_attn, d_qkv, d_up, d_down = factors
            layer_sums[at] = (
                reduce_rows(matdot(a_one.T, d_qkv)),
                reduce_rows(matdot(merged.T, d_attn)),
                reduce_rows(matdot(a_two.T, d_up)),
                reduce_rows(matdot(active.T, d_down)),
            )
            modul_grads[at] = d_mod.reshape(6, images, D).transpose(1, 0, 2).reshape(images, 6 * D)
            layer_bias_grads[at] = d_bias.reshape(-1)
        d_mod_own = jnp.concatenate(
            modul_grads + [d_final_shift, d_final_scale], axis=1
        ).astype(jnp.bfloat16)
        d_patch = d_stream.astype(jnp.bfloat16)
        d_modulation = lax.all_gather(d_mod_own, ("dp", "seq"), axis=0, tiled=True)
        (
            d_bias_patch,
            d_bias_mod,
            d_bias_layers,
            d_bias_head,
            loss_sum,
            loss_count,
            g_patch,
            g_head,
        ) = lax.psum(
            (
                column_sum(d_patch),
                column_sum(d_mod_own),
                jnp.concatenate(layer_bias_grads),
                d_bias_head,
                loss_part,
                count_part,
                matdot(flat_in.T, d_patch),
                matdot(a_final.T, d_head),
            ),
            ("seq", "dp"),
        )
        s_patch = lax.dynamic_slice(g_patch, (0, own_place), (PATCH_IN, own_cols))
        s_head = lax.dynamic_slice(g_head, (own_place, 0), (own_cols, OUT_CH))
    d_cond_act = dot_nt(d_modulation, cond_own)
    _, silu_back = jax.vjp(jax.nn.silu, condition)
    d_condition = silu_back(d_cond_act)[0]
    d_time_own = d_condition.astype(jnp.bfloat16)
    if by_kernel:
        d_time = gather_small(
            jnp.pad(d_time_own.T, ((0, 0), (0, everyone))), lines, 5
        )
        d_time = d_time[:, :everyone].T
    else:
        d_time = lax.all_gather(d_time_own, "dp", axis=1, tiled=True)
    d_time_hidden = dot_nt(d_time, time_full)
    _, time_back = jax.vjp(jax.nn.silu, time_pre)
    d_time_pre = time_back(d_time_hidden)[0].astype(jnp.bfloat16)
    s_cond = matdot(cond_act.T, d_modulation)
    s_table = jnp.dot(onehot.T, d_condition, precision=lax.Precision.HIGHEST)
    g_time = matdot(time_hidden.T, d_time_own)
    g_freq = matdot(
        features.T, lax.dynamic_slice(d_time_pre, (0, own_place), (everyone, own_cols))
    )
    bias_grad = jnp.concatenate(
        [
            d_bias_patch,
            column_sum(d_time_pre),
            column_sum(d_time),
            d_bias_mod,
            d_bias_layers,
            d_bias_head,
        ]
    )
    s_embed = jnp.concatenate([s_patch, g_freq, g_time], axis=0)
    new_embed, new_first_embed, new_second_embed = adamw(
        embed_rows, s_embed, first_embed, second_embed, RATE_MATRIX
    )
    new_table, new_first_table, new_second_table = adamw(
        class_table, s_table, first_table, second_table, RATE_TABLE
    )
    if by_kernel:
        new_qkv, new_first_qkv, new_second_qkv = unit_adamw(
            qkv_weight, units, first_qkv, second_qkv, 9, False
        )
        new_proj, new_first_proj, new_second_proj = unit_adamw(
            proj_weight, units, first_proj, second_proj, 8, False
        )
        new_up, new_first_up, new_second_up = unit_adamw(
            up_weight, units, first_up, second_up, 4, False
        )
        new_down, new_first_down, new_second_down = unit_adamw(
            down_weight, units, first_down, second_down, 0, True
        )
    else:
        s_qkv = jnp.stack([layer_sums[at][0] for at in range(LAYERS)])
        s_proj = jnp.stack([layer_sums[at][1] for at in range(LAYERS)])
        s_up = jnp.stack([layer_sums[at][2] for at in range(LAYERS)])
        s_down = jnp.stack([layer_sums[at][3] for at in range(LAYERS)])
        new_qkv, new_first_qkv, new_second_qkv = adamw(
            qkv_weight, s_qkv, first_qkv, second_qkv, RATE_MATRIX
        )
        new_proj, new_first_proj, new_second_proj = adamw(
            proj_weight, s_proj, first_proj, second_proj, RATE_MATRIX
        )
        new_up, new_first_up, new_second_up = adamw(up_weight, s_up, first_up, second_up, RATE_MATRIX)
        new_down, new_first_down, new_second_down = adamw(
            down_weight, s_down, first_down, second_down, RATE_MATRIX
        )
    new_cond, new_first_cond, new_second_cond = adamw(
        cond_weight, s_cond, first_cond, second_cond, RATE_MATRIX
    )
    new_head, new_first_head, new_second_head = adamw(
        head_weight, s_head, first_head, second_head, RATE_MATRIX
    )
    new_bias, new_first_bias, new_second_bias = adamw(
        all_biases, bias_grad, first_bias, second_bias, RATE_BIAS
    )
    return (
        loss_sum,
        loss_count,
        new_embed,
        new_first_embed,
        new_second_embed,
        new_table,
        new_first_table,
        new_second_table,
        new_qkv,
        new_first_qkv,
        new_second_qkv,
        new_proj,
        new_first_proj,
        new_second_proj,
        new_up,
        new_first_up,
        new_second_up,
        new_down,
        new_first_down,
        new_second_down,
        new_cond,
        new_first_cond,
        new_second_cond,
        new_head,
        new_first_head,
        new_second_head,
        new_bias,
        new_first_bias,
        new_second_bias,
    )


def solution(mesh):
    placed = (
        P("dp", "seq", None),
        P("dp", "seq", None),
        P("dp", "seq"),
        P("dp"),
        P("dp"),
        P(None, "dp"),
        P(None, "dp"),
        P(None, "dp"),
        P(None, "dp"),
        P(None, "dp"),
        P(None, "dp"),
        P(None, "dp", None),
        P(None, "dp", None),
        P(None, "dp", None),
        P(None, "dp", None),
        P(None, "dp", None),
        P(None, "dp", None),
        P(None, "dp", None),
        P(None, "dp", None),
        P(None, "dp", None),
        P(None, "dp", None),
        P(None, "dp", None),
        P(None, "dp", None),
        P("dp", None),
        P("dp", None),
        P("dp", None),
        P("dp", None),
        P("dp", None),
        P("dp", None),
        P(),
        P(),
        P(),
    )
    return jax.shard_map(
        body,
        mesh=mesh,
        in_specs=placed,
        out_specs=(
            P(),
            P(),
            P(None, "dp"),
            P(None, "dp"),
            P(None, "dp"),
            P(None, "dp"),
            P(None, "dp"),
            P(None, "dp"),
            P(None, "dp", None),
            P(None, "dp", None),
            P(None, "dp", None),
            P(None, "dp", None),
            P(None, "dp", None),
            P(None, "dp", None),
            P(None, "dp", None),
            P(None, "dp", None),
            P(None, "dp", None),
            P(None, "dp", None),
            P(None, "dp", None),
            P(None, "dp", None),
            P("dp", None),
            P("dp", None),
            P("dp", None),
            P("dp", None),
            P("dp", None),
            P("dp", None),
            P(),
            P(),
            P(),
        ),
        check_vma=False,
    )
```

```python
import functools
import math

import jax
import jax.numpy as jnp
from jax import lax
from jax.experimental import pallas as pl
from jax.experimental.pallas import tpu as pltpu
from jax.sharding import PartitionSpec as P

D = 1024
HEADS = 16
HEAD_DIM = 64
FF = 4096
NCLASS = 1001
FREQ = 256
OUT_CH = 32
PATCH_IN = 16
GRID = 16
LAYERS = 2
STEP = 10
NBIAS = 35872


BETA_ONE = 0.9
BETA_TWO = 0.999
EPSILON = 1e-08
DECAY = 0.01
RATE_MATRIX = 0.06
RATE_TABLE = 0.4
RATE_BIAS = 0.2

MESH = pl.DeviceIdType.MESH
TILE = 256
PARTS = 4
SHARED = 640
SHARED_ROWS = 80
GATHER_LAGS = (2, 2, 2, 1)
HALF = 512
GELU_IN = math.sqrt(2.0 / math.pi)
GELU_CUBE = 0.044715
FORWARD_STEPS = 30
BACKWARD_STEPS = 27


def matdot(left, right):
    return jnp.dot(left, right, preferred_element_type=jnp.float32)


def layer_norm(stream):
    row_mean = jnp.mean(stream, axis=-1, keepdims=True)
    centered = stream - row_mean
    variance = jnp.mean(centered * centered, axis=-1, keepdims=True)
    return centered * lax.rsqrt(variance + 1e-06)


def modulate(stream, shift_by, scale_by):
    return layer_norm(stream) * (1.0 + scale_by[:, None, :]) + shift_by[:, None, :]


def position_table(position_ids, feature_width, grid_side):
    quarter_width = feature_width // 4
    omegas = 1.0 / 10000.0 ** (jnp.arange(quarter_width, dtype=jnp.float32) / quarter_width)
    col_angle = (position_ids % grid_side).astype(jnp.float32)[:, None] * omegas[None, :]
    row_angle = (position_ids // grid_side).astype(jnp.float32)[:, None] * omegas[None, :]
    return jnp.concatenate(
        [jnp.sin(col_angle), jnp.cos(col_angle), jnp.sin(row_angle), jnp.cos(row_angle)], axis=1
    )


def time_features(timesteps, feature_width):
    half_width = feature_width // 2
    frequencies = jnp.exp(
        -math.log(10000.0) * jnp.arange(half_width, dtype=jnp.float32) / half_width
    )
    angles = timesteps.astype(jnp.float32)[:, None] * frequencies[None, :]
    return jnp.concatenate([jnp.cos(angles), jnp.sin(angles)], axis=1)


def column_sum(grad_bf):
    return jnp.sum(grad_bf.astype(jnp.float32), axis=0)


def dot_nn(left, right):
    return jnp.dot(left, right, preferred_element_type=jnp.float32)


def dot_nt(left, right):
    return lax.dot_general(
        left, right, (((1,), (1,)), ((), ())), preferred_element_type=jnp.float32
    )


def dot_tn(left, right):
    return lax.dot_general(
        left, right, (((0,), (0,)), ((), ())), preferred_element_type=jnp.float32
    )


def wide_sum(one, other):
    return one.astype(jnp.float32) + other.astype(jnp.float32)


def column_tile(at, size=HALF):
    return pl.ds(pl.multiple_of(at * size, size), size)


def normalized(rows):
    centered = rows - jnp.mean(rows, axis=-1, keepdims=True)
    variance = jnp.mean(centered * centered, axis=-1, keepdims=True)
    inverse = lax.rsqrt(variance + 1e-06)
    return centered * inverse, inverse


def head_probs(queries, keys, keep):
    scores = jnp.where(keep > 0, dot_nt(queries, keys), -1000000000.0)
    raised = jnp.exp(scores - jnp.max(scores, axis=-1, keepdims=True))
    return raised * (1.0 / jnp.sum(raised, axis=-1, keepdims=True))


def within(at, first, size):
    return jnp.logical_and(at >= first, at < first + size)


def forward_pieces(refs, mod_at):
    (
        x_ref,
        mod_ref,
        bias_ref,
        keep_ref,
        w_qkv,
        w_proj,
        w_up,
        w_down,
        a_one_out,
        qkv_out,
        merged_out,
        attn_out,
        x_one_out,
        a_two_out,
        pre_out,
        act_out,
        down_out,
        x_two_out,
        a_buf,
        qkv_buf,
        merged_buf,
        attn_buf,
        x_one_buf,
        a_two_buf,
        pre_buf,
        act_buf,
        down_buf,
        x_two_buf,
        wide_buf,
        tall_buf,
        load_sem,
        tile_sem,
        save_sem,
    ) = refs
    images, toks = keep_ref.shape
    bf = jnp.bfloat16

    def save(at, source, target):
        return pltpu.make_async_copy(source, target, save_sem.at[at])

    saves = [
        save(at, *pair)
        for at, pair in enumerate(
            [
                (a_buf, a_one_out),
                (qkv_buf, qkv_out),
                (merged_buf, merged_out),
                (attn_buf, attn_out),
                (x_one_buf, x_one_out),
                (a_two_buf, a_two_out),
                (down_buf, down_out),
                (x_two_buf, x_two_out),
                (act_buf, act_out),
            ]
        )
    ]

    def wide_load(source, tile, slot):
        return pltpu.make_async_copy(
            source.at[:, :, :, :, column_tile(tile)], wide_buf.at[slot], load_sem.at[0, slot]
        )

    def tall_load(tile, slot):
        return pltpu.make_async_copy(
            w_down.at[:, :, :, :, column_tile(tile, TILE)], tall_buf.at[slot], load_sem.at[1, slot]
        )

    def tile_saves(tile, slot):
        return [
            pltpu.make_async_copy(
                pre_buf.at[slot], pre_out.at[:, column_tile(tile)], tile_sem.at[0, slot]
            ),
        ]

    def wide_tile(slot):
        return wide_buf[slot].reshape(D, HALF)

    def tall_tile(slot):
        return tall_buf[slot].reshape(FF, TILE)

    def loads(at, run):
        slot = lax.rem(at, 2)

        @pl.when(within(at, 1, 6))
        def _():
            run(wide_load(w_qkv, at - 1, slot))

        @pl.when(within(at, 15, 2))
        def _():
            run(wide_load(w_proj, at - 15, slot))

        @pl.when(within(at, 18, 8))
        def _():
            run(wide_load(w_up, at - 18, slot))

        @pl.when(within(at, 26, 4))
        def _():
            run(tall_load(at - 26, slot))

    def modulated(source, target, piece):
        def rows_of(block, carry):
            image = block // 4
            rows = pl.ds(pl.multiple_of(block * 64, 64), 64)
            shift = mod_ref[pl.ds(mod_at + 2 * piece + image, 1), :]
            scale = mod_ref[pl.ds(mod_at + 2 * piece + 2 + image, 1), :]
            unit, _ = normalized(source[rows, :])
            target[rows, :] = (unit * (1.0 + scale) + shift).astype(bf)
            return carry

        lax.fori_loop(0, images * toks // 64, rows_of, 0)

    def attend(image, pair):
        rows = pl.ds(pl.multiple_of(image * toks, toks), toks)
        low = lax.broadcasted_iota(jnp.int32, (toks, 128), 1) < 64
        queries = qkv_buf[rows, column_tile(pair, 128)] * jnp.asarray(0.125, bf)
        keys = qkv_buf[rows, column_tile(8 + pair, 128)]
        values = qkv_buf[rows, column_tile(16 + pair, 128)]
        keep = keep_ref[pl.ds(image, 1), :]
        zero = jnp.zeros_like(queries)
        total = jnp.zeros((toks, 128), jnp.float32)
        for own in (low, jnp.logical_not(low)):
            probs = head_probs(jnp.where(own, queries, zero), keys, keep)
            total = total + dot_nn(probs.astype(bf), jnp.where(own, values, zero))
        merged_buf[rows, column_tile(pair, 128)] = total.astype(bf)

    def step(at):
        slot = lax.rem(at, 2)
        loads(at + 1, lambda copy: copy.start())
        loads(at, lambda copy: copy.wait())

        @pl.when(at == 0)
        def _():
            modulated(x_ref, a_buf, 0)
            saves[0].start()

        @pl.when(within(at, 1, 6))
        def _():
            cols = column_tile(at - 1)
            for image in range(images):
                rows = pl.ds(image * toks, toks)
                qkv_buf[rows, cols] = (
                    dot_nn(a_buf[rows, :], wide_tile(slot)) + bias_ref[:, cols]
                ).astype(bf)

        @pl.when(at == 7)
        def _():
            saves[1].start()

        @pl.when(within(at, 7, 8))
        def _():
            for turn in range(2):
                item = (at - 7) * 2 + turn
                attend(item // 8, lax.rem(item, 8))

        @pl.when(within(at, 15, 2))
        def _():
            cols = column_tile(at - 15)
            for image in range(images):
                rows = pl.ds(image * toks, toks)
                attn = dot_nn(merged_buf[rows, :], wide_tile(slot)) + bias_ref[
                    :, column_tile(at - 15 + 6)
                ]
                attn_buf[rows, cols] = attn
                gate = mod_ref[mod_at + 4 + image : mod_at + 5 + image, cols]
                x_one_buf[rows, cols] = x_ref[rows, cols] + gate * attn

        @pl.when(at == 17)
        def _():
            for which in (2, 3, 4):
                saves[which].start()
            modulated(x_one_buf, a_two_buf, 3)
            saves[5].start()

        @pl.when(within(at, 18, 8))
        def _():
            tile = at - 18

            @pl.when(tile >= 2)
            def _():
                for copy in tile_saves(tile - 2, slot):
                    copy.wait()

            for image in range(images):
                rows = pl.ds(image * toks, toks)
                pre = dot_nn(a_two_buf[rows, :], wide_tile(slot)) + bias_ref[:, column_tile(tile + 8)]
                pre_buf[slot, rows, :] = pre
                inner = jnp.tanh(GELU_IN * (pre + GELU_CUBE * pre * pre * pre))
                active = (0.5 * pre * (1.0 + inner)).astype(bf)
                act_buf[rows, column_tile(tile)] = active

            for copy in tile_saves(tile, slot):
                copy.start()

        @pl.when(at == 26)
        def _():
            saves[8].start()

        @pl.when(within(at, 26, 4))
        def _():
            cols = column_tile(at - 26, TILE)
            bias_cols = column_tile(at - 26 + 32, TILE)
            for image in range(images):
                rows = pl.ds(image * toks, toks)
                down = dot_nn(act_buf[rows, :], tall_tile(slot)) + bias_ref[:, bias_cols]
                down_buf[rows, cols] = down
                gate = mod_ref[mod_at + 10 + image : mod_at + 11 + image, cols]
                x_two_buf[rows, cols] = x_one_buf[rows, cols] + gate * down

        @pl.when(at == FORWARD_STEPS - 1)
        def _():
            saves[6].start()
            saves[7].start()

    def finish():
        for tile in (6, 7):
            for copy in tile_saves(tile, tile % 2):
                copy.wait()
        for copy in saves:
            copy.wait()

    return step, finish


FORWARD_OUTS = [
    (D, jnp.bfloat16),
    (3 * D, jnp.bfloat16),
    (D, jnp.bfloat16),
    (D, jnp.float32),
    (D, jnp.float32),
    (D, jnp.bfloat16),
    (FF, jnp.float32),
    (FF, jnp.bfloat16),
    (D, jnp.float32),
    (D, jnp.float32),
]


def forward_scratch(toks):
    bf, f32 = jnp.bfloat16, jnp.float32
    return [
        pltpu.VMEM((toks, D), bf),
        pltpu.VMEM((toks, 3 * D), bf),
        pltpu.VMEM((toks, D), bf),
        pltpu.VMEM((toks, D), f32),
        pltpu.VMEM((toks, D), f32),
        pltpu.VMEM((toks, D), bf),
        pltpu.VMEM((2, toks, HALF), f32),
        pltpu.VMEM((toks, FF), bf),
        pltpu.VMEM((toks, D), f32),
        pltpu.VMEM((toks, D), f32),
        pltpu.VMEM((2, 4, 2, 2, 64, HALF), bf),
        pltpu.VMEM((2, 4, 2, 2, 256, TILE), bf),
        pltpu.SemaphoreType.DMA((2, 2)),
        pltpu.SemaphoreType.DMA((2, 2)),
        pltpu.SemaphoreType.DMA((9,)),
    ]


def forward_kernel(mod_at, *refs):
    step, finish = forward_pieces(refs, mod_at)

    def turn(at, carry):
        step(at)
        return carry

    lax.fori_loop(0, FORWARD_STEPS, turn, 0)
    finish()


def grouped(weights):
    return [each.reshape(4, 2, 2, -1, each.shape[-1]) for each in weights]


def forward_layer(x, mods, mod_at, biases, keep, weights):
    toks = x.shape[0]
    return pl.pallas_call(
        functools.partial(forward_kernel, mod_at),
        out_shape=[jax.ShapeDtypeStruct((toks, width), kind) for width, kind in FORWARD_OUTS],
        in_specs=[pl.BlockSpec(memory_space=pltpu.VMEM)] * 4
        + [pl.BlockSpec(memory_space=pl.ANY)] * 4,
        out_specs=[pl.BlockSpec(memory_space=pl.ANY)] * len(FORWARD_OUTS),
        scratch_shapes=forward_scratch(toks),
        compiler_params=pltpu.CompilerParams(vmem_limit_bytes=56 * 1024 * 1024),
        cost_estimate=pl.CostEstimate(
            flops=24 * toks * D * D, bytes_accessed=60 * 1024 * 1024, transcendentals=4 * toks * D
        ),
    )(x, mods, biases, keep, *grouped(weights))


def backward_pieces(ins, outs, scratch, mod_at):
    (
        x_hbm,
        x_one_hbm,
        attn_hbm,
        down_hbm,
        qkv_hbm,
        pre_hbm,
        w_qkv,
        w_proj,
        w_up,
        w_down,
        mod_ref,
        keep_ref,
    ) = ins
    d_down_out, d_up_out, d_attn_out, d_qkv_out = outs
    (
        d_mod_ref,
        d_bias_ref,
        grad_ref,
        side_ref,
        x_one_ref,
        attn_ref,
        qkv_ref,
        total_buf,
        d_x_one_buf,
        d_down_buf,
        d_up_buf,
        d_attn_buf,
        d_heads_buf,
        d_qkv_buf,
        pre_buf,
        wide_buf,
        tall_buf,
        load_sem,
        tile_sem,
        save_sem,
        in_sem,
    ) = scratch
    images, toks = keep_ref.shape
    bf = jnp.bfloat16
    blocks = toks // 64
    saves = [
        pltpu.make_async_copy(source, target, save_sem.at[at])
        for at, (source, target) in enumerate(
            [
                (d_down_buf, d_down_out),
                (d_attn_buf, d_attn_out),
                (d_qkv_buf, d_qkv_out),
            ]
        )
    ]

    in_down, in_x_one, in_attn, in_qkv, in_x = [
        pltpu.make_async_copy(source, target, in_sem.at[at])
        for at, (source, target) in enumerate(
            [
                (down_hbm, side_ref),
                (x_one_hbm, x_one_ref),
                (attn_hbm, attn_ref),
                (qkv_hbm, qkv_ref),
                (x_hbm, side_ref),
            ]
        )
    ]

    def begin():
        for copy in (in_down, in_x_one, in_attn, in_qkv):
            copy.start()

    def wide_load(source, tile, slot):
        return pltpu.make_async_copy(
            source.at[:, :, :, :, column_tile(tile)], wide_buf.at[slot], load_sem.at[0, slot]
        )

    def tall_load(tile, slot):
        return pltpu.make_async_copy(
            w_down.at[tile // 2, lax.rem(tile, 2)], tall_buf.at[slot], load_sem.at[1, slot]
        )

    def pre_load(tile, slot):
        return pltpu.make_async_copy(
            pre_hbm.at[:, column_tile(tile)], pre_buf.at[slot], load_sem.at[2, slot]
        )

    def up_save(tile, slot):
        return pltpu.make_async_copy(
            d_up_buf.at[slot], d_up_out.at[:, column_tile(tile)], tile_sem.at[slot]
        )

    def wide_tile(slot):
        return wide_buf[slot].reshape(D, HALF)

    def tall_tile(slot):
        return tall_buf[slot].reshape(HALF, D)

    def loads(at, run):
        slot = lax.rem(at, 2)

        @pl.when(within(at, 1, 8))
        def _():
            run(tall_load(at - 1, slot))
            run(wide_load(w_up, at - 1, slot))
            run(pre_load(at - 1, slot))

        @pl.when(within(at, 10, 2))
        def _():
            run(wide_load(w_proj, at - 10, slot))

        @pl.when(within(at, 20, 6))
        def _():
            run(wide_load(w_qkv, at - 20, slot))

    def column_sums(rows):
        return jnp.sum(rows.astype(jnp.float32), axis=0, keepdims=True)

    def gated(image, gate_row, gradient, branch, target, bias_cols):
        def rows_of(block, sums):
            rows = pl.ds(pl.multiple_of(image * toks + block * 64, 64), 64)
            upper = gradient[rows, :]
            gate = mod_ref[mod_at + gate_row + image : mod_at + gate_row + image + 1, :]
            lower = (upper * gate).astype(bf)
            target[rows, :] = lower
            return sums[0] + column_sums(upper * branch[rows, :]), sums[1] + column_sums(lower)

        zero = jnp.zeros((1, D), jnp.float32)
        gate, bias = lax.fori_loop(0, blocks, rows_of, (zero, zero))
        gate_at = mod_at + gate_row + image
        d_mod_ref[gate_at : gate_at + 1, :] = gate
        if image == 0:
            d_bias_ref[:, bias_cols] = bias
        else:
            d_bias_ref[:, bias_cols] += bias

    def modulate_back(image, first_row, source, passed, target):
        def rows_of(block, sums):
            rows = pl.ds(pl.multiple_of(image * toks + block * 64, 64), 64)
            scale_row = mod_at + first_row + 2 + image
            scale = mod_ref[scale_row : scale_row + 1, :]
            unit, inverse = normalized(source[rows, :])
            upper = total_buf[rows, :]
            inner = upper * (1.0 + scale)
            back = inverse * (
                inner
                - jnp.mean(inner, axis=-1, keepdims=True)
                - unit * jnp.mean(inner * unit, axis=-1, keepdims=True)
            )
            target[rows, :] = back + passed[rows, :]
            return sums[0] + column_sums(upper), sums[1] + column_sums(upper * unit)

        zero = jnp.zeros((1, D), jnp.float32)
        shift, scale = lax.fori_loop(0, blocks, rows_of, (zero, zero))
        shift_at = mod_at + first_row + image
        d_mod_ref[shift_at : shift_at + 1, :] = shift
        d_mod_ref[shift_at + 2 : shift_at + 3, :] = scale

    def attend_back(image, pair):
        rows = pl.ds(pl.multiple_of(image * toks, toks), toks)
        low = lax.broadcasted_iota(jnp.int32, (toks, 128), 1) < 64
        eighth = jnp.asarray(0.125, bf)
        queries = qkv_ref[rows, column_tile(pair, 128)] * eighth
        keys = qkv_ref[rows, column_tile(8 + pair, 128)]
        values = qkv_ref[rows, column_tile(16 + pair, 128)]
        upper = d_heads_buf[rows, column_tile(pair, 128)]
        keep = keep_ref[pl.ds(image, 1), :]
        zero = jnp.zeros_like(queries)
        total = jnp.zeros((toks, 128), jnp.float32)
        d_q, d_k, d_v = total, total, total
        for own in (low, jnp.logical_not(low)):
            own_q = jnp.where(own, queries, zero)
            own_up = jnp.where(own, upper, zero)
            probs = head_probs(own_q, keys, keep)
            d_probs = dot_nt(own_up, values)
            mean = jnp.sum(probs * d_probs, axis=-1, keepdims=True)
            d_scores = (probs * (d_probs - mean)).astype(bf)
            d_v = d_v + dot_tn(probs.astype(bf), own_up)
            d_q = d_q + dot_nn(d_scores, jnp.where(own, keys * eighth, zero))
            d_k = d_k + dot_tn(d_scores, own_q)
        d_qkv_buf[rows, column_tile(pair, 128)] = d_q.astype(bf)
        d_qkv_buf[rows, column_tile(8 + pair, 128)] = d_k.astype(bf)
        d_qkv_buf[rows, column_tile(16 + pair, 128)] = d_v.astype(bf)

    def add_product(first, image_rows, part):
        @pl.when(first)
        def _():
            total_buf[image_rows, :] = part

        @pl.when(jnp.logical_not(first))
        def _():
            total_buf[image_rows, :] += part

    def step(at):
        slot = lax.rem(at, 2)
        loads(at + 1, lambda copy: copy.start())
        loads(at, lambda copy: copy.wait())

        @pl.when(at == 0)
        def _():
            in_down.wait()
            for image in range(images):
                gated(image, 10, grad_ref, side_ref, d_down_buf, slice(8 * D, 9 * D))
            saves[0].start()

        @pl.when(within(at, 1, 8))
        def _():
            tile = at - 1
            bias = jnp.zeros((1, HALF), jnp.float32)
            for image in range(images):
                rows = pl.ds(image * toks, toks)
                upper = dot_nt(d_down_buf[rows, :], tall_tile(slot))
                pre = pre_buf[slot, rows, :]
                square = pre * pre
                inner = jnp.tanh(GELU_IN * (pre + GELU_CUBE * square * pre))
                slope = 0.5 * (1.0 + inner) + 0.5 * pre * (1.0 - inner * inner) * (
                    GELU_IN * (1.0 + 3.0 * GELU_CUBE * square)
                )
                lower = (upper * slope).astype(bf)
                d_up_buf[slot, rows, :] = lower
                bias = bias + column_sums(lower)
                add_product(tile == 0, rows, dot_nt(lower, wide_tile(slot)))
            d_bias_ref[:, column_tile(tile + 8)] = bias
            up_save(tile, slot).start()

            @pl.when(tile == 0)
            def _():
                saves[0].wait()

            @pl.when(tile >= 1)
            def _():
                up_save(tile - 1, 1 - slot).wait()

        @pl.when(at == 9)
        def _():
            up_save(7, 0).wait()
            in_x_one.wait()
            in_attn.wait()
            for image in range(images):
                modulate_back(image, 6, x_one_ref, grad_ref, d_x_one_buf)
                gated(image, 4, d_x_one_buf, attn_ref, d_attn_buf, slice(3 * D, 4 * D))
            saves[1].start()

        @pl.when(within(at, 10, 2))
        def _():
            for image in range(images):
                rows = pl.ds(image * toks, toks)
                part = dot_nt(d_attn_buf[rows, column_tile(at - 10)], wide_tile(slot))
                add_product(at == 10, rows, part)

            @pl.when(at == 10)
            def _():
                in_x.start()
                saves[1].wait()

            @pl.when(at == 11)
            def _():
                in_qkv.wait()
                d_heads_buf[...] = total_buf[...].astype(bf)

        @pl.when(within(at, 12, 8))
        def _():
            for turn in range(2):
                item = (at - 12) * 2 + turn
                attend_back(item // 8, lax.rem(item, 8))

        @pl.when(at == 20)
        def _():
            saves[2].start()

        @pl.when(within(at, 20, 6))
        def _():
            cols = column_tile(at - 20)
            bias = jnp.zeros((1, HALF), jnp.float32)
            for image in range(images):
                rows = pl.ds(image * toks, toks)
                lower = d_qkv_buf[rows, cols]
                bias = bias + column_sums(lower)
                add_product(at == 20, rows, dot_nt(lower, wide_tile(slot)))
            d_bias_ref[:, cols] = bias

            @pl.when(at == 21)
            def _():
                saves[2].wait()

        @pl.when(at == BACKWARD_STEPS - 1)
        def _():
            in_x.wait()
            for image in range(images):
                modulate_back(image, 0, side_ref, d_x_one_buf, grad_ref)

    return begin, step


BACKWARD_OUTS = [(D, jnp.bfloat16), (FF, jnp.bfloat16), (D, jnp.bfloat16), (3 * D, jnp.bfloat16)]


def backward_scratch(toks):
    bf, f32 = jnp.bfloat16, jnp.float32
    return [
        pltpu.VMEM((toks, D), f32),
        pltpu.VMEM((toks, D), f32),
        pltpu.VMEM((toks, D), f32),
        pltpu.VMEM((toks, D), f32),
        pltpu.VMEM((toks, 3 * D), bf),
        pltpu.VMEM((toks, D), f32),
        pltpu.VMEM((toks, D), f32),
        pltpu.VMEM((toks, D), bf),
        pltpu.VMEM((2, toks, HALF), bf),
        pltpu.VMEM((toks, D), bf),
        pltpu.VMEM((toks, D), bf),
        pltpu.VMEM((toks, 3 * D), bf),
        pltpu.VMEM((2, toks, HALF), f32),
        pltpu.VMEM((2, 4, 2, 2, 64, HALF), bf),
        pltpu.VMEM((2, 2, 256, D), bf),
        pltpu.SemaphoreType.DMA((3, 2)),
        pltpu.SemaphoreType.DMA((2,)),
        pltpu.SemaphoreType.DMA((3,)),
        pltpu.SemaphoreType.DMA((5,)),
    ]


def backward_kernel(mod_at, *refs):
    grad_in, ins, outs = refs[0], refs[1:13], refs[13:17]
    d_x_out, d_mod_ref, d_bias_ref = refs[17:20]
    scratch, sem = refs[20:-1], refs[-1]
    begin, step = backward_pieces(ins, outs, (d_mod_ref, d_bias_ref) + scratch, mod_at)
    begin()
    copy = pltpu.make_async_copy(grad_in, scratch[0], sem.at[0])
    copy.start()
    copy.wait()

    def turn(at, carry):
        step(at)
        return carry

    lax.fori_loop(0, BACKWARD_STEPS, turn, 0)
    copy = pltpu.make_async_copy(scratch[0], d_x_out, sem.at[1])
    copy.start()
    copy.wait()


def backward_operands(x, saved, weights):
    _, qkv, _, attn, x_one, _, pre, _, down, _ = saved
    return (x, x_one, attn, down, qkv, pre, *weights)


def backward_layer(grad, x, saved, mods, mod_at, keep, weights):
    a_one, _, merged, _, _, a_two, _, act, _, _ = saved
    toks = x.shape[0]
    vmem = pl.BlockSpec(memory_space=pltpu.VMEM)
    hbm = pl.BlockSpec(memory_space=pl.ANY)
    outs = pl.pallas_call(
        functools.partial(backward_kernel, mod_at),
        out_shape=[jax.ShapeDtypeStruct((toks, width), kind) for width, kind in BACKWARD_OUTS]
        + [
            jax.ShapeDtypeStruct((toks, D), jnp.float32),
            jax.ShapeDtypeStruct((mod_at + 12, D), jnp.float32),
            jax.ShapeDtypeStruct((1, 9 * D), jnp.float32),
        ],
        in_specs=[hbm] * 11 + [vmem] * 2,
        out_specs=[hbm] * 5 + [vmem] * 2,
        scratch_shapes=backward_scratch(toks) + [pltpu.SemaphoreType.DMA((2,))],
        compiler_params=pltpu.CompilerParams(vmem_limit_bytes=56 * 1024 * 1024),
        cost_estimate=pl.CostEstimate(
            flops=28 * toks * D * D, bytes_accessed=80 * 1024 * 1024, transcendentals=4 * toks * D
        ),
    )(grad, *backward_operands(x, saved, grouped(weights)), mods, keep)
    d_down, d_up, d_attn, d_qkv, d_x, d_mod, d_bias = outs
    factors = (merged, a_one, a_two, act, d_attn, d_qkv, d_up, d_down)
    return d_x, d_mod[mod_at:], factors, d_bias


def gather_pieces(lines, refs):
    layers = (len(refs) - 7) // 8
    pairs = list(zip(refs[: 4 * layers], refs[4 * layers : 8 * layers]))
    own_sem, zp_sem, zq_sem, yp_sem, yq_sem, x_sem, core_sem = refs[8 * layers :]
    firsts = [12 * layer + first for layer in range(layers) for first in (0, 3, 4, 8)]
    total = 12 * layers
    seq = lax.axis_index("seq")
    dp = lax.axis_index("dp")
    core = lax.rem(dp, 2)
    why = lax.rem(dp // 2, 2)
    zed = dp // 4
    core_peer = {"seq": seq, "dp": dp + 1 - 2 * core}
    x_peer = {"seq": 1 - seq, "dp": dp}
    y_peer = {"seq": seq, "dp": dp + 2 - 4 * why}
    z_peers = [
        {"seq": seq, "dp": lax.rem(zed + step, lines) * 4 + 2 * why + core}
        for step in range(1, lines)
    ]
    keeps = [
        pltpu.make_async_copy(own, every.at[zed, why, core], own_sem.at[at])
        for at, (own, every) in enumerate(pairs)
    ]
    for keep in keeps:
        keep.start()
    for keep in keeps:
        keep.wait()
    barrier = pltpu.get_barrier_semaphore()
    for peer in [core_peer, x_peer, y_peer] + z_peers:
        pl.semaphore_signal(barrier, inc=1, device_id=peer, device_id_type=MESH)
    pl.semaphore_wait(barrier, 2 + lines)

    def views(kind, unit):
        at = unit - firsts[kind]
        if kind % 4 == 3:
            cols = column_tile(at, TILE)
            mine = pl.ds(pl.multiple_of(seq * SHARED_ROWS, 16), SHARED_ROWS)
            rest = pl.ds(2 * SHARED_ROWS, PARTS * 64 - 2 * SHARED_ROWS)
            return (mine, cols), (rest, cols), (slice(None), cols)
        first = pl.multiple_of(at * D, D)
        halved = pl.ds(first, SHARED)
        rest = pl.ds(pl.multiple_of(first + SHARED, 128), D - SHARED)
        mine = pl.ds(pl.multiple_of(seq * 32, 32), 32)
        return (mine, halved), (slice(None), rest), (slice(None), pl.ds(first, D))

    def copies(stage, kind, unit):
        slot = unit
        own, every = pairs[kind]
        shared, rest, whole = views(kind, unit)

        def remote(source, target, sems, peer):
            return pltpu.make_async_remote_copy(
                src_ref=source,
                dst_ref=target,
                send_sem=sems.at[0],
                recv_sem=sems.at[1],
                device_id=peer,
                device_id_type=MESH,
            )

        def same(view, sems, peer):
            return remote(view, view, sems, peer)

        if stage == 0:
            return [
                remote(own.at[view], every.at[(zed, why, core) + view], sems, peer)
                for view, kinds in ((shared, zp_sem), (rest, zq_sem))
                for sems, peer in [(kinds.at[slot, at], z_peers[at]) for at in range(lines - 1)]
            ]
        if stage == 1:
            return [
                same(every.at[(slice(None), why, core) + shared], yp_sem.at[slot], y_peer),
                same(every.at[(slice(None), why, core) + rest], yq_sem.at[slot], y_peer),
            ]
        if stage == 2:
            return [same(every.at[(slice(None), slice(None), core) + shared], x_sem.at[slot], x_peer)]
        return [same(every.at[(slice(None), slice(None), core) + whole], core_sem.at[slot], core_peer)]

    def each_kind(unit, run):
        ends = firsts[1:] + [total]
        for kind in range(len(firsts)):

            @pl.when(jnp.logical_and(unit >= firsts[kind], unit < ends[kind]))
            def _():
                run(kind)

    def begin(stage, unit):
        def run(kind):
            for copy in copies(stage, kind, unit):
                copy.start()

        each_kind(unit, run)

    def finish(stage, unit):
        def run(kind):
            for copy in copies(stage, kind, unit):
                copy.wait()

        each_kind(unit, run)

    def step(at):
        finish(3, at - sum(GATHER_LAGS))
        for stage in (3, 2, 1):
            behind = sum(GATHER_LAGS[:stage])
            finish(stage - 1, at - behind)
            begin(stage, at - behind)
        begin(0, at)

    return step, total + sum(GATHER_LAGS)


def gather_scratch(lines, layers):
    dma = pltpu.SemaphoreType.DMA
    units = 12 * layers
    return [
        dma((4 * layers,)),
        dma((units, lines - 1, 2)),
        dma((units, lines - 1, 2)),
        dma((units, 2)),
        dma((units, 2)),
        dma((units, 2)),
        dma((units, 2)),
    ]


def modulation_pieces(lines, refs):
    (
        partial_ref,
        bias_ref,
        mods_ref,
        core_in,
        core_total,
        y_in,
        y_total,
        z_in,
        core_sem,
        y_sem,
        z_sem,
    ) = refs
    seq = lax.axis_index("seq")
    dp = lax.axis_index("dp")
    core = lax.rem(dp, 2)
    why = lax.rem(dp // 2, 2)
    zed = dp // 4

    def remote(source, target, sems, peer):
        return pltpu.make_async_remote_copy(
            src_ref=source,
            dst_ref=target,
            send_sem=sems.at[0],
            recv_sem=sems.at[1],
            device_id={"seq": seq, "dp": peer},
            device_id_type=MESH,
        )

    to_core = remote(partial_ref.at[:, :, 1 - core], core_in, core_sem, dp + 1 - 2 * core)
    to_y = remote(core_total.at[:, 1 - why], y_in, y_sem, dp + 2 - 4 * why)
    to_z = []
    for ahead in range(1, lines):
        there = lax.rem(zed + ahead, lines)
        to_z.append(
            remote(
                y_total.at[there],
                z_in.at[ahead - 1],
                z_sem.at[ahead - 1],
                there * 4 + 2 * why + core,
            )
        )

    def step(at):
        @pl.when(at == 0)
        def _():
            to_core.start()

        @pl.when(at == 1)
        def _():
            to_core.wait()
            core_total[...] = wide_sum(partial_ref[:, :, core], core_in[...]).astype(jnp.bfloat16)
            to_y.start()

        @pl.when(at == 4)
        def _():
            to_y.wait()
            y_total[...] = wide_sum(core_total[:, why], y_in[...]).astype(jnp.bfloat16)
            for copy in to_z:
                copy.start()

        @pl.when(at == 8)
        def _():
            total = y_total[zed].astype(jnp.float32)
            for ahead, copy in enumerate(to_z):
                copy.wait()
                total = total + z_in[ahead].astype(jnp.float32)
            for image in range(2):
                for piece in range(mods_ref.shape[0] // 2):
                    row, source = 2 * piece + image, 16 * image + piece
                    mods_ref[row : row + 1, :] = (
                        total[source : source + 1, :] + bias_ref[row : row + 1, :]
                    )

    return step


def modulation_scratch(lines):
    dma = pltpu.SemaphoreType.DMA
    bf = jnp.bfloat16
    return [
        pltpu.VMEM((lines, 2, 32, D), bf),
        pltpu.VMEM((lines, 2, 32, D), bf),
        pltpu.VMEM((lines, 32, D), bf),
        pltpu.VMEM((lines, 32, D), bf),
        pltpu.VMEM((lines - 1, 32, D), bf),
        dma((2,)),
        dma((2,)),
        dma((lines - 1, 2)),
    ]


def whole_forward_kernel(lines, *refs):
    refs = list(refs)

    def take(count):
        taken, refs[:] = tuple(refs[:count]), refs[count:]
        return taken

    own = take(8)
    partial_ref, mod_bias, x_ref, first_bias, second_bias, keep = take(6)
    every = take(8)
    first_outs, second_outs = take(len(FORWARD_OUTS)), take(len(FORWARD_OUTS))
    (mods,) = take(1)
    gather_sems = take(7)
    mod_scratch = take(8)
    scratch = tuple(refs)
    gather, steps = gather_pieces(lines, own + every + gather_sems)
    modulate_step = modulation_pieces(lines, (partial_ref, mod_bias, mods) + mod_scratch)
    first, first_finish = forward_pieces(
        (x_ref, mods, first_bias, keep) + every[:4] + first_outs + scratch, 0
    )
    second, second_finish = forward_pieces(
        (scratch[9], mods, second_bias, keep) + every[4:] + second_outs + scratch, 12
    )

    def run(step, begin, end):
        def one(at, carry):
            step(at)
            return carry

        lax.fori_loop(begin, end, one, 0)

    def turn(at, carry):
        gather(at)
        modulate_step(at)

        @pl.when(within(at, 10, 13))
        def _():
            run(first, 5 * (at - 10) // 2, 5 * (at - 9) // 2)

        @pl.when(at == 23)
        def _():
            first_finish()

        @pl.when(at >= 23)
        def _():
            run(second, 13 * (at - 23) // 4, 13 * (at - 22) // 4)

        return carry

    lax.fori_loop(0, steps + 2, turn, 0)
    second_finish()


def whole_forward(own, partial, mod_bias, x, biases, keep, lines):
    toks = x.shape[0]
    rows = mod_bias.shape[0]
    vmem = pl.BlockSpec(memory_space=pltpu.VMEM)
    hbm = pl.BlockSpec(memory_space=pl.ANY)
    layer_outs = [jax.ShapeDtypeStruct((toks, width), kind) for width, kind in FORWARD_OUTS]
    outs = pl.pallas_call(
        functools.partial(whole_forward_kernel, lines),
        out_shape=[
            jax.ShapeDtypeStruct((lines, 2, 2) + each.shape, jnp.bfloat16) for each in own
        ]
        + layer_outs
        + layer_outs
        + [jax.ShapeDtypeStruct((rows, D), jnp.float32)],
        in_specs=[vmem] * 14,
        out_specs=[hbm] * (8 + 2 * len(FORWARD_OUTS)) + [vmem],
        scratch_shapes=gather_scratch(lines, 2)
        + modulation_scratch(lines)
        + forward_scratch(toks),
        compiler_params=pltpu.CompilerParams(
            collective_id=2, has_side_effects=True, vmem_limit_bytes=58 * 1024 * 1024
        ),
        cost_estimate=pl.CostEstimate(
            flops=48 * toks * D * D,
            bytes_accessed=24 * 4 * lines * 64 * D * 8,
            transcendentals=8 * toks * D,
        ),
    )(*own, partial, mod_bias, x, *biases, keep)
    weights = outs[:8]
    count = len(FORWARD_OUTS)
    saved = [outs[8 : 8 + count], outs[8 + count : 8 + 2 * count]]
    return [weights[:4], weights[4:]], saved, outs[-1]


def gather_small_kernel(lines, own_ref, every_ref, z_sem, y_sem, core_sem):
    seq = lax.axis_index("seq")
    dp = lax.axis_index("dp")
    core = lax.rem(dp, 2)
    why = lax.rem(dp // 2, 2)
    zed = dp // 4
    core_peer = {"seq": seq, "dp": dp + 1 - 2 * core}
    y_peer = {"seq": seq, "dp": dp + 2 - 4 * why}
    z_peers = [
        {"seq": seq, "dp": lax.rem(zed + step, lines) * 4 + 2 * why + core}
        for step in range(1, lines)
    ]
    barrier = pltpu.get_barrier_semaphore()
    for peer in [core_peer, y_peer] + z_peers:
        pl.semaphore_signal(barrier, inc=1, device_id=peer, device_id_type=MESH)
    every_ref[zed, why, core] = own_ref[...]
    pl.semaphore_wait(barrier, 1 + lines)

    def remote(source, target, sems, peer):
        return pltpu.make_async_remote_copy(
            src_ref=source,
            dst_ref=target,
            send_sem=sems.at[0],
            recv_sem=sems.at[1],
            device_id=peer,
            device_id_type=MESH,
        )

    copies = [
        remote(own_ref, every_ref.at[zed, why, core], z_sem.at[at], peer)
        for at, peer in enumerate(z_peers)
    ]
    for copy in copies:
        copy.start()
    for copy in copies:
        copy.wait()
    for view, sems, peer in (
        (every_ref.at[:, why, core], y_sem, y_peer),
        (every_ref.at[:, :, core], core_sem, core_peer),
    ):
        copy = remote(view, view, sems, peer)
        copy.start()
        copy.wait()


def gather_small(own, lines, collective_id):
    dma = pltpu.SemaphoreType.DMA
    every = pl.pallas_call(
        functools.partial(gather_small_kernel, lines),
        out_shape=jax.ShapeDtypeStruct((lines, 2, 2) + own.shape, own.dtype),
        in_specs=[pl.BlockSpec(memory_space=pltpu.VMEM)],
        out_specs=pl.BlockSpec(memory_space=pltpu.VMEM),
        scratch_shapes=[dma((lines - 1, 2)), dma((2,)), dma((2,))],
        compiler_params=pltpu.CompilerParams(collective_id=collective_id, has_side_effects=True),
        cost_estimate=pl.CostEstimate(
            flops=0, bytes_accessed=own.size * 32 * lines, transcendentals=0
        ),
    )(own)
    return every.reshape(-1, own.shape[-1])


def scatter_pieces(lines, sources, scratch):
    per_layer = 12
    total = len(sources) * per_layer
    (
    out_ref,
    lhs_buf,
    act_buf,
    wide_buf,
    down_buf,
    load_sem,
    made,
    core_in,
    x_out,
    x_in,
    p_keep,
    yq_out,
    yq_in,
    q_keep,
    yp_out,
    yp_in,
    p_line,
    zq_out,
    zq_in,
    zp_out,
    zp_in,
    xq_out,
    xq_in,
    xp_out,
    xp_in,
    core_sem,
    x_sem,
    yq_sem,
    yp_sem,
    zq_sem,
    zp_sem,
    xq_sem,
    xp_sem,
    out_buf,
    out_sem,
    ) = scratch
    seq = lax.axis_index("seq")
    dp = lax.axis_index("dp")
    core = lax.rem(dp, 2)
    why = lax.rem(dp // 2, 2)
    zed = dp // 4
    core_peer = {"seq": seq, "dp": dp + 1 - 2 * core}
    x_peer = {"seq": 1 - seq, "dp": dp}
    y_peer = {"seq": seq, "dp": dp + 2 - 4 * why}

    def z_place(step):
        return lax.rem(zed + step, lines)

    def z_peer(step):
        return {"seq": seq, "dp": z_place(step) * 4 + 2 * why + core}

    def remote(source, target, sems, peer):
        return pltpu.make_async_remote_copy(
            src_ref=source,
            dst_ref=target,
            send_sem=sems.at[0],
            recv_sem=sems.at[1],
            device_id=peer,
            device_id_type=MESH,
        )

    def core_copy(slot):
        return remote(made.at[slot, 1 - core], core_in.at[slot], core_sem.at[slot], core_peer)

    def x_copy(slot):
        return remote(x_out.at[slot], x_in.at[slot], x_sem.at[slot], x_peer)

    def yq_copy(slot):
        return remote(yq_out.at[slot], yq_in.at[slot], yq_sem.at[slot], y_peer)

    def yp_copy(slot):
        return remote(yp_out.at[slot], yp_in.at[slot], yp_sem.at[slot], y_peer)

    def zq_copy(slot, step):
        return remote(
            zq_out.at[slot, z_place(step)],
            zq_in.at[slot, step - 1],
            zq_sem.at[slot, step - 1],
            z_peer(step),
        )

    def zp_copy(slot, step):
        return remote(
            zp_out.at[slot, z_place(step)],
            zp_in.at[slot, step - 1],
            zp_sem.at[slot, step - 1],
            z_peer(step),
        )

    def xq_copy(slot):
        return remote(xq_out.at[slot], xq_in.at[slot], xq_sem.at[slot], x_peer)

    def xp_copy(slot):
        return remote(xp_out.at[slot], xp_in.at[slot], xp_sem.at[slot], x_peer)

    def loads(unit, slot):
        found = []
        for layer in range(len(sources)):
            merged, a_one, a_two, act, d_attn, d_qkv, d_up, d_down = sources[layer]
            at = unit - layer * per_layer

            def slab(ref, index, size):
                return ref.at[:, pl.ds(pl.multiple_of(index * size, size), size)]

            wide_to = wide_buf.at[slot], load_sem.at[1, slot]
            lhs_to = lhs_buf.at[slot], load_sem.at[0, slot]
            found += [
                (
                    jnp.logical_and(at >= 0, at < 4),
                    (slab(d_down, at, TILE), down_buf.at[slot], load_sem.at[2, slot]),
                ),
                (at == 0, (act, act_buf, load_sem.at[3, 0])),
                (
                    jnp.logical_and(at >= 4, at < 8),
                    (a_two, *lhs_to),
                    (slab(d_up, at - 4, D), *wide_to),
                ),
                (at == 8, (merged, *lhs_to), (d_attn, *wide_to)),
                (
                    jnp.logical_and(at >= 9, at < per_layer),
                    (a_one, *lhs_to),
                    (slab(d_qkv, at - 9, D), *wide_to),
                ),
            ]
        return found

    def prefetch(unit):
        for due, *moves in loads(unit, lax.rem(unit, 2)):

            @pl.when(due)
            def _():
                for move in moves:
                    pltpu.make_async_copy(*move).start()

    def fetched(unit):
        for due, *moves in loads(unit, lax.rem(unit, 2)):

            @pl.when(due)
            def _():
                for move in moves:
                    pltpu.make_async_copy(*move).wait()

    def dot_rows(left, right):
        return lax.dot_general(
            left, right, (((0,), (0,)), ((), ())), preferred_element_type=jnp.float32
        )

    def compute(unit):
        at = lax.rem(unit, per_layer)
        slot = lax.rem(unit, 2)
        fetched(unit)

        @pl.when(at >= 4)
        def _():
            def rows(pair, carry):
                left = lhs_buf[slot, :, pl.ds(pl.multiple_of(pair * 128, 128), 128)]
                block = dot_rows(left, wide_buf[slot]).astype(jnp.bfloat16)
                for own in range(2):
                    for part in range(PARTS):
                        made[slot, own, part, pair // 2, lax.rem(pair, 2)] = block[
                            own * 64 : own * 64 + 64, part * TILE : part * TILE + TILE
                        ]
                return carry

            lax.fori_loop(0, 2 * lines, rows, 0)

        @pl.when(at < 4)
        def _():
            def rows(pair, carry):
                left = act_buf[:, pl.ds(pl.multiple_of(pair * 512, 512), 512)]
                block = dot_rows(left, down_buf[slot]).astype(jnp.bfloat16)
                for own in range(2):
                    for part in range(PARTS):
                        first = own * 256 + part * 64
                        made[slot, own, part, pair // 2, lax.rem(pair, 2)] = block[
                            first : first + 64
                        ]
                return carry

            lax.fori_loop(0, 2 * lines, rows, 0)

    def out_copy(unit, slot):
        return pltpu.make_async_copy(out_buf.at[slot], out_ref.at[unit], out_sem.at[slot])

    def stage_two(slot):
        core_copy(slot).wait()

        def rows(line, carry):
            for side in range(2):
                x_out[slot, line, side] = wide_sum(
                    made[slot, core, 1 - seq, line, side], core_in[slot, 1 - seq, line, side]
                ).astype(jnp.bfloat16)
                p_keep[slot, line, side] = wide_sum(
                    made[slot, core, seq, line, side], core_in[slot, seq, line, side]
                ).astype(jnp.bfloat16)
            for part in range(2):
                yq_out[slot, line, part] = wide_sum(
                    made[slot, core, 2 + part, line, 1 - why],
                    core_in[slot, 2 + part, line, 1 - why],
                ).astype(jnp.bfloat16)
                q_keep[slot, line, part] = wide_sum(
                    made[slot, core, 2 + part, line, why], core_in[slot, 2 + part, line, why]
                ).astype(jnp.bfloat16)
            return carry

        lax.fori_loop(0, lines, rows, 0)
        x_copy(slot).start()
        yq_copy(slot).start()

    def stage_three(slot):
        x_copy(slot).wait()
        yq_copy(slot).wait()

        def rows(line, carry):
            yp_out[slot, line] = wide_sum(
                p_keep[slot, line, 1 - why], x_in[slot, line, 1 - why]
            ).astype(jnp.bfloat16)
            p_line[slot, line] = wide_sum(p_keep[slot, line, why], x_in[slot, line, why]).astype(
                jnp.bfloat16
            )
            for part in range(2):
                zq_out[slot, line, part] = wide_sum(
                    q_keep[slot, line, part], yq_in[slot, line, part]
                ).astype(jnp.bfloat16)
            return carry

        lax.fori_loop(0, lines, rows, 0)
        yp_copy(slot).start()
        for step in range(1, lines):
            zq_copy(slot, step).start()

    def stage_four(slot):
        yp_copy(slot).wait()
        for step in range(1, lines):
            zq_copy(slot, step).wait()

        def rows(line, carry):
            zp_out[slot, line] = wide_sum(p_line[slot, line], yp_in[slot, line]).astype(
                jnp.bfloat16
            )
            return carry

        lax.fori_loop(0, lines, rows, 0)
        total_q = zq_out[slot, zed].astype(jnp.float32)
        for step in range(1, lines):
            total_q = total_q + zq_in[slot, step - 1].astype(jnp.float32)
        xq_out[slot] = total_q.astype(jnp.bfloat16)
        for step in range(1, lines):
            zp_copy(slot, step).start()
        xq_copy(slot).start()

    def stage_five(unit, slot):
        for step in range(1, lines):
            zp_copy(slot, step).wait()
        xq_copy(slot).wait()
        total_p = zp_out[slot, zed].astype(jnp.float32)
        for step in range(1, lines):
            total_p = total_p + zp_in[slot, step - 1].astype(jnp.float32)
        rounded = total_p.astype(jnp.bfloat16)
        xp_out[slot] = rounded
        xp_copy(slot).start()
        @pl.when(unit >= 2)
        def _():
            out_copy(unit - 2, slot).wait()

        out_buf[slot, seq] = rounded.astype(jnp.float32)
        for part in range(2):
            out_buf[slot, 2 + part] = wide_sum(xq_out[slot, part], xq_in[slot, part])

    def stage_six(unit, slot):
        xp_copy(slot).wait()
        out_buf[slot, 1 - seq] = xp_in[slot].astype(jnp.float32)
        out_copy(unit, slot).start()

    def turn(at):
        def when_due(behind, run):
            unit = at - behind

            @pl.when(jnp.logical_and(unit >= 0, unit < total))
            def _():
                run(unit, lax.rem(unit, 2))

        when_due(5, stage_six)
        when_due(4, stage_five)
        when_due(3, lambda unit, slot: stage_four(slot))
        when_due(2, lambda unit, slot: stage_three(slot))
        when_due(1, lambda unit, slot: stage_two(slot))

        @pl.when(at < total)
        def _():
            compute(at)
            core_copy(lax.rem(at, 2)).start()

    def finish():
        for unit in (total - 2, total - 1):
            out_copy(unit, unit % 2).wait()

    return prefetch, turn, finish, total + 5


def scatter_scratch(toks, lines):
    bf = jnp.bfloat16
    dma = pltpu.SemaphoreType.DMA

    buf_f32 = pltpu.VMEM((2, PARTS, 64, TILE), jnp.float32)

    def buf(*shape):
        return pltpu.VMEM((2,) + shape, bf)

    return [
        buf(toks, D),
        pltpu.VMEM((toks, FF), bf),
        buf(toks, D),
        buf(toks, TILE),
        dma((4, 2)),
        buf(2, PARTS, lines, 2, 64, TILE),
        buf(PARTS, lines, 2, 64, TILE),
        buf(lines, 2, 64, TILE),
        buf(lines, 2, 64, TILE),
        buf(lines, 2, 64, TILE),
        buf(lines, 2, 64, TILE),
        buf(lines, 2, 64, TILE),
        buf(lines, 2, 64, TILE),
        buf(lines, 64, TILE),
        buf(lines, 64, TILE),
        buf(lines, 64, TILE),
        buf(lines, 2, 64, TILE),
        buf(lines - 1, 2, 64, TILE),
        buf(lines, 64, TILE),
        buf(lines - 1, 64, TILE),
        buf(2, 64, TILE),
        buf(2, 64, TILE),
        buf(64, TILE),
        buf(64, TILE),
        dma((2, 2)),
        dma((2, 2)),
        dma((2, 2)),
        dma((2, 2)),
        dma((2, lines - 1, 2)),
        dma((2, lines - 1, 2)),
        dma((2, 2)),
        dma((2, 2)),
        buf_f32,
        dma((2,)),
    ]


def summary_pieces(lines, refs):
    (
        flat_own,
        mod_own,
        flat_all,
        mod_all,
        core_in,
        core_total,
        x_in,
        x_total,
        y_in,
        y_total,
        z_in,
        pair_sem,
        line_sem,
    ) = refs
    seq = lax.axis_index("seq")
    dp = lax.axis_index("dp")
    core = lax.rem(dp, 2)
    why = lax.rem(dp // 2, 2)
    zed = dp // 4
    core_peer = {"seq": seq, "dp": dp + 1 - 2 * core}
    x_peer = {"seq": 1 - seq, "dp": dp}
    y_peer = {"seq": seq, "dp": dp + 2 - 4 * why}
    places = [lax.rem(zed + ahead, lines) for ahead in range(1, lines)]
    z_peers = [{"seq": seq, "dp": there * 4 + 2 * why + core} for there in places]

    def remote(source, target, sems, peer):
        return pltpu.make_async_remote_copy(
            src_ref=source,
            dst_ref=target,
            send_sem=sems.at[0],
            recv_sem=sems.at[1],
            device_id=peer,
            device_id_type=MESH,
        )

    def same(view, sems, peer):
        return remote(view, view, sems, peer)

    flat_core = remote(flat_own.at[1 - core], core_in, pair_sem.at[0], core_peer)
    flat_x = remote(core_total, x_in, pair_sem.at[1], x_peer)
    flat_y = remote(x_total, y_in, pair_sem.at[2], y_peer)
    flat_z = [
        remote(y_total.at[there], z_in.at[at], line_sem.at[0, at], peer)
        for at, (there, peer) in enumerate(zip(places, z_peers))
    ]
    back_z = [
        same(flat_all.at[core, zed], line_sem.at[1, at], peer) for at, peer in enumerate(z_peers)
    ]
    back_core = same(flat_all.at[core], pair_sem.at[3], core_peer)
    mod_x = remote(mod_own, mod_all.at[zed, why, core, seq], pair_sem.at[4], x_peer)
    mod_z = [
        same(mod_all.at[zed, why, core], line_sem.at[2, at], peer)
        for at, peer in enumerate(z_peers)
    ]
    mod_y = same(mod_all.at[:, why, core], pair_sem.at[5], y_peer)
    mod_core = same(mod_all.at[:, :, core], pair_sem.at[6], core_peer)

    def first():
        mod_all[zed, why, core, seq] = mod_own[...]
        flat_core.start()
        mod_x.start()

    def second():
        flat_core.wait()
        core_total[...] = flat_own[core] + core_in[...]
        flat_x.start()
        mod_x.wait()
        for copy in mod_z:
            copy.start()

    def third():
        flat_x.wait()
        x_total[...] = core_total[...] + x_in[...]
        flat_y.start()
        for copy in mod_z:
            copy.wait()
        mod_y.start()

    def fourth():
        flat_y.wait()
        y_total[...] = x_total[...] + y_in[...]
        for copy in flat_z:
            copy.start()

    def fifth():
        total = y_total[zed]
        for at, copy in enumerate(flat_z):
            copy.wait()
            total = total + z_in[at]
        flat_all[core, zed] = total
        for copy in back_z:
            copy.start()
        mod_y.wait()
        mod_core.start()

    def sixth():
        for copy in back_z:
            copy.wait()
        back_core.start()
        mod_core.wait()

    def seventh():
        back_core.wait()

    return [first, second, third, fourth, fifth, sixth, seventh]


def summary_scratch(lines):
    f32 = jnp.float32
    part = pltpu.VMEM((lines, 8, D), f32)
    return [
        pltpu.VMEM((2, lines, 8, D), f32),
        pltpu.VMEM((32, D), jnp.bfloat16),
        part,
        part,
        part,
        part,
        part,
        part,
        pltpu.VMEM((lines - 1, 8, D), f32),
        pltpu.SemaphoreType.DMA((7, 2)),
        pltpu.SemaphoreType.DMA((3, lines - 1, 2)),
    ]


def whole_backward_kernel(lines, *refs):
    refs = list(refs)

    def take(count):
        taken, refs[:] = tuple(refs[:count]), refs[count:]
        return taken

    (grad_in,) = take(1)
    operands = [take(10), take(10)]
    kept = [take(4), take(4)]
    mod_ref, keep_ref, final_rows, head_rows, misc_row, flat_in = take(6)
    units_out = take(1)
    outs = [take(4), take(4)]
    flat_all, mod_all = take(2)
    back_scratch = take(19)
    d_mod_ref, *d_bias_refs = take(3)
    (grad_sem,) = take(1)
    summary = take(11)
    scatter_refs = tuple(refs)

    dp = lax.axis_index("dp")
    seq = lax.axis_index("seq")
    core = lax.rem(dp, 2)
    why = lax.rem(dp // 2, 2)
    zed = dp // 4
    barrier = pltpu.get_barrier_semaphore()
    peers = [dp + 1 - 2 * core, dp + 2 - 4 * why]
    peers += [lax.rem(zed + ahead, lines) * 4 + 2 * why + core for ahead in range(1, lines)]
    for peer in [{"seq": seq, "dp": peer} for peer in peers] + [{"seq": 1 - seq, "dp": dp}]:
        pl.semaphore_signal(barrier, inc=1, device_id=peer, device_id_type=MESH)

    load = pltpu.make_async_copy(grad_in, back_scratch[0], grad_sem.at[0])
    load.start()
    begins, steps = [], []
    for at, mod_at in ((0, 12), (1, 0)):
        begin, step = backward_pieces(
            operands[at] + (mod_ref, keep_ref),
            outs[at],
            (d_mod_ref, d_bias_refs[at]) + back_scratch,
            mod_at,
        )
        begins.append(begin)
        steps.append(step)
    begins[0]()
    load.wait()

    sources = []
    for at in range(2):
        merged, a_one, a_two, act = kept[at]
        d_down, d_up, d_attn, d_qkv = outs[at]
        sources.append((merged, a_one, a_two, act, d_attn, d_qkv, d_up, d_down))
    prefetch, scatter, scatter_finish, turns = scatter_pieces(
        lines, sources, units_out + scatter_refs
    )
    flat_own, mod_own = summary[:2]
    summary_steps = summary_pieces(
        lines, (flat_own, mod_own, flat_all, mod_all) + summary[2:]
    )

    def put(row, value):
        flat_own[row // (8 * lines), row // 8 % lines, row % 8 : row % 8 + 1, :] = value

    def collect():
        d_patch = back_scratch[0][...].astype(jnp.bfloat16)
        for layer in range(2):
            for row in range(9):
                put(9 * layer + row, d_bias_refs[1 - layer][:, row * D : (row + 1) * D])
        put(18, jnp.sum(d_patch.astype(jnp.float32), axis=0, keepdims=True))
        g_patch = dot_nn(flat_in[...], d_patch)
        for row in range(16):
            put(19 + row, g_patch[row : row + 1, :])
            put(35 + row, head_rows[row : row + 1, :])
        put(51, misc_row[...])
        for row in range(52, 16 * lines):
            put(row, jnp.zeros((1, D), jnp.float32))
        d_mod_ref[24:28, :] = final_rows[...]
        d_mod_ref[28:32, :] = jnp.zeros((4, D), jnp.float32)
        mod_own[...] = d_mod_ref[...].astype(jnp.bfloat16)

    def back(at, carry):
        @pl.when(at < BACKWARD_STEPS)
        def _():
            steps[0](at)

        @pl.when(at == BACKWARD_STEPS)
        def _():
            begins[1]()

        @pl.when(jnp.logical_and(at >= BACKWARD_STEPS, at < 2 * BACKWARD_STEPS))
        def _():
            steps[1](at - BACKWARD_STEPS)

        return carry

    lax.fori_loop(0, 2, back, 0)
    prefetch(jnp.int32(0))
    pl.semaphore_wait(barrier, 2 + lines)

    def turn(at, carry):
        @pl.when(at <= 20)
        def _():
            lax.fori_loop(2 + at * 5 // 2, 2 + (at + 1) * 5 // 2, back, 0)

        prefetch(at + 1)
        scatter(at)

        @pl.when(at == 21)
        def _():
            collect()

        for offset, run in enumerate(summary_steps):

            @pl.when(at == 21 + offset)
            def _():
                run()

        return carry

    lax.fori_loop(0, turns, turn, 0)
    scatter_finish()


def whole_backward(
    grad, inputs, saved, weights, mods, keep, final_rows, head_rows, misc_row, flat_in, lines
):
    toks = grad.shape[0]
    vmem = pl.BlockSpec(memory_space=pltpu.VMEM)
    hbm = pl.BlockSpec(memory_space=pl.ANY)
    operands = [grad]
    for at in (1, 0):
        operands += backward_operands(inputs[at], saved[at], weights[at])
    for at in (1, 0):
        a_one, _, merged, _, _, a_two, _, act, _, _ = saved[at]
        operands += [merged, a_one, a_two, act]
    layer_outs = [jax.ShapeDtypeStruct((toks, width), kind) for width, kind in BACKWARD_OUTS]
    outs = pl.pallas_call(
        functools.partial(whole_backward_kernel, lines),
        out_shape=[jax.ShapeDtypeStruct((24, PARTS, 64, TILE), jnp.float32)]
        + layer_outs
        + layer_outs
        + [
            jax.ShapeDtypeStruct((2, lines, 8, D), jnp.float32),
            jax.ShapeDtypeStruct((lines, 2, 2, 2, 32, D), jnp.bfloat16),
        ],
        in_specs=[hbm] * len(operands) + [vmem] * 6,
        out_specs=[hbm] * 9 + [vmem] * 2,
        scratch_shapes=backward_scratch(toks)
        + [
            pltpu.VMEM((32, D), jnp.float32),
            pltpu.VMEM((1, 9 * D), jnp.float32),
            pltpu.VMEM((1, 9 * D), jnp.float32),
            pltpu.SemaphoreType.DMA((1,)),
        ]
        + summary_scratch(lines)
        + scatter_scratch(toks, lines),
        compiler_params=pltpu.CompilerParams(
            collective_id=1, has_side_effects=True, vmem_limit_bytes=61 * 1024 * 1024
        ),
        cost_estimate=pl.CostEstimate(
            flops=104 * toks * D * D,
            bytes_accessed=300 * 1024 * 1024,
            transcendentals=8 * toks * D,
        ),
    )(*operands, mods, keep, final_rows, head_rows, misc_row, flat_in)
    return outs[0], outs[9], outs[10]


def gather_rows(shard):
    return lax.all_gather(shard.astype(jnp.bfloat16), "dp", axis=0, tiled=True)


def kernels_fit():
    dp_parts = lax.axis_size("dp")
    return (
        lax.axis_size("seq") == 2
        and dp_parts % 4 == 0
        and D // dp_parts == 64
        and FF // dp_parts == PARTS * 64
    )


def reduce_rows(partial):
    owned = lax.psum_scatter(
        partial.astype(jnp.bfloat16), "dp", scatter_dimension=0, tiled=True
    )
    return lax.psum(owned, "seq").astype(jnp.float32)


def adamw(weight, gradient, first, second, rate):
    first_new = BETA_ONE * first + (1.0 - BETA_ONE) * gradient
    second_new = BETA_TWO * second + (1.0 - BETA_TWO) * gradient * gradient
    first_hat = first_new / (1.0 - BETA_ONE**STEP)
    second_hat = second_new / (1.0 - BETA_TWO**STEP)
    return (
        weight - rate * (first_hat / (jnp.sqrt(second_hat) + EPSILON) + DECAY * weight),
        first_new,
        second_new,
    )


def unit_adamw_kernel(by_rows, grad_ref, weight_ref, first_ref, second_ref, *outs):
    for part in range(PARTS):
        if by_rows:
            place = (0, slice(part * 64, part * 64 + 64), slice(None))
        else:
            place = (0, slice(None), slice(part * TILE, part * TILE + TILE))
        moved = adamw(
            weight_ref[place], grad_ref[0, part], first_ref[place], second_ref[place], RATE_MATRIX
        )
        for out, value in zip(outs, moved):
            out[place] = value


def unit_adamw(weight, units, first, second, first_unit, by_rows):
    layers, rows, width = weight.shape
    block = (1, rows, TILE) if by_rows else (1, rows, D)
    spec = pl.BlockSpec(block, lambda layer, at: (layer, 0, at))
    per_layer = units.shape[0] // layers
    grad_spec = pl.BlockSpec(
        (1, PARTS, 64, TILE),
        lambda layer, at: ((layers - 1 - layer) * per_layer + first_unit + at, 0, 0, 0),
    )
    return pl.pallas_call(
        functools.partial(unit_adamw_kernel, by_rows),
        out_shape=[jax.ShapeDtypeStruct(weight.shape, jnp.float32)] * 3,
        grid=(layers, width // block[2]),
        in_specs=[grad_spec, spec, spec, spec],
        out_specs=[spec] * 3,
        compiler_params=pltpu.CompilerParams(vmem_limit_bytes=32 * 1024 * 1024),
        cost_estimate=pl.CostEstimate(
            flops=16 * weight.size, bytes_accessed=28 * weight.size, transcendentals=weight.size
        ),
    )(units, weight, first, second)


def body(
    latents,
    noise_target,
    pad_mask,
    labels,
    timesteps,
    embed_rows,
    first_embed,
    second_embed,
    class_table,
    first_table,
    second_table,
    qkv_weight,
    first_qkv,
    second_qkv,
    proj_weight,
    first_proj,
    second_proj,
    up_weight,
    first_up,
    second_up,
    down_weight,
    first_down,
    second_down,
    cond_weight,
    first_cond,
    second_cond,
    head_weight,
    first_head,
    second_head,
    all_biases,
    first_bias,
    second_bias,
):
    seq_parts = lax.axis_size("seq")
    dp_parts = lax.axis_size("dp")
    seq_at = lax.axis_index("seq")
    dp_at = lax.axis_index("dp")
    lines = dp_parts // 4
    group, half_rows, _ = latents.shape
    images = group // seq_parts
    everyone = group * dp_parts
    own_cols = embed_rows.shape[1]
    own_place = dp_at * own_cols
    cond_cols = cond_weight.shape[1]
    pieces = cond_cols // D
    bias_base = 3 * D + cond_cols
    by_kernel = kernels_fit()
    packed = jnp.concatenate(
        [latents, noise_target, pad_mask.astype(jnp.float32)[:, :, None]], axis=2
    )
    shards = [
        weight[at].astype(jnp.bfloat16)
        for at in range(LAYERS)
        for weight in (qkv_weight, proj_weight, up_weight, down_weight)
    ]
    narrow = jnp.concatenate(
        [embed_rows[: PATCH_IN + FREQ].T, head_weight], axis=1
    ).astype(jnp.bfloat16)
    if by_kernel:
        ids = jnp.stack([labels, timesteps])
        parts = jnp.stack([ids // 32, ids % 32]).astype(jnp.bfloat16).reshape(-1, 1)
        parts = jnp.pad(parts, ((0, own_cols - parts.shape[0]), (0, 0)))
        width = narrow.shape[1]
        block = jnp.concatenate(
            [narrow, parts, jnp.zeros((own_cols, 383 - width), jnp.bfloat16)], axis=1
        )
        small = gather_small(block, lines, 4)
        parts = small[:, width].astype(jnp.float32).reshape(dp_parts, own_cols)[:, : 4 * group]
        parts = parts.reshape(dp_parts, 2, 2, group)
        ids = (parts[:, 0] * 32.0 + parts[:, 1]).astype(jnp.int32)
        ids = ids.transpose(1, 0, 2).reshape(2, everyone)
        theirs = lax.dynamic_slice(
            packed, ((1 - seq_at) * images, 0, 0), (images,) + packed.shape[1:]
        )
        mine = lax.dynamic_slice(packed, (seq_at * images, 0, 0), (images,) + packed.shape[1:])
        came = lax.ppermute(theirs, "seq", [(0, 1), (1, 0)])
        packed = jnp.concatenate(
            [jnp.where(seq_at == 0, mine, came), jnp.where(seq_at == 0, came, mine)], axis=1
        )
    else:
        small = lax.all_gather(narrow, "dp", axis=0, tiled=True)
        ids = lax.all_gather(jnp.stack([labels, timesteps]), "dp", axis=1, tiled=True)
        packed = lax.all_to_all(packed, "seq", split_axis=0, concat_axis=1, tiled=True)
    tok_rows = packed.shape[1]
    toks = images * tok_rows
    latents, noise_target, keep_rows = (
        packed[:, :, :PATCH_IN],
        packed[:, :, PATCH_IN : 2 * PATCH_IN],
        packed[:, :, 2 * PATCH_IN],
    )
    patch_part = small[:, :PATCH_IN]
    freq_part = small[:, PATCH_IN : PATCH_IN + FREQ]
    head_full = small[:, PATCH_IN + FREQ : PATCH_IN + FREQ + OUT_CH]
    time_own = embed_rows[PATCH_IN + FREQ :].astype(jnp.bfloat16)
    cond_own = cond_weight.astype(jnp.bfloat16)

    features = time_features(ids[1], FREQ).astype(jnp.bfloat16)
    time_pre = dot_nt(features, freq_part) + all_biases[D : 2 * D]
    time_hidden = jax.nn.silu(time_pre).astype(jnp.bfloat16)
    second_bias_own = lax.dynamic_slice(all_biases, (2 * D + own_place,), (own_cols,))
    onehot = (ids[0][:, None] == jnp.arange(NCLASS, dtype=jnp.int32)[None, :]).astype(jnp.float32)
    condition = (
        matdot(time_hidden, time_own)
        + second_bias_own
        + matdot(onehot.astype(jnp.bfloat16), class_table.astype(jnp.bfloat16))
    )
    cond_act = jax.nn.silu(condition).astype(jnp.bfloat16)
    plane_act = lax.dynamic_index_in_dim(
        cond_act.reshape(dp_parts, seq_parts, images, own_cols), seq_at, 1, keepdims=False
    ).reshape(dp_parts * images, own_cols)
    partial = matdot(plane_act, cond_own)
    mod_bias = jnp.repeat(all_biases[3 * D : bias_base].reshape(pieces, D), images, axis=0)

    position = position_table(jnp.arange(tok_rows, dtype=jnp.int32), D, GRID)
    flat_in = latents.astype(jnp.bfloat16).reshape(toks, PATCH_IN)
    stream = (dot_nt(flat_in, patch_part) + all_biases[:D]).reshape(
        images, tok_rows, D
    ) + position[None]
    stream = stream.reshape(toks, D)
    layer_bias = [
        all_biases[bias_base + at * 9 * D : bias_base + (at + 1) * 9 * D].reshape(1, 9 * D)
        for at in range(LAYERS)
    ]
    if by_kernel:
        partial = partial.astype(jnp.bfloat16).reshape(dp_parts * images, pieces, D)
        partial = jnp.pad(partial, ((0, 0), (0, 16 - pieces), (0, 0)))
        weights_kept, saved_kept, mods = whole_forward(
            shards,
            partial.reshape(lines, 2, 2, 16 * images, D),
            mod_bias,
            stream,
            layer_bias,
            keep_rows,
            lines,
        )
    else:
        partial = partial.reshape(dp_parts, images, pieces, D).transpose(0, 2, 1, 3)
        partial = partial.reshape(dp_parts, pieces * images, D)
        mods = mod_bias + lax.psum_scatter(
            partial, "dp", scatter_dimension=0, tiled=True
        ).reshape(pieces * images, D)
        weights_kept = [
            [gather_rows(shard) for shard in shards[4 * at : 4 * at + 4]] for at in range(LAYERS)
        ]
        saved_kept = []
        upper = stream
        for at in range(LAYERS):
            saved_kept.append(
                forward_layer(
                    upper, mods, 6 * images * at, layer_bias[at], keep_rows, weights_kept[at]
                )
            )
            upper = saved_kept[at][-1]
    inputs_kept = [stream] + [saved[-1] for saved in saved_kept]
    final, time_own = lax.optimization_barrier((inputs_kept[-1], time_own))
    time_full = lax.all_gather(time_own, "dp", axis=1, tiled=True)
    final_at = 6 * LAYERS * images
    final_shift = mods[final_at : final_at + images]
    final_scale = mods[final_at + images :]
    moved, final_back = jax.vjp(
        modulate, final.reshape(images, tok_rows, D), final_shift, final_scale
    )
    a_final = moved.astype(jnp.bfloat16).reshape(toks, D)
    head_out = matdot(a_final, head_full) + all_biases[NBIAS - OUT_CH :]
    split_out = head_out.reshape(images, tok_rows, 4, 2, OUT_CH // 8)
    predicted = split_out[:, :, :, 0, :].reshape(images, tok_rows, PATCH_IN)
    errors = predicted - noise_target
    loss_part = jnp.sum(keep_rows[:, :, None] * errors * errors)
    count_part = PATCH_IN * jnp.sum(keep_rows)
    d_pred = (2.0 * keep_rows[:, :, None] * errors).reshape(images, tok_rows, 4, 1, OUT_CH // 8)
    d_head = (
        jnp.concatenate([d_pred, jnp.zeros_like(d_pred)], axis=3)
        .reshape(toks, OUT_CH)
        .astype(jnp.bfloat16)
    )
    d_a_final = dot_nt(d_head, head_full).reshape(images, tok_rows, D)
    d_stream, d_final_shift, d_final_scale = final_back(d_a_final)
    d_stream = d_stream.reshape(toks, D)
    d_bias_head = column_sum(d_head)
    if by_kernel:
        d_noise = d_pred.astype(jnp.bfloat16).reshape(toks, PATCH_IN)
        misc_row = jnp.concatenate([d_bias_head, loss_part[None], count_part[None]])
        misc_row = jnp.pad(misc_row, (0, D - misc_row.shape[0])).reshape(1, D)
        units, flat, mod_all = whole_backward(
            d_stream,
            inputs_kept,
            saved_kept,
            weights_kept,
            mods,
            keep_rows,
            jnp.concatenate([d_final_shift, d_final_scale], axis=0),
            matdot(d_noise.T, a_final),
            misc_row,
            flat_in.T,
            lines,
        )
        d_modulation = (
            mod_all[..., : pieces * images, :]
            .reshape(dp_parts * seq_parts, pieces, images, D)
            .transpose(0, 2, 1, 3)
            .reshape(everyone, cond_cols)
        )
        flat = flat.reshape(64, D)
        d_bias_mod = column_sum(d_modulation)
        d_bias_patch = flat[18]
        d_bias_layers = flat[:18].reshape(-1)
        d_bias_head, loss_sum, loss_count = (
            flat[51, :OUT_CH],
            flat[51, OUT_CH],
            flat[51, OUT_CH + 1],
        )
        own_flat = lax.dynamic_slice(flat, (0, own_place), (64, own_cols))
        s_patch = own_flat[19:35]
        s_head = own_flat[35:51].T.reshape(own_cols, 4, 1, OUT_CH // 8)
        s_head = jnp.concatenate([s_head, jnp.zeros_like(s_head)], axis=2)
        s_head = s_head.reshape(own_cols, OUT_CH)
    else:
        layer_sums = [None] * LAYERS
        layer_bias_grads = [None] * LAYERS
        modul_grads = [None] * LAYERS
        for at in reversed(range(LAYERS)):
            d_stream, d_mod, factors, d_bias = backward_layer(
                d_stream,
                inputs_kept[at],
                saved_kept[at],
                mods,
                6 * images * at,
                keep_rows,
                weights_kept[at],
            )
            merged, a_one, a_two, active, d_attn, d_qkv, d_up, d_down = factors
            layer_sums[at] = (
                reduce_rows(matdot(a_one.T, d_qkv)),
                reduce_rows(matdot(merged.T, d_attn)),
                reduce_rows(matdot(a_two.T, d_up)),
                reduce_rows(matdot(active.T, d_down)),
            )
            modul_grads[at] = d_mod.reshape(6, images, D).transpose(1, 0, 2).reshape(images, 6 * D)
            layer_bias_grads[at] = d_bias.reshape(-1)
        d_mod_own = jnp.concatenate(
            modul_grads + [d_final_shift, d_final_scale], axis=1
        ).astype(jnp.bfloat16)
        d_patch = d_stream.astype(jnp.bfloat16)
        d_modulation = lax.all_gather(d_mod_own, ("dp", "seq"), axis=0, tiled=True)
        (
            d_bias_patch,
            d_bias_mod,
            d_bias_layers,
            d_bias_head,
            loss_sum,
            loss_count,
            g_patch,
            g_head,
        ) = lax.psum(
            (
                column_sum(d_patch),
                column_sum(d_mod_own),
                jnp.concatenate(layer_bias_grads),
                d_bias_head,
                loss_part,
                count_part,
                matdot(flat_in.T, d_patch),
                matdot(a_final.T, d_head),
            ),
            ("seq", "dp"),
        )
        s_patch = lax.dynamic_slice(g_patch, (0, own_place), (PATCH_IN, own_cols))
        s_head = lax.dynamic_slice(g_head, (own_place, 0), (own_cols, OUT_CH))
    d_cond_act = dot_nt(d_modulation, cond_own)
    _, silu_back = jax.vjp(jax.nn.silu, condition)
    d_condition = silu_back(d_cond_act)[0]
    d_time_own = d_condition.astype(jnp.bfloat16)
    if by_kernel:
        d_time = gather_small(
            jnp.pad(d_time_own.T, ((0, 0), (0, everyone))), lines, 5
        )
        d_time = d_time[:, :everyone].T
    else:
        d_time = lax.all_gather(d_time_own, "dp", axis=1, tiled=True)
    d_time_hidden = dot_nt(d_time, time_full)
    _, time_back = jax.vjp(jax.nn.silu, time_pre)
    d_time_pre = time_back(d_time_hidden)[0].astype(jnp.bfloat16)
    s_cond = matdot(cond_act.T, d_modulation)
    s_table = jnp.dot(onehot.T, d_condition, precision=lax.Precision.HIGHEST)
    g_time = matdot(time_hidden.T, d_time_own)
    g_freq = matdot(
        features.T, lax.dynamic_slice(d_time_pre, (0, own_place), (everyone, own_cols))
    )
    bias_grad = jnp.concatenate(
        [
            d_bias_patch,
            column_sum(d_time_pre),
            column_sum(d_time),
            d_bias_mod,
            d_bias_layers,
            d_bias_head,
        ]
    )
    s_embed = jnp.concatenate([s_patch, g_freq, g_time], axis=0)
    new_embed, new_first_embed, new_second_embed = adamw(
        embed_rows, s_embed, first_embed, second_embed, RATE_MATRIX
    )
    new_table, new_first_table, new_second_table = adamw(
        class_table, s_table, first_table, second_table, RATE_TABLE
    )
    if by_kernel:
        new_qkv, new_first_qkv, new_second_qkv = unit_adamw(
            qkv_weight, units, first_qkv, second_qkv, 9, False
        )
        new_proj, new_first_proj, new_second_proj = unit_adamw(
            proj_weight, units, first_proj, second_proj, 8, False
        )
        new_up, new_first_up, new_second_up = unit_adamw(
            up_weight, units, first_up, second_up, 4, False
        )
        new_down, new_first_down, new_second_down = unit_adamw(
            down_weight, units, first_down, second_down, 0, True
        )
    else:
        s_qkv = jnp.stack([layer_sums[at][0] for at in range(LAYERS)])
        s_proj = jnp.stack([layer_sums[at][1] for at in range(LAYERS)])
        s_up = jnp.stack([layer_sums[at][2] for at in range(LAYERS)])
        s_down = jnp.stack([layer_sums[at][3] for at in range(LAYERS)])
        new_qkv, new_first_qkv, new_second_qkv = adamw(
            qkv_weight, s_qkv, first_qkv, second_qkv, RATE_MATRIX
        )
        new_proj, new_first_proj, new_second_proj = adamw(
            proj_weight, s_proj, first_proj, second_proj, RATE_MATRIX
        )
        new_up, new_first_up, new_second_up = adamw(up_weight, s_up, first_up, second_up, RATE_MATRIX)
        new_down, new_first_down, new_second_down = adamw(
            down_weight, s_down, first_down, second_down, RATE_MATRIX
        )
    new_cond, new_first_cond, new_second_cond = adamw(
        cond_weight, s_cond, first_cond, second_cond, RATE_MATRIX
    )
    new_head, new_first_head, new_second_head = adamw(
        head_weight, s_head, first_head, second_head, RATE_MATRIX
    )
    new_bias, new_first_bias, new_second_bias = adamw(
        all_biases, bias_grad, first_bias, second_bias, RATE_BIAS
    )
    return (
        loss_sum,
        loss_count,
        new_embed,
        new_first_embed,
        new_second_embed,
        new_table,
        new_first_table,
        new_second_table,
        new_qkv,
        new_first_qkv,
        new_second_qkv,
        new_proj,
        new_first_proj,
        new_second_proj,
        new_up,
        new_first_up,
        new_second_up,
        new_down,
        new_first_down,
        new_second_down,
        new_cond,
        new_first_cond,
        new_second_cond,
        new_head,
        new_first_head,
        new_second_head,
        new_bias,
        new_first_bias,
        new_second_bias,
    )


def solution(mesh):
    placed = (
        P("dp", "seq", None),
        P("dp", "seq", None),
        P("dp", "seq"),
        P("dp"),
        P("dp"),
        P(None, "dp"),
        P(None, "dp"),
        P(None, "dp"),
        P(None, "dp"),
        P(None, "dp"),
        P(None, "dp"),
        P(None, "dp", None),
        P(None, "dp", None),
        P(None, "dp", None),
        P(None, "dp", None),
        P(None, "dp", None),
        P(None, "dp", None),
        P(None, "dp", None),
        P(None, "dp", None),
        P(None, "dp", None),
        P(None, "dp", None),
        P(None, "dp", None),
        P(None, "dp", None),
        P("dp", None),
        P("dp", None),
        P("dp", None),
        P("dp", None),
        P("dp", None),
        P("dp", None),
        P(),
        P(),
        P(),
    )
    return jax.shard_map(
        body,
        mesh=mesh,
        in_specs=placed,
        out_specs=(
            P(),
            P(),
            P(None, "dp"),
            P(None, "dp"),
            P(None, "dp"),
            P(None, "dp"),
            P(None, "dp"),
            P(None, "dp"),
            P(None, "dp", None),
            P(None, "dp", None),
            P(None, "dp", None),
            P(None, "dp", None),
            P(None, "dp", None),
            P(None, "dp", None),
            P(None, "dp", None),
            P(None, "dp", None),
            P(None, "dp", None),
            P(None, "dp", None),
            P(None, "dp", None),
            P(None, "dp", None),
            P("dp", None),
            P("dp", None),
            P("dp", None),
            P("dp", None),
            P("dp", None),
            P("dp", None),
            P(),
            P(),
            P(),
        ),
        check_vma=False,
    )
```

```python
import functools
import math

import jax
import jax.numpy as jnp
from jax import lax
from jax.experimental import pallas as pl
from jax.experimental.pallas import tpu as pltpu
from jax.sharding import PartitionSpec as P

D = 1024
HEADS = 16
HEAD_DIM = 64
FF = 4096
NCLASS = 1001
FREQ = 256
OUT_CH = 32
PATCH_IN = 16
GRID = 16
LAYERS = 2
STEP = 10
NBIAS = 35872


BETA_ONE = 0.9
BETA_TWO = 0.999
EPSILON = 1e-08
DECAY = 0.01
RATE_MATRIX = 0.06
RATE_TABLE = 0.4
RATE_BIAS = 0.2

MESH = pl.DeviceIdType.MESH
TILE = 256
PARTS = 4
SHARED = 640
SHARED_ROWS = 80
GATHER_LAGS = (2, 2, 2, 1)
HALF = 512
GELU_IN = math.sqrt(2.0 / math.pi)
GELU_CUBE = 0.044715
FORWARD_STEPS = 30
BACKWARD_STEPS = 27


def matdot(left, right):
    return jnp.dot(left, right, preferred_element_type=jnp.float32)


def layer_norm(stream):
    row_mean = jnp.mean(stream, axis=-1, keepdims=True)
    centered = stream - row_mean
    variance = jnp.mean(centered * centered, axis=-1, keepdims=True)
    return centered * lax.rsqrt(variance + 1e-06)


def modulate(stream, shift_by, scale_by):
    return layer_norm(stream) * (1.0 + scale_by[:, None, :]) + shift_by[:, None, :]


def position_table(position_ids, feature_width, grid_side):
    quarter_width = feature_width // 4
    omegas = 1.0 / 10000.0 ** (jnp.arange(quarter_width, dtype=jnp.float32) / quarter_width)
    col_angle = (position_ids % grid_side).astype(jnp.float32)[:, None] * omegas[None, :]
    row_angle = (position_ids // grid_side).astype(jnp.float32)[:, None] * omegas[None, :]
    return jnp.concatenate(
        [jnp.sin(col_angle), jnp.cos(col_angle), jnp.sin(row_angle), jnp.cos(row_angle)], axis=1
    )


def time_features(timesteps, feature_width):
    half_width = feature_width // 2
    frequencies = jnp.exp(
        -math.log(10000.0) * jnp.arange(half_width, dtype=jnp.float32) / half_width
    )
    angles = timesteps.astype(jnp.float32)[:, None] * frequencies[None, :]
    return jnp.concatenate([jnp.cos(angles), jnp.sin(angles)], axis=1)


def column_sum(grad_bf):
    return jnp.sum(grad_bf.astype(jnp.float32), axis=0)


def dot_nn(left, right):
    return jnp.dot(left, right, preferred_element_type=jnp.float32)


def dot_nt(left, right):
    return lax.dot_general(
        left, right, (((1,), (1,)), ((), ())), preferred_element_type=jnp.float32
    )


def dot_tn(left, right):
    return lax.dot_general(
        left, right, (((0,), (0,)), ((), ())), preferred_element_type=jnp.float32
    )


def wide_sum(one, other):
    return one.astype(jnp.float32) + other.astype(jnp.float32)


def column_tile(at, size=HALF):
    return pl.ds(pl.multiple_of(at * size, size), size)


def normalized(rows):
    centered = rows - jnp.mean(rows, axis=-1, keepdims=True)
    variance = jnp.mean(centered * centered, axis=-1, keepdims=True)
    inverse = lax.rsqrt(variance + 1e-06)
    return centered * inverse, inverse


def head_probs(queries, keys, keep):
    scores = jnp.where(keep > 0, dot_nt(queries, keys), -1000000000.0)
    raised = jnp.exp(scores - jnp.max(scores, axis=-1, keepdims=True))
    return raised * (1.0 / jnp.sum(raised, axis=-1, keepdims=True))


def within(at, first, size):
    return jnp.logical_and(at >= first, at < first + size)


def forward_pieces(refs, mod_at):
    (
        x_ref,
        mod_ref,
        bias_ref,
        keep_ref,
        w_qkv,
        w_proj,
        w_up,
        w_down,
        a_one_out,
        qkv_out,
        merged_out,
        attn_out,
        x_one_out,
        a_two_out,
        pre_out,
        act_out,
        down_out,
        x_two_out,
        a_buf,
        qkv_buf,
        merged_buf,
        attn_buf,
        x_one_buf,
        a_two_buf,
        pre_buf,
        act_buf,
        down_buf,
        x_two_buf,
        wide_buf,
        tall_buf,
        load_sem,
        tile_sem,
        save_sem,
    ) = refs
    images, toks = keep_ref.shape
    bf = jnp.bfloat16

    def save(at, source, target):
        return pltpu.make_async_copy(source, target, save_sem.at[at])

    saves = [
        save(at, *pair)
        for at, pair in enumerate(
            [
                (a_buf, a_one_out),
                (qkv_buf, qkv_out),
                (merged_buf, merged_out),
                (attn_buf, attn_out),
                (x_one_buf, x_one_out),
                (a_two_buf, a_two_out),
                (down_buf, down_out),
                (x_two_buf, x_two_out),
                (act_buf, act_out),
            ]
        )
    ]

    def wide_load(source, tile, slot):
        return pltpu.make_async_copy(
            source.at[:, :, :, :, column_tile(tile)], wide_buf.at[slot], load_sem.at[0, slot]
        )

    def tall_load(tile, slot):
        return pltpu.make_async_copy(
            w_down.at[:, :, :, :, column_tile(tile, TILE)], tall_buf.at[slot], load_sem.at[1, slot]
        )

    def tile_saves(tile, slot):
        return [
            pltpu.make_async_copy(
                pre_buf.at[slot], pre_out.at[:, column_tile(tile)], tile_sem.at[0, slot]
            ),
        ]

    def wide_tile(slot):
        return wide_buf[slot].reshape(D, HALF)

    def tall_tile(slot):
        return tall_buf[slot].reshape(FF, TILE)

    def loads(at, run):
        slot = lax.rem(at, 2)

        @pl.when(within(at, 1, 6))
        def _():
            run(wide_load(w_qkv, at - 1, slot))

        @pl.when(within(at, 15, 2))
        def _():
            run(wide_load(w_proj, at - 15, slot))

        @pl.when(within(at, 18, 8))
        def _():
            run(wide_load(w_up, at - 18, slot))

        @pl.when(within(at, 26, 4))
        def _():
            run(tall_load(at - 26, slot))

    def modulated(source, target, piece):
        def rows_of(block, carry):
            image = block // 4
            rows = pl.ds(pl.multiple_of(block * 64, 64), 64)
            shift = mod_ref[pl.ds(mod_at + 2 * piece + image, 1), :]
            scale = mod_ref[pl.ds(mod_at + 2 * piece + 2 + image, 1), :]
            unit, _ = normalized(source[rows, :])
            target[rows, :] = (unit * (1.0 + scale) + shift).astype(bf)
            return carry

        lax.fori_loop(0, images * toks // 64, rows_of, 0)

    def attend(image, pair):
        rows = pl.ds(pl.multiple_of(image * toks, toks), toks)
        low = lax.broadcasted_iota(jnp.int32, (toks, 128), 1) < 64
        queries = qkv_buf[rows, column_tile(pair, 128)] * jnp.asarray(0.125, bf)
        keys = qkv_buf[rows, column_tile(8 + pair, 128)]
        values = qkv_buf[rows, column_tile(16 + pair, 128)]
        keep = keep_ref[pl.ds(image, 1), :]
        zero = jnp.zeros_like(queries)
        total = jnp.zeros((toks, 128), jnp.float32)
        for own in (low, jnp.logical_not(low)):
            probs = head_probs(jnp.where(own, queries, zero), keys, keep)
            total = total + dot_nn(probs.astype(bf), jnp.where(own, values, zero))
        merged_buf[rows, column_tile(pair, 128)] = total.astype(bf)

    def step(at):
        slot = lax.rem(at, 2)
        loads(at + 1, lambda copy: copy.start())
        loads(at, lambda copy: copy.wait())

        @pl.when(at == 0)
        def _():
            modulated(x_ref, a_buf, 0)
            saves[0].start()

        @pl.when(within(at, 1, 6))
        def _():
            cols = column_tile(at - 1)
            for image in range(images):
                rows = pl.ds(image * toks, toks)
                qkv_buf[rows, cols] = (
                    dot_nn(a_buf[rows, :], wide_tile(slot)) + bias_ref[:, cols]
                ).astype(bf)

        @pl.when(at == 7)
        def _():
            saves[1].start()

        @pl.when(within(at, 7, 8))
        def _():
            for turn in range(2):
                item = (at - 7) * 2 + turn
                attend(item // 8, lax.rem(item, 8))

        @pl.when(within(at, 15, 2))
        def _():
            cols = column_tile(at - 15)
            for image in range(images):
                rows = pl.ds(image * toks, toks)
                attn = dot_nn(merged_buf[rows, :], wide_tile(slot)) + bias_ref[
                    :, column_tile(at - 15 + 6)
                ]
                attn_buf[rows, cols] = attn
                gate = mod_ref[mod_at + 4 + image : mod_at + 5 + image, cols]
                x_one_buf[rows, cols] = x_ref[rows, cols] + gate * attn

        @pl.when(at == 17)
        def _():
            for which in (2, 3, 4):
                saves[which].start()
            modulated(x_one_buf, a_two_buf, 3)
            saves[5].start()

        @pl.when(within(at, 18, 8))
        def _():
            tile = at - 18

            @pl.when(tile >= 2)
            def _():
                for copy in tile_saves(tile - 2, slot):
                    copy.wait()

            for image in range(images):
                rows = pl.ds(image * toks, toks)
                pre = dot_nn(a_two_buf[rows, :], wide_tile(slot)) + bias_ref[:, column_tile(tile + 8)]
                pre_buf[slot, rows, :] = pre
                inner = jnp.tanh(GELU_IN * (pre + GELU_CUBE * pre * pre * pre))
                active = (0.5 * pre * (1.0 + inner)).astype(bf)
                act_buf[rows, column_tile(tile)] = active

            for copy in tile_saves(tile, slot):
                copy.start()

        @pl.when(at == 26)
        def _():
            saves[8].start()

        @pl.when(within(at, 26, 4))
        def _():
            cols = column_tile(at - 26, TILE)
            bias_cols = column_tile(at - 26 + 32, TILE)
            for image in range(images):
                rows = pl.ds(image * toks, toks)
                down = dot_nn(act_buf[rows, :], tall_tile(slot)) + bias_ref[:, bias_cols]
                down_buf[rows, cols] = down
                gate = mod_ref[mod_at + 10 + image : mod_at + 11 + image, cols]
                x_two_buf[rows, cols] = x_one_buf[rows, cols] + gate * down

        @pl.when(at == FORWARD_STEPS - 1)
        def _():
            saves[6].start()
            saves[7].start()

    def finish():
        for tile in (6, 7):
            for copy in tile_saves(tile, tile % 2):
                copy.wait()
        for copy in saves:
            copy.wait()

    return step, finish


FORWARD_OUTS = [
    (D, jnp.bfloat16),
    (3 * D, jnp.bfloat16),
    (D, jnp.bfloat16),
    (D, jnp.float32),
    (D, jnp.float32),
    (D, jnp.bfloat16),
    (FF, jnp.float32),
    (FF, jnp.bfloat16),
    (D, jnp.float32),
    (D, jnp.float32),
]


def forward_scratch(toks):
    bf, f32 = jnp.bfloat16, jnp.float32
    return [
        pltpu.VMEM((toks, D), bf),
        pltpu.VMEM((toks, 3 * D), bf),
        pltpu.VMEM((toks, D), bf),
        pltpu.VMEM((toks, D), f32),
        pltpu.VMEM((toks, D), f32),
        pltpu.VMEM((toks, D), bf),
        pltpu.VMEM((2, toks, HALF), f32),
        pltpu.VMEM((toks, FF), bf),
        pltpu.VMEM((toks, D), f32),
        pltpu.VMEM((toks, D), f32),
        pltpu.VMEM((2, 4, 2, 2, 64, HALF), bf),
        pltpu.VMEM((2, 4, 2, 2, 256, TILE), bf),
        pltpu.SemaphoreType.DMA((2, 2)),
        pltpu.SemaphoreType.DMA((2, 2)),
        pltpu.SemaphoreType.DMA((9,)),
    ]


def forward_kernel(mod_at, *refs):
    step, finish = forward_pieces(refs, mod_at)

    def turn(at, carry):
        step(at)
        return carry

    lax.fori_loop(0, FORWARD_STEPS, turn, 0)
    finish()


def grouped(weights):
    return [each.reshape(4, 2, 2, -1, each.shape[-1]) for each in weights]


def forward_layer(x, mods, mod_at, biases, keep, weights):
    toks = x.shape[0]
    return pl.pallas_call(
        functools.partial(forward_kernel, mod_at),
        out_shape=[jax.ShapeDtypeStruct((toks, width), kind) for width, kind in FORWARD_OUTS],
        in_specs=[pl.BlockSpec(memory_space=pltpu.VMEM)] * 4
        + [pl.BlockSpec(memory_space=pl.ANY)] * 4,
        out_specs=[pl.BlockSpec(memory_space=pl.ANY)] * len(FORWARD_OUTS),
        scratch_shapes=forward_scratch(toks),
        compiler_params=pltpu.CompilerParams(vmem_limit_bytes=56 * 1024 * 1024),
        cost_estimate=pl.CostEstimate(
            flops=24 * toks * D * D, bytes_accessed=60 * 1024 * 1024, transcendentals=4 * toks * D
        ),
    )(x, mods, biases, keep, *grouped(weights))


def backward_pieces(ins, outs, scratch, mod_at):
    (
        x_hbm,
        x_one_hbm,
        attn_hbm,
        down_hbm,
        qkv_hbm,
        pre_hbm,
        w_qkv,
        w_proj,
        w_up,
        w_down,
        mod_ref,
        keep_ref,
    ) = ins
    d_down_out, d_up_out, d_attn_out, d_qkv_out = outs
    (
        d_mod_ref,
        d_bias_ref,
        grad_ref,
        side_ref,
        x_one_ref,
        attn_ref,
        qkv_ref,
        total_buf,
        d_x_one_buf,
        d_down_buf,
        d_up_buf,
        d_attn_buf,
        d_heads_buf,
        d_qkv_buf,
        pre_buf,
        wide_buf,
        tall_buf,
        load_sem,
        tile_sem,
        save_sem,
        in_sem,
    ) = scratch
    images, toks = keep_ref.shape
    bf = jnp.bfloat16
    blocks = toks // 64
    saves = [
        pltpu.make_async_copy(source, target, save_sem.at[at])
        for at, (source, target) in enumerate(
            [
                (d_down_buf, d_down_out),
                (d_attn_buf, d_attn_out),
                (d_qkv_buf, d_qkv_out),
            ]
        )
    ]

    in_down, in_x_one, in_attn, in_qkv, in_x = [
        pltpu.make_async_copy(source, target, in_sem.at[at])
        for at, (source, target) in enumerate(
            [
                (down_hbm, side_ref),
                (x_one_hbm, x_one_ref),
                (attn_hbm, attn_ref),
                (qkv_hbm, qkv_ref),
                (x_hbm, side_ref),
            ]
        )
    ]

    def begin():
        for copy in (in_down, in_x_one, in_attn, in_qkv):
            copy.start()

    def wide_load(source, tile, slot):
        return pltpu.make_async_copy(
            source.at[:, :, :, :, column_tile(tile)], wide_buf.at[slot], load_sem.at[0, slot]
        )

    def tall_load(tile, slot):
        return pltpu.make_async_copy(
            w_down.at[tile // 2, lax.rem(tile, 2)], tall_buf.at[slot], load_sem.at[1, slot]
        )

    def pre_load(tile, slot):
        return pltpu.make_async_copy(
            pre_hbm.at[:, column_tile(tile)], pre_buf.at[slot], load_sem.at[2, slot]
        )

    def up_save(tile, slot):
        return pltpu.make_async_copy(
            d_up_buf.at[slot], d_up_out.at[:, column_tile(tile)], tile_sem.at[slot]
        )

    def wide_tile(slot):
        return wide_buf[slot].reshape(D, HALF)

    def tall_tile(slot):
        return tall_buf[slot].reshape(HALF, D)

    def loads(at, run):
        slot = lax.rem(at, 2)

        @pl.when(within(at, 1, 8))
        def _():
            run(tall_load(at - 1, slot))
            run(wide_load(w_up, at - 1, slot))
            run(pre_load(at - 1, slot))

        @pl.when(within(at, 10, 2))
        def _():
            run(wide_load(w_proj, at - 10, slot))

        @pl.when(within(at, 20, 6))
        def _():
            run(wide_load(w_qkv, at - 20, slot))

    def column_sums(rows):
        return jnp.sum(rows.astype(jnp.float32), axis=0, keepdims=True)

    def gated(image, gate_row, gradient, branch, target, bias_cols):
        def rows_of(block, sums):
            rows = pl.ds(pl.multiple_of(image * toks + block * 64, 64), 64)
            upper = gradient[rows, :]
            gate = mod_ref[mod_at + gate_row + image : mod_at + gate_row + image + 1, :]
            lower = (upper * gate).astype(bf)
            target[rows, :] = lower
            return sums[0] + column_sums(upper * branch[rows, :]), sums[1] + column_sums(lower)

        zero = jnp.zeros((1, D), jnp.float32)
        gate, bias = lax.fori_loop(0, blocks, rows_of, (zero, zero))
        gate_at = mod_at + gate_row + image
        d_mod_ref[gate_at : gate_at + 1, :] = gate
        if image == 0:
            d_bias_ref[:, bias_cols] = bias
        else:
            d_bias_ref[:, bias_cols] += bias

    def modulate_back(image, first_row, source, passed, target):
        def rows_of(block, sums):
            rows = pl.ds(pl.multiple_of(image * toks + block * 64, 64), 64)
            scale_row = mod_at + first_row + 2 + image
            scale = mod_ref[scale_row : scale_row + 1, :]
            unit, inverse = normalized(source[rows, :])
            upper = total_buf[rows, :]
            inner = upper * (1.0 + scale)
            back = inverse * (
                inner
                - jnp.mean(inner, axis=-1, keepdims=True)
                - unit * jnp.mean(inner * unit, axis=-1, keepdims=True)
            )
            target[rows, :] = back + passed[rows, :]
            return sums[0] + column_sums(upper), sums[1] + column_sums(upper * unit)

        zero = jnp.zeros((1, D), jnp.float32)
        shift, scale = lax.fori_loop(0, blocks, rows_of, (zero, zero))
        shift_at = mod_at + first_row + image
        d_mod_ref[shift_at : shift_at + 1, :] = shift
        d_mod_ref[shift_at + 2 : shift_at + 3, :] = scale

    def attend_back(image, pair):
        rows = pl.ds(pl.multiple_of(image * toks, toks), toks)
        low = lax.broadcasted_iota(jnp.int32, (toks, 128), 1) < 64
        eighth = jnp.asarray(0.125, bf)
        queries = qkv_ref[rows, column_tile(pair, 128)] * eighth
        keys = qkv_ref[rows, column_tile(8 + pair, 128)]
        values = qkv_ref[rows, column_tile(16 + pair, 128)]
        upper = d_heads_buf[rows, column_tile(pair, 128)]
        keep = keep_ref[pl.ds(image, 1), :]
        zero = jnp.zeros_like(queries)
        total = jnp.zeros((toks, 128), jnp.float32)
        d_q, d_k, d_v = total, total, total
        for own in (low, jnp.logical_not(low)):
            own_q = jnp.where(own, queries, zero)
            own_up = jnp.where(own, upper, zero)
            probs = head_probs(own_q, keys, keep)
            d_probs = dot_nt(own_up, values)
            mean = jnp.sum(probs * d_probs, axis=-1, keepdims=True)
            d_scores = (probs * (d_probs - mean)).astype(bf)
            d_v = d_v + dot_tn(probs.astype(bf), own_up)
            d_q = d_q + dot_nn(d_scores, jnp.where(own, keys * eighth, zero))
            d_k = d_k + dot_tn(d_scores, own_q)
        d_qkv_buf[rows, column_tile(pair, 128)] = d_q.astype(bf)
        d_qkv_buf[rows, column_tile(8 + pair, 128)] = d_k.astype(bf)
        d_qkv_buf[rows, column_tile(16 + pair, 128)] = d_v.astype(bf)

    def add_product(first, image_rows, part):
        @pl.when(first)
        def _():
            total_buf[image_rows, :] = part

        @pl.when(jnp.logical_not(first))
        def _():
            total_buf[image_rows, :] += part

    def step(at):
        slot = lax.rem(at, 2)
        loads(at + 1, lambda copy: copy.start())
        loads(at, lambda copy: copy.wait())

        @pl.when(at == 0)
        def _():
            in_down.wait()
            for image in range(images):
                gated(image, 10, grad_ref, side_ref, d_down_buf, slice(8 * D, 9 * D))
            saves[0].start()

        @pl.when(within(at, 1, 8))
        def _():
            tile = at - 1
            bias = jnp.zeros((1, HALF), jnp.float32)
            for image in range(images):
                rows = pl.ds(image * toks, toks)
                upper = dot_nt(d_down_buf[rows, :], tall_tile(slot))
                pre = pre_buf[slot, rows, :]
                square = pre * pre
                inner = jnp.tanh(GELU_IN * (pre + GELU_CUBE * square * pre))
                slope = 0.5 * (1.0 + inner) + 0.5 * pre * (1.0 - inner * inner) * (
                    GELU_IN * (1.0 + 3.0 * GELU_CUBE * square)
                )
                lower = (upper * slope).astype(bf)
                d_up_buf[slot, rows, :] = lower
                bias = bias + column_sums(lower)
                add_product(tile == 0, rows, dot_nt(lower, wide_tile(slot)))
            d_bias_ref[:, column_tile(tile + 8)] = bias
            up_save(tile, slot).start()

            @pl.when(tile == 0)
            def _():
                saves[0].wait()

            @pl.when(tile >= 1)
            def _():
                up_save(tile - 1, 1 - slot).wait()

        @pl.when(at == 9)
        def _():
            up_save(7, 0).wait()
            in_x_one.wait()
            in_attn.wait()
            for image in range(images):
                modulate_back(image, 6, x_one_ref, grad_ref, d_x_one_buf)
                gated(image, 4, d_x_one_buf, attn_ref, d_attn_buf, slice(3 * D, 4 * D))
            saves[1].start()

        @pl.when(within(at, 10, 2))
        def _():
            for image in range(images):
                rows = pl.ds(image * toks, toks)
                part = dot_nt(d_attn_buf[rows, column_tile(at - 10)], wide_tile(slot))
                add_product(at == 10, rows, part)

            @pl.when(at == 10)
            def _():
                in_x.start()
                saves[1].wait()

            @pl.when(at == 11)
            def _():
                in_qkv.wait()
                d_heads_buf[...] = total_buf[...].astype(bf)

        @pl.when(within(at, 12, 8))
        def _():
            for turn in range(2):
                item = (at - 12) * 2 + turn
                attend_back(item // 8, lax.rem(item, 8))

        @pl.when(at == 20)
        def _():
            saves[2].start()

        @pl.when(within(at, 20, 6))
        def _():
            cols = column_tile(at - 20)
            bias = jnp.zeros((1, HALF), jnp.float32)
            for image in range(images):
                rows = pl.ds(image * toks, toks)
                lower = d_qkv_buf[rows, cols]
                bias = bias + column_sums(lower)
                add_product(at == 20, rows, dot_nt(lower, wide_tile(slot)))
            d_bias_ref[:, cols] = bias

            @pl.when(at == 21)
            def _():
                saves[2].wait()

        @pl.when(at == BACKWARD_STEPS - 1)
        def _():
            in_x.wait()
            for image in range(images):
                modulate_back(image, 0, side_ref, d_x_one_buf, grad_ref)

    return begin, step


BACKWARD_OUTS = [(D, jnp.bfloat16), (FF, jnp.bfloat16), (D, jnp.bfloat16), (3 * D, jnp.bfloat16)]


def backward_scratch(toks):
    bf, f32 = jnp.bfloat16, jnp.float32
    return [
        pltpu.VMEM((toks, D), f32),
        pltpu.VMEM((toks, D), f32),
        pltpu.VMEM((toks, D), f32),
        pltpu.VMEM((toks, D), f32),
        pltpu.VMEM((toks, 3 * D), bf),
        pltpu.VMEM((toks, D), f32),
        pltpu.VMEM((toks, D), f32),
        pltpu.VMEM((toks, D), bf),
        pltpu.VMEM((2, toks, HALF), bf),
        pltpu.VMEM((toks, D), bf),
        pltpu.VMEM((toks, D), bf),
        pltpu.VMEM((toks, 3 * D), bf),
        pltpu.VMEM((2, toks, HALF), f32),
        pltpu.VMEM((2, 4, 2, 2, 64, HALF), bf),
        pltpu.VMEM((2, 2, 256, D), bf),
        pltpu.SemaphoreType.DMA((3, 2)),
        pltpu.SemaphoreType.DMA((2,)),
        pltpu.SemaphoreType.DMA((3,)),
        pltpu.SemaphoreType.DMA((5,)),
    ]


def backward_kernel(mod_at, *refs):
    grad_in, ins, outs = refs[0], refs[1:13], refs[13:17]
    d_x_out, d_mod_ref, d_bias_ref = refs[17:20]
    scratch, sem = refs[20:-1], refs[-1]
    begin, step = backward_pieces(ins, outs, (d_mod_ref, d_bias_ref) + scratch, mod_at)
    begin()
    copy = pltpu.make_async_copy(grad_in, scratch[0], sem.at[0])
    copy.start()
    copy.wait()

    def turn(at, carry):
        step(at)
        return carry

    lax.fori_loop(0, BACKWARD_STEPS, turn, 0)
    copy = pltpu.make_async_copy(scratch[0], d_x_out, sem.at[1])
    copy.start()
    copy.wait()


def backward_operands(x, saved, weights):
    _, qkv, _, attn, x_one, _, pre, _, down, _ = saved
    return (x, x_one, attn, down, qkv, pre, *weights)


def backward_layer(grad, x, saved, mods, mod_at, keep, weights):
    a_one, _, merged, _, _, a_two, _, act, _, _ = saved
    toks = x.shape[0]
    vmem = pl.BlockSpec(memory_space=pltpu.VMEM)
    hbm = pl.BlockSpec(memory_space=pl.ANY)
    outs = pl.pallas_call(
        functools.partial(backward_kernel, mod_at),
        out_shape=[jax.ShapeDtypeStruct((toks, width), kind) for width, kind in BACKWARD_OUTS]
        + [
            jax.ShapeDtypeStruct((toks, D), jnp.float32),
            jax.ShapeDtypeStruct((mod_at + 12, D), jnp.float32),
            jax.ShapeDtypeStruct((1, 9 * D), jnp.float32),
        ],
        in_specs=[hbm] * 11 + [vmem] * 2,
        out_specs=[hbm] * 5 + [vmem] * 2,
        scratch_shapes=backward_scratch(toks) + [pltpu.SemaphoreType.DMA((2,))],
        compiler_params=pltpu.CompilerParams(vmem_limit_bytes=56 * 1024 * 1024),
        cost_estimate=pl.CostEstimate(
            flops=28 * toks * D * D, bytes_accessed=80 * 1024 * 1024, transcendentals=4 * toks * D
        ),
    )(grad, *backward_operands(x, saved, grouped(weights)), mods, keep)
    d_down, d_up, d_attn, d_qkv, d_x, d_mod, d_bias = outs
    factors = (merged, a_one, a_two, act, d_attn, d_qkv, d_up, d_down)
    return d_x, d_mod[mod_at:], factors, d_bias


def gather_pieces(lines, refs):
    layers = (len(refs) - 7) // 8
    pairs = list(zip(refs[: 4 * layers], refs[4 * layers : 8 * layers]))
    own_sem, zp_sem, zq_sem, yp_sem, yq_sem, x_sem, core_sem = refs[8 * layers :]
    firsts = [12 * layer + first for layer in range(layers) for first in (0, 3, 4, 8)]
    total = 12 * layers
    seq = lax.axis_index("seq")
    dp = lax.axis_index("dp")
    core = lax.rem(dp, 2)
    why = lax.rem(dp // 2, 2)
    zed = dp // 4
    core_peer = {"seq": seq, "dp": dp + 1 - 2 * core}
    x_peer = {"seq": 1 - seq, "dp": dp}
    y_peer = {"seq": seq, "dp": dp + 2 - 4 * why}
    z_peers = [
        {"seq": seq, "dp": lax.rem(zed + step, lines) * 4 + 2 * why + core}
        for step in range(1, lines)
    ]
    keeps = [
        pltpu.make_async_copy(own, every.at[zed, why, core], own_sem.at[at])
        for at, (own, every) in enumerate(pairs)
    ]
    for keep in keeps:
        keep.start()
    for keep in keeps:
        keep.wait()
    barrier = pltpu.get_barrier_semaphore()
    for peer in [core_peer, x_peer, y_peer] + z_peers:
        pl.semaphore_signal(barrier, inc=1, device_id=peer, device_id_type=MESH)
    pl.semaphore_wait(barrier, 2 + lines)

    def views(kind, unit):
        at = unit - firsts[kind]
        if kind % 4 == 3:
            cols = column_tile(at, TILE)
            mine = pl.ds(pl.multiple_of(seq * SHARED_ROWS, 16), SHARED_ROWS)
            rest = pl.ds(2 * SHARED_ROWS, PARTS * 64 - 2 * SHARED_ROWS)
            return (mine, cols), (rest, cols), (slice(None), cols)
        first = pl.multiple_of(at * D, D)
        halved = pl.ds(first, SHARED)
        rest = pl.ds(pl.multiple_of(first + SHARED, 128), D - SHARED)
        mine = pl.ds(pl.multiple_of(seq * 32, 32), 32)
        return (mine, halved), (slice(None), rest), (slice(None), pl.ds(first, D))

    def copies(stage, kind, unit):
        slot = unit
        own, every = pairs[kind]
        shared, rest, whole = views(kind, unit)

        def remote(source, target, sems, peer):
            return pltpu.make_async_remote_copy(
                src_ref=source,
                dst_ref=target,
                send_sem=sems.at[0],
                recv_sem=sems.at[1],
                device_id=peer,
                device_id_type=MESH,
            )

        def same(view, sems, peer):
            return remote(view, view, sems, peer)

        if stage == 0:
            return [
                remote(own.at[view], every.at[(zed, why, core) + view], sems, peer)
                for view, kinds in ((shared, zp_sem), (rest, zq_sem))
                for sems, peer in [(kinds.at[slot, at], z_peers[at]) for at in range(lines - 1)]
            ]
        if stage == 1:
            return [
                same(every.at[(slice(None), why, core) + shared], yp_sem.at[slot], y_peer),
                same(every.at[(slice(None), why, core) + rest], yq_sem.at[slot], y_peer),
            ]
        if stage == 2:
            return [same(every.at[(slice(None), slice(None), core) + shared], x_sem.at[slot], x_peer)]
        return [same(every.at[(slice(None), slice(None), core) + whole], core_sem.at[slot], core_peer)]

    def each_kind(unit, run):
        ends = firsts[1:] + [total]
        for kind in range(len(firsts)):

            @pl.when(jnp.logical_and(unit >= firsts[kind], unit < ends[kind]))
            def _():
                run(kind)

    def begin(stage, unit):
        def run(kind):
            for copy in copies(stage, kind, unit):
                copy.start()

        each_kind(unit, run)

    def finish(stage, unit):
        def run(kind):
            for copy in copies(stage, kind, unit):
                copy.wait()

        each_kind(unit, run)

    def step(at):
        finish(3, at - sum(GATHER_LAGS))
        for stage in (3, 2, 1):
            behind = sum(GATHER_LAGS[:stage])
            finish(stage - 1, at - behind)
            begin(stage, at - behind)
        begin(0, at)

    return step, total + sum(GATHER_LAGS)


def gather_scratch(lines, layers):
    dma = pltpu.SemaphoreType.DMA
    units = 12 * layers
    return [
        dma((4 * layers,)),
        dma((units, lines - 1, 2)),
        dma((units, lines - 1, 2)),
        dma((units, 2)),
        dma((units, 2)),
        dma((units, 2)),
        dma((units, 2)),
    ]


def modulation_pieces(lines, refs):
    (
        partial_ref,
        bias_ref,
        mods_ref,
        core_in,
        core_total,
        y_in,
        y_total,
        z_in,
        core_sem,
        y_sem,
        z_sem,
    ) = refs
    seq = lax.axis_index("seq")
    dp = lax.axis_index("dp")
    core = lax.rem(dp, 2)
    why = lax.rem(dp // 2, 2)
    zed = dp // 4

    def remote(source, target, sems, peer):
        return pltpu.make_async_remote_copy(
            src_ref=source,
            dst_ref=target,
            send_sem=sems.at[0],
            recv_sem=sems.at[1],
            device_id={"seq": seq, "dp": peer},
            device_id_type=MESH,
        )

    to_core = remote(partial_ref.at[:, :, 1 - core], core_in, core_sem, dp + 1 - 2 * core)
    to_y = remote(core_total.at[:, 1 - why], y_in, y_sem, dp + 2 - 4 * why)
    to_z = []
    for ahead in range(1, lines):
        there = lax.rem(zed + ahead, lines)
        to_z.append(
            remote(
                y_total.at[there],
                z_in.at[ahead - 1],
                z_sem.at[ahead - 1],
                there * 4 + 2 * why + core,
            )
        )

    def step(at):
        @pl.when(at == 0)
        def _():
            to_core.start()

        @pl.when(at == 1)
        def _():
            to_core.wait()
            core_total[...] = wide_sum(partial_ref[:, :, core], core_in[...]).astype(jnp.bfloat16)
            to_y.start()

        @pl.when(at == 4)
        def _():
            to_y.wait()
            y_total[...] = wide_sum(core_total[:, why], y_in[...]).astype(jnp.bfloat16)
            for copy in to_z:
                copy.start()

        @pl.when(at == 8)
        def _():
            total = y_total[zed].astype(jnp.float32)
            for ahead, copy in enumerate(to_z):
                copy.wait()
                total = total + z_in[ahead].astype(jnp.float32)
            for image in range(2):
                for piece in range(mods_ref.shape[0] // 2):
                    row, source = 2 * piece + image, 16 * image + piece
                    mods_ref[row : row + 1, :] = (
                        total[source : source + 1, :] + bias_ref[row : row + 1, :]
                    )

    return step


def modulation_scratch(lines):
    dma = pltpu.SemaphoreType.DMA
    bf = jnp.bfloat16
    return [
        pltpu.VMEM((lines, 2, 32, D), bf),
        pltpu.VMEM((lines, 2, 32, D), bf),
        pltpu.VMEM((lines, 32, D), bf),
        pltpu.VMEM((lines, 32, D), bf),
        pltpu.VMEM((lines - 1, 32, D), bf),
        dma((2,)),
        dma((2,)),
        dma((lines - 1, 2)),
    ]


def whole_forward_kernel(lines, *refs):
    refs = list(refs)

    def take(count):
        taken, refs[:] = tuple(refs[:count]), refs[count:]
        return taken

    own = take(8)
    partial_ref, mod_bias, x_ref, first_bias, second_bias, keep = take(6)
    every = take(8)
    first_outs, second_outs = take(len(FORWARD_OUTS)), take(len(FORWARD_OUTS))
    (mods,) = take(1)
    gather_sems = take(7)
    mod_scratch = take(8)
    scratch = tuple(refs)
    gather, steps = gather_pieces(lines, own + every + gather_sems)
    modulate_step = modulation_pieces(lines, (partial_ref, mod_bias, mods) + mod_scratch)
    first, first_finish = forward_pieces(
        (x_ref, mods, first_bias, keep) + every[:4] + first_outs + scratch, 0
    )
    second, second_finish = forward_pieces(
        (scratch[9], mods, second_bias, keep) + every[4:] + second_outs + scratch, 12
    )

    def run(step, begin, end):
        def one(at, carry):
            step(at)
            return carry

        lax.fori_loop(begin, end, one, 0)

    def turn(at, carry):
        gather(at)
        modulate_step(at)

        @pl.when(within(at, 10, 13))
        def _():
            run(first, 5 * (at - 10) // 2, 5 * (at - 9) // 2)

        @pl.when(at == 23)
        def _():
            first_finish()

        @pl.when(at >= 23)
        def _():
            run(second, 13 * (at - 23) // 4, 13 * (at - 22) // 4)

        return carry

    lax.fori_loop(0, steps + 2, turn, 0)
    second_finish()


def whole_forward(own, partial, mod_bias, x, biases, keep, lines):
    toks = x.shape[0]
    rows = mod_bias.shape[0]
    vmem = pl.BlockSpec(memory_space=pltpu.VMEM)
    hbm = pl.BlockSpec(memory_space=pl.ANY)
    layer_outs = [jax.ShapeDtypeStruct((toks, width), kind) for width, kind in FORWARD_OUTS]
    outs = pl.pallas_call(
        functools.partial(whole_forward_kernel, lines),
        out_shape=[
            jax.ShapeDtypeStruct((lines, 2, 2) + each.shape, jnp.bfloat16) for each in own
        ]
        + layer_outs
        + layer_outs
        + [jax.ShapeDtypeStruct((rows, D), jnp.float32)],
        in_specs=[vmem] * 14,
        out_specs=[hbm] * (8 + 2 * len(FORWARD_OUTS)) + [vmem],
        scratch_shapes=gather_scratch(lines, 2)
        + modulation_scratch(lines)
        + forward_scratch(toks),
        compiler_params=pltpu.CompilerParams(
            collective_id=2, has_side_effects=True, vmem_limit_bytes=58 * 1024 * 1024
        ),
        cost_estimate=pl.CostEstimate(
            flops=48 * toks * D * D,
            bytes_accessed=24 * 4 * lines * 64 * D * 8,
            transcendentals=8 * toks * D,
        ),
    )(*own, partial, mod_bias, x, *biases, keep)
    weights = outs[:8]
    count = len(FORWARD_OUTS)
    saved = [outs[8 : 8 + count], outs[8 + count : 8 + 2 * count]]
    return [weights[:4], weights[4:]], saved, outs[-1]


def gather_small_kernel(lines, own_ref, every_ref, z_sem, y_sem, core_sem):
    seq = lax.axis_index("seq")
    dp = lax.axis_index("dp")
    core = lax.rem(dp, 2)
    why = lax.rem(dp // 2, 2)
    zed = dp // 4
    core_peer = {"seq": seq, "dp": dp + 1 - 2 * core}
    y_peer = {"seq": seq, "dp": dp + 2 - 4 * why}
    z_peers = [
        {"seq": seq, "dp": lax.rem(zed + step, lines) * 4 + 2 * why + core}
        for step in range(1, lines)
    ]
    barrier = pltpu.get_barrier_semaphore()
    for peer in [core_peer, y_peer] + z_peers:
        pl.semaphore_signal(barrier, inc=1, device_id=peer, device_id_type=MESH)
    every_ref[zed, why, core] = own_ref[...]
    pl.semaphore_wait(barrier, 1 + lines)

    def remote(source, target, sems, peer):
        return pltpu.make_async_remote_copy(
            src_ref=source,
            dst_ref=target,
            send_sem=sems.at[0],
            recv_sem=sems.at[1],
            device_id=peer,
            device_id_type=MESH,
        )

    copies = [
        remote(own_ref, every_ref.at[zed, why, core], z_sem.at[at], peer)
        for at, peer in enumerate(z_peers)
    ]
    for copy in copies:
        copy.start()
    for copy in copies:
        copy.wait()
    for view, sems, peer in (
        (every_ref.at[:, why, core], y_sem, y_peer),
        (every_ref.at[:, :, core], core_sem, core_peer),
    ):
        copy = remote(view, view, sems, peer)
        copy.start()
        copy.wait()


def gather_small(own, lines, collective_id):
    dma = pltpu.SemaphoreType.DMA
    every = pl.pallas_call(
        functools.partial(gather_small_kernel, lines),
        out_shape=jax.ShapeDtypeStruct((lines, 2, 2) + own.shape, own.dtype),
        in_specs=[pl.BlockSpec(memory_space=pltpu.VMEM)],
        out_specs=pl.BlockSpec(memory_space=pltpu.VMEM),
        scratch_shapes=[dma((lines - 1, 2)), dma((2,)), dma((2,))],
        compiler_params=pltpu.CompilerParams(collective_id=collective_id, has_side_effects=True),
        cost_estimate=pl.CostEstimate(
            flops=0, bytes_accessed=own.size * 32 * lines, transcendentals=0
        ),
    )(own)
    return every.reshape(-1, own.shape[-1])


def scatter_pieces(lines, sources, scratch):
    per_layer = 12
    total = len(sources) * per_layer
    (
    out_ref,
    lhs_buf,
    act_buf,
    wide_buf,
    down_buf,
    load_sem,
    made,
    core_in,
    x_out,
    x_in,
    p_keep,
    yq_out,
    yq_in,
    q_keep,
    yp_out,
    yp_in,
    p_line,
    zq_out,
    zq_in,
    zp_out,
    zp_in,
    xq_out,
    xq_in,
    xp_out,
    xp_in,
    core_sem,
    x_sem,
    yq_sem,
    yp_sem,
    zq_sem,
    zp_sem,
    xq_sem,
    xp_sem,
    out_buf,
    out_sem,
    ) = scratch
    seq = lax.axis_index("seq")
    dp = lax.axis_index("dp")
    core = lax.rem(dp, 2)
    why = lax.rem(dp // 2, 2)
    zed = dp // 4
    core_peer = {"seq": seq, "dp": dp + 1 - 2 * core}
    x_peer = {"seq": 1 - seq, "dp": dp}
    y_peer = {"seq": seq, "dp": dp + 2 - 4 * why}

    def z_place(step):
        return lax.rem(zed + step, lines)

    def z_peer(step):
        return {"seq": seq, "dp": z_place(step) * 4 + 2 * why + core}

    def remote(source, target, sems, peer):
        return pltpu.make_async_remote_copy(
            src_ref=source,
            dst_ref=target,
            send_sem=sems.at[0],
            recv_sem=sems.at[1],
            device_id=peer,
            device_id_type=MESH,
        )

    def core_copy(slot):
        return remote(made.at[slot, 1 - core], core_in.at[slot], core_sem.at[slot], core_peer)

    def x_copy(slot):
        return remote(x_out.at[slot], x_in.at[slot], x_sem.at[slot], x_peer)

    def yq_copy(slot):
        return remote(yq_out.at[slot], yq_in.at[slot], yq_sem.at[slot], y_peer)

    def yp_copy(slot):
        return remote(yp_out.at[slot], yp_in.at[slot], yp_sem.at[slot], y_peer)

    def zq_copy(slot, step):
        return remote(
            zq_out.at[slot, z_place(step)],
            zq_in.at[slot, step - 1],
            zq_sem.at[slot, step - 1],
            z_peer(step),
        )

    def zp_copy(slot, step):
        return remote(
            zp_out.at[slot, z_place(step)],
            zp_in.at[slot, step - 1],
            zp_sem.at[slot, step - 1],
            z_peer(step),
        )

    def xq_copy(slot):
        return remote(xq_out.at[slot], xq_in.at[slot], xq_sem.at[slot], x_peer)

    def xp_copy(slot):
        return remote(xp_out.at[slot], xp_in.at[slot], xp_sem.at[slot], x_peer)

    def loads(unit, slot):
        found = []
        for layer in range(len(sources)):
            merged, a_one, a_two, act, d_attn, d_qkv, d_up, d_down = sources[layer]
            at = unit - layer * per_layer

            def slab(ref, index, size):
                return ref.at[:, pl.ds(pl.multiple_of(index * size, size), size)]

            wide_to = wide_buf.at[slot], load_sem.at[1, slot]
            lhs_to = lhs_buf.at[slot], load_sem.at[0, slot]
            found += [
                (
                    jnp.logical_and(at >= 0, at < 4),
                    (slab(d_down, at, TILE), down_buf.at[slot], load_sem.at[2, slot]),
                ),
                (at == 0, (act, act_buf, load_sem.at[3, 0])),
                (
                    jnp.logical_and(at >= 4, at < 8),
                    (a_two, *lhs_to),
                    (slab(d_up, at - 4, D), *wide_to),
                ),
                (at == 8, (merged, *lhs_to), (d_attn, *wide_to)),
                (
                    jnp.logical_and(at >= 9, at < per_layer),
                    (a_one, *lhs_to),
                    (slab(d_qkv, at - 9, D), *wide_to),
                ),
            ]
        return found

    def prefetch(unit):
        for due, *moves in loads(unit, lax.rem(unit, 2)):

            @pl.when(due)
            def _():
                for move in moves:
                    pltpu.make_async_copy(*move).start()

    def fetched(unit):
        for due, *moves in loads(unit, lax.rem(unit, 2)):

            @pl.when(due)
            def _():
                for move in moves:
                    pltpu.make_async_copy(*move).wait()

    def dot_rows(left, right):
        return lax.dot_general(
            left, right, (((0,), (0,)), ((), ())), preferred_element_type=jnp.float32
        )

    def compute(unit):
        at = lax.rem(unit, per_layer)
        slot = lax.rem(unit, 2)
        fetched(unit)

        @pl.when(at >= 4)
        def _():
            def rows(pair, carry):
                left = lhs_buf[slot, :, pl.ds(pl.multiple_of(pair * 128, 128), 128)]
                block = dot_rows(left, wide_buf[slot]).astype(jnp.bfloat16)
                for own in range(2):
                    for part in range(PARTS):
                        made[slot, own, part, pair // 2, lax.rem(pair, 2)] = block[
                            own * 64 : own * 64 + 64, part * TILE : part * TILE + TILE
                        ]
                return carry

            lax.fori_loop(0, 2 * lines, rows, 0)

        @pl.when(at < 4)
        def _():
            def rows(pair, carry):
                left = act_buf[:, pl.ds(pl.multiple_of(pair * 512, 512), 512)]
                block = dot_rows(left, down_buf[slot]).astype(jnp.bfloat16)
                for own in range(2):
                    for part in range(PARTS):
                        first = own * 256 + part * 64
                        made[slot, own, part, pair // 2, lax.rem(pair, 2)] = block[
                            first : first + 64
                        ]
                return carry

            lax.fori_loop(0, 2 * lines, rows, 0)

    def out_copy(unit, slot):
        return pltpu.make_async_copy(out_buf.at[slot], out_ref.at[unit], out_sem.at[slot])

    def stage_two(slot):
        core_copy(slot).wait()

        def rows(line, carry):
            for side in range(2):
                x_out[slot, line, side] = wide_sum(
                    made[slot, core, 1 - seq, line, side], core_in[slot, 1 - seq, line, side]
                ).astype(jnp.bfloat16)
                p_keep[slot, line, side] = wide_sum(
                    made[slot, core, seq, line, side], core_in[slot, seq, line, side]
                ).astype(jnp.bfloat16)
            for part in range(2):
                yq_out[slot, line, part] = wide_sum(
                    made[slot, core, 2 + part, line, 1 - why],
                    core_in[slot, 2 + part, line, 1 - why],
                ).astype(jnp.bfloat16)
                q_keep[slot, line, part] = wide_sum(
                    made[slot, core, 2 + part, line, why], core_in[slot, 2 + part, line, why]
                ).astype(jnp.bfloat16)
            return carry

        lax.fori_loop(0, lines, rows, 0)
        x_copy(slot).start()
        yq_copy(slot).start()

    def stage_three(slot):
        x_copy(slot).wait()
        yq_copy(slot).wait()

        def rows(line, carry):
            yp_out[slot, line] = wide_sum(
                p_keep[slot, line, 1 - why], x_in[slot, line, 1 - why]
            ).astype(jnp.bfloat16)
            p_line[slot, line] = wide_sum(p_keep[slot, line, why], x_in[slot, line, why]).astype(
                jnp.bfloat16
            )
            for part in range(2):
                zq_out[slot, line, part] = wide_sum(
                    q_keep[slot, line, part], yq_in[slot, line, part]
                ).astype(jnp.bfloat16)
            return carry

        lax.fori_loop(0, lines, rows, 0)
        yp_copy(slot).start()
        for step in range(1, lines):
            zq_copy(slot, step).start()

    def stage_four(slot):
        yp_copy(slot).wait()
        for step in range(1, lines):
            zq_copy(slot, step).wait()

        def rows(line, carry):
            zp_out[slot, line] = wide_sum(p_line[slot, line], yp_in[slot, line]).astype(
                jnp.bfloat16
            )
            return carry

        lax.fori_loop(0, lines, rows, 0)
        total_q = zq_out[slot, zed].astype(jnp.float32)
        for step in range(1, lines):
            total_q = total_q + zq_in[slot, step - 1].astype(jnp.float32)
        xq_out[slot] = total_q.astype(jnp.bfloat16)
        for step in range(1, lines):
            zp_copy(slot, step).start()
        xq_copy(slot).start()

    def stage_five(unit, slot):
        for step in range(1, lines):
            zp_copy(slot, step).wait()
        xq_copy(slot).wait()
        total_p = zp_out[slot, zed].astype(jnp.float32)
        for step in range(1, lines):
            total_p = total_p + zp_in[slot, step - 1].astype(jnp.float32)
        rounded = total_p.astype(jnp.bfloat16)
        xp_out[slot] = rounded
        xp_copy(slot).start()
        @pl.when(unit >= 2)
        def _():
            out_copy(unit - 2, slot).wait()

        out_buf[slot, seq] = rounded.astype(jnp.float32)
        for part in range(2):
            out_buf[slot, 2 + part] = wide_sum(xq_out[slot, part], xq_in[slot, part])

    def stage_six(unit, slot):
        xp_copy(slot).wait()
        out_buf[slot, 1 - seq] = xp_in[slot].astype(jnp.float32)
        out_copy(unit, slot).start()

    def turn(at):
        def when_due(behind, run):
            unit = at - behind

            @pl.when(jnp.logical_and(unit >= 0, unit < total))
            def _():
                run(unit, lax.rem(unit, 2))

        when_due(5, stage_six)
        when_due(4, stage_five)
        when_due(3, lambda unit, slot: stage_four(slot))
        when_due(2, lambda unit, slot: stage_three(slot))
        when_due(1, lambda unit, slot: stage_two(slot))

        @pl.when(at < total)
        def _():
            compute(at)
            core_copy(lax.rem(at, 2)).start()

    def finish():
        for unit in (total - 2, total - 1):
            out_copy(unit, unit % 2).wait()

    return prefetch, turn, finish, total + 5


def scatter_scratch(toks, lines):
    bf = jnp.bfloat16
    dma = pltpu.SemaphoreType.DMA

    buf_f32 = pltpu.VMEM((2, PARTS, 64, TILE), jnp.float32)

    def buf(*shape):
        return pltpu.VMEM((2,) + shape, bf)

    return [
        buf(toks, D),
        pltpu.VMEM((toks, FF), bf),
        buf(toks, D),
        buf(toks, TILE),
        dma((4, 2)),
        buf(2, PARTS, lines, 2, 64, TILE),
        buf(PARTS, lines, 2, 64, TILE),
        buf(lines, 2, 64, TILE),
        buf(lines, 2, 64, TILE),
        buf(lines, 2, 64, TILE),
        buf(lines, 2, 64, TILE),
        buf(lines, 2, 64, TILE),
        buf(lines, 2, 64, TILE),
        buf(lines, 64, TILE),
        buf(lines, 64, TILE),
        buf(lines, 64, TILE),
        buf(lines, 2, 64, TILE),
        buf(lines - 1, 2, 64, TILE),
        buf(lines, 64, TILE),
        buf(lines - 1, 64, TILE),
        buf(2, 64, TILE),
        buf(2, 64, TILE),
        buf(64, TILE),
        buf(64, TILE),
        dma((2, 2)),
        dma((2, 2)),
        dma((2, 2)),
        dma((2, 2)),
        dma((2, lines - 1, 2)),
        dma((2, lines - 1, 2)),
        dma((2, 2)),
        dma((2, 2)),
        buf_f32,
        dma((2,)),
    ]


def summary_pieces(lines, refs):
    (
        flat_own,
        mod_own,
        flat_all,
        mod_all,
        core_in,
        core_total,
        x_in,
        x_total,
        y_in,
        y_total,
        z_in,
        pair_sem,
        line_sem,
    ) = refs
    seq = lax.axis_index("seq")
    dp = lax.axis_index("dp")
    core = lax.rem(dp, 2)
    why = lax.rem(dp // 2, 2)
    zed = dp // 4
    core_peer = {"seq": seq, "dp": dp + 1 - 2 * core}
    x_peer = {"seq": 1 - seq, "dp": dp}
    y_peer = {"seq": seq, "dp": dp + 2 - 4 * why}
    places = [lax.rem(zed + ahead, lines) for ahead in range(1, lines)]
    z_peers = [{"seq": seq, "dp": there * 4 + 2 * why + core} for there in places]

    def remote(source, target, sems, peer):
        return pltpu.make_async_remote_copy(
            src_ref=source,
            dst_ref=target,
            send_sem=sems.at[0],
            recv_sem=sems.at[1],
            device_id=peer,
            device_id_type=MESH,
        )

    def same(view, sems, peer):
        return remote(view, view, sems, peer)

    flat_core = remote(flat_own.at[1 - core], core_in, pair_sem.at[0], core_peer)
    flat_x = remote(core_total, x_in, pair_sem.at[1], x_peer)
    flat_y = remote(x_total, y_in, pair_sem.at[2], y_peer)
    flat_z = [
        remote(y_total.at[there], z_in.at[at], line_sem.at[0, at], peer)
        for at, (there, peer) in enumerate(zip(places, z_peers))
    ]
    back_z = [
        same(flat_all.at[core, zed], line_sem.at[1, at], peer) for at, peer in enumerate(z_peers)
    ]
    back_core = same(flat_all.at[core], pair_sem.at[3], core_peer)
    mod_x = remote(mod_own, mod_all.at[zed, why, core, seq], pair_sem.at[4], x_peer)
    mod_z = [
        same(mod_all.at[zed, why, core], line_sem.at[2, at], peer)
        for at, peer in enumerate(z_peers)
    ]
    mod_y = same(mod_all.at[:, why, core], pair_sem.at[5], y_peer)
    mod_core = same(mod_all.at[:, :, core], pair_sem.at[6], core_peer)

    def first():
        mod_all[zed, why, core, seq] = mod_own[...]
        flat_core.start()
        mod_x.start()

    def second():
        flat_core.wait()
        core_total[...] = flat_own[core] + core_in[...]
        flat_x.start()
        mod_x.wait()
        for copy in mod_z:
            copy.start()

    def third():
        flat_x.wait()
        x_total[...] = core_total[...] + x_in[...]
        flat_y.start()
        for copy in mod_z:
            copy.wait()
        mod_y.start()

    def fourth():
        flat_y.wait()
        y_total[...] = x_total[...] + y_in[...]
        for copy in flat_z:
            copy.start()

    def fifth():
        total = y_total[zed]
        for at, copy in enumerate(flat_z):
            copy.wait()
            total = total + z_in[at]
        flat_all[core, zed] = total
        for copy in back_z:
            copy.start()
        mod_y.wait()
        mod_core.start()

    def sixth():
        for copy in back_z:
            copy.wait()
        back_core.start()
        mod_core.wait()

    def seventh():
        back_core.wait()

    return [first, second, third, fourth, fifth, sixth, seventh]


def summary_scratch(lines):
    f32 = jnp.float32
    part = pltpu.VMEM((lines, 8, D), f32)
    return [
        pltpu.VMEM((2, lines, 8, D), f32),
        pltpu.VMEM((32, D), jnp.bfloat16),
        part,
        part,
        part,
        part,
        part,
        part,
        pltpu.VMEM((lines - 1, 8, D), f32),
        pltpu.SemaphoreType.DMA((7, 2)),
        pltpu.SemaphoreType.DMA((3, lines - 1, 2)),
    ]


def whole_backward_kernel(lines, *refs):
    refs = list(refs)

    def take(count):
        taken, refs[:] = tuple(refs[:count]), refs[count:]
        return taken

    (grad_in,) = take(1)
    operands = [take(10), take(10)]
    kept = [take(4), take(4)]
    mod_ref, keep_ref, final_rows, head_rows, misc_row, flat_in = take(6)
    units_out = take(1)
    outs = [take(4), take(4)]
    flat_all, mod_all = take(2)
    back_scratch = take(19)
    d_mod_ref, *d_bias_refs = take(3)
    (grad_sem,) = take(1)
    summary = take(11)
    scatter_refs = tuple(refs)

    dp = lax.axis_index("dp")
    seq = lax.axis_index("seq")
    core = lax.rem(dp, 2)
    why = lax.rem(dp // 2, 2)
    zed = dp // 4
    barrier = pltpu.get_barrier_semaphore()
    peers = [dp + 1 - 2 * core, dp + 2 - 4 * why]
    peers += [lax.rem(zed + ahead, lines) * 4 + 2 * why + core for ahead in range(1, lines)]
    for peer in [{"seq": seq, "dp": peer} for peer in peers] + [{"seq": 1 - seq, "dp": dp}]:
        pl.semaphore_signal(barrier, inc=1, device_id=peer, device_id_type=MESH)

    load = pltpu.make_async_copy(grad_in, back_scratch[0], grad_sem.at[0])
    load.start()
    begins, steps = [], []
    for at, mod_at in ((0, 12), (1, 0)):
        begin, step = backward_pieces(
            operands[at] + (mod_ref, keep_ref),
            outs[at],
            (d_mod_ref, d_bias_refs[at]) + back_scratch,
            mod_at,
        )
        begins.append(begin)
        steps.append(step)
    begins[0]()
    load.wait()

    sources = []
    for at in range(2):
        merged, a_one, a_two, act = kept[at]
        d_down, d_up, d_attn, d_qkv = outs[at]
        sources.append((merged, a_one, a_two, act, d_attn, d_qkv, d_up, d_down))
    prefetch, scatter, scatter_finish, turns = scatter_pieces(
        lines, sources, units_out + scatter_refs
    )
    flat_own, mod_own = summary[:2]
    summary_steps = summary_pieces(
        lines, (flat_own, mod_own, flat_all, mod_all) + summary[2:]
    )

    def put(row, value):
        flat_own[row // (8 * lines), row // 8 % lines, row % 8 : row % 8 + 1, :] = value

    def collect():
        d_patch = back_scratch[0][...].astype(jnp.bfloat16)
        for layer in range(2):
            for row in range(9):
                put(9 * layer + row, d_bias_refs[1 - layer][:, row * D : (row + 1) * D])
        put(18, jnp.sum(d_patch.astype(jnp.float32), axis=0, keepdims=True))
        g_patch = dot_nn(flat_in[...], d_patch)
        for row in range(16):
            put(19 + row, g_patch[row : row + 1, :])
            put(35 + row, head_rows[row : row + 1, :])
        put(51, misc_row[...])
        for row in range(52, 16 * lines):
            put(row, jnp.zeros((1, D), jnp.float32))
        d_mod_ref[24:28, :] = final_rows[...]
        by_image = back_scratch[5]
        for image in range(2):
            for piece in range(16):
                row = 2 * piece + image
                value = d_mod_ref[row : row + 1, :] if piece < 14 else jnp.zeros((1, D), jnp.float32)
                by_image[16 * image + piece : 16 * image + piece + 1, :] = value
        mod_own[...] = by_image[:32, :].astype(jnp.bfloat16)

    def back(at, carry):
        @pl.when(at < BACKWARD_STEPS)
        def _():
            steps[0](at)

        @pl.when(at == BACKWARD_STEPS)
        def _():
            begins[1]()

        @pl.when(jnp.logical_and(at >= BACKWARD_STEPS, at < 2 * BACKWARD_STEPS))
        def _():
            steps[1](at - BACKWARD_STEPS)

        return carry

    lax.fori_loop(0, 2, back, 0)
    prefetch(jnp.int32(0))
    pl.semaphore_wait(barrier, 2 + lines)

    def turn(at, carry):
        @pl.when(at <= 20)
        def _():
            lax.fori_loop(2 + at * 5 // 2, 2 + (at + 1) * 5 // 2, back, 0)

        prefetch(at + 1)
        scatter(at)

        @pl.when(at == 21)
        def _():
            collect()

        for offset, run in enumerate(summary_steps):

            @pl.when(at == 21 + offset)
            def _():
                run()

        return carry

    lax.fori_loop(0, turns, turn, 0)
    scatter_finish()


def whole_backward(
    grad, inputs, saved, weights, mods, keep, final_rows, head_rows, misc_row, flat_in, lines
):
    toks = grad.shape[0]
    vmem = pl.BlockSpec(memory_space=pltpu.VMEM)
    hbm = pl.BlockSpec(memory_space=pl.ANY)
    operands = [grad]
    for at in (1, 0):
        operands += backward_operands(inputs[at], saved[at], weights[at])
    for at in (1, 0):
        a_one, _, merged, _, _, a_two, _, act, _, _ = saved[at]
        operands += [merged, a_one, a_two, act]
    layer_outs = [jax.ShapeDtypeStruct((toks, width), kind) for width, kind in BACKWARD_OUTS]
    outs = pl.pallas_call(
        functools.partial(whole_backward_kernel, lines),
        out_shape=[jax.ShapeDtypeStruct((24, PARTS, 64, TILE), jnp.float32)]
        + layer_outs
        + layer_outs
        + [
            jax.ShapeDtypeStruct((2, lines, 8, D), jnp.float32),
            jax.ShapeDtypeStruct((lines, 2, 2, 2, 32, D), jnp.bfloat16),
        ],
        in_specs=[hbm] * len(operands) + [vmem] * 6,
        out_specs=[hbm] * 9 + [vmem] * 2,
        scratch_shapes=backward_scratch(toks)
        + [
            pltpu.VMEM((32, D), jnp.float32),
            pltpu.VMEM((1, 9 * D), jnp.float32),
            pltpu.VMEM((1, 9 * D), jnp.float32),
            pltpu.SemaphoreType.DMA((1,)),
        ]
        + summary_scratch(lines)
        + scatter_scratch(toks, lines),
        compiler_params=pltpu.CompilerParams(
            collective_id=1, has_side_effects=True, vmem_limit_bytes=61 * 1024 * 1024
        ),
        cost_estimate=pl.CostEstimate(
            flops=104 * toks * D * D,
            bytes_accessed=300 * 1024 * 1024,
            transcendentals=8 * toks * D,
        ),
    )(*operands, mods, keep, final_rows, head_rows, misc_row, flat_in)
    return outs[0], outs[9], outs[10]


def gather_rows(shard):
    return lax.all_gather(shard.astype(jnp.bfloat16), "dp", axis=0, tiled=True)


def kernels_fit():
    dp_parts = lax.axis_size("dp")
    return (
        lax.axis_size("seq") == 2
        and dp_parts % 4 == 0
        and D // dp_parts == 64
        and FF // dp_parts == PARTS * 64
    )


def reduce_rows(partial):
    owned = lax.psum_scatter(
        partial.astype(jnp.bfloat16), "dp", scatter_dimension=0, tiled=True
    )
    return lax.psum(owned, "seq").astype(jnp.float32)


def adamw(weight, gradient, first, second, rate):
    first_new = BETA_ONE * first + (1.0 - BETA_ONE) * gradient
    second_new = BETA_TWO * second + (1.0 - BETA_TWO) * gradient * gradient
    first_hat = first_new / (1.0 - BETA_ONE**STEP)
    second_hat = second_new / (1.0 - BETA_TWO**STEP)
    return (
        weight - rate * (first_hat / (jnp.sqrt(second_hat) + EPSILON) + DECAY * weight),
        first_new,
        second_new,
    )


def unit_adamw_kernel(by_rows, grad_ref, weight_ref, first_ref, second_ref, *outs):
    for part in range(PARTS):
        if by_rows:
            place = (0, slice(part * 64, part * 64 + 64), slice(None))
        else:
            place = (0, slice(None), slice(part * TILE, part * TILE + TILE))
        moved = adamw(
            weight_ref[place], grad_ref[0, part], first_ref[place], second_ref[place], RATE_MATRIX
        )
        for out, value in zip(outs, moved):
            out[place] = value


def unit_adamw(weight, units, first, second, first_unit, by_rows):
    layers, rows, width = weight.shape
    block = (1, rows, TILE) if by_rows else (1, rows, D)
    spec = pl.BlockSpec(block, lambda layer, at: (layer, 0, at))
    per_layer = units.shape[0] // layers
    grad_spec = pl.BlockSpec(
        (1, PARTS, 64, TILE),
        lambda layer, at: ((layers - 1 - layer) * per_layer + first_unit + at, 0, 0, 0),
    )
    return pl.pallas_call(
        functools.partial(unit_adamw_kernel, by_rows),
        out_shape=[jax.ShapeDtypeStruct(weight.shape, jnp.float32)] * 3,
        grid=(layers, width // block[2]),
        in_specs=[grad_spec, spec, spec, spec],
        out_specs=[spec] * 3,
        compiler_params=pltpu.CompilerParams(vmem_limit_bytes=32 * 1024 * 1024),
        cost_estimate=pl.CostEstimate(
            flops=16 * weight.size, bytes_accessed=28 * weight.size, transcendentals=weight.size
        ),
    )(units, weight, first, second)


def body(
    latents,
    noise_target,
    pad_mask,
    labels,
    timesteps,
    embed_rows,
    first_embed,
    second_embed,
    class_table,
    first_table,
    second_table,
    qkv_weight,
    first_qkv,
    second_qkv,
    proj_weight,
    first_proj,
    second_proj,
    up_weight,
    first_up,
    second_up,
    down_weight,
    first_down,
    second_down,
    cond_weight,
    first_cond,
    second_cond,
    head_weight,
    first_head,
    second_head,
    all_biases,
    first_bias,
    second_bias,
):
    seq_parts = lax.axis_size("seq")
    dp_parts = lax.axis_size("dp")
    seq_at = lax.axis_index("seq")
    dp_at = lax.axis_index("dp")
    lines = dp_parts // 4
    group, half_rows, _ = latents.shape
    images = group // seq_parts
    everyone = group * dp_parts
    own_cols = embed_rows.shape[1]
    own_place = dp_at * own_cols
    cond_cols = cond_weight.shape[1]
    pieces = cond_cols // D
    bias_base = 3 * D + cond_cols
    by_kernel = kernels_fit()
    packed = jnp.concatenate(
        [latents, noise_target, pad_mask.astype(jnp.float32)[:, :, None]], axis=2
    )
    shards = [
        weight[at].astype(jnp.bfloat16)
        for at in range(LAYERS)
        for weight in (qkv_weight, proj_weight, up_weight, down_weight)
    ]
    narrow = jnp.concatenate(
        [embed_rows[: PATCH_IN + FREQ].T, head_weight], axis=1
    ).astype(jnp.bfloat16)
    if by_kernel:
        ids = jnp.stack([labels, timesteps])
        parts = jnp.stack([ids // 32, ids % 32]).astype(jnp.bfloat16).reshape(-1, 1)
        parts = jnp.pad(parts, ((0, own_cols - parts.shape[0]), (0, 0)))
        width = narrow.shape[1]
        block = jnp.concatenate(
            [narrow, parts, jnp.zeros((own_cols, 383 - width), jnp.bfloat16)], axis=1
        )
        small = gather_small(block, lines, 4)
        parts = small[:, width].astype(jnp.float32).reshape(dp_parts, own_cols)[:, : 4 * group]
        parts = parts.reshape(dp_parts, 2, 2, group)
        ids = (parts[:, 0] * 32.0 + parts[:, 1]).astype(jnp.int32)
        ids = ids.transpose(1, 0, 2).reshape(2, everyone)
        theirs = lax.dynamic_slice(
            packed, ((1 - seq_at) * images, 0, 0), (images,) + packed.shape[1:]
        )
        mine = lax.dynamic_slice(packed, (seq_at * images, 0, 0), (images,) + packed.shape[1:])
        came = lax.ppermute(theirs, "seq", [(0, 1), (1, 0)])
        packed = jnp.concatenate(
            [jnp.where(seq_at == 0, mine, came), jnp.where(seq_at == 0, came, mine)], axis=1
        )
    else:
        small = lax.all_gather(narrow, "dp", axis=0, tiled=True)
        ids = lax.all_gather(jnp.stack([labels, timesteps]), "dp", axis=1, tiled=True)
        packed = lax.all_to_all(packed, "seq", split_axis=0, concat_axis=1, tiled=True)
    tok_rows = packed.shape[1]
    toks = images * tok_rows
    latents, noise_target, keep_rows = (
        packed[:, :, :PATCH_IN],
        packed[:, :, PATCH_IN : 2 * PATCH_IN],
        packed[:, :, 2 * PATCH_IN],
    )
    patch_part = small[:, :PATCH_IN]
    freq_part = small[:, PATCH_IN : PATCH_IN + FREQ]
    head_full = small[:, PATCH_IN + FREQ : PATCH_IN + FREQ + OUT_CH]
    time_own = embed_rows[PATCH_IN + FREQ :].astype(jnp.bfloat16)
    cond_own = cond_weight.astype(jnp.bfloat16)

    features = time_features(ids[1], FREQ).astype(jnp.bfloat16)
    time_pre = dot_nt(features, freq_part) + all_biases[D : 2 * D]
    time_hidden = jax.nn.silu(time_pre).astype(jnp.bfloat16)
    second_bias_own = lax.dynamic_slice(all_biases, (2 * D + own_place,), (own_cols,))
    onehot = (ids[0][:, None] == jnp.arange(NCLASS, dtype=jnp.int32)[None, :]).astype(jnp.float32)
    condition = (
        matdot(time_hidden, time_own)
        + second_bias_own
        + matdot(onehot.astype(jnp.bfloat16), class_table.astype(jnp.bfloat16))
    )
    cond_act = jax.nn.silu(condition).astype(jnp.bfloat16)
    plane_act = lax.dynamic_index_in_dim(
        cond_act.reshape(dp_parts, seq_parts, images, own_cols), seq_at, 1, keepdims=False
    ).reshape(dp_parts * images, own_cols)
    partial = matdot(plane_act, cond_own)
    mod_bias = jnp.repeat(all_biases[3 * D : bias_base].reshape(pieces, D), images, axis=0)

    position = position_table(jnp.arange(tok_rows, dtype=jnp.int32), D, GRID)
    flat_in = latents.astype(jnp.bfloat16).reshape(toks, PATCH_IN)
    stream = (dot_nt(flat_in, patch_part) + all_biases[:D]).reshape(
        images, tok_rows, D
    ) + position[None]
    stream = stream.reshape(toks, D)
    layer_bias = [
        all_biases[bias_base + at * 9 * D : bias_base + (at + 1) * 9 * D].reshape(1, 9 * D)
        for at in range(LAYERS)
    ]
    if by_kernel:
        partial = partial.astype(jnp.bfloat16).reshape(dp_parts * images, pieces, D)
        partial = jnp.pad(partial, ((0, 0), (0, 16 - pieces), (0, 0)))
        weights_kept, saved_kept, mods = whole_forward(
            shards,
            partial.reshape(lines, 2, 2, 16 * images, D),
            mod_bias,
            stream,
            layer_bias,
            keep_rows,
            lines,
        )
    else:
        partial = partial.reshape(dp_parts, images, pieces, D).transpose(0, 2, 1, 3)
        partial = partial.reshape(dp_parts, pieces * images, D)
        mods = mod_bias + lax.psum_scatter(
            partial, "dp", scatter_dimension=0, tiled=True
        ).reshape(pieces * images, D)
        weights_kept = [
            [gather_rows(shard) for shard in shards[4 * at : 4 * at + 4]] for at in range(LAYERS)
        ]
        saved_kept = []
        upper = stream
        for at in range(LAYERS):
            saved_kept.append(
                forward_layer(
                    upper, mods, 6 * images * at, layer_bias[at], keep_rows, weights_kept[at]
                )
            )
            upper = saved_kept[at][-1]
    inputs_kept = [stream] + [saved[-1] for saved in saved_kept]
    final, time_own = lax.optimization_barrier((inputs_kept[-1], time_own))
    time_full = lax.all_gather(time_own, "dp", axis=1, tiled=True)
    final_at = 6 * LAYERS * images
    final_shift = mods[final_at : final_at + images]
    final_scale = mods[final_at + images :]
    moved, final_back = jax.vjp(
        modulate, final.reshape(images, tok_rows, D), final_shift, final_scale
    )
    a_final = moved.astype(jnp.bfloat16).reshape(toks, D)
    head_out = matdot(a_final, head_full) + all_biases[NBIAS - OUT_CH :]
    split_out = head_out.reshape(images, tok_rows, 4, 2, OUT_CH // 8)
    predicted = split_out[:, :, :, 0, :].reshape(images, tok_rows, PATCH_IN)
    errors = predicted - noise_target
    loss_part = jnp.sum(keep_rows[:, :, None] * errors * errors)
    count_part = PATCH_IN * jnp.sum(keep_rows)
    d_pred = (2.0 * keep_rows[:, :, None] * errors).reshape(images, tok_rows, 4, 1, OUT_CH // 8)
    d_head = (
        jnp.concatenate([d_pred, jnp.zeros_like(d_pred)], axis=3)
        .reshape(toks, OUT_CH)
        .astype(jnp.bfloat16)
    )
    d_a_final = dot_nt(d_head, head_full).reshape(images, tok_rows, D)
    d_stream, d_final_shift, d_final_scale = final_back(d_a_final)
    d_stream = d_stream.reshape(toks, D)
    d_bias_head = column_sum(d_head)
    if by_kernel:
        d_noise = d_pred.astype(jnp.bfloat16).reshape(toks, PATCH_IN)
        misc_row = jnp.concatenate([d_bias_head, loss_part[None], count_part[None]])
        misc_row = jnp.pad(misc_row, (0, D - misc_row.shape[0])).reshape(1, D)
        units, flat, mod_all = whole_backward(
            d_stream,
            inputs_kept,
            saved_kept,
            weights_kept,
            mods,
            keep_rows,
            jnp.concatenate([d_final_shift, d_final_scale], axis=0),
            matdot(d_noise.T, a_final),
            misc_row,
            flat_in.T,
            lines,
        )
        d_modulation = mod_all.reshape(everyone, 16 * D)[:, :cond_cols]
        flat = flat.reshape(64, D)
        d_bias_mod = column_sum(d_modulation)
        d_bias_patch = flat[18]
        d_bias_layers = flat[:18].reshape(-1)
        d_bias_head, loss_sum, loss_count = (
            flat[51, :OUT_CH],
            flat[51, OUT_CH],
            flat[51, OUT_CH + 1],
        )
        own_flat = lax.dynamic_slice(flat, (0, own_place), (64, own_cols))
        s_patch = own_flat[19:35]
        s_head = own_flat[35:51].T.reshape(own_cols, 4, 1, OUT_CH // 8)
        s_head = jnp.concatenate([s_head, jnp.zeros_like(s_head)], axis=2)
        s_head = s_head.reshape(own_cols, OUT_CH)
    else:
        layer_sums = [None] * LAYERS
        layer_bias_grads = [None] * LAYERS
        modul_grads = [None] * LAYERS
        for at in reversed(range(LAYERS)):
            d_stream, d_mod, factors, d_bias = backward_layer(
                d_stream,
                inputs_kept[at],
                saved_kept[at],
                mods,
                6 * images * at,
                keep_rows,
                weights_kept[at],
            )
            merged, a_one, a_two, active, d_attn, d_qkv, d_up, d_down = factors
            layer_sums[at] = (
                reduce_rows(matdot(a_one.T, d_qkv)),
                reduce_rows(matdot(merged.T, d_attn)),
                reduce_rows(matdot(a_two.T, d_up)),
                reduce_rows(matdot(active.T, d_down)),
            )
            modul_grads[at] = d_mod.reshape(6, images, D).transpose(1, 0, 2).reshape(images, 6 * D)
            layer_bias_grads[at] = d_bias.reshape(-1)
        d_mod_own = jnp.concatenate(
            modul_grads + [d_final_shift, d_final_scale], axis=1
        ).astype(jnp.bfloat16)
        d_patch = d_stream.astype(jnp.bfloat16)
        d_modulation = lax.all_gather(d_mod_own, ("dp", "seq"), axis=0, tiled=True)
        (
            d_bias_patch,
            d_bias_mod,
            d_bias_layers,
            d_bias_head,
            loss_sum,
            loss_count,
            g_patch,
            g_head,
        ) = lax.psum(
            (
                column_sum(d_patch),
                column_sum(d_mod_own),
                jnp.concatenate(layer_bias_grads),
                d_bias_head,
                loss_part,
                count_part,
                matdot(flat_in.T, d_patch),
                matdot(a_final.T, d_head),
            ),
            ("seq", "dp"),
        )
        s_patch = lax.dynamic_slice(g_patch, (0, own_place), (PATCH_IN, own_cols))
        s_head = lax.dynamic_slice(g_head, (own_place, 0), (own_cols, OUT_CH))
    d_cond_act = dot_nt(d_modulation, cond_own)
    _, silu_back = jax.vjp(jax.nn.silu, condition)
    d_condition = silu_back(d_cond_act)[0]
    d_time_own = d_condition.astype(jnp.bfloat16)
    if by_kernel:
        d_time = gather_small(
            jnp.pad(d_time_own.T, ((0, 0), (0, everyone))), lines, 5
        )
        d_time = d_time[:, :everyone].T
    else:
        d_time = lax.all_gather(d_time_own, "dp", axis=1, tiled=True)
    d_time_hidden = dot_nt(d_time, time_full)
    _, time_back = jax.vjp(jax.nn.silu, time_pre)
    d_time_pre = time_back(d_time_hidden)[0].astype(jnp.bfloat16)
    s_cond = matdot(cond_act.T, d_modulation)
    s_table = jnp.dot(onehot.T, d_condition, precision=lax.Precision.HIGHEST)
    g_time = matdot(time_hidden.T, d_time_own)
    g_freq = matdot(
        features.T, lax.dynamic_slice(d_time_pre, (0, own_place), (everyone, own_cols))
    )
    bias_grad = jnp.concatenate(
        [
            d_bias_patch,
            column_sum(d_time_pre),
            column_sum(d_time),
            d_bias_mod,
            d_bias_layers,
            d_bias_head,
        ]
    )
    s_embed = jnp.concatenate([s_patch, g_freq, g_time], axis=0)
    new_embed, new_first_embed, new_second_embed = adamw(
        embed_rows, s_embed, first_embed, second_embed, RATE_MATRIX
    )
    new_table, new_first_table, new_second_table = adamw(
        class_table, s_table, first_table, second_table, RATE_TABLE
    )
    if by_kernel:
        new_qkv, new_first_qkv, new_second_qkv = unit_adamw(
            qkv_weight, units, first_qkv, second_qkv, 9, False
        )
        new_proj, new_first_proj, new_second_proj = unit_adamw(
            proj_weight, units, first_proj, second_proj, 8, False
        )
        new_up, new_first_up, new_second_up = unit_adamw(
            up_weight, units, first_up, second_up, 4, False
        )
        new_down, new_first_down, new_second_down = unit_adamw(
            down_weight, units, first_down, second_down, 0, True
        )
    else:
        s_qkv = jnp.stack([layer_sums[at][0] for at in range(LAYERS)])
        s_proj = jnp.stack([layer_sums[at][1] for at in range(LAYERS)])
        s_up = jnp.stack([layer_sums[at][2] for at in range(LAYERS)])
        s_down = jnp.stack([layer_sums[at][3] for at in range(LAYERS)])
        new_qkv, new_first_qkv, new_second_qkv = adamw(
            qkv_weight, s_qkv, first_qkv, second_qkv, RATE_MATRIX
        )
        new_proj, new_first_proj, new_second_proj = adamw(
            proj_weight, s_proj, first_proj, second_proj, RATE_MATRIX
        )
        new_up, new_first_up, new_second_up = adamw(up_weight, s_up, first_up, second_up, RATE_MATRIX)
        new_down, new_first_down, new_second_down = adamw(
            down_weight, s_down, first_down, second_down, RATE_MATRIX
        )
    new_cond, new_first_cond, new_second_cond = adamw(
        cond_weight, s_cond, first_cond, second_cond, RATE_MATRIX
    )
    new_head, new_first_head, new_second_head = adamw(
        head_weight, s_head, first_head, second_head, RATE_MATRIX
    )
    new_bias, new_first_bias, new_second_bias = adamw(
        all_biases, bias_grad, first_bias, second_bias, RATE_BIAS
    )
    return (
        loss_sum,
        loss_count,
        new_embed,
        new_first_embed,
        new_second_embed,
        new_table,
        new_first_table,
        new_second_table,
        new_qkv,
        new_first_qkv,
        new_second_qkv,
        new_proj,
        new_first_proj,
        new_second_proj,
        new_up,
        new_first_up,
        new_second_up,
        new_down,
        new_first_down,
        new_second_down,
        new_cond,
        new_first_cond,
        new_second_cond,
        new_head,
        new_first_head,
        new_second_head,
        new_bias,
        new_first_bias,
        new_second_bias,
    )


def solution(mesh):
    placed = (
        P("dp", "seq", None),
        P("dp", "seq", None),
        P("dp", "seq"),
        P("dp"),
        P("dp"),
        P(None, "dp"),
        P(None, "dp"),
        P(None, "dp"),
        P(None, "dp"),
        P(None, "dp"),
        P(None, "dp"),
        P(None, "dp", None),
        P(None, "dp", None),
        P(None, "dp", None),
        P(None, "dp", None),
        P(None, "dp", None),
        P(None, "dp", None),
        P(None, "dp", None),
        P(None, "dp", None),
        P(None, "dp", None),
        P(None, "dp", None),
        P(None, "dp", None),
        P(None, "dp", None),
        P("dp", None),
        P("dp", None),
        P("dp", None),
        P("dp", None),
        P("dp", None),
        P("dp", None),
        P(),
        P(),
        P(),
    )
    return jax.shard_map(
        body,
        mesh=mesh,
        in_specs=placed,
        out_specs=(
            P(),
            P(),
            P(None, "dp"),
            P(None, "dp"),
            P(None, "dp"),
            P(None, "dp"),
            P(None, "dp"),
            P(None, "dp"),
            P(None, "dp", None),
            P(None, "dp", None),
            P(None, "dp", None),
            P(None, "dp", None),
            P(None, "dp", None),
            P(None, "dp", None),
            P(None, "dp", None),
            P(None, "dp", None),
            P(None, "dp", None),
            P(None, "dp", None),
            P(None, "dp", None),
            P(None, "dp", None),
            P("dp", None),
            P("dp", None),
            P("dp", None),
            P("dp", None),
            P("dp", None),
            P("dp", None),
            P(),
            P(),
            P(),
        ),
        check_vma=False,
    )
```
